128 devices in a mesh: row: 8 (over x, core), col: 16 (over z, y).
Axes of the slice: x: 4, y: 4, z: 4, core: 2. Of those that a mesh axis runs over, the one named last changes fastest.
Arguments:
- amplitudes: bfloat16 [1792, 23040], P('col', 'row'), may hold values from -6 to 6
- integrals: bfloat16 [23040, 23040], P('row', 'col'), may hold values from -0.026352314 to 0.026352314, as said below
- row_gap: float32 [1792], replicated, may hold values from 0.25 to 1
- col_gap: float32 [23040], replicated, may hold values from 0.25 to 1
Outputs:
- updated: bfloat16 [1792, 23040], P(None, ('row', 'col'))
The draws below stay inside these ranges and needn't reach their ends.
Inputs may be any that keep to these rules, and one draw needn't show every extreme that they name: integrals is symmetric: entry (p, q) equals entry (q, p).
All inputs are finite; a program needn't handle non-finite values.
Results may differ from the reference program's by a relative error of at most 0.022.
Values may be sent and summed in bfloat16 or wider, within the bound.
A program may use at most 64 MiB of HBM per device.

```python
import math
import jax
import jax.numpy as jnp
from jax import lax

P_SIZE = 23040
ROWS = 1792
N_ROW = 8
N_COL = 16


def draw_integrals(key, part):
    key = jax.random.fold_in(key, 11)
    spread_scale = P_SIZE ** (-0.5)
    raw_values = jnp.clip(jax.random.normal(key, (P_SIZE, P_SIZE), jnp.float32), -3.98, 3.98) * spread_scale
    first_index = lax.broadcasted_iota(jnp.int32, (P_SIZE, P_SIZE), 0)
    second_index = lax.broadcasted_iota(jnp.int32, (P_SIZE, P_SIZE), 1)
    return jnp.where(first_index <= second_index, raw_values, raw_values.T).astype(jnp.bfloat16)


def steps_of(stream_key, dims, split, least, largest):
    factor_of, own = 1.0, jax.random.fold_in(stream_key, 6)
    for position, blocks in split:
        heights = jnp.exp(jax.random.uniform(jax.random.fold_in(own, position), (blocks,), jnp.float32, least / len(split), largest / len(split)))
        factor_of = factor_of * jnp.repeat(heights, dims[position] // blocks).reshape([-1 if axis == position else 1 for axis in range(len(dims))])
    return factor_of


def centred(rng, extent, spread, most, shards=(), kind=jnp.bfloat16):
    entries = jax.random.normal(rng, extent, jnp.float32) * spread
    if len(shards) > 0:
        entries = steps_of(rng, extent, shards, -0.22, 0.18) * entries
    return jnp.clip(entries, min=-most, max=most).astype(kind)


def setup_inputs(seed: int = 0) -> dict:
    arg_keys = jax.random.split(jax.random.key(seed), 5)
    amplitudes = centred(arg_keys[0], (ROWS, P_SIZE), 1.0, 6.0, ((0, 16), (1, 8)))
    integrals = draw_integrals(jax.random.fold_in(arg_keys[4], 71), 0)
    row_gap = jnp.clip(jnp.exp(jax.random.uniform(arg_keys[2], (ROWS,), jnp.float32, math.log(0.25), math.log(1.0))), 0.25, 1.0)
    col_gap = jnp.clip(jnp.exp(jax.random.uniform(arg_keys[3], (P_SIZE,), jnp.float32, math.log(0.25), math.log(1.0))), 0.25, 1.0)
    return {"amplitudes": amplitudes, "integrals": integrals, "row_gap": row_gap, "col_gap": col_gap}


def split_product(left_matrix, right_matrix, pieces_count):
    span_width = left_matrix.shape[1] // pieces_count

    def add_range(carried, range_index):
        left_part = lax.dynamic_slice_in_dim(left_matrix, (range_index * span_width).astype(jnp.int32), span_width, 1)
        right_part = lax.dynamic_slice_in_dim(right_matrix, (range_index * span_width).astype(jnp.int32), span_width, 0)
        summed = jnp.dot(left_part, right_part, preferred_element_type=jnp.float32)
        rounded = lax.optimization_barrier(summed.astype(jnp.bfloat16))
        return carried + rounded.astype(jnp.float32), None

    initial = jnp.zeros((left_matrix.shape[0], right_matrix.shape[1]), jnp.float32)
    result, _ = lax.scan(add_range, initial, jnp.arange(pieces_count, dtype=jnp.int32))
    return result


def reference(amplitudes, integrals, row_gap, col_gap):
    denominator = row_gap[:, None] + col_gap[None, :]
    cycle_one = split_product(amplitudes, integrals, N_ROW)
    section_one = (cycle_one / denominator).astype(jnp.bfloat16)
    cycle_two = split_product(section_one, integrals, N_COL)
    return (cycle_two / denominator).astype(jnp.bfloat16)
```

```python
import functools

import jax
import jax.numpy as jnp
from jax import lax
from jax.experimental import pallas as pl
from jax.experimental.pallas import tpu as pltpu
from jax.sharding import PartitionSpec as P

MESH = pl.DeviceIdType.MESH
F32 = jnp.float32
BF16 = jnp.bfloat16

BLOCK = 16
SPLIT = 1408
WINDOW = 192
STRIDE = 176
X_KIND = 14
RS_KIND = 22
KINDS = 38

PLAN = (
    ("a0", 0),
    ("r1", 3),
    ("b1", 2),
    ("a1", 0),
    ("r3", 4),
    ("b2", 2),
    ("a3", 1),
    ("r2", 3),
    ("b3", 2),
    ("a2", 0),
    ("r4", 4),
    ("m2", 2),
    ("m1", 1),
    ("sw", 5),
)


def kernel(
    a_ref, v_hbm, dn_ref, o_ref,
    v, ap, aq, c1, cx, xr, sg, w, ro1, rn1, ro2, rn2, lsem, send, recv,
):
    chunks = ap.shape[0]
    depth, width = v.shape
    group = depth // 4
    row, col = lax.axis_index("row"), lax.axis_index("col")
    x, core = row // 2, row % 2
    z, y = col // 4, col % 4
    half = core * 128
    other = 128 - half
    mine = half + x * 32

    def device(dx=0, dcore=0, dz=0, dy=0):
        return (
            ((x + dx + 4) % 4) * 2 + (core + dcore) % 2,
            ((z + dz + 4) % 4) * 4 + (y + dy + 4) % 4,
        )

    def along(axis, step):
        return device(dz=step) if axis == "z" else device(dy=step)

    place = {"z": z, "y": y}
    gather = ((ap, "y", "z"), (aq, "z", "y"))
    scatter = (("z", "y"), ("y", "z"))

    def copy(c, kind, src, dst, to):
        return pltpu.make_async_remote_copy(
            src_ref=src, dst_ref=dst, send_sem=send.at[c, kind], recv_sem=recv.at[c, kind],
            device_id=to, device_id_type=MESH,
        )

    def arrived(c, kind, dst):
        copy(c, kind, dst, dst, device(dcore=1)).wait_recv()

    def sent(c, kind, src):
        copy(c, kind, src, src, device(dcore=1)).wait_send()

    def block(s, c, step):
        buf, first, second = gather[s]
        f = (place[first] + step + 4) % 4
        return buf.at[c, z, f] if first == "y" else buf.at[c, f, y]

    def line(s, c, step, start=0, size=4):
        buf, first, second = gather[s]
        g = (place[second] + step + 4) % 4
        return buf.at[c, g, pl.ds(start, size)] if first == "y" else buf.at[c, pl.ds(start, size), g]

    def turn(c):
        return 1 - 2 * (c % 2)

    def a_sends(c, s):
        d = turn(c)
        return (
            (block(s, c, 0), along(gather[s][1], 1)),
            (block(s, c, 0), along(gather[s][1], -1)),
            (block(s, c, -d), along(gather[s][1], d)),
            (line(s, c, 0), along(gather[s][2], 1)),
            (line(s, c, 0), along(gather[s][2], -1)),
            (line(s, c, -1, 0, 2), along(gather[s][2], 1)),
            (line(s, c, 1, 2, 2), along(gather[s][2], -1)),
        )

    def a_lands(c, s):
        return (
            block(s, c, -1), block(s, c, 1), block(s, c, 2),
            line(s, c, -1), line(s, c, 1), line(s, c, 2, 0, 2), line(s, c, 2, 2, 2),
        )

    def a_start(c, s, k):
        src, to = a_sends(c, s)[k]
        copy(c, s * 7 + k, src, src, to).start()

    def a_wait(c, s, k):
        arrived(c, s * 7 + k, a_lands(c, s)[k])

    def a0(c):
        for s in range(2):
            a_start(c, s, 0)
            a_start(c, s, 1)

    def a1(c):
        def forward(k):
            for s in range(2):
                a_wait(c, s, k)
                a_start(c, s, 2)

        pl.when(c % 2 == 0)(lambda: forward(0))
        pl.when(c % 2 == 1)(lambda: forward(1))

    def a2(c):
        pl.when(c % 2 == 0)(lambda: [a_wait(c, s, 1) for s in range(2)] and None)
        pl.when(c % 2 == 1)(lambda: [a_wait(c, s, 0) for s in range(2)] and None)
        for s in range(2):
            a_wait(c, s, 2)
            a_start(c, s, 3)
            a_start(c, s, 4)

    def a3(c):
        for s in range(2):
            a_wait(c, s, 3)
            a_start(c, s, 5)
            a_wait(c, s, 4)
            a_start(c, s, 6)

    def m1(c):
        @pl.when(c == 0)
        def _():
            pltpu.make_async_copy(v_hbm, v, lsem).wait()

        for s in range(2):
            a_wait(c, s, 5)
            a_wait(c, s, 6)
        left = ap[c].reshape(16 * BLOCK, SPLIT)
        right = aq[c].reshape(16 * BLOCK, depth - SPLIT)
        for lo in range(0, width, 512):
            hi = min(lo + 512, width)
            part = jnp.dot(left, v[:SPLIT, lo:hi], preferred_element_type=F32)
            part = part + jnp.dot(right, v[SPLIT:, lo:hi], preferred_element_type=F32)
            c1[c, :, lo:hi] = part.astype(BF16)
        copy(c, X_KIND, c1.at[c, pl.ds(other, 128)], cx.at[c], device(dcore=1)).start()

    def b1(c):
        arrived(c, X_KIND, cx.at[c])
        rows = pl.ds(half, 128)
        c1[c, rows, :] = (c1[c, rows, :].astype(F32) + cx[c].astype(F32)).astype(BF16)
        for k in (2, 1, 3):
            src = c1.at[c, pl.ds(half + ((x + k) % 4) * 32, 32)]
            copy(c, X_KIND + k, src, xr.at[c, k - 1], device(dx=k)).start()

    def b2(c):
        for k in (1, 2, 3):
            arrived(c, X_KIND + k, xr.at[c, k - 1])
        rows = pl.ds(mine, 32)
        total = c1[c, rows, :].astype(F32)
        for k in range(3):
            total = total + xr[c, k].astype(F32)
        sg[c, rows, :] = (total / dn_ref[c]).astype(BF16)
        src = sg.at[c, rows]
        for k in (2, 1, 3):
            copy(c, X_KIND + 3 + k, src, src, device(dx=k)).start()

    def b3(c):
        for k in (1, 2, 3):
            arrived(c, X_KIND + 3 + k, sg.at[c, pl.ds(half + ((x + 4 - k) % 4) * 32, 32)])
        src = sg.at[c, pl.ds(half, 128)]
        copy(c, X_KIND + 7, src, src, device(dcore=1)).start()

    def r_moves(c, s):
        first, second = scatter[s]
        f, g = place[first], place[second]
        own = w.at[s, c, f]
        far, far2 = (f + 2) % 4, (g + 2) % 4
        h = WINDOW // 2
        return (
            (w.at[s, c, far, pl.ds(0, 2)], ro1.at[s, c, pl.ds(0, 2)], along(first, 1)),
            (w.at[s, c, far, pl.ds(2, 2)], ro1.at[s, c, pl.ds(2, 2)], along(first, -1)),
            (w.at[s, c, (f + 1) % 4], rn1.at[s, c, 0], along(first, 1)),
            (w.at[s, c, (f + 3) % 4], rn1.at[s, c, 1], along(first, -1)),
            (own.at[far2, pl.ds(0, h)], ro2.at[s, c, pl.ds(0, h)], along(second, 1)),
            (own.at[far2, pl.ds(h, h)], ro2.at[s, c, pl.ds(h, h)], along(second, -1)),
            (own.at[(g + 1) % 4], rn2.at[s, c, 0], along(second, 1)),
            (own.at[(g + 3) % 4], rn2.at[s, c, 1], along(second, -1)),
        )

    def r_start(c, s, k):
        src, dst, to = r_moves(c, s)[k]
        copy(c, RS_KIND + s * 8 + k, src, dst, to).start()

    def r_wait(c, s, k):
        arrived(c, RS_KIND + s * 8 + k, r_moves(c, s)[k][1])

    def m2(c):
        arrived(c, X_KIND + 7, sg.at[c, pl.ds(other, 128)])

        def rows_of(q, carry):
            part = lax.dot_general(
                v[pl.ds(pl.multiple_of(q * group, 16), group), :], sg[c], (((1,), (1,)), ((), ())),
                preferred_element_type=F32,
            ).astype(BF16)
            for p in range(4):
                piece = part[p * STRIDE : p * STRIDE + WINDOW]
                w[0, c, q, p] = piece[:, :128]
                w[1, c, p, q] = piece[:, 128:]
            return carry

        lax.fori_loop(0, 4, rows_of, 0)
        for s in range(2):
            r_start(c, s, 0)
            r_start(c, s, 1)

    def r1(c):
        for s in range(2):
            f = place[scatter[s][0]]
            up, down = (f + 1) % 4, (f + 3) % 4
            r_wait(c, s, 0)
            w[s, c, up, 0:2] = (w[s, c, up, 0:2].astype(F32) + ro1[s, c, 0:2].astype(F32)).astype(BF16)
            r_start(c, s, 2)
            r_wait(c, s, 1)
            w[s, c, down, 2:4] = (w[s, c, down, 2:4].astype(F32) + ro1[s, c, 2:4].astype(F32)).astype(BF16)
            r_start(c, s, 3)

    def r2(c):
        for s in range(2):
            f = place[scatter[s][0]]
            r_wait(c, s, 2)
            r_wait(c, s, 3)
            total = w[s, c, f].astype(F32) + rn1[s, c, 0].astype(F32) + rn1[s, c, 1].astype(F32)
            w[s, c, f] = total.astype(BF16)
            r_start(c, s, 4)
            r_start(c, s, 5)

    def r3(c):
        h = WINDOW // 2
        for s in range(2):
            f, g = place[scatter[s][0]], place[scatter[s][1]]
            up, down = (g + 1) % 4, (g + 3) % 4
            r_wait(c, s, 4)
            w[s, c, f, up, :h] = (w[s, c, f, up, :h].astype(F32) + ro2[s, c, :h].astype(F32)).astype(BF16)
            r_start(c, s, 6)
            r_wait(c, s, 5)
            w[s, c, f, down, h:] = (w[s, c, f, down, h:].astype(F32) + ro2[s, c, h:].astype(F32)).astype(BF16)
            r_start(c, s, 7)

    def r4(c):
        sums = []
        for s in range(2):
            f, g = place[scatter[s][0]], place[scatter[s][1]]
            r_wait(c, s, 6)
            r_wait(c, s, 7)
            sums.append(w[s, c, f, g].astype(F32) + rn2[s, c, 0].astype(F32) + rn2[s, c, 1].astype(F32))
        total = jnp.concatenate(sums, axis=1)
        total = jnp.concatenate([total, jnp.zeros((256 - WINDOW, 256), F32)], axis=0)
        total = pltpu.roll(total, (256 - 4 * y) % 256, 0)
        flat = total.T[:, : o_ref.shape[-1]]
        o_ref[:, c] = flat.reshape(16, BLOCK, o_ref.shape[-1])

    def sw(c):
        for s in range(2):
            for k, move in enumerate(a_sends(c, s)):
                sent(c, s * 7 + k, move[0])
            for k, move in enumerate(r_moves(c, s)):
                sent(c, RS_KIND + s * 8 + k, move[0])
        sent(c, X_KIND, c1.at[c, pl.ds(other, 128)])
        for k in (1, 2, 3):
            sent(c, X_KIND + k, c1.at[c, pl.ds(half + ((x + k) % 4) * 32, 32)])
            sent(c, X_KIND + 3 + k, sg.at[c, pl.ds(mine, 32)])
        sent(c, X_KIND + 7, sg.at[c, pl.ds(half, 128)])

    pltpu.make_async_copy(v_hbm, v, lsem).start()
    for c in range(chunks):
        ap[c, z, y] = a_ref[c * BLOCK : (c + 1) * BLOCK, :SPLIT]
        aq[c, z, y] = a_ref[c * BLOCK : (c + 1) * BLOCK, SPLIT:]

    peers = [device(dy=1), device(dy=-1), device(dz=1), device(dz=-1), device(dcore=1)]
    peers += [device(dx=k) for k in (1, 2, 3)]
    barrier = pltpu.get_barrier_semaphore()
    for peer in peers:
        pl.semaphore_signal(barrier, inc=1, device_id=peer, device_id_type=MESH)
    pl.semaphore_wait(barrier, len(peers))

    ops = dict(a0=a0, a1=a1, a2=a2, a3=a3, m1=m1, b1=b1, b2=b2, b3=b3, m2=m2, r1=r1, r2=r2, r3=r3, r4=r4, sw=sw)

    def step(t, carry):
        for name, late in PLAN:
            c = t - late
            pl.when(jnp.logical_and(c >= 0, c < chunks))(functools.partial(ops[name], c))
        return carry

    lax.fori_loop(0, chunks + max(late for _, late in PLAN), step, 0)


def on_device(amplitudes, integrals, row_gap, col_gap):
    rows, depth = amplitudes.shape
    width = integrals.shape[1]
    chunks = rows // BLOCK
    final = depth // 16
    row, col = lax.axis_index("row"), lax.axis_index("col")
    gaps = row_gap.reshape(16, chunks, BLOCK)
    near = lax.dynamic_slice_in_dim(gaps, (row % 2) * 8 + (row // 2) * 2, 2, 0)
    near = near.transpose(1, 0, 2).reshape(chunks, 2 * BLOCK, 1)
    denominators = near + lax.dynamic_slice_in_dim(col_gap, col * width, width)

    vm = pl.BlockSpec(memory_space=pltpu.VMEM)
    cycle_two = pl.pallas_call(
        kernel,
        out_shape=jax.ShapeDtypeStruct((16, chunks, BLOCK, final), F32),
        in_specs=[vm, pl.BlockSpec(memory_space=pl.ANY), vm],
        out_specs=vm,
        scratch_shapes=[
            pltpu.VMEM((depth, width), BF16),
            pltpu.VMEM((chunks, 4, 4, BLOCK, SPLIT), BF16),
            pltpu.VMEM((chunks, 4, 4, BLOCK, depth - SPLIT), BF16),
            pltpu.VMEM((chunks, 256, width), BF16),
            pltpu.VMEM((chunks, 128, width), BF16),
            pltpu.VMEM((chunks, 3, 32, width), BF16),
            pltpu.VMEM((chunks, 256, width), BF16),
            pltpu.VMEM((2, chunks, 4, 4, WINDOW, 128), BF16),
            pltpu.VMEM((2, chunks, 4, WINDOW, 128), BF16),
            pltpu.VMEM((2, chunks, 2, 4, WINDOW, 128), BF16),
            pltpu.VMEM((2, chunks, WINDOW, 128), BF16),
            pltpu.VMEM((2, chunks, 2, WINDOW, 128), BF16),
            pltpu.SemaphoreType.DMA,
            pltpu.SemaphoreType.DMA((chunks, KINDS)),
            pltpu.SemaphoreType.DMA((chunks, KINDS)),
        ],
        compiler_params=pltpu.CompilerParams(
            collective_id=0, has_side_effects=True, vmem_limit_bytes=62 * 1024 * 1024
        ),
        cost_estimate=pl.CostEstimate(
            flops=4 * 16 * rows * depth * width, bytes_accessed=2 * depth * width, transcendentals=0
        ),
    )(amplitudes, integrals, denominators)
    start = (row * 16 + col) * final
    here = lax.dynamic_slice_in_dim(col_gap, start, final)
    cycle_two = cycle_two.reshape(16 * rows, final)
    return (cycle_two / (row_gap[:, None] + here[None, :])).astype(BF16)


def solution(mesh):
    return jax.shard_map(
        on_device,
        mesh=mesh,
        in_specs=(P("col", "row"), P("row", "col"), P(), P()),
        out_specs=P(None, ("row", "col")),
        check_vma=False,
    )
```

```python
import functools

import jax
import jax.numpy as jnp
from jax import lax
from jax.experimental import pallas as pl
from jax.experimental.pallas import tpu as pltpu
from jax.sharding import PartitionSpec as P

MESH = pl.DeviceIdType.MESH
F32 = jnp.float32
BF16 = jnp.bfloat16

BLOCK = 16
SPLIT = 1408
WINDOW = 192
STRIDE = 176
TILE = 128
X_KIND = 14
RS_KIND = 22
KINDS = 38

PLAN = (
    ("r2", 11),
    ("r3", 12),
    ("r4", 14),
    ("sw", 14),
    ("r1", 9),
    ("m2", 8),
    ("b2", 6),
    ("a2", 2),
    ("a1", 1),
    ("b3", 7),
    ("a0", 0),
    ("b1", 4),
    ("m1", 3),
    ("a3", 2),
    ("tv", 0),
)


def kernel(
    a_ref, vt_hbm, dn_ref, o_ref,
    v, stage, ap, aq, c1, cx, xr, sg, w, ro1, rn1, ro2, rn2, lsem, send, recv,
):
    chunks = ap.shape[0]
    depth, width = v.shape
    group = depth // 4
    row, col = lax.axis_index("row"), lax.axis_index("col")
    x, core = row // 2, row % 2
    z, y = col // 4, col % 4
    half = core * 128
    other = 128 - half
    mine = half + x * 32

    def device(dx=0, dcore=0, dz=0, dy=0):
        return (
            ((x + dx + 4) % 4) * 2 + (core + dcore) % 2,
            ((z + dz + 4) % 4) * 4 + (y + dy + 4) % 4,
        )

    def along(axis, step):
        return device(dz=step) if axis == "z" else device(dy=step)

    place = {"z": z, "y": y}
    gather = ((ap, "y", "z"), (aq, "z", "y"))
    scatter = (("z", "y"), ("y", "z"))

    def copy(c, kind, src, dst, to):
        return pltpu.make_async_remote_copy(
            src_ref=src, dst_ref=dst, send_sem=send.at[c, kind], recv_sem=recv.at[c, kind],
            device_id=to, device_id_type=MESH,
        )

    def arrived(c, kind, dst):
        copy(c, kind, dst, dst, device(dcore=1)).wait_recv()

    def sent(c, kind, src):
        copy(c, kind, src, src, device(dcore=1)).wait_send()

    def block(s, c, step):
        buf, first, second = gather[s]
        f = (place[first] + step + 4) % 4
        return buf.at[c, z, f] if first == "y" else buf.at[c, f, y]

    def line(s, c, step, start=0, size=4):
        buf, first, second = gather[s]
        g = (place[second] + step + 4) % 4
        return buf.at[c, g, pl.ds(start, size)] if first == "y" else buf.at[c, pl.ds(start, size), g]

    def turn(c):
        return 1 - 2 * (c % 2)

    def a_sends(c, s):
        d = turn(c)
        return (
            (block(s, c, 0), along(gather[s][1], 1)),
            (block(s, c, 0), along(gather[s][1], -1)),
            (block(s, c, -d), along(gather[s][1], d)),
            (line(s, c, 0), along(gather[s][2], 1)),
            (line(s, c, 0), along(gather[s][2], -1)),
            (line(s, c, -1, 0, 2), along(gather[s][2], 1)),
            (line(s, c, 1, 2, 2), along(gather[s][2], -1)),
        )

    def a_lands(c, s):
        return (
            block(s, c, -1), block(s, c, 1), block(s, c, 2),
            line(s, c, -1), line(s, c, 1), line(s, c, 2, 0, 2), line(s, c, 2, 2, 2),
        )

    def a_start(c, s, k):
        src, to = a_sends(c, s)[k]
        copy(c, s * 7 + k, src, src, to).start()

    def a_wait(c, s, k):
        arrived(c, s * 7 + k, a_lands(c, s)[k])

    def a0(c):
        for s in range(2):
            a_start(c, s, 0)
            a_start(c, s, 1)

    def a1(c):
        def forward(k):
            for s in range(2):
                a_wait(c, s, k)
                a_start(c, s, 2)

        pl.when(c % 2 == 0)(lambda: forward(0))
        pl.when(c % 2 == 1)(lambda: forward(1))

    def a2(c):
        pl.when(c % 2 == 0)(lambda: [a_wait(c, s, 1) for s in range(2)] and None)
        pl.when(c % 2 == 1)(lambda: [a_wait(c, s, 0) for s in range(2)] and None)
        for s in range(2):
            a_wait(c, s, 2)
            a_start(c, s, 3)
            a_start(c, s, 4)

    def a3(c):
        for s in range(2):
            a_wait(c, s, 3)
            a_start(c, s, 5)
            a_wait(c, s, 4)
            a_start(c, s, 6)

    def m1(c):
        for s in range(2):
            a_wait(c, s, 5)
            a_wait(c, s, 6)
        left = ap[c].reshape(16 * BLOCK, SPLIT)
        right = aq[c].reshape(16 * BLOCK, depth - SPLIT)
        for lo in range(0, width, 512):
            hi = min(lo + 512, width)
            part = jnp.dot(left, v[:SPLIT, lo:hi], preferred_element_type=F32)
            part = part + jnp.dot(right, v[SPLIT:, lo:hi], preferred_element_type=F32)
            c1[c, :, lo:hi] = part.astype(BF16)
        copy(c, X_KIND, c1.at[c, pl.ds(other, 128)], cx.at[c], device(dcore=1)).start()

    def b1(c):
        arrived(c, X_KIND, cx.at[c])
        rows = pl.ds(half, 128)
        c1[c, rows, :] = (c1[c, rows, :].astype(F32) + cx[c].astype(F32)).astype(BF16)
        for k in (2, 1, 3):
            src = c1.at[c, pl.ds(half + ((x + k) % 4) * 32, 32)]
            copy(c, X_KIND + k, src, xr.at[c, k - 1], device(dx=k)).start()

    def b2(c):
        for k in (1, 2, 3):
            arrived(c, X_KIND + k, xr.at[c, k - 1])
        rows = pl.ds(mine, 32)
        total = c1[c, rows, :].astype(F32)
        for k in range(3):
            total = total + xr[c, k].astype(F32)
        sg[c, rows, :] = (total / dn_ref[c]).astype(BF16)
        src = sg.at[c, rows]
        for k in (2, 1, 3):
            copy(c, X_KIND + 3 + k, src, src, device(dx=k)).start()

    def b3(c):
        for k in (1, 2, 3):
            arrived(c, X_KIND + 3 + k, sg.at[c, pl.ds(half + ((x + 4 - k) % 4) * 32, 32)])
        src = sg.at[c, pl.ds(half, 128)]
        copy(c, X_KIND + 7, src, src, device(dcore=1)).start()

    def r_moves(c, s):
        first, second = scatter[s]
        f, g = place[first], place[second]
        own = w.at[s, c, f]
        far, far2 = (f + 2) % 4, (g + 2) % 4
        h = WINDOW // 2
        return (
            (w.at[s, c, far, pl.ds(0, 2)], ro1.at[s, c, pl.ds(0, 2)], along(first, 1)),
            (w.at[s, c, far, pl.ds(2, 2)], ro1.at[s, c, pl.ds(2, 2)], along(first, -1)),
            (w.at[s, c, (f + 1) % 4], rn1.at[s, c, 0], along(first, 1)),
            (w.at[s, c, (f + 3) % 4], rn1.at[s, c, 1], along(first, -1)),
            (own.at[far2, pl.ds(0, h)], ro2.at[s, c, pl.ds(0, h)], along(second, 1)),
            (own.at[far2, pl.ds(h, h)], ro2.at[s, c, pl.ds(h, h)], along(second, -1)),
            (own.at[(g + 1) % 4], rn2.at[s, c, 0], along(second, 1)),
            (own.at[(g + 3) % 4], rn2.at[s, c, 1], along(second, -1)),
        )

    def r_start(c, s, k):
        src, dst, to = r_moves(c, s)[k]
        copy(c, RS_KIND + s * 8 + k, src, dst, to).start()

    def r_wait(c, s, k):
        arrived(c, RS_KIND + s * 8 + k, r_moves(c, s)[k][1])

    def m2(c):
        arrived(c, X_KIND + 7, sg.at[c, pl.ds(other, 128)])

        def rows_of(q, carry):
            part = lax.dot_general(
                v[pl.ds(pl.multiple_of(q * group, 16), group), :], sg[c], (((1,), (1,)), ((), ())),
                preferred_element_type=F32,
            ).astype(BF16)
            for p in range(4):
                piece = part[p * STRIDE : p * STRIDE + WINDOW]
                w[0, c, q, p] = piece[:, :128]
                w[1, c, p, q] = piece[:, 128:]
            return carry

        lax.fori_loop(0, 4, rows_of, 0)
        for s in range(2):
            r_start(c, s, 0)
            r_start(c, s, 1)

    def r1(c):
        for s in range(2):
            f = place[scatter[s][0]]
            up, down = (f + 1) % 4, (f + 3) % 4
            r_wait(c, s, 0)
            w[s, c, up, 0:2] = (w[s, c, up, 0:2].astype(F32) + ro1[s, c, 0:2].astype(F32)).astype(BF16)
            r_start(c, s, 2)
            r_wait(c, s, 1)
            w[s, c, down, 2:4] = (w[s, c, down, 2:4].astype(F32) + ro1[s, c, 2:4].astype(F32)).astype(BF16)
            r_start(c, s, 3)

    def r2(c):
        for s in range(2):
            f = place[scatter[s][0]]
            r_wait(c, s, 2)
            r_wait(c, s, 3)
            total = w[s, c, f].astype(F32) + rn1[s, c, 0].astype(F32) + rn1[s, c, 1].astype(F32)
            w[s, c, f] = total.astype(BF16)
            r_start(c, s, 4)
            r_start(c, s, 5)

    def r3(c):
        h = WINDOW // 2
        for s in range(2):
            f, g = place[scatter[s][0]], place[scatter[s][1]]
            up, down = (g + 1) % 4, (g + 3) % 4
            r_wait(c, s, 4)
            w[s, c, f, up, :h] = (w[s, c, f, up, :h].astype(F32) + ro2[s, c, :h].astype(F32)).astype(BF16)
            r_start(c, s, 6)
            r_wait(c, s, 5)
            w[s, c, f, down, h:] = (w[s, c, f, down, h:].astype(F32) + ro2[s, c, h:].astype(F32)).astype(BF16)
            r_start(c, s, 7)

    def r4(c):
        sums = []
        for s in range(2):
            f, g = place[scatter[s][0]], place[scatter[s][1]]
            r_wait(c, s, 6)
            r_wait(c, s, 7)
            sums.append(w[s, c, f, g].astype(F32) + rn2[s, c, 0].astype(F32) + rn2[s, c, 1].astype(F32))
        total = jnp.concatenate(sums, axis=1)
        total = jnp.concatenate([total, jnp.zeros((256 - WINDOW, 256), F32)], axis=0)
        total = pltpu.roll(total, (256 - 4 * y) % 256, 0)
        flat = total.T[:, : o_ref.shape[-1]]
        o_ref[:, c] = flat.reshape(16, BLOCK, o_ref.shape[-1])

    def sw(c):
        for s in range(2):
            for k, move in enumerate(a_sends(c, s)):
                sent(c, s * 7 + k, move[0])
            for k, move in enumerate(r_moves(c, s)):
                sent(c, RS_KIND + s * 8 + k, move[0])
        sent(c, X_KIND, c1.at[c, pl.ds(other, 128)])
        for k in (1, 2, 3):
            sent(c, X_KIND + k, c1.at[c, pl.ds(half + ((x + k) % 4) * 32, 32)])
            sent(c, X_KIND + 3 + k, sg.at[c, pl.ds(mine, 32)])
        sent(c, X_KIND + 7, sg.at[c, pl.ds(half, 128)])

    def load(i, size):
        slot = i % 2
        return pltpu.make_async_copy(
            vt_hbm.at[pl.ds(pl.multiple_of(i * TILE, TILE), size)], stage.at[slot, pl.ds(0, size)], lsem.at[slot]
        )

    tiles, rest = width // TILE, width % TILE
    third = (tiles + 1) // 3

    def tv(c):
        def turned(i, carry):
            load(i, TILE).wait()
            v[:, pl.ds(pl.multiple_of(i * TILE, TILE), TILE)] = stage[i % 2].T
            pl.when(i + 2 < tiles)(lambda: load(i + 2, TILE).start())
            pl.when(i + 2 == tiles)(lambda: load(tiles, rest).start())
            return carry

        lax.fori_loop(c * third, jnp.minimum((c + 1) * third, tiles), turned, 0)

        @pl.when(c == 2)
        def _():
            load(tiles, rest).wait()
            v[:, tiles * TILE :] = stage[tiles % 2, :rest].T

    load(0, TILE).start()
    load(1, TILE).start()
    for c in range(chunks):
        ap[c, z, y] = a_ref[c * BLOCK : (c + 1) * BLOCK, :SPLIT]
        aq[c, z, y] = a_ref[c * BLOCK : (c + 1) * BLOCK, SPLIT:]

    peers = [device(dy=1), device(dy=-1), device(dz=1), device(dz=-1), device(dcore=1)]
    peers += [device(dx=k) for k in (1, 2, 3)]
    barrier = pltpu.get_barrier_semaphore()
    for peer in peers:
        pl.semaphore_signal(barrier, inc=1, device_id=peer, device_id_type=MESH)
    pl.semaphore_wait(barrier, len(peers))

    ops = dict(tv=tv, a0=a0, a1=a1, a2=a2, a3=a3, m1=m1, b1=b1, b2=b2, b3=b3, m2=m2, r1=r1, r2=r2, r3=r3, r4=r4, sw=sw)

    def step(t, carry):
        for name, late in PLAN:
            c = t - late
            pl.when(jnp.logical_and(c >= 0, c < (3 if name == "tv" else chunks)))(functools.partial(ops[name], c))
        return carry

    lax.fori_loop(0, chunks + max(late for _, late in PLAN), step, 0)


def on_device(amplitudes, integrals, row_gap, col_gap):
    rows, depth = amplitudes.shape
    width = integrals.shape[1]
    chunks = rows // BLOCK
    final = depth // 16
    row, col = lax.axis_index("row"), lax.axis_index("col")
    gaps = row_gap.reshape(16, chunks, BLOCK)
    near = lax.dynamic_slice_in_dim(gaps, (row % 2) * 8 + (row // 2) * 2, 2, 0)
    near = near.transpose(1, 0, 2).reshape(chunks, 2 * BLOCK, 1)
    denominators = near + lax.dynamic_slice_in_dim(col_gap, col * width, width)

    vm = pl.BlockSpec(memory_space=pltpu.VMEM)
    cycle_two = pl.pallas_call(
        kernel,
        out_shape=jax.ShapeDtypeStruct((16, chunks, BLOCK, final), F32),
        in_specs=[vm, pl.BlockSpec(memory_space=pl.ANY), vm],
        out_specs=vm,
        scratch_shapes=[
            pltpu.VMEM((depth, width), BF16),
            pltpu.VMEM((2, TILE, depth), BF16),
            pltpu.VMEM((chunks, 4, 4, BLOCK, SPLIT), BF16),
            pltpu.VMEM((chunks, 4, 4, BLOCK, depth - SPLIT), BF16),
            pltpu.VMEM((chunks, 256, width), BF16),
            pltpu.VMEM((chunks, 128, width), BF16),
            pltpu.VMEM((chunks, 3, 32, width), BF16),
            pltpu.VMEM((chunks, 256, width), BF16),
            pltpu.VMEM((2, chunks, 4, 4, WINDOW, 128), BF16),
            pltpu.VMEM((2, chunks, 4, WINDOW, 128), BF16),
            pltpu.VMEM((2, chunks, 2, 4, WINDOW, 128), BF16),
            pltpu.VMEM((2, chunks, WINDOW, 128), BF16),
            pltpu.VMEM((2, chunks, 2, WINDOW, 128), BF16),
            pltpu.SemaphoreType.DMA((2,)),
            pltpu.SemaphoreType.DMA((chunks, KINDS)),
            pltpu.SemaphoreType.DMA((chunks, KINDS)),
        ],
        compiler_params=pltpu.CompilerParams(
            collective_id=0, has_side_effects=True, vmem_limit_bytes=62 * 1024 * 1024
        ),
        cost_estimate=pl.CostEstimate(
            flops=4 * 16 * rows * depth * width, bytes_accessed=2 * depth * width, transcendentals=0
        ),
    )(amplitudes, integrals.T, denominators)
    start = (row * 16 + col) * final
    here = lax.dynamic_slice_in_dim(col_gap, start, final)
    cycle_two = cycle_two.reshape(16 * rows, final)
    return (cycle_two / (row_gap[:, None] + here[None, :])).astype(BF16)


def solution(mesh):
    return jax.shard_map(
        on_device,
        mesh=mesh,
        in_specs=(P("col", "row"), P("row", "col"), P(), P()),
        out_specs=P(None, ("row", "col")),
        check_vma=False,
    )
```

```python
import functools

import jax
import jax.numpy as jnp
from jax import lax
from jax.experimental import pallas as pl
from jax.experimental.pallas import tpu as pltpu
from jax.sharding import PartitionSpec as P

MESH = pl.DeviceIdType.MESH
F32 = jnp.float32
BF16 = jnp.bfloat16

BLOCK = 16
SPLIT = 1408
WINDOW = 192
STRIDE = 176
TILE = 128
X_KIND = 14
RS_KIND = 24
KINDS = 40

PLAN = (
    ("r1", 8),
    ("r2", 10),
    ("a0", 0),
    ("m1", 3),
    ("b2", 4),
    ("b4", 5),
    ("r3", 12),
    ("a3", 2),
    ("a2", 1),
    ("r4", 14),
    ("sw", 14),
    ("tv", 0),
    ("a1", 0),
    ("m2", 6),
    ("b1", 3),
    ("b3", 4),
    ("b5", 5),
)


def kernel(
    a_ref, vt_hbm, row_hbm, col_hbm, o_ref, final_ref,
    rg, near, cg, v, stage, ap, aq, c1, cx, xo, xn, sg, w, ro1, rn1, ro2, rn2, gsem, lsem, send, recv,
):
    chunks = ap.shape[0]
    depth, width = v.shape
    group = depth // 4
    row, col = lax.axis_index("row"), lax.axis_index("col")
    x, core = row // 2, row % 2
    z, y = col // 4, col % 4
    half = core * 128
    other = 128 - half

    def device(dx=0, dcore=0, dz=0, dy=0):
        return (
            ((x + dx + 4) % 4) * 2 + (core + dcore) % 2,
            ((z + dz + 4) % 4) * 4 + (y + dy + 4) % 4,
        )

    def along(axis, step):
        return device(dz=step) if axis == "z" else device(dy=step)

    place = {"z": z, "y": y}
    gather = ((ap, "y", "z"), (aq, "z", "y"))
    scatter = (("z", "y"), ("y", "z"))

    def copy(c, kind, src, dst, to):
        return pltpu.make_async_remote_copy(
            src_ref=src, dst_ref=dst, send_sem=send.at[c, kind], recv_sem=recv.at[c, kind],
            device_id=to, device_id_type=MESH,
        )

    def arrived(c, kind, dst):
        copy(c, kind, dst, dst, device(dcore=1)).wait_recv()

    def sent(c, kind, src):
        copy(c, kind, src, src, device(dcore=1)).wait_send()

    def block(s, c, step):
        buf, first, second = gather[s]
        f = (place[first] + step + 4) % 4
        return buf.at[c, z, f] if first == "y" else buf.at[c, f, y]

    def line(s, c, step, start=0, size=4):
        buf, first, second = gather[s]
        g = (place[second] + step + 4) % 4
        return buf.at[c, g, pl.ds(start, size)] if first == "y" else buf.at[c, pl.ds(start, size), g]

    def turn(c):
        return 1 - 2 * (c % 2)

    def a_sends(c, s):
        d = turn(c)
        return (
            (block(s, c, 0), along(gather[s][1], 1)),
            (block(s, c, 0), along(gather[s][1], -1)),
            (block(s, c, -d), along(gather[s][1], d)),
            (line(s, c, 0), along(gather[s][2], 1)),
            (line(s, c, 0), along(gather[s][2], -1)),
            (line(s, c, -1, 0, 2), along(gather[s][2], 1)),
            (line(s, c, 1, 2, 2), along(gather[s][2], -1)),
        )

    def a_lands(c, s):
        return (
            block(s, c, -1), block(s, c, 1), block(s, c, 2),
            line(s, c, -1), line(s, c, 1), line(s, c, 2, 0, 2), line(s, c, 2, 2, 2),
        )

    def a_start(c, s, k):
        src, to = a_sends(c, s)[k]
        copy(c, s * 7 + k, src, src, to).start()

    def a_wait(c, s, k):
        arrived(c, s * 7 + k, a_lands(c, s)[k])

    def a0(c):
        for s in range(2):
            a_start(c, s, 0)
            a_start(c, s, 1)

    def a1(c):
        def forward(k):
            for s in range(2):
                a_wait(c, s, k)
                a_start(c, s, 2)

        pl.when(c % 2 == 0)(lambda: forward(0))
        pl.when(c % 2 == 1)(lambda: forward(1))

    def a2(c):
        pl.when(c % 2 == 0)(lambda: [a_wait(c, s, 1) for s in range(2)] and None)
        pl.when(c % 2 == 1)(lambda: [a_wait(c, s, 0) for s in range(2)] and None)
        for s in range(2):
            a_wait(c, s, 2)
            a_start(c, s, 3)
            a_start(c, s, 4)

    def a3(c):
        for s in range(2):
            a_wait(c, s, 3)
            a_start(c, s, 5)
            a_wait(c, s, 4)
            a_start(c, s, 6)

    def m1(c):
        for s in range(2):
            a_wait(c, s, 5)
            a_wait(c, s, 6)
        left = ap[c].reshape(16 * BLOCK, SPLIT)
        right = aq[c].reshape(16 * BLOCK, depth - SPLIT)
        for lo in range(0, width, 512):
            hi = min(lo + 512, width)
            part = jnp.dot(left, v[:SPLIT, lo:hi], preferred_element_type=F32)
            part = part + jnp.dot(right, v[SPLIT:, lo:hi], preferred_element_type=F32)
            c1[c, :, lo:hi] = part.astype(BF16)
        x_start(c, 0)

    def piece(c, step, start=0, size=32):
        return pl.ds(half + ((x + step + 4) % 4) * 32 + start, size)

    def x_sends(c):
        return (
            (c1.at[c, pl.ds(other, 128)], cx.at[c], device(dcore=1)),
            (c1.at[c, piece(c, 2, 0, 16)], xo.at[c, pl.ds(0, 16)], device(dx=1)),
            (c1.at[c, piece(c, 2, 16, 16)], xo.at[c, pl.ds(16, 16)], device(dx=-1)),
            (c1.at[c, piece(c, 1)], xn.at[c, 0], device(dx=1)),
            (c1.at[c, piece(c, -1)], xn.at[c, 1], device(dx=-1)),
            (sg.at[c, piece(c, 0)], sg.at[c, piece(c, 0)], device(dx=1)),
            (sg.at[c, piece(c, 0)], sg.at[c, piece(c, 0)], device(dx=-1)),
            (sg.at[c, piece(c, -1, 0, 16)], sg.at[c, piece(c, -1, 0, 16)], device(dx=1)),
            (sg.at[c, piece(c, 1, 16, 16)], sg.at[c, piece(c, 1, 16, 16)], device(dx=-1)),
            (sg.at[c, pl.ds(half, 128)], sg.at[c, pl.ds(half, 128)], device(dcore=1)),
        )

    def x_lands(c):
        return tuple(move[1] for move in x_sends(c)[:5]) + (
            sg.at[c, piece(c, -1)], sg.at[c, piece(c, 1)],
            sg.at[c, piece(c, 2, 0, 16)], sg.at[c, piece(c, 2, 16, 16)],
            sg.at[c, pl.ds(other, 128)],
        )

    def x_start(c, k):
        src, dst, to = x_sends(c)[k]
        copy(c, X_KIND + k, src, dst, to).start()

    def x_wait(c, k):
        arrived(c, X_KIND + k, x_lands(c)[k])

    def b1(c):
        x_wait(c, 0)
        rows = pl.ds(half, 128)
        c1[c, rows, :] = (c1[c, rows, :].astype(F32) + cx[c].astype(F32)).astype(BF16)
        x_start(c, 1)
        x_start(c, 2)

    def b2(c):
        for k, step in ((1, 1), (2, -1)):
            x_wait(c, k)
            part, rows = pl.ds(16 * (k - 1), 16), piece(c, step, 16 * (k - 1), 16)
            c1[c, rows, :] = (c1[c, rows, :].astype(F32) + xo[c, part].astype(F32)).astype(BF16)
            x_start(c, k + 2)

    def b3(c):
        gap = jnp.zeros((32, 128), F32)
        index = lax.broadcasted_iota(jnp.int32, (32, 128), 0)
        for k in range(32):
            value = rg[(core * 8 + x * 2 + k // BLOCK) * (chunks * BLOCK) + c * BLOCK + k % BLOCK]
            gap = jnp.where(index == k, value, gap)
        x_wait(c, 3)
        x_wait(c, 4)
        rows = piece(c, 0)
        total = c1[c, rows, :].astype(F32) + xn[c, 0].astype(F32) + xn[c, 1].astype(F32)
        sg[c, rows, :] = (total / (gap[:, :1] + cg[0:1, :width])).astype(BF16)
        x_start(c, 5)
        x_start(c, 6)

    def b4(c):
        for k in (5, 6):
            x_wait(c, k)
            x_start(c, k + 2)

    def b5(c):
        x_wait(c, 7)
        x_wait(c, 8)
        x_start(c, 9)

    def r_moves(c, s):
        first, second = scatter[s]
        f, g = place[first], place[second]
        own = w.at[s, c, f]
        far, far2 = (f + 2) % 4, (g + 2) % 4
        h = WINDOW // 2
        return (
            (w.at[s, c, far, pl.ds(0, 2)], ro1.at[s, c, pl.ds(0, 2)], along(first, 1)),
            (w.at[s, c, far, pl.ds(2, 2)], ro1.at[s, c, pl.ds(2, 2)], along(first, -1)),
            (w.at[s, c, (f + 1) % 4], rn1.at[s, c, 0], along(first, 1)),
            (w.at[s, c, (f + 3) % 4], rn1.at[s, c, 1], along(first, -1)),
            (own.at[far2, pl.ds(0, h)], ro2.at[s, c, pl.ds(0, h)], along(second, 1)),
            (own.at[far2, pl.ds(h, h)], ro2.at[s, c, pl.ds(h, h)], along(second, -1)),
            (own.at[(g + 1) % 4], rn2.at[s, c, 0], along(second, 1)),
            (own.at[(g + 3) % 4], rn2.at[s, c, 1], along(second, -1)),
        )

    def r_start(c, s, k):
        src, dst, to = r_moves(c, s)[k]
        copy(c, RS_KIND + s * 8 + k, src, dst, to).start()

    def r_wait(c, s, k):
        arrived(c, RS_KIND + s * 8 + k, r_moves(c, s)[k][1])

    def m2(c):
        x_wait(c, 9)

        def rows_of(q, carry):
            part = lax.dot_general(
                v[pl.ds(pl.multiple_of(q * group, 16), group), :], sg[c], (((1,), (1,)), ((), ())),
                preferred_element_type=F32,
            ).astype(BF16)
            for p in range(4):
                piece = part[p * STRIDE : p * STRIDE + WINDOW]
                w[0, c, q, p] = piece[:, :128]
                w[1, c, p, q] = piece[:, 128:]
            return carry

        lax.fori_loop(0, 4, rows_of, 0)
        for s in range(2):
            r_start(c, s, 0)
            r_start(c, s, 1)

    def r1(c):
        for s in range(2):
            f = place[scatter[s][0]]
            up, down = (f + 1) % 4, (f + 3) % 4
            r_wait(c, s, 0)
            w[s, c, up, 0:2] = (w[s, c, up, 0:2].astype(F32) + ro1[s, c, 0:2].astype(F32)).astype(BF16)
            r_start(c, s, 2)
            r_wait(c, s, 1)
            w[s, c, down, 2:4] = (w[s, c, down, 2:4].astype(F32) + ro1[s, c, 2:4].astype(F32)).astype(BF16)
            r_start(c, s, 3)

    def r2(c):
        for s in range(2):
            f = place[scatter[s][0]]
            r_wait(c, s, 2)
            r_wait(c, s, 3)
            total = w[s, c, f].astype(F32) + rn1[s, c, 0].astype(F32) + rn1[s, c, 1].astype(F32)
            w[s, c, f] = total.astype(BF16)
            r_start(c, s, 4)
            r_start(c, s, 5)

    def r3(c):
        h = WINDOW // 2
        for s in range(2):
            f, g = place[scatter[s][0]], place[scatter[s][1]]
            up, down = (g + 1) % 4, (g + 3) % 4
            r_wait(c, s, 4)
            w[s, c, f, up, :h] = (w[s, c, f, up, :h].astype(F32) + ro2[s, c, :h].astype(F32)).astype(BF16)
            r_start(c, s, 6)
            r_wait(c, s, 5)
            w[s, c, f, down, h:] = (w[s, c, f, down, h:].astype(F32) + ro2[s, c, h:].astype(F32)).astype(BF16)
            r_start(c, s, 7)

    def r4(c):
        sums = []
        for s in range(2):
            f, g = place[scatter[s][0]], place[scatter[s][1]]
            r_wait(c, s, 6)
            r_wait(c, s, 7)
            sums.append(w[s, c, f, g].astype(F32) + rn2[s, c, 0].astype(F32) + rn2[s, c, 1].astype(F32))
        total = jnp.concatenate(sums, axis=1)
        total = jnp.concatenate([total, jnp.zeros((256 - WINDOW, 256), F32)], axis=0)
        total = pltpu.roll(total, (256 - 4 * y) % 256, 0)
        flat = total.T[:, : o_ref.shape[-1]]
        o_ref[:, c] = flat.reshape(16, BLOCK, o_ref.shape[-1])

    def sw(c):
        for s in range(2):
            for k, move in enumerate(a_sends(c, s)):
                sent(c, s * 7 + k, move[0])
            for k, move in enumerate(r_moves(c, s)):
                sent(c, RS_KIND + s * 8 + k, move[0])
        for k, move in enumerate(x_sends(c)):
            sent(c, X_KIND + k, move[0])

    def load(i, size):
        slot = i % 2
        return pltpu.make_async_copy(
            vt_hbm.at[pl.ds(pl.multiple_of(i * TILE, TILE), size)], stage.at[slot, pl.ds(0, size)], lsem.at[slot]
        )

    tiles, rest = width // TILE, width % TILE
    third = (tiles + 1) // 3

    def tv(c):
        def turned(i, carry):
            load(i, TILE).wait()
            v[:, pl.ds(pl.multiple_of(i * TILE, TILE), TILE)] = stage[i % 2].T
            pl.when(i + 2 < tiles)(lambda: load(i + 2, TILE).start())
            pl.when(i + 2 == tiles)(lambda: load(tiles, rest).start())
            return carry

        lax.fori_loop(c * third, jnp.minimum((c + 1) * third, tiles), turned, 0)

        @pl.when(c == 2)
        def _():
            load(tiles, rest).wait()
            v[:, tiles * TILE :] = stage[tiles % 2, :rest].T

    load(0, TILE).start()
    load(1, TILE).start()
    final = o_ref.shape[-1]
    inner, outer = col * width, (row * 16 + col) * final
    inner_base = inner // 128 * 128
    outer_base = jnp.minimum(outer // 128, col_hbm.shape[1] // 128 - 3) * 128
    gaps = [
        pltpu.make_async_copy(row_hbm, rg, gsem.at[0]),
        pltpu.make_async_copy(col_hbm.at[:, pl.ds(pl.multiple_of(inner_base, 128), 1536)], near.at[:, :1536], gsem.at[1]),
        pltpu.make_async_copy(col_hbm.at[:, pl.ds(pl.multiple_of(outer_base, 128), 384)], near.at[:, 1536:], gsem.at[2]),
    ]
    for gap in gaps:
        gap.start()
    for c in range(chunks):
        ap[c, z, y] = a_ref[c * BLOCK : (c + 1) * BLOCK, :SPLIT]
        aq[c, z, y] = a_ref[c * BLOCK : (c + 1) * BLOCK, SPLIT:]

    peers = [device(dy=1), device(dy=-1), device(dz=1), device(dz=-1), device(dcore=1)]
    peers += [device(dx=1), device(dx=-1)]
    barrier = pltpu.get_barrier_semaphore()
    for peer in peers:
        pl.semaphore_signal(barrier, inc=1, device_id=peer, device_id_type=MESH)
    pl.semaphore_wait(barrier, len(peers))

    for gap in gaps:
        gap.wait()
    cg[...] = pltpu.roll(jnp.broadcast_to(near[:, :1536], (8, 1536)), (1536 - (inner - inner_base)) % 1536, 1)
    shifted = pltpu.roll(jnp.broadcast_to(near[:, 1536:], (8, 384)), (384 - (outer - outer_base)) % 384, 1)
    final_ref[...] = shifted[0:1, :final]

    ops = dict(tv=tv, a0=a0, a1=a1, a2=a2, a3=a3, m1=m1, b1=b1, b2=b2, b3=b3, b4=b4, b5=b5, m2=m2, r1=r1, r2=r2, r3=r3, r4=r4, sw=sw)

    def step(t, carry):
        for name, late in PLAN:
            c = t - late
            pl.when(jnp.logical_and(c >= 0, c < (3 if name == "tv" else chunks)))(functools.partial(ops[name], c))
        return carry

    lax.fori_loop(0, chunks + max(late for _, late in PLAN), step, 0)


def on_device(amplitudes, integrals, row_gap, col_gap):
    rows, depth = amplitudes.shape
    width = integrals.shape[1]
    chunks = rows // BLOCK
    final = depth // 16

    vm = pl.BlockSpec(memory_space=pltpu.VMEM)
    anywhere = pl.BlockSpec(memory_space=pl.ANY)
    cycle_two, here = pl.pallas_call(
        kernel,
        out_shape=(
            jax.ShapeDtypeStruct((16, chunks, BLOCK, final), F32),
            jax.ShapeDtypeStruct((1, final), F32),
        ),
        in_specs=[vm, anywhere, anywhere, anywhere],
        out_specs=(vm, vm),
        scratch_shapes=[
            pltpu.SMEM((16 * rows,), F32),
            pltpu.VMEM((1, 1920), F32),
            pltpu.VMEM((8, 1536), F32),
            pltpu.VMEM((depth, width), BF16),
            pltpu.VMEM((2, TILE, depth), BF16),
            pltpu.VMEM((chunks, 4, 4, BLOCK, SPLIT), BF16),
            pltpu.VMEM((chunks, 4, 4, BLOCK, depth - SPLIT), BF16),
            pltpu.VMEM((chunks, 256, width), BF16),
            pltpu.VMEM((chunks, 128, width), BF16),
            pltpu.VMEM((chunks, 32, width), BF16),
            pltpu.VMEM((chunks, 2, 32, width), BF16),
            pltpu.VMEM((chunks, 256, width), BF16),
            pltpu.VMEM((2, chunks, 4, 4, WINDOW, 128), BF16),
            pltpu.VMEM((2, chunks, 4, WINDOW, 128), BF16),
            pltpu.VMEM((2, chunks, 2, 4, WINDOW, 128), BF16),
            pltpu.VMEM((2, chunks, WINDOW, 128), BF16),
            pltpu.VMEM((2, chunks, 2, WINDOW, 128), BF16),
            pltpu.SemaphoreType.DMA((3,)),
            pltpu.SemaphoreType.DMA((2,)),
            pltpu.SemaphoreType.DMA((chunks, KINDS)),
            pltpu.SemaphoreType.DMA((chunks, KINDS)),
        ],
        compiler_params=pltpu.CompilerParams(
            collective_id=0, has_side_effects=True, vmem_limit_bytes=62 * 1024 * 1024
        ),
        cost_estimate=pl.CostEstimate(
            flops=4 * 16 * rows * depth * width, bytes_accessed=2 * depth * width, transcendentals=0
        ),
    )(amplitudes, integrals.T, row_gap, col_gap[None])
    cycle_two = cycle_two.reshape(16 * rows, final)
    return (cycle_two / (row_gap[:, None] + here)).astype(BF16)


def solution(mesh):
    return jax.shard_map(
        on_device,
        mesh=mesh,
        in_specs=(P("col", "row"), P("row", "col"), P(), P()),
        out_specs=P(None, ("row", "col")),
        check_vma=False,
    )
```

```python
import functools

import jax
import jax.numpy as jnp
from jax import lax
from jax.experimental import pallas as pl
from jax.experimental.pallas import tpu as pltpu
from jax.sharding import PartitionSpec as P

MESH = pl.DeviceIdType.MESH
F32 = jnp.float32
BF16 = jnp.bfloat16

BLOCK = 16
SPLIT = 1408
WINDOW = 192
STRIDE = 176
TILE = 128
X_KIND = 14
RS_KIND = 24
KINDS = 40

PLAN = (
    ("r1", 8),
    ("r2", 10),
    ("a0", 0),
    ("m1", 3),
    ("b2", 4),
    ("b4", 5),
    ("r3", 12),
    ("a3", 2),
    ("a2", 1),
    ("r4", 14),
    ("sw", 14),
    ("tv", 0),
    ("a1", 0),
    ("m2", 6),
    ("b1", 3),
    ("b3", 4),
    ("b5", 5),
)


def kernel(
    a_ref, vt_hbm, row_hbm, col_ref, o_ref, final_ref,
    rg, near, cg, v, stage, ag, c1, cx, xo, xn, sg, w, ro1, rn1, ro2, rn2, out, gsem, lsem, send, recv,
):
    chunks = ag.shape[0]
    depth, width = a_ref.shape[1], v.shape[1]
    group = depth // 4
    row, col = lax.axis_index("row"), lax.axis_index("col")
    x, core = row // 2, row % 2
    z, y = col // 4, col % 4
    half = core * 128
    other = 128 - half

    def around(index):
        return {0: index, 1: lax.rem(index + 1, 4), 2: lax.rem(index + 2, 4), -1: lax.rem(index + 3, 4)}

    xs, ys, zs = around(x), around(y), around(z)
    at = {"z": zs, "y": ys}
    peer = {
        ("x", 1): (xs[1] * 2 + core, col),
        ("x", -1): (xs[-1] * 2 + core, col),
        ("y", 1): (row, z * 4 + ys[1]),
        ("y", -1): (row, z * 4 + ys[-1]),
        ("z", 1): (row, zs[1] * 4 + y),
        ("z", -1): (row, zs[-1] * 4 + y),
        "core": (x * 2 + 1 - core, col),
    }
    strips = {step: half + index * 32 for step, index in xs.items()}
    gather = (("y", "z", pl.ds(0, SPLIT)), ("z", "y", pl.ds(SPLIT, ag.shape[-1] - SPLIT)))
    scatter = (("z", "y"), ("y", "z"))

    def copy(c, kind, src, dst, to):
        return pltpu.make_async_remote_copy(
            src_ref=src, dst_ref=dst, send_sem=send.at[c, kind], recv_sem=recv.at[c, kind],
            device_id=to, device_id_type=MESH,
        )

    def arrived(c, kind, dst):
        copy(c, kind, dst, dst, peer["core"]).wait_recv()

    def sent(c, kind, src):
        copy(c, kind, src, src, peer["core"]).wait_send()

    def block(s, c, step):
        first, _, lanes = gather[s]
        f = at[first][step]
        return ag.at[c, z, f, :, lanes] if first == "y" else ag.at[c, f, y, :, lanes]

    def line(s, c, step, start=0, size=4):
        first, second, lanes = gather[s]
        g, part = at[second][step], pl.ds(start, size)
        return ag.at[c, g, part, :, lanes] if first == "y" else ag.at[c, part, g, :, lanes]

    def a_send(c, s, k, d=1):
        first, second, _ = gather[s]
        if k == 0:
            return block(s, c, 0), peer[first, 1]
        if k == 1:
            return block(s, c, 0), peer[first, -1]
        if k == 2:
            return block(s, c, -d), peer[first, d]
        if k == 3:
            return line(s, c, 0), peer[second, 1]
        if k == 4:
            return line(s, c, 0), peer[second, -1]
        if k == 5:
            return line(s, c, -1, 0, 2), peer[second, 1]
        return line(s, c, 1, 2, 2), peer[second, -1]

    def a_land(c, s, k):
        if k < 3:
            return block(s, c, (-1, 1, 2)[k])
        if k < 5:
            return line(s, c, (-1, 1)[k - 3])
        return line(s, c, 2, 2 * (k - 5), 2)

    def a_start(c, s, k, d=1):
        src, to = a_send(c, s, k, d)
        copy(c, s * 7 + k, src, src, to).start()

    def a_wait(c, s, k):
        arrived(c, s * 7 + k, a_land(c, s, k))

    def a0(c):
        for s in range(2):
            a_start(c, s, 0)
            a_start(c, s, 1)

    def a1(c):
        def forward(d):
            for s in range(2):
                a_wait(c, s, 0 if d == 1 else 1)
                a_start(c, s, 2, d)

        pl.when(c % 2 == 0)(lambda: forward(1))
        pl.when(c % 2 == 1)(lambda: forward(-1))

    def a2(c):
        pl.when(c % 2 == 0)(lambda: [a_wait(c, s, 1) for s in range(2)] and None)
        pl.when(c % 2 == 1)(lambda: [a_wait(c, s, 0) for s in range(2)] and None)
        for s in range(2):
            a_wait(c, s, 2)
            a_start(c, s, 3)
            a_start(c, s, 4)

    def a3(c):
        for s in range(2):
            a_wait(c, s, 3)
            a_start(c, s, 5)
            a_wait(c, s, 4)
            a_start(c, s, 6)

    def m1(c):
        for s in range(2):
            a_wait(c, s, 5)
            a_wait(c, s, 6)
        rows = ag[c].reshape(16 * BLOCK, ag.shape[-1])
        for lo in range(0, width, 512):
            hi = min(lo + 512, width)
            c1[c, :, lo:hi] = jnp.dot(rows, v[:, lo:hi], preferred_element_type=F32).astype(BF16)
        x_start(c, 0)

    def piece(step, start=0, size=32):
        return pl.ds(pl.multiple_of(strips[step] + start, 16), size)

    def x_send(c, k):
        if k == 0:
            return c1.at[c, pl.ds(pl.multiple_of(other, 128), 128)], cx.at[c], peer["core"]
        if k == 9:
            src = sg.at[c, pl.ds(pl.multiple_of(half, 128), 128)]
            return src, src, peer["core"]
        d = 1 if k % 2 == 1 else -1
        part = pl.ds(8 - 8 * d, 16)
        if k < 3:
            return c1.at[c, piece(2, 8 - 8 * d, 16)], xo.at[c, part], peer["x", d]
        if k < 5:
            return c1.at[c, piece(d)], xn.at[c, (k - 3)], peer["x", d]
        src = sg.at[c, piece(0) if k < 7 else piece(-d, 8 - 8 * d, 16)]
        return src, src, peer["x", d]

    def x_land(c, k):
        if k < 5:
            return x_send(c, k)[1]
        if k == 9:
            return sg.at[c, pl.ds(pl.multiple_of(other, 128), 128)]
        d = 1 if k % 2 == 1 else -1
        return sg.at[c, piece(-d) if k < 7 else piece(2, 8 - 8 * d, 16)]

    def x_start(c, k):
        src, dst, to = x_send(c, k)
        copy(c, X_KIND + k, src, dst, to).start()

    def x_wait(c, k):
        arrived(c, X_KIND + k, x_land(c, k))

    def b1(c):
        x_wait(c, 0)
        rows = pl.ds(pl.multiple_of(half, 128), 128)
        c1[c, rows, :] = (c1[c, rows, :].astype(F32) + cx[c].astype(F32)).astype(BF16)
        x_start(c, 1)
        x_start(c, 2)

    def b2(c):
        for k, step in ((1, 1), (2, -1)):
            x_wait(c, k)
            part, rows = pl.ds(16 * (k - 1), 16), piece(step, 16 * (k - 1), 16)
            c1[c, rows, :] = (c1[c, rows, :].astype(F32) + xo[c, part].astype(F32)).astype(BF16)
            x_start(c, k + 2)

    first_row = (core * 8 + x * 2) * (chunks * BLOCK)

    def b3(c):
        gap = jnp.zeros((32, 128), F32)
        index = lax.broadcasted_iota(jnp.int32, (32, 128), 0)
        for k in range(32):
            value = rg[first_row + (k // BLOCK) * (chunks * BLOCK) + c * BLOCK + k % BLOCK]
            gap = jnp.where(index == k, value, gap)
        x_wait(c, 3)
        x_wait(c, 4)
        rows = piece(0)
        total = c1[c, rows, :].astype(F32) + xn[c, 0].astype(F32) + xn[c, 1].astype(F32)
        sg[c, rows, :] = (total / (gap[:, :1] + cg[0:1, :width])).astype(BF16)
        x_start(c, 5)
        x_start(c, 6)

    def b4(c):
        for k in (5, 6):
            x_wait(c, k)
            x_start(c, k + 2)

    def b5(c):
        x_wait(c, 7)
        x_wait(c, 8)
        x_start(c, 9)

    def r_move(c, s, k):
        first, second = scatter[s]
        fs, gs = at[first], at[second]
        d = 1 if k % 2 == 0 else -1
        if k < 2:
            part = pl.ds(2 * k, 2)
            return w.at[s, c, fs[2], part], ro1.at[s, c, part], peer[first, d]
        if k < 4:
            return w.at[s, c, fs[d]], rn1.at[s, c, k - 2], peer[first, d]
        if k < 6:
            part = pl.ds((k - 4) * (WINDOW // 2), WINDOW // 2)
            return w.at[s, c, fs[0], gs[2], part], ro2.at[s, c, part], peer[second, d]
        return w.at[s, c, fs[0], gs[d]], rn2.at[s, c, k - 6], peer[second, d]

    def r_start(c, s, k):
        src, dst, to = r_move(c, s, k)
        copy(c, RS_KIND + s * 8 + k, src, dst, to).start()

    def r_wait(c, s, k):
        arrived(c, RS_KIND + s * 8 + k, r_move(c, s, k)[1])

    def m2(c):
        x_wait(c, 9)

        def rows_of(q, carry):
            part = lax.dot_general(
                v[pl.ds(pl.multiple_of(q * group, 16), group), :], sg[c], (((1,), (1,)), ((), ())),
                preferred_element_type=F32,
            ).astype(BF16)
            for p in range(4):
                piece = part[p * STRIDE : p * STRIDE + WINDOW]
                w[0, c, q, p] = piece[:, :128]
                w[1, c, p, q] = piece[:, 128:]
            return carry

        lax.fori_loop(0, 4, rows_of, 0)
        for s in range(2):
            r_start(c, s, 0)
            r_start(c, s, 1)

    def r1(c):
        for s in range(2):
            up, down = at[scatter[s][0]][1], at[scatter[s][0]][-1]
            r_wait(c, s, 0)
            w[s, c, up, 0:2] = (w[s, c, up, 0:2].astype(F32) + ro1[s, c, 0:2].astype(F32)).astype(BF16)
            r_start(c, s, 2)
            r_wait(c, s, 1)
            w[s, c, down, 2:4] = (w[s, c, down, 2:4].astype(F32) + ro1[s, c, 2:4].astype(F32)).astype(BF16)
            r_start(c, s, 3)

    def r2(c):
        for s in range(2):
            f = at[scatter[s][0]][0]
            r_wait(c, s, 2)
            r_wait(c, s, 3)
            total = w[s, c, f].astype(F32) + rn1[s, c, 0].astype(F32) + rn1[s, c, 1].astype(F32)
            w[s, c, f] = total.astype(BF16)
            r_start(c, s, 4)
            r_start(c, s, 5)

    def r3(c):
        h = WINDOW // 2
        for s in range(2):
            f, gs = at[scatter[s][0]][0], at[scatter[s][1]]
            up, down = gs[1], gs[-1]
            r_wait(c, s, 4)
            w[s, c, f, up, :h] = (w[s, c, f, up, :h].astype(F32) + ro2[s, c, :h].astype(F32)).astype(BF16)
            r_start(c, s, 6)
            r_wait(c, s, 5)
            w[s, c, f, down, h:] = (w[s, c, f, down, h:].astype(F32) + ro2[s, c, h:].astype(F32)).astype(BF16)
            r_start(c, s, 7)

    def r4(c):
        sums = []
        for s in range(2):
            f, g = at[scatter[s][0]][0], at[scatter[s][1]][0]
            r_wait(c, s, 6)
            r_wait(c, s, 7)
            sums.append(w[s, c, f, g].astype(F32) + rn2[s, c, 0].astype(F32) + rn2[s, c, 1].astype(F32))
        total = jnp.concatenate(sums, axis=1)
        total = jnp.concatenate([total, jnp.zeros((256 - WINDOW, 256), F32)], axis=0)
        total = pltpu.roll(total, (256 - 4 * y) % 256, 0)
        out[:, c] = total.T.reshape(16, BLOCK, 256)

    def sw(c):
        for s in range(2):
            for k in range(7):
                sent(c, s * 7 + k, a_send(c, s, k)[0])
            for k in range(8):
                sent(c, RS_KIND + s * 8 + k, r_move(c, s, k)[0])
        for k in range(10):
            sent(c, X_KIND + k, x_send(c, k)[0])

    def load(i, size):
        slot = i % 2
        return pltpu.make_async_copy(
            vt_hbm.at[pl.ds(pl.multiple_of(i * TILE, TILE), size)], stage.at[slot, pl.ds(0, size)], lsem.at[slot]
        )

    tiles, rest = width // TILE, width % TILE
    third = (tiles + 1) // 3

    def tv(c):
        def turned(i, carry):
            load(i, TILE).wait()
            v[:depth, pl.ds(pl.multiple_of(i * TILE, TILE), TILE)] = stage[i % 2].T
            pl.when(i + 2 < tiles)(lambda: load(i + 2, TILE).start())
            pl.when(i + 2 == tiles)(lambda: load(tiles, rest).start())
            return carry

        lax.fori_loop(c * third, jnp.minimum((c + 1) * third, tiles), turned, 0)

        @pl.when(c == 2)
        def _():
            load(tiles, rest).wait()
            v[:depth, tiles * TILE :] = stage[tiles % 2, :rest].T

    load(0, TILE).start()
    load(1, TILE).start()
    rows_gap = pltpu.make_async_copy(row_hbm, rg, gsem)
    rows_gap.start()
    v[depth:, :] = jnp.zeros((v.shape[0] - depth, width), BF16)
    for c in range(chunks):
        ag[c, z, y, :, :depth] = a_ref[c * BLOCK : (c + 1) * BLOCK, :]
        ag[c, z, y, :, depth:] = jnp.zeros((BLOCK, ag.shape[-1] - depth), BF16)

    barrier = pltpu.get_barrier_semaphore()
    for to in peer.values():
        pl.semaphore_signal(barrier, inc=1, device_id=to, device_id_type=MESH)
    pl.semaphore_wait(barrier, len(peer))

    final = final_ref.shape[-1]
    inner, outer = col * width, (row * 16 + col) * final
    inner_row = inner // 128
    outer_row = jnp.minimum(outer // 128, col_ref.shape[0] - 3)
    for k in range(12):
        near[:, 128 * k : 128 * (k + 1)] = col_ref[pl.ds(inner_row + k, 1), :]
    for k in range(3):
        near[:, 1536 + 128 * k : 1664 + 128 * k] = col_ref[pl.ds(outer_row + k, 1), :]
    cg[...] = pltpu.roll(jnp.broadcast_to(near[:, :1536], (8, 1536)), (1536 - (inner - inner_row * 128)) % 1536, 1)
    shifted = pltpu.roll(jnp.broadcast_to(near[:, 1536:], (8, 384)), (384 - (outer - outer_row * 128)) % 384, 1)
    final_ref[...] = shifted[0:1, :final]
    rows_gap.wait()

    ops = dict(tv=tv, a0=a0, a1=a1, a2=a2, a3=a3, m1=m1, b1=b1, b2=b2, b3=b3, b4=b4, b5=b5, m2=m2, r1=r1, r2=r2, r3=r3, r4=r4, sw=sw)

    def step(t, carry):
        for name, late in PLAN:
            c = t - late
            pl.when(jnp.logical_and(c >= 0, c < (3 if name == "tv" else chunks)))(functools.partial(ops[name], c))
        return carry

    lax.fori_loop(0, chunks + max(late for _, late in PLAN), step, 0)
    for k in range(chunks):
        lanes = pl.ds(k * 256, 256)
        rows = out.reshape(16 * chunks * BLOCK, 256)[lanes, :]
        o_ref[:, lanes] = rows.T[:final]


def on_device(amplitudes, integrals, row_gap, col_gap):
    rows, depth = amplitudes.shape
    width = integrals.shape[1]
    chunks = rows // BLOCK
    final = depth // 16
    padded = (depth + 127) // 128 * 128

    vm = pl.BlockSpec(memory_space=pltpu.VMEM)
    anywhere = pl.BlockSpec(memory_space=pl.ANY)
    cycle_two, here = pl.pallas_call(
        kernel,
        out_shape=(
            jax.ShapeDtypeStruct((final, 16 * rows), F32),
            jax.ShapeDtypeStruct((1, final), F32),
        ),
        in_specs=[vm, anywhere, anywhere, vm],
        out_specs=(vm, vm),
        scratch_shapes=[
            pltpu.SMEM((16 * rows,), F32),
            pltpu.VMEM((1, 1920), F32),
            pltpu.VMEM((8, 1536), F32),
            pltpu.VMEM((padded, width), BF16),
            pltpu.VMEM((2, TILE, depth), BF16),
            pltpu.VMEM((chunks, 4, 4, BLOCK, padded), BF16),
            pltpu.VMEM((chunks, 256, width), BF16),
            pltpu.VMEM((chunks, 128, width), BF16),
            pltpu.VMEM((chunks, 32, width), BF16),
            pltpu.VMEM((chunks, 2, 32, width), BF16),
            pltpu.VMEM((chunks, 256, width), BF16),
            pltpu.VMEM((2, chunks, 4, 4, WINDOW, 128), BF16),
            pltpu.VMEM((2, chunks, 4, WINDOW, 128), BF16),
            pltpu.VMEM((2, chunks, 2, 4, WINDOW, 128), BF16),
            pltpu.VMEM((2, chunks, WINDOW, 128), BF16),
            pltpu.VMEM((2, chunks, 2, WINDOW, 128), BF16),
            pltpu.VMEM((16, chunks, BLOCK, 256), F32),
            pltpu.SemaphoreType.DMA,
            pltpu.SemaphoreType.DMA((2,)),
            pltpu.SemaphoreType.DMA((chunks, KINDS)),
            pltpu.SemaphoreType.DMA((chunks, KINDS)),
        ],
        compiler_params=pltpu.CompilerParams(
            collective_id=0, has_side_effects=True, vmem_limit_bytes=62 * 1024 * 1024
        ),
        cost_estimate=pl.CostEstimate(
            flops=4 * 16 * rows * depth * width, bytes_accessed=2 * depth * width, transcendentals=0
        ),
    )(amplitudes, integrals.T, row_gap, col_gap.reshape(-1, 128))
    return (cycle_two.T / (row_gap[:, None] + here)).astype(BF16)


def solution(mesh):
    return jax.shard_map(
        on_device,
        mesh=mesh,
        in_specs=(P("col", "row"), P("row", "col"), P(), P()),
        out_specs=P(None, ("row", "col")),
        check_vma=False,
    )
```

```python
import functools

import jax
import jax.numpy as jnp
from jax import lax
from jax.experimental import pallas as pl
from jax.experimental.pallas import tpu as pltpu
from jax.sharding import PartitionSpec as P

MESH = pl.DeviceIdType.MESH
F32 = jnp.float32
BF16 = jnp.bfloat16

BLOCK = 16
SPLIT = 1408
WINDOW = 192
STRIDE = 176
TILE = 128
X_KIND = 14
RS_KIND = 24
KINDS = 40

PLAN = (
    ("r1", 8),
    ("r2", 10),
    ("a0", 0),
    ("m1", 3),
    ("b2", 4),
    ("b4", 5),
    ("r3", 12),
    ("a3", 2),
    ("a2", 1),
    ("r4", 14),
    ("sw", 14),
    ("tv", 0),
    ("a1", 0),
    ("m2", 6),
    ("b1", 3),
    ("b3", 4),
    ("b5", 5),
)


def kernel(
    a_ref, vt_hbm, row_hbm, col_ref, o_ref, final_ref,
    rg, near, cg, v, stage, turned, ag, c1, cx, xo, xn, sg, w, ro1, rn1, ro2, rn2, out, gsem, lsem, send, recv,
):
    chunks = ag.shape[0]
    depth, width = a_ref.shape[1], v.shape[1]
    group = depth // 4
    row, col = lax.axis_index("row"), lax.axis_index("col")
    x, core = row // 2, row % 2
    z, y = col // 4, col % 4
    half = core * 128
    other = 128 - half

    def around(index):
        return {0: index, 1: lax.rem(index + 1, 4), 2: lax.rem(index + 2, 4), -1: lax.rem(index + 3, 4)}

    xs, ys, zs = around(x), around(y), around(z)
    at = {"z": zs, "y": ys}
    peer = {
        ("x", 1): (xs[1] * 2 + core, col),
        ("x", -1): (xs[-1] * 2 + core, col),
        ("y", 1): (row, z * 4 + ys[1]),
        ("y", -1): (row, z * 4 + ys[-1]),
        ("z", 1): (row, zs[1] * 4 + y),
        ("z", -1): (row, zs[-1] * 4 + y),
        "core": (x * 2 + 1 - core, col),
    }
    strips = {step: half + index * 32 for step, index in xs.items()}
    gather = (("y", "z", pl.ds(0, SPLIT)), ("z", "y", pl.ds(SPLIT, ag.shape[-1] - SPLIT)))
    scatter = (("z", "y"), ("y", "z"))

    def copy(c, kind, src, dst, to):
        return pltpu.make_async_remote_copy(
            src_ref=src, dst_ref=dst, send_sem=send.at[c, kind], recv_sem=recv.at[c, kind],
            device_id=to, device_id_type=MESH,
        )

    def arrived(c, kind, dst):
        copy(c, kind, dst, dst, peer["core"]).wait_recv()

    def sent(c, kind, src):
        copy(c, kind, src, src, peer["core"]).wait_send()

    def block(s, c, step):
        first, _, lanes = gather[s]
        f = at[first][step]
        return ag.at[c, z, f, :, lanes] if first == "y" else ag.at[c, f, y, :, lanes]

    def line(s, c, step, start=0, size=4):
        first, second, lanes = gather[s]
        g, part = at[second][step], pl.ds(start, size)
        return ag.at[c, g, part, :, lanes] if first == "y" else ag.at[c, part, g, :, lanes]

    def a_send(c, s, k, d=1):
        first, second, _ = gather[s]
        if k == 0:
            return block(s, c, 0), peer[first, 1]
        if k == 1:
            return block(s, c, 0), peer[first, -1]
        if k == 2:
            return block(s, c, -d), peer[first, d]
        if k == 3:
            return line(s, c, 0), peer[second, 1]
        if k == 4:
            return line(s, c, 0), peer[second, -1]
        if k == 5:
            return line(s, c, -1, 0, 2), peer[second, 1]
        return line(s, c, 1, 2, 2), peer[second, -1]

    def a_land(c, s, k):
        if k < 3:
            return block(s, c, (-1, 1, 2)[k])
        if k < 5:
            return line(s, c, (-1, 1)[k - 3])
        return line(s, c, 2, 2 * (k - 5), 2)

    def a_start(c, s, k, d=1):
        src, to = a_send(c, s, k, d)
        copy(c, s * 7 + k, src, src, to).start()

    def a_wait(c, s, k):
        arrived(c, s * 7 + k, a_land(c, s, k))

    def a0(c):
        for s in range(2):
            a_start(c, s, 0)
            a_start(c, s, 1)

    def a1(c):
        def forward(d):
            for s in range(2):
                a_wait(c, s, 0 if d == 1 else 1)
                a_start(c, s, 2, d)

        pl.when(c % 2 == 0)(lambda: forward(1))
        pl.when(c % 2 == 1)(lambda: forward(-1))

    def a2(c):
        pl.when(c % 2 == 0)(lambda: [a_wait(c, s, 1) for s in range(2)] and None)
        pl.when(c % 2 == 1)(lambda: [a_wait(c, s, 0) for s in range(2)] and None)
        for s in range(2):
            a_wait(c, s, 2)
            a_start(c, s, 3)
            a_start(c, s, 4)

    def a3(c):
        for s in range(2):
            a_wait(c, s, 3)
            a_start(c, s, 5)
            a_wait(c, s, 4)
            a_start(c, s, 6)

    def m1(c):
        for s in range(2):
            a_wait(c, s, 5)
            a_wait(c, s, 6)
        rows = ag[c].reshape(16 * BLOCK, ag.shape[-1])
        for lo in range(0, width, 512):
            hi = min(lo + 512, width)
            c1[c, :, lo:hi] = jnp.dot(rows, v[:, lo:hi], preferred_element_type=F32).astype(BF16)
        x_start(c, 0)

    def piece(step, start=0, size=32):
        return pl.ds(pl.multiple_of(strips[step] + start, 16), size)

    def x_send(c, k):
        if k == 0:
            return c1.at[c, pl.ds(pl.multiple_of(other, 128), 128)], cx.at[c], peer["core"]
        if k == 9:
            src = sg.at[c, pl.ds(pl.multiple_of(half, 128), 128)]
            return src, src, peer["core"]
        d = 1 if k % 2 == 1 else -1
        part = pl.ds(8 - 8 * d, 16)
        if k < 3:
            return c1.at[c, piece(2, 8 - 8 * d, 16)], xo.at[c, part], peer["x", d]
        if k < 5:
            return c1.at[c, piece(d)], xn.at[c, (k - 3)], peer["x", d]
        src = sg.at[c, piece(0) if k < 7 else piece(-d, 8 - 8 * d, 16)]
        return src, src, peer["x", d]

    def x_land(c, k):
        if k < 5:
            return x_send(c, k)[1]
        if k == 9:
            return sg.at[c, pl.ds(pl.multiple_of(other, 128), 128)]
        d = 1 if k % 2 == 1 else -1
        return sg.at[c, piece(-d) if k < 7 else piece(2, 8 - 8 * d, 16)]

    def x_start(c, k):
        src, dst, to = x_send(c, k)
        copy(c, X_KIND + k, src, dst, to).start()

    def x_wait(c, k):
        arrived(c, X_KIND + k, x_land(c, k))

    def b1(c):
        x_wait(c, 0)
        rows = pl.ds(pl.multiple_of(half, 128), 128)
        c1[c, rows, :] = (c1[c, rows, :].astype(F32) + cx[c].astype(F32)).astype(BF16)
        x_start(c, 1)
        x_start(c, 2)

    def b2(c):
        for k, step in ((1, 1), (2, -1)):
            x_wait(c, k)
            part, rows = pl.ds(16 * (k - 1), 16), piece(step, 16 * (k - 1), 16)
            c1[c, rows, :] = (c1[c, rows, :].astype(F32) + xo[c, part].astype(F32)).astype(BF16)
            x_start(c, k + 2)

    first_row = (core * 8 + x * 2) * (chunks * BLOCK)

    def b3(c):
        gap = jnp.zeros((32, 128), F32)
        index = lax.broadcasted_iota(jnp.int32, (32, 128), 0)
        for k in range(32):
            value = rg[first_row + (k // BLOCK) * (chunks * BLOCK) + c * BLOCK + k % BLOCK]
            gap = jnp.where(index == k, value, gap)
        x_wait(c, 3)
        x_wait(c, 4)
        rows = piece(0)
        total = c1[c, rows, :].astype(F32) + xn[c, 0].astype(F32) + xn[c, 1].astype(F32)
        sg[c, rows, :] = (total / (gap[:, :1] + cg[0:1, :width])).astype(BF16)
        x_start(c, 5)
        x_start(c, 6)

    def b4(c):
        for k in (5, 6):
            x_wait(c, k)
            x_start(c, k + 2)

    def b5(c):
        x_wait(c, 7)
        x_wait(c, 8)
        x_start(c, 9)

    def r_move(c, s, k):
        first, second = scatter[s]
        fs, gs = at[first], at[second]
        d = 1 if k % 2 == 0 else -1
        if k < 2:
            part = pl.ds(2 * k, 2)
            return w.at[s, c, fs[2], part], ro1.at[s, c, part], peer[first, d]
        if k < 4:
            return w.at[s, c, fs[d]], rn1.at[s, c, k - 2], peer[first, d]
        if k < 6:
            part = pl.ds((k - 4) * (WINDOW // 2), WINDOW // 2)
            return w.at[s, c, fs[0], gs[2], part], ro2.at[s, c, part], peer[second, d]
        return w.at[s, c, fs[0], gs[d]], rn2.at[s, c, k - 6], peer[second, d]

    def r_start(c, s, k):
        src, dst, to = r_move(c, s, k)
        copy(c, RS_KIND + s * 8 + k, src, dst, to).start()

    def r_wait(c, s, k):
        arrived(c, RS_KIND + s * 8 + k, r_move(c, s, k)[1])

    def m2(c):
        x_wait(c, 9)

        turned[...] = sg[c].T

        def rows_of(q, carry):
            part = jnp.dot(
                v[pl.ds(pl.multiple_of(q * group, 16), group), :], turned[...], preferred_element_type=F32
            ).astype(BF16)
            for p in range(4):
                piece = part[p * STRIDE : p * STRIDE + WINDOW]
                w[0, c, q, p] = piece[:, :128]
                w[1, c, p, q] = piece[:, 128:]
            return carry

        lax.fori_loop(0, 4, rows_of, 0)
        for s in range(2):
            r_start(c, s, 0)
            r_start(c, s, 1)

    def r1(c):
        for s in range(2):
            up, down = at[scatter[s][0]][1], at[scatter[s][0]][-1]
            r_wait(c, s, 0)
            w[s, c, up, 0:2] = (w[s, c, up, 0:2].astype(F32) + ro1[s, c, 0:2].astype(F32)).astype(BF16)
            r_start(c, s, 2)
            r_wait(c, s, 1)
            w[s, c, down, 2:4] = (w[s, c, down, 2:4].astype(F32) + ro1[s, c, 2:4].astype(F32)).astype(BF16)
            r_start(c, s, 3)

    def r2(c):
        for s in range(2):
            f = at[scatter[s][0]][0]
            r_wait(c, s, 2)
            r_wait(c, s, 3)
            total = w[s, c, f].astype(F32) + rn1[s, c, 0].astype(F32) + rn1[s, c, 1].astype(F32)
            w[s, c, f] = total.astype(BF16)
            r_start(c, s, 4)
            r_start(c, s, 5)

    def r3(c):
        h = WINDOW // 2
        for s in range(2):
            f, gs = at[scatter[s][0]][0], at[scatter[s][1]]
            up, down = gs[1], gs[-1]
            r_wait(c, s, 4)
            w[s, c, f, up, :h] = (w[s, c, f, up, :h].astype(F32) + ro2[s, c, :h].astype(F32)).astype(BF16)
            r_start(c, s, 6)
            r_wait(c, s, 5)
            w[s, c, f, down, h:] = (w[s, c, f, down, h:].astype(F32) + ro2[s, c, h:].astype(F32)).astype(BF16)
            r_start(c, s, 7)

    def r4(c):
        sums = []
        for s in range(2):
            f, g = at[scatter[s][0]][0], at[scatter[s][1]][0]
            r_wait(c, s, 6)
            r_wait(c, s, 7)
            sums.append(w[s, c, f, g].astype(F32) + rn2[s, c, 0].astype(F32) + rn2[s, c, 1].astype(F32))
        total = jnp.concatenate(sums, axis=1)
        total = jnp.concatenate([total, jnp.zeros((256 - WINDOW, 256), F32)], axis=0)
        total = pltpu.roll(total, (256 - 4 * y) % 256, 0)
        out[:, c] = total.T.reshape(16, BLOCK, 256)

    def sw(c):
        for s in range(2):
            for k in range(7):
                sent(c, s * 7 + k, a_send(c, s, k)[0])
            for k in range(8):
                sent(c, RS_KIND + s * 8 + k, r_move(c, s, k)[0])
        for k in range(10):
            sent(c, X_KIND + k, x_send(c, k)[0])

    def load(i, size):
        slot = i % 2
        return pltpu.make_async_copy(
            vt_hbm.at[pl.ds(pl.multiple_of(i * TILE, TILE), size)], stage.at[slot, pl.ds(0, size)], lsem.at[slot]
        )

    tiles, rest = width // TILE, width % TILE
    third = (tiles + 1) // 3

    def tv(c):
        def turn(i, carry):
            load(i, TILE).wait()
            v[:depth, pl.ds(pl.multiple_of(i * TILE, TILE), TILE)] = stage[i % 2].T
            pl.when(i + 2 < tiles)(lambda: load(i + 2, TILE).start())
            pl.when(i + 2 == tiles)(lambda: load(tiles, rest).start())
            return carry

        lax.fori_loop(c * third, jnp.minimum((c + 1) * third, tiles), turn, 0)

        @pl.when(c == 2)
        def _():
            load(tiles, rest).wait()
            v[:depth, tiles * TILE :] = stage[tiles % 2, :rest].T

    load(0, TILE).start()
    load(1, TILE).start()
    rows_gap = pltpu.make_async_copy(row_hbm, rg, gsem)
    rows_gap.start()
    v[depth:, :] = jnp.zeros((v.shape[0] - depth, width), BF16)
    for c in range(chunks):
        ag[c, z, y, :, :depth] = a_ref[c * BLOCK : (c + 1) * BLOCK, :]
        ag[c, z, y, :, depth:] = jnp.zeros((BLOCK, ag.shape[-1] - depth), BF16)

    barrier = pltpu.get_barrier_semaphore()
    for to in peer.values():
        pl.semaphore_signal(barrier, inc=1, device_id=to, device_id_type=MESH)
    pl.semaphore_wait(barrier, len(peer))

    final = final_ref.shape[-1]
    inner, outer = col * width, (row * 16 + col) * final
    inner_row = inner // 128
    outer_row = jnp.minimum(outer // 128, col_ref.shape[0] - 3)
    for k in range(12):
        near[:, 128 * k : 128 * (k + 1)] = col_ref[pl.ds(inner_row + k, 1), :]
    for k in range(3):
        near[:, 1536 + 128 * k : 1664 + 128 * k] = col_ref[pl.ds(outer_row + k, 1), :]
    cg[...] = pltpu.roll(jnp.broadcast_to(near[:, :1536], (8, 1536)), (1536 - (inner - inner_row * 128)) % 1536, 1)
    shifted = pltpu.roll(jnp.broadcast_to(near[:, 1536:], (8, 384)), (384 - (outer - outer_row * 128)) % 384, 1)
    final_ref[...] = shifted[0:1, :final]
    rows_gap.wait()

    ops = dict(tv=tv, a0=a0, a1=a1, a2=a2, a3=a3, m1=m1, b1=b1, b2=b2, b3=b3, b4=b4, b5=b5, m2=m2, r1=r1, r2=r2, r3=r3, r4=r4, sw=sw)

    def step(t, carry):
        for name, late in PLAN:
            c = t - late
            pl.when(jnp.logical_and(c >= 0, c < (3 if name == "tv" else chunks)))(functools.partial(ops[name], c))
        return carry

    lax.fori_loop(0, chunks + max(late for _, late in PLAN), step, 0)
    for k in range(chunks):
        lanes = pl.ds(k * 256, 256)
        rows = out.reshape(16 * chunks * BLOCK, 256)[lanes, :]
        o_ref[:, lanes] = rows.T[:final]


def on_device(amplitudes, integrals, row_gap, col_gap):
    rows, depth = amplitudes.shape
    width = integrals.shape[1]
    chunks = rows // BLOCK
    final = depth // 16
    padded = (depth + 127) // 128 * 128

    vm = pl.BlockSpec(memory_space=pltpu.VMEM)
    anywhere = pl.BlockSpec(memory_space=pl.ANY)
    cycle_two, here = pl.pallas_call(
        kernel,
        out_shape=(
            jax.ShapeDtypeStruct((final, 16 * rows), F32),
            jax.ShapeDtypeStruct((1, final), F32),
        ),
        in_specs=[vm, anywhere, anywhere, vm],
        out_specs=(vm, vm),
        scratch_shapes=[
            pltpu.SMEM((16 * rows,), F32),
            pltpu.VMEM((1, 1920), F32),
            pltpu.VMEM((8, 1536), F32),
            pltpu.VMEM((padded, width), BF16),
            pltpu.VMEM((2, TILE, depth), BF16),
            pltpu.VMEM((width, 256), BF16),
            pltpu.VMEM((chunks, 4, 4, BLOCK, padded), BF16),
            pltpu.VMEM((chunks, 256, width), BF16),
            pltpu.VMEM((chunks, 128, width), BF16),
            pltpu.VMEM((chunks, 32, width), BF16),
            pltpu.VMEM((chunks, 2, 32, width), BF16),
            pltpu.VMEM((chunks, 256, width), BF16),
            pltpu.VMEM((2, chunks, 4, 4, WINDOW, 128), BF16),
            pltpu.VMEM((2, chunks, 4, WINDOW, 128), BF16),
            pltpu.VMEM((2, chunks, 2, 4, WINDOW, 128), BF16),
            pltpu.VMEM((2, chunks, WINDOW, 128), BF16),
            pltpu.VMEM((2, chunks, 2, WINDOW, 128), BF16),
            pltpu.VMEM((16, chunks, BLOCK, 256), F32),
            pltpu.SemaphoreType.DMA,
            pltpu.SemaphoreType.DMA((2,)),
            pltpu.SemaphoreType.DMA((chunks, KINDS)),
            pltpu.SemaphoreType.DMA((chunks, KINDS)),
        ],
        compiler_params=pltpu.CompilerParams(
            collective_id=0, has_side_effects=True, vmem_limit_bytes=62 * 1024 * 1024
        ),
        cost_estimate=pl.CostEstimate(
            flops=4 * 16 * rows * depth * width, bytes_accessed=2 * depth * width, transcendentals=0
        ),
    )(amplitudes, integrals.T, row_gap, col_gap.reshape(-1, 128))
    return (cycle_two.T / (row_gap[:, None] + here)).astype(BF16)


def solution(mesh):
    return jax.shard_map(
        on_device,
        mesh=mesh,
        in_specs=(P("col", "row"), P("row", "col"), P(), P()),
        out_specs=P(None, ("row", "col")),
        check_vma=False,
    )
```

```python
import functools

import jax
import jax.numpy as jnp
from jax import lax
from jax.experimental import pallas as pl
from jax.experimental.pallas import tpu as pltpu
from jax.sharding import PartitionSpec as P

MESH = pl.DeviceIdType.MESH
F32 = jnp.float32
BF16 = jnp.bfloat16

BLOCK = 16
SPLIT = 1408
WINDOW = 192
STRIDE = 176
TILE = 128
CUT = 368
SLOTS = 4
X_KIND = 14
RS_KIND = 24
KINDS = 40

PLAN = (
    ("r1", 8),
    ("r2", 10),
    ("a0", 0),
    ("cw", 7),
    ("m1", 3),
    ("b2", 4),
    ("b4", 5),
    ("r3", 12),
    ("a3", 2),
    ("a2", 1),
    ("r4", 14),
    ("sw", 14),
    ("tv", 0),
    ("a1", 0),
    ("m2", 6),
    ("b1", 3),
    ("b3", 4),
    ("b5", 5),
)


def kernel(
    a_ref, vt_hbm, row_ref, col_ref, o_ref,
    near, cg, cf, rc, v, stage, turned, ag, c1, cx, xo, xn, sg, wq, w1, w2, ro1, rn1, ro2, rn2, out, lsem, send, recv,
):
    chunks = ag.shape[0]
    depth, width = a_ref.shape[1], v.shape[1]
    group, final = depth // 4, o_ref.shape[0]
    row, col = lax.axis_index("row"), lax.axis_index("col")
    x, core = row // 2, row % 2
    z, y = col // 4, col % 4
    half = core * 128
    other = 128 - half

    def around(index):
        return {0: index, 1: lax.rem(index + 1, 4), 2: lax.rem(index + 2, 4), -1: lax.rem(index + 3, 4)}

    xs, ys, zs = around(x), around(y), around(z)
    at = {"z": zs, "y": ys}
    peer = {
        ("x", 1): (xs[1] * 2 + core, col),
        ("x", -1): (xs[-1] * 2 + core, col),
        ("y", 1): (row, z * 4 + ys[1]),
        ("y", -1): (row, z * 4 + ys[-1]),
        ("z", 1): (row, zs[1] * 4 + y),
        ("z", -1): (row, zs[-1] * 4 + y),
        "core": (x * 2 + 1 - core, col),
    }
    strips = {step: half + index * 32 for step, index in xs.items()}
    gather = (("y", "z", pl.ds(0, SPLIT)), ("z", "y", pl.ds(SPLIT, ag.shape[-1] - SPLIT)))
    scatter = (("z", "y"), ("y", "z"))

    def copy(c, kind, src, dst, to):
        return pltpu.make_async_remote_copy(
            src_ref=src, dst_ref=dst, send_sem=send.at[c, kind], recv_sem=recv.at[c, kind],
            device_id=to, device_id_type=MESH,
        )

    def arrived(c, kind, dst):
        copy(c, kind, dst, dst, peer["core"]).wait_recv()

    def sent(c, kind, src):
        copy(c, kind, src, src, peer["core"]).wait_send()

    def block(s, c, step):
        first, _, lanes = gather[s]
        f = at[first][step]
        return ag.at[c, z, f, :, lanes] if first == "y" else ag.at[c, f, y, :, lanes]

    def line(s, c, step, start=0, size=4):
        first, second, lanes = gather[s]
        g, part = at[second][step], pl.ds(start, size)
        return ag.at[c, g, part, :, lanes] if first == "y" else ag.at[c, part, g, :, lanes]

    def a_send(c, s, k, d=1):
        first, second, _ = gather[s]
        if k == 0:
            return block(s, c, 0), peer[first, 1]
        if k == 1:
            return block(s, c, 0), peer[first, -1]
        if k == 2:
            return block(s, c, -d), peer[first, d]
        if k == 3:
            return line(s, c, 0), peer[second, 1]
        if k == 4:
            return line(s, c, 0), peer[second, -1]
        if k == 5:
            return line(s, c, -1, 0, 2), peer[second, 1]
        return line(s, c, 1, 2, 2), peer[second, -1]

    def a_land(c, s, k):
        if k < 3:
            return block(s, c, (-1, 1, 2)[k])
        if k < 5:
            return line(s, c, (-1, 1)[k - 3])
        return line(s, c, 2, 2 * (k - 5), 2)

    def a_start(c, s, k, d=1):
        src, to = a_send(c, s, k, d)
        copy(c, s * 7 + k, src, src, to).start()

    def a_wait(c, s, k):
        arrived(c, s * 7 + k, a_land(c, s, k))

    def a0(c):
        for s in range(2):
            a_start(c, s, 0)
            a_start(c, s, 1)

    def a1(c):
        def forward(d):
            for s in range(2):
                a_wait(c, s, 0 if d == 1 else 1)
                a_start(c, s, 2, d)

        pl.when(c % 2 == 0)(lambda: forward(1))
        pl.when(c % 2 == 1)(lambda: forward(-1))

    def a2(c):
        pl.when(c % 2 == 0)(lambda: [a_wait(c, s, 1) for s in range(2)] and None)
        pl.when(c % 2 == 1)(lambda: [a_wait(c, s, 0) for s in range(2)] and None)
        for s in range(2):
            a_wait(c, s, 2)
            a_start(c, s, 3)
            a_start(c, s, 4)

    def a3(c):
        for s in range(2):
            a_wait(c, s, 3)
            a_start(c, s, 5)
            a_wait(c, s, 4)
            a_start(c, s, 6)

    def m1(c):
        for s in range(2):
            a_wait(c, s, 5)
            a_wait(c, s, 6)
        rows = ag[c].reshape(16 * BLOCK, ag.shape[-1])
        for lo in range(0, width, 512):
            hi = min(lo + 512, width)
            c1[c % SLOTS, :, lo:hi] = jnp.dot(rows, v[:, lo:hi], preferred_element_type=F32).astype(BF16)
        x_start(c, 0)

    def piece(step, start=0, size=32):
        return pl.ds(pl.multiple_of(strips[step] + start, 16), size)

    def x_send(c, k):
        if k == 0:
            return c1.at[c % SLOTS, pl.ds(pl.multiple_of(other, 128), 128)], cx.at[c], peer["core"]
        if k == 9:
            src = sg.at[c, pl.ds(pl.multiple_of(half, 128), 128)]
            return src, src, peer["core"]
        d = 1 if k % 2 == 1 else -1
        part = pl.ds(8 - 8 * d, 16)
        if k < 3:
            return c1.at[c % SLOTS, piece(2, 8 - 8 * d, 16)], xo.at[c, part], peer["x", d]
        if k < 5:
            return c1.at[c % SLOTS, piece(d)], xn.at[c, (k - 3)], peer["x", d]
        src = sg.at[c, piece(0) if k < 7 else piece(-d, 8 - 8 * d, 16)]
        return src, src, peer["x", d]

    def x_land(c, k):
        if k < 5:
            return x_send(c, k)[1]
        if k == 9:
            return sg.at[c, pl.ds(pl.multiple_of(other, 128), 128)]
        d = 1 if k % 2 == 1 else -1
        return sg.at[c, piece(-d) if k < 7 else piece(2, 8 - 8 * d, 16)]

    def x_start(c, k):
        src, dst, to = x_send(c, k)
        copy(c, X_KIND + k, src, dst, to).start()

    def x_wait(c, k):
        arrived(c, X_KIND + k, x_land(c, k))

    def b1(c):
        x_wait(c, 0)
        rows = pl.ds(pl.multiple_of(half, 128), 128)
        c1[c % SLOTS, rows, :] = (c1[c % SLOTS, rows, :].astype(F32) + cx[c].astype(F32)).astype(BF16)
        x_start(c, 1)
        x_start(c, 2)

    def b2(c):
        for k, step in ((1, 1), (2, -1)):
            x_wait(c, k)
            part, rows = pl.ds(16 * (k - 1), 16), piece(step, 16 * (k - 1), 16)
            c1[c % SLOTS, rows, :] = (c1[c % SLOTS, rows, :].astype(F32) + xo[c, part].astype(F32)).astype(BF16)
            x_start(c, k + 2)

    def b3(c):
        gap = rc[pl.ds(core * 8 + x * 2, 2), c].reshape(32, 128)
        x_wait(c, 3)
        x_wait(c, 4)
        rows = piece(0)
        total = c1[c % SLOTS, rows, :].astype(F32) + xn[c, 0].astype(F32) + xn[c, 1].astype(F32)
        sg[c, rows, :] = (total / (gap[:, :1] + cg[0:1, :width])).astype(BF16)
        x_start(c, 5)
        x_start(c, 6)

    def b4(c):
        for k in (5, 6):
            x_wait(c, k)
            x_start(c, k + 2)

    def b5(c):
        x_wait(c, 7)
        x_wait(c, 8)
        x_start(c, 9)

    def r_move(c, s, k):
        first, second = scatter[s]
        fs, gs = at[first], at[second]
        d = 1 if k % 2 == 0 else -1
        if k < 2:
            part = pl.ds(0, CUT) if k == 0 else pl.ds(CUT, group - CUT)
            return w1.at[s, c, fs[2], part], ro1.at[s, c, part], peer[first, d]
        if k < 4:
            return w1.at[s, c, fs[d]], rn1.at[s, c, k - 2], peer[first, d]
        if k < 6:
            part = pl.ds((k - 4) * (WINDOW // 2), WINDOW // 2)
            return w2.at[s, c, gs[2], part], ro2.at[s, c, part], peer[second, d]
        return w2.at[s, c, gs[d]], rn2.at[s, c, k - 6], peer[second, d]

    def r_start(c, s, k):
        src, dst, to = r_move(c, s, k)
        copy(c, RS_KIND + s * 8 + k, src, dst, to).start()

    def r_wait(c, s, k):
        arrived(c, RS_KIND + s * 8 + k, r_move(c, s, k)[1])

    def m2(c):
        x_wait(c, 9)

        turned[...] = sg[c].T

        for q in range(4):
            part = jnp.dot(v[q * group : (q + 1) * group, :], turned[...], preferred_element_type=F32)
            w1[0, c, q] = part[:, :128].astype(BF16)
            for p in range(4):
                wq[p, q * final : (q + 1) * final] = part[p * final : (p + 1) * final, 128:]
        for p in range(4):
            w1[1, c, p] = wq[p].astype(BF16)
        for s in range(2):
            r_start(c, s, 0)
            r_start(c, s, 1)

    def r1(c):
        for s in range(2):
            up, down = at[scatter[s][0]][1], at[scatter[s][0]][-1]
            r_wait(c, s, 0)
            w1[s, c, up, :CUT] = (w1[s, c, up, :CUT].astype(F32) + ro1[s, c, :CUT].astype(F32)).astype(BF16)
            r_start(c, s, 2)
            r_wait(c, s, 1)
            w1[s, c, down, CUT:] = (w1[s, c, down, CUT:].astype(F32) + ro1[s, c, CUT:].astype(F32)).astype(BF16)
            r_start(c, s, 3)

    def r2(c):
        for s in range(2):
            f = at[scatter[s][0]][0]
            r_wait(c, s, 2)
            r_wait(c, s, 3)
            total = w1[s, c, f].astype(F32) + rn1[s, c, 0].astype(F32) + rn1[s, c, 1].astype(F32)
            total = total.astype(BF16)
            for p in range(4):
                w2[s, c, p] = total[p * STRIDE : p * STRIDE + WINDOW]
            r_start(c, s, 4)
            r_start(c, s, 5)

    def r3(c):
        h = WINDOW // 2
        for s in range(2):
            up, down = at[scatter[s][1]][1], at[scatter[s][1]][-1]
            r_wait(c, s, 4)
            w2[s, c, up, :h] = (w2[s, c, up, :h].astype(F32) + ro2[s, c, :h].astype(F32)).astype(BF16)
            r_start(c, s, 6)
            r_wait(c, s, 5)
            w2[s, c, down, h:] = (w2[s, c, down, h:].astype(F32) + ro2[s, c, h:].astype(F32)).astype(BF16)
            r_start(c, s, 7)

    def r4(c):
        sums = []
        for s in range(2):
            g = at[scatter[s][1]][0]
            r_wait(c, s, 6)
            r_wait(c, s, 7)
            total = w2[s, c, g].astype(F32) + rn2[s, c, 0].astype(F32) + rn2[s, c, 1].astype(F32)
            sums.append(pltpu.roll(total, lax.rem(WINDOW - 4 * g, WINDOW), 0))
        total = jnp.concatenate(sums, axis=1)
        total = jnp.concatenate([total, jnp.zeros((256 - WINDOW, 256), F32)], axis=0)
        gap = rc[:, c].reshape(256, 128)
        gap = jnp.concatenate([gap, gap], axis=1) + cf[0:1, :]
        out[:, c] = (total.T / gap).astype(BF16).reshape(16, BLOCK, 256)

    def cw(c):
        for k in range(5):
            sent(c, X_KIND + k, x_send(c, k)[0])

    def sw(c):
        for s in range(2):
            for k in range(7):
                sent(c, s * 7 + k, a_send(c, s, k)[0])
            for k in range(8):
                sent(c, RS_KIND + s * 8 + k, r_move(c, s, k)[0])
        for k in range(5, 10):
            sent(c, X_KIND + k, x_send(c, k)[0])

    def load(i, size):
        slot = i % 2
        return pltpu.make_async_copy(
            vt_hbm.at[pl.ds(pl.multiple_of(i * TILE, TILE), size)], stage.at[slot, pl.ds(0, size)], lsem.at[slot]
        )

    tiles, rest = width // TILE, width % TILE
    third = (tiles + 1) // 3

    def tv(c):
        def turn(i, carry):
            load(i, TILE).wait()
            v[:depth, pl.ds(pl.multiple_of(i * TILE, TILE), TILE)] = stage[i % 2].T
            pl.when(i + 2 < tiles)(lambda: load(i + 2, TILE).start())
            pl.when(i + 2 == tiles)(lambda: load(tiles, rest).start())
            return carry

        lax.fori_loop(c * third, jnp.minimum((c + 1) * third, tiles), turn, 0)

        @pl.when(c == 2)
        def _():
            load(tiles, rest).wait()
            v[:depth, tiles * TILE :] = stage[tiles % 2, :rest].T

    load(0, TILE).start()
    load(1, TILE).start()
    v[depth:, :] = jnp.zeros((v.shape[0] - depth, width), BF16)
    for c in range(chunks):
        ag[c, z, y, :, :depth] = a_ref[c * BLOCK : (c + 1) * BLOCK, :]
        ag[c, z, y, :, depth:] = jnp.zeros((BLOCK, ag.shape[-1] - depth), BF16)

    barrier = pltpu.get_barrier_semaphore()
    for to in peer.values():
        pl.semaphore_signal(barrier, inc=1, device_id=to, device_id_type=MESH)
    pl.semaphore_wait(barrier, len(peer))

    inner, outer = col * width, (row * 16 + col) * final
    inner_row = inner // 128
    outer_row = jnp.minimum(outer // 128, col_ref.shape[0] - 3)
    for k in range(12):
        near[:, 128 * k : 128 * (k + 1)] = col_ref[pl.ds(inner_row + k, 1), :]
    for k in range(3):
        near[:, 1536 + 128 * k : 1664 + 128 * k] = col_ref[pl.ds(outer_row + k, 1), :]
    cg[...] = pltpu.roll(jnp.broadcast_to(near[:, :1536], (8, 1536)), (1536 - (inner - inner_row * 128)) % 1536, 1)
    shifted = pltpu.roll(jnp.broadcast_to(near[:, 1536:], (8, 384)), (384 - (outer - outer_row * 128)) % 384, 1)
    cf[...] = shifted[:, :256]
    flat = rc.reshape(16 * chunks * BLOCK, 128)
    for k in range(row_ref.shape[0]):
        flat[k * 128 : (k + 1) * 128, :] = jnp.broadcast_to(row_ref[k : k + 1, :], (128, 128)).T

    ops = dict(tv=tv, cw=cw, a0=a0, a1=a1, a2=a2, a3=a3, m1=m1, b1=b1, b2=b2, b3=b3, b4=b4, b5=b5, m2=m2, r1=r1, r2=r2, r3=r3, r4=r4, sw=sw)

    def step(t, carry):
        for name, late in PLAN:
            c = t - late
            pl.when(jnp.logical_and(c >= 0, c < (3 if name == "tv" else chunks)))(functools.partial(ops[name], c))
        return carry

    lax.fori_loop(0, chunks + max(late for _, late in PLAN), step, 0)
    for k in range(chunks):
        lanes = pl.ds(k * 256, 256)
        rows = out.reshape(16 * chunks * BLOCK, 256)[lanes, :]
        o_ref[:, lanes] = rows.T[:final]


def on_device(amplitudes, integrals, row_gap, col_gap):
    rows, depth = amplitudes.shape
    width = integrals.shape[1]
    chunks = rows // BLOCK
    final = depth // 16
    padded = (depth + 127) // 128 * 128

    vm = pl.BlockSpec(memory_space=pltpu.VMEM)
    anywhere = pl.BlockSpec(memory_space=pl.ANY)
    updated = pl.pallas_call(
        kernel,
        out_shape=jax.ShapeDtypeStruct((final, 16 * rows), BF16),
        in_specs=[vm, anywhere, vm, vm],
        out_specs=vm,
        scratch_shapes=[
            pltpu.VMEM((1, 1920), F32),
            pltpu.VMEM((8, 1536), F32),
            pltpu.VMEM((8, 256), F32),
            pltpu.VMEM((16, chunks, BLOCK, 128), F32),
            pltpu.VMEM((padded, width), BF16),
            pltpu.VMEM((2, TILE, depth), BF16),
            pltpu.VMEM((width, 256), BF16),
            pltpu.VMEM((chunks, 4, 4, BLOCK, padded), BF16),
            pltpu.VMEM((SLOTS, 256, width), BF16),
            pltpu.VMEM((chunks, 128, width), BF16),
            pltpu.VMEM((chunks, 32, width), BF16),
            pltpu.VMEM((chunks, 2, 32, width), BF16),
            pltpu.VMEM((chunks, 256, width), BF16),
            pltpu.VMEM((4, depth // 4, 128), F32),
            pltpu.VMEM((2, chunks, 4, depth // 4, 128), BF16),
            pltpu.VMEM((2, chunks, 4, WINDOW, 128), BF16),
            pltpu.VMEM((2, chunks, depth // 4, 128), BF16),
            pltpu.VMEM((2, chunks, 2, depth // 4, 128), BF16),
            pltpu.VMEM((2, chunks, WINDOW, 128), BF16),
            pltpu.VMEM((2, chunks, 2, WINDOW, 128), BF16),
            pltpu.VMEM((16, chunks, BLOCK, 256), BF16),
            pltpu.SemaphoreType.DMA((2,)),
            pltpu.SemaphoreType.DMA((chunks, KINDS)),
            pltpu.SemaphoreType.DMA((chunks, KINDS)),
        ],
        compiler_params=pltpu.CompilerParams(
            collective_id=0, has_side_effects=True, vmem_limit_bytes=62 * 1024 * 1024
        ),
        cost_estimate=pl.CostEstimate(
            flops=4 * 16 * rows * depth * width, bytes_accessed=2 * depth * width, transcendentals=0
        ),
    )(amplitudes, integrals.T, row_gap.reshape(-1, 128), col_gap.reshape(-1, 128))
    return updated.T


def solution(mesh):
    return jax.shard_map(
        on_device,
        mesh=mesh,
        in_specs=(P("col", "row"), P("row", "col"), P(), P()),
        out_specs=P(None, ("row", "col")),
        check_vma=False,
    )
```

```python
import functools

import jax
import jax.numpy as jnp
from jax import lax
from jax.experimental import pallas as pl
from jax.experimental.pallas import tpu as pltpu
from jax.sharding import PartitionSpec as P

MESH = pl.DeviceIdType.MESH
F32 = jnp.float32
BF16 = jnp.bfloat16

BLOCK = 16
WINDOW = 192
STRIDE = 176
TILE = 128
CUT = 368
SLOTS = 4
X_KIND = 14
RS_KIND = 24
KINDS = 40

PLAN = (
    ("r1", 8),
    ("r2", 10),
    ("a0", 0),
    ("cw", 7),
    ("m1", 3),
    ("b2", 4),
    ("b4", 5),
    ("r3", 12),
    ("a3", 2),
    ("a2", 1),
    ("r4", 14),
    ("sw", 14),
    ("tv", 0),
    ("gp", 3),
    ("a1", 0),
    ("m2", 6),
    ("b1", 3),
    ("b3", 4),
    ("b5", 5),
)


def kernel(
    a_ref, vt_hbm, row_ref, col_ref, o_ref,
    near, cg, cf, rc, v, stage, turned, ag, tg, c1, cx, xo, xn, sg, wq, w1, w2, ro1, rn1, ro2, rn2, out, lsem, tsend, trecv, send, recv,
):
    chunks = ag.shape[0]
    depth, width = a_ref.shape[1], v.shape[1]
    group, final = depth // 4, o_ref.shape[0]
    row, col = lax.axis_index("row"), lax.axis_index("col")
    x, core = row // 2, row % 2
    z, y = col // 4, col % 4
    half = core * 128
    other = 128 - half

    def around(index):
        return {0: index, 1: lax.rem(index + 1, 4), 2: lax.rem(index + 2, 4), -1: lax.rem(index + 3, 4)}

    xs, ys, zs = around(x), around(y), around(z)
    at = {"z": zs, "y": ys}
    peer = {
        ("x", 1): (xs[1] * 2 + core, col),
        ("x", -1): (xs[-1] * 2 + core, col),
        ("y", 1): (row, z * 4 + ys[1]),
        ("y", -1): (row, z * 4 + ys[-1]),
        ("z", 1): (row, zs[1] * 4 + y),
        ("z", -1): (row, zs[-1] * 4 + y),
        "core": (x * 2 + 1 - core, col),
    }
    strips = {step: half + index * 32 for step, index in xs.items()}
    main = ag.shape[-1]
    gather = (("y", "z", pl.ds(0, main // 2)), ("z", "y", pl.ds(main // 2, main // 2)))
    scatter = (("z", "y"), ("y", "z"))

    barrier = pltpu.get_barrier_semaphore()
    for to in peer.values():
        pl.semaphore_signal(barrier, inc=1, device_id=to, device_id_type=MESH)

    def copy(c, kind, src, dst, to):
        return pltpu.make_async_remote_copy(
            src_ref=src, dst_ref=dst, send_sem=send.at[c, kind], recv_sem=recv.at[c, kind],
            device_id=to, device_id_type=MESH,
        )

    def arrived(c, kind, dst):
        copy(c, kind, dst, dst, peer["core"]).wait_recv()

    def sent(c, kind, src):
        copy(c, kind, src, src, peer["core"]).wait_send()

    def block(s, c, step):
        first, _, lanes = gather[s]
        f = at[first][step]
        return ag.at[c, z, f, :, lanes] if first == "y" else ag.at[c, f, y, :, lanes]

    def line(s, c, step, start=0, size=4):
        first, second, lanes = gather[s]
        g, part = at[second][step], pl.ds(start, size)
        return ag.at[c, g, part, :, lanes] if first == "y" else ag.at[c, part, g, :, lanes]

    def a_send(c, s, k, d=1):
        first, second, _ = gather[s]
        if k == 0:
            return block(s, c, 0), peer[first, 1]
        if k == 1:
            return block(s, c, 0), peer[first, -1]
        if k == 2:
            return block(s, c, -d), peer[first, d]
        if k == 3:
            return line(s, c, 0), peer[second, 1]
        if k == 4:
            return line(s, c, 0), peer[second, -1]
        if k == 5:
            return line(s, c, -1, 0, 2), peer[second, 1]
        return line(s, c, 1, 2, 2), peer[second, -1]

    def a_land(c, s, k):
        if k < 3:
            return block(s, c, (-1, 1, 2)[k])
        if k < 5:
            return line(s, c, (-1, 1)[k - 3])
        return line(s, c, 2, 2 * (k - 5), 2)

    def a_start(c, s, k, d=1):
        src, to = a_send(c, s, k, d)
        copy(c, s * 7 + k, src, src, to).start()

    def a_wait(c, s, k):
        arrived(c, s * 7 + k, a_land(c, s, k))

    def t_line(step, start=0, size=4):
        return tg.at[zs[step], pl.ds(start, size)]

    def t_send(k):
        return (
            (tg.at[z, y], peer["y", 1]),
            (tg.at[z, y], peer["y", -1]),
            (tg.at[z, ys[-1]], peer["y", 1]),
            (t_line(0), peer["z", 1]),
            (t_line(0), peer["z", -1]),
            (t_line(-1, 0, 2), peer["z", 1]),
            (t_line(1, 2, 2), peer["z", -1]),
        )[k]

    def t_land(k):
        return (
            tg.at[z, ys[-1]], tg.at[z, ys[1]], tg.at[z, ys[2]],
            t_line(-1), t_line(1), t_line(2, 0, 2), t_line(2, 2, 2),
        )[k]

    def t_copy(k, src, to):
        return pltpu.make_async_remote_copy(
            src_ref=src, dst_ref=src, send_sem=tsend.at[k], recv_sem=trecv.at[k], device_id=to, device_id_type=MESH
        )

    def t_start(*kinds):
        for k in kinds:
            t_copy(k, *t_send(k)).start()

    def t_wait(*kinds):
        for k in kinds:
            t_copy(k, t_land(k), peer["core"]).wait_recv()

    def a0(c):
        ag[c, z, y] = a_ref[pl.ds(pl.multiple_of(c * BLOCK, BLOCK), BLOCK), :main]
        for s in range(2):
            a_start(c, s, 0)
            a_start(c, s, 1)
        pl.when(c == 0)(lambda: t_start(0, 1))

    def a1(c):
        def forward(d):
            for s in range(2):
                a_wait(c, s, 0 if d == 1 else 1)
                a_start(c, s, 2, d)

        @pl.when(c == 0)
        def _():
            t_wait(0)
            t_start(2)

        pl.when(c % 2 == 0)(lambda: forward(1))
        pl.when(c % 2 == 1)(lambda: forward(-1))

    def a2(c):
        pl.when(c % 2 == 0)(lambda: [a_wait(c, s, 1) for s in range(2)] and None)
        pl.when(c % 2 == 1)(lambda: [a_wait(c, s, 0) for s in range(2)] and None)
        for s in range(2):
            a_wait(c, s, 2)
            a_start(c, s, 3)
            a_start(c, s, 4)

        @pl.when(c == 0)
        def _():
            t_wait(1, 2)
            t_start(3, 4)

    def a3(c):
        for s in range(2):
            a_wait(c, s, 3)
            a_start(c, s, 5)
            a_wait(c, s, 4)
            a_start(c, s, 6)

        @pl.when(c == 0)
        def _():
            t_wait(3)
            t_start(5)
            t_wait(4)
            t_start(6)

    def m1(c):
        for s in range(2):
            a_wait(c, s, 5)
            a_wait(c, s, 6)
        pl.when(c == 0)(lambda: t_wait(5, 6))
        ends = tg[:, :, pl.ds(pl.multiple_of(c // 2 * BLOCK, BLOCK), BLOCK), :].reshape(16 * BLOCK, 128)
        mine = lax.broadcasted_iota(jnp.int32, (16 * BLOCK, 128), 1) // 64 == c % 2
        ends = jnp.where(mine, ends.astype(F32), 0.0).astype(BF16)
        rows = jnp.concatenate([ag[c].reshape(16 * BLOCK, main), ends], axis=1)
        for lo in range(0, width, 512):
            hi = min(lo + 512, width)
            c1[c % SLOTS, :, lo:hi] = jnp.dot(rows, v[:, lo:hi], preferred_element_type=F32).astype(BF16)
        x_start(c, 0)

    def piece(step, start=0, size=32):
        return pl.ds(pl.multiple_of(strips[step] + start, 16), size)

    def x_send(c, k):
        if k == 0:
            return c1.at[c % SLOTS, pl.ds(pl.multiple_of(other, 128), 128)], cx.at[c], peer["core"]
        if k == 9:
            src = sg.at[c, pl.ds(pl.multiple_of(half, 128), 128)]
            return src, src, peer["core"]
        d = 1 if k % 2 == 1 else -1
        part = pl.ds(8 - 8 * d, 16)
        if k < 3:
            return c1.at[c % SLOTS, piece(2, 8 - 8 * d, 16)], xo.at[c, part], peer["x", d]
        if k < 5:
            return c1.at[c % SLOTS, piece(d)], xn.at[c, (k - 3)], peer["x", d]
        src = sg.at[c, piece(0) if k < 7 else piece(-d, 8 - 8 * d, 16)]
        return src, src, peer["x", d]

    def x_land(c, k):
        if k < 5:
            return x_send(c, k)[1]
        if k == 9:
            return sg.at[c, pl.ds(pl.multiple_of(other, 128), 128)]
        d = 1 if k % 2 == 1 else -1
        return sg.at[c, piece(-d) if k < 7 else piece(2, 8 - 8 * d, 16)]

    def x_start(c, k):
        src, dst, to = x_send(c, k)
        copy(c, X_KIND + k, src, dst, to).start()

    def x_wait(c, k):
        arrived(c, X_KIND + k, x_land(c, k))

    def b1(c):
        x_wait(c, 0)
        rows = pl.ds(pl.multiple_of(half, 128), 128)
        c1[c % SLOTS, rows, :] = (c1[c % SLOTS, rows, :].astype(F32) + cx[c].astype(F32)).astype(BF16)
        x_start(c, 1)
        x_start(c, 2)

    def b2(c):
        for k, step in ((1, 1), (2, -1)):
            x_wait(c, k)
            part, rows = pl.ds(16 * (k - 1), 16), piece(step, 16 * (k - 1), 16)
            c1[c % SLOTS, rows, :] = (c1[c % SLOTS, rows, :].astype(F32) + xo[c, part].astype(F32)).astype(BF16)
            x_start(c, k + 2)

    def b3(c):
        gap = rc[pl.ds(core * 8 + x * 2, 2), c].reshape(32, 128)
        x_wait(c, 3)
        x_wait(c, 4)
        rows = piece(0)
        total = c1[c % SLOTS, rows, :].astype(F32) + xn[c, 0].astype(F32) + xn[c, 1].astype(F32)
        sg[c, rows, :] = (total / (gap[:, :1] + cg[0:1, :width])).astype(BF16)
        x_start(c, 5)
        x_start(c, 6)

    def b4(c):
        for k in (5, 6):
            x_wait(c, k)
            x_start(c, k + 2)

    def b5(c):
        x_wait(c, 7)
        x_wait(c, 8)
        x_start(c, 9)

    def r_move(c, s, k):
        first, second = scatter[s]
        fs, gs = at[first], at[second]
        d = 1 if k % 2 == 0 else -1
        if k < 2:
            part = pl.ds(0, CUT) if k == 0 else pl.ds(CUT, group - CUT)
            return w1.at[s, c, fs[2], part], ro1.at[s, c, part], peer[first, d]
        if k < 4:
            return w1.at[s, c, fs[d]], rn1.at[s, c, k - 2], peer[first, d]
        if k < 6:
            part = pl.ds((k - 4) * (WINDOW // 2), WINDOW // 2)
            return w2.at[s, c, gs[2], part], ro2.at[s, c, part], peer[second, d]
        return w2.at[s, c, gs[d]], rn2.at[s, c, k - 6], peer[second, d]

    def r_start(c, s, k):
        src, dst, to = r_move(c, s, k)
        copy(c, RS_KIND + s * 8 + k, src, dst, to).start()

    def r_wait(c, s, k):
        arrived(c, RS_KIND + s * 8 + k, r_move(c, s, k)[1])

    def m2(c):
        x_wait(c, 9)

        turned[...] = sg[c].T

        for q in range(4):
            part = jnp.dot(v[q * group : (q + 1) * group, :], turned[...], preferred_element_type=F32)
            w1[0, c, q] = part[:, :128].astype(BF16)
            for p in range(4):
                wq[p, q * final : (q + 1) * final] = part[p * final : (p + 1) * final, 128:]
        for p in range(4):
            w1[1, c, p] = wq[p].astype(BF16)
        for s in range(2):
            r_start(c, s, 0)
            r_start(c, s, 1)

    def r1(c):
        for s in range(2):
            up, down = at[scatter[s][0]][1], at[scatter[s][0]][-1]
            r_wait(c, s, 0)
            w1[s, c, up, :CUT] = (w1[s, c, up, :CUT].astype(F32) + ro1[s, c, :CUT].astype(F32)).astype(BF16)
            r_start(c, s, 2)
            r_wait(c, s, 1)
            w1[s, c, down, CUT:] = (w1[s, c, down, CUT:].astype(F32) + ro1[s, c, CUT:].astype(F32)).astype(BF16)
            r_start(c, s, 3)

    def r2(c):
        for s in range(2):
            f = at[scatter[s][0]][0]
            r_wait(c, s, 2)
            r_wait(c, s, 3)
            total = w1[s, c, f].astype(F32) + rn1[s, c, 0].astype(F32) + rn1[s, c, 1].astype(F32)
            total = total.astype(BF16)
            for p in range(4):
                w2[s, c, p] = total[p * STRIDE : p * STRIDE + WINDOW]
            r_start(c, s, 4)
            r_start(c, s, 5)

    def r3(c):
        h = WINDOW // 2
        for s in range(2):
            up, down = at[scatter[s][1]][1], at[scatter[s][1]][-1]
            r_wait(c, s, 4)
            w2[s, c, up, :h] = (w2[s, c, up, :h].astype(F32) + ro2[s, c, :h].astype(F32)).astype(BF16)
            r_start(c, s, 6)
            r_wait(c, s, 5)
            w2[s, c, down, h:] = (w2[s, c, down, h:].astype(F32) + ro2[s, c, h:].astype(F32)).astype(BF16)
            r_start(c, s, 7)

    def r4(c):
        sums = []
        for s in range(2):
            g = at[scatter[s][1]][0]
            r_wait(c, s, 6)
            r_wait(c, s, 7)
            total = w2[s, c, g].astype(F32) + rn2[s, c, 0].astype(F32) + rn2[s, c, 1].astype(F32)
            sums.append(pltpu.roll(total, lax.rem(WINDOW - 4 * g, WINDOW), 0))
        total = jnp.concatenate(sums, axis=1)
        total = jnp.concatenate([total, jnp.zeros((256 - WINDOW, 256), F32)], axis=0)
        gap = rc[:, c].reshape(256, 128)
        gap = jnp.concatenate([gap, gap], axis=1) + cf[0:1, :]
        out[:, c] = (total.T / gap).astype(BF16).reshape(16, BLOCK, 256)

    def cw(c):
        for k in range(5):
            sent(c, X_KIND + k, x_send(c, k)[0])

    def sw(c):
        @pl.when(c == 0)
        def _():
            for k in range(7):
                t_copy(k, t_send(k)[0], peer["core"]).wait_send()

        for s in range(2):
            for k in range(7):
                sent(c, s * 7 + k, a_send(c, s, k)[0])
            for k in range(8):
                sent(c, RS_KIND + s * 8 + k, r_move(c, s, k)[0])
        for k in range(5, 10):
            sent(c, X_KIND + k, x_send(c, k)[0])

    def load(i, size):
        slot = i % 2
        return pltpu.make_async_copy(
            vt_hbm.at[pl.ds(pl.multiple_of(i * TILE, TILE), size)], stage.at[slot, pl.ds(0, size)], lsem.at[slot]
        )

    tiles, rest = width // TILE, width % TILE
    third = (tiles + 1) // 3

    def tv(c):
        def turn(i, carry):
            load(i, TILE).wait()
            turned_tile = stage[i % 2].T
            lanes = pl.ds(pl.multiple_of(i * TILE, TILE), TILE)
            v[:depth, lanes] = turned_tile
            v[depth:, lanes] = turned_tile[main:]
            pl.when(i + 2 < tiles)(lambda: load(i + 2, TILE).start())
            pl.when(i + 2 == tiles)(lambda: load(tiles, rest).start())
            return carry

        lax.fori_loop(c * third, jnp.minimum((c + 1) * third, tiles), turn, 0)

        @pl.when(c == 2)
        def _():
            load(tiles, rest).wait()
            turned_tile = stage[tiles % 2, :rest].T
            v[:depth, tiles * TILE :] = turned_tile
            v[depth:, tiles * TILE :] = turned_tile[main:]

    load(0, TILE).start()
    load(1, TILE).start()
    for k in range(0, chunks, 2):
        pair = [a_ref[i * BLOCK : (i + 1) * BLOCK, main:] for i in (k, k + 1) if i < chunks]
        if len(pair) == 1:
            pair.append(jnp.zeros_like(pair[0]))
        tg[z, y, k // 2 * BLOCK : (k // 2 + 1) * BLOCK, :] = jnp.concatenate(pair, axis=1)

    def gp(c):
        inner, outer = col * width, (row * 16 + col) * final
        inner_row = inner // 128
        outer_row = jnp.minimum(outer // 128, col_ref.shape[0] - 3)
        for k in range(12):
            near[:, 128 * k : 128 * (k + 1)] = col_ref[pl.ds(inner_row + k, 1), :]
        for k in range(3):
            near[:, 1536 + 128 * k : 1664 + 128 * k] = col_ref[pl.ds(outer_row + k, 1), :]
        cg[...] = pltpu.roll(jnp.broadcast_to(near[:, :1536], (8, 1536)), (1536 - (inner - inner_row * 128)) % 1536, 1)
        shifted = pltpu.roll(jnp.broadcast_to(near[:, 1536:], (8, 384)), (384 - (outer - outer_row * 128)) % 384, 1)
        cf[...] = shifted[:, :256]
        flat = rc.reshape(16 * chunks * BLOCK, 128)
        for k in range(row_ref.shape[0]):
            flat[k * 128 : (k + 1) * 128, :] = jnp.broadcast_to(row_ref[k : k + 1, :], (128, 128)).T

    pl.semaphore_wait(barrier, len(peer))

    ops = dict(tv=tv, cw=cw, gp=gp, a0=a0, a1=a1, a2=a2, a3=a3, m1=m1, b1=b1, b2=b2, b3=b3, b4=b4, b5=b5, m2=m2, r1=r1, r2=r2, r3=r3, r4=r4, sw=sw)

    def step(t, carry):
        for name, late in PLAN:
            c = t - late
            pl.when(jnp.logical_and(c >= 0, c < {"tv": 3, "gp": 1}.get(name, chunks)))(functools.partial(ops[name], c))
        return carry

    lax.fori_loop(0, chunks + max(late for _, late in PLAN), step, 0)
    for k in range(chunks):
        lanes = pl.ds(k * 256, 256)
        rows = out.reshape(16 * chunks * BLOCK, 256)[lanes, :]
        o_ref[:, lanes] = rows.T[:final]


def finish(src, dst, sem):
    step = src.shape[0] // 64 * 16
    starts = range(0, src.shape[0], step)
    copies = [
        pltpu.make_async_copy(src.at[pl.ds(i, min(step, src.shape[0] - i))], dst.at[pl.ds(i, min(step, src.shape[0] - i))], sem.at[k])
        for k, i in enumerate(starts)
    ]
    for copy in copies:
        copy.start()
    for copy in copies:
        copy.wait()


def on_device(amplitudes, integrals, row_gap, col_gap):
    rows, depth = amplitudes.shape
    width = integrals.shape[1]
    chunks = rows // BLOCK
    final = depth // 16
    padded = (depth + 127) // 128 * 128

    vm = pl.BlockSpec(memory_space=pltpu.VMEM)
    anywhere = pl.BlockSpec(memory_space=pl.ANY)
    updated = pl.pallas_call(
        kernel,
        out_shape=jax.ShapeDtypeStruct((final, 16 * rows), BF16),
        in_specs=[vm, anywhere, vm, vm],
        out_specs=vm,
        scratch_shapes=[
            pltpu.VMEM((1, 1920), F32),
            pltpu.VMEM((8, 1536), F32),
            pltpu.VMEM((8, 256), F32),
            pltpu.VMEM((16, chunks, BLOCK, 128), F32),
            pltpu.VMEM((padded, width), BF16),
            pltpu.VMEM((2, TILE, depth), BF16),
            pltpu.VMEM((width, 256), BF16),
            pltpu.VMEM((chunks, 4, 4, BLOCK, depth // 128 * 128), BF16),
            pltpu.VMEM((4, 4, (chunks + 1) // 2 * BLOCK, 128), BF16),
            pltpu.VMEM((SLOTS, 256, width), BF16),
            pltpu.VMEM((chunks, 128, width), BF16),
            pltpu.VMEM((chunks, 32, width), BF16),
            pltpu.VMEM((chunks, 2, 32, width), BF16),
            pltpu.VMEM((chunks, 256, width), BF16),
            pltpu.VMEM((4, depth // 4, 128), F32),
            pltpu.VMEM((2, chunks, 4, depth // 4, 128), BF16),
            pltpu.VMEM((2, chunks, 4, WINDOW, 128), BF16),
            pltpu.VMEM((2, chunks, depth // 4, 128), BF16),
            pltpu.VMEM((2, chunks, 2, depth // 4, 128), BF16),
            pltpu.VMEM((2, chunks, WINDOW, 128), BF16),
            pltpu.VMEM((2, chunks, 2, WINDOW, 128), BF16),
            pltpu.VMEM((16, chunks, BLOCK, 256), BF16),
            pltpu.SemaphoreType.DMA((2,)),
            pltpu.SemaphoreType.DMA((7,)),
            pltpu.SemaphoreType.DMA((7,)),
            pltpu.SemaphoreType.DMA((chunks, KINDS)),
            pltpu.SemaphoreType.DMA((chunks, KINDS)),
        ],
        compiler_params=pltpu.CompilerParams(
            collective_id=0, has_side_effects=True, vmem_limit_bytes=62 * 1024 * 1024
        ),
        cost_estimate=pl.CostEstimate(
            flops=4 * 16 * rows * depth * width, bytes_accessed=2 * depth * width, transcendentals=0
        ),
    )(amplitudes, integrals.T, row_gap.reshape(-1, 128), col_gap.reshape(-1, 128))
    updated = pl.pallas_call(
        finish,
        out_shape=jax.ShapeDtypeStruct(updated.shape, updated.dtype),
        in_specs=[anywhere],
        out_specs=anywhere,
        scratch_shapes=[pltpu.SemaphoreType.DMA((8,))],
    )(updated)
    return updated.T


def solution(mesh):
    return jax.shard_map(
        on_device,
        mesh=mesh,
        in_specs=(P("col", "row"), P("row", "col"), P(), P()),
        out_specs=P(None, ("row", "col")),
        check_vma=False,
    )
```

```python
import functools

import jax
import jax.numpy as jnp
from jax import lax
from jax.experimental import pallas as pl
from jax.experimental.pallas import tpu as pltpu
from jax.sharding import PartitionSpec as P

MESH = pl.DeviceIdType.MESH
F32 = jnp.float32
BF16 = jnp.bfloat16

BLOCK = 16
WINDOW = 192
STRIDE = 176
TILE = 128
CUT = 368
SLOTS = 4
X_KIND = 14
RS_KIND = 24
KINDS = 40

PLAN = (
    ("r1", 8),
    ("r2", 10),
    ("a0", 0),
    ("cw", 7),
    ("m1", 3),
    ("b2", 4),
    ("b4", 5),
    ("r3", 12),
    ("a3", 2),
    ("a2", 1),
    ("r4", 14),
    ("sw", 14),
    ("tv", 0),
    ("gp", 3),
    ("a1", 0),
    ("rw", 10),
    ("m2", 6),
    ("gw", 7),
    ("b1", 3),
    ("b3", 4),
    ("b5", 5),
)


def kernel(
    a_ref, vt_hbm, row_ref, col_ref, o_ref,
    near, cg, cf, rc, v, vt, vtail, turned, ag, tg, c1, cx, xo, xn, sg, wq, w1, w2, ro1, rn1, ro2, rn2, out, lsem, tsend, trecv, send, recv,
):
    chunks = ag.shape[0]
    depth, width = a_ref.shape[1], v.shape[1]
    group, final = depth // 4, o_ref.shape[0]
    row, col = lax.axis_index("row"), lax.axis_index("col")
    x, core = row // 2, row % 2
    z, y = col // 4, col % 4
    half = core * 128
    other = 128 - half

    def around(index):
        return {0: index, 1: lax.rem(index + 1, 4), 2: lax.rem(index + 2, 4), -1: lax.rem(index + 3, 4)}

    xs, ys, zs = around(x), around(y), around(z)
    at = {"z": zs, "y": ys}
    peer = {
        ("x", 1): (xs[1] * 2 + core, col),
        ("x", -1): (xs[-1] * 2 + core, col),
        ("y", 1): (row, z * 4 + ys[1]),
        ("y", -1): (row, z * 4 + ys[-1]),
        ("z", 1): (row, zs[1] * 4 + y),
        ("z", -1): (row, zs[-1] * 4 + y),
        "core": (x * 2 + 1 - core, col),
    }
    strips = {step: half + index * 32 for step, index in xs.items()}
    main = ag.shape[-1]
    gather = (("y", "z", pl.ds(0, main // 2)), ("z", "y", pl.ds(main // 2, main // 2)))
    scatter = (("z", "y"), ("y", "z"))

    barrier = pltpu.get_barrier_semaphore()
    for to in peer.values():
        pl.semaphore_signal(barrier, inc=1, device_id=to, device_id_type=MESH)

    def copy(c, kind, src, dst, to):
        return pltpu.make_async_remote_copy(
            src_ref=src, dst_ref=dst, send_sem=send.at[c, kind], recv_sem=recv.at[c, kind],
            device_id=to, device_id_type=MESH,
        )

    def arrived(c, kind, dst):
        copy(c, kind, dst, dst, peer["core"]).wait_recv()

    def sent(c, kind, src):
        copy(c, kind, src, src, peer["core"]).wait_send()

    def block(s, c, step):
        first, _, lanes = gather[s]
        f = at[first][step]
        return ag.at[c, z, f, :, lanes] if first == "y" else ag.at[c, f, y, :, lanes]

    def line(s, c, step, start=0, size=4):
        first, second, lanes = gather[s]
        g, part = at[second][step], pl.ds(start, size)
        return ag.at[c, g, part, :, lanes] if first == "y" else ag.at[c, part, g, :, lanes]

    def a_send(c, s, k, d=1):
        first, second, _ = gather[s]
        if k == 0:
            return block(s, c, 0), peer[first, 1]
        if k == 1:
            return block(s, c, 0), peer[first, -1]
        if k == 2:
            return block(s, c, -d), peer[first, d]
        if k == 3:
            return line(s, c, 0), peer[second, 1]
        if k == 4:
            return line(s, c, 0), peer[second, -1]
        if k == 5:
            return line(s, c, -1, 0, 2), peer[second, 1]
        return line(s, c, 1, 2, 2), peer[second, -1]

    def a_land(c, s, k):
        if k < 3:
            return block(s, c, (-1, 1, 2)[k])
        if k < 5:
            return line(s, c, (-1, 1)[k - 3])
        return line(s, c, 2, 2 * (k - 5), 2)

    def a_start(c, s, k, d=1):
        src, to = a_send(c, s, k, d)
        copy(c, s * 7 + k, src, src, to).start()

    def a_wait(c, s, k):
        arrived(c, s * 7 + k, a_land(c, s, k))

    def t_line(step, start=0, size=4):
        return tg.at[zs[step], pl.ds(start, size)]

    def t_send(k):
        return (
            (tg.at[z, y], peer["y", 1]),
            (tg.at[z, y], peer["y", -1]),
            (tg.at[z, ys[-1]], peer["y", 1]),
            (t_line(0), peer["z", 1]),
            (t_line(0), peer["z", -1]),
            (t_line(-1, 0, 2), peer["z", 1]),
            (t_line(1, 2, 2), peer["z", -1]),
        )[k]

    def t_land(k):
        return (
            tg.at[z, ys[-1]], tg.at[z, ys[1]], tg.at[z, ys[2]],
            t_line(-1), t_line(1), t_line(2, 0, 2), t_line(2, 2, 2),
        )[k]

    def t_copy(k, src, to):
        return pltpu.make_async_remote_copy(
            src_ref=src, dst_ref=src, send_sem=tsend.at[k], recv_sem=trecv.at[k], device_id=to, device_id_type=MESH
        )

    def t_start(*kinds):
        for k in kinds:
            t_copy(k, *t_send(k)).start()

    def t_wait(*kinds):
        for k in kinds:
            t_copy(k, t_land(k), peer["core"]).wait_recv()

    def a0(c):
        ag[c, z, y] = a_ref[pl.ds(pl.multiple_of(c * BLOCK, BLOCK), BLOCK), :main]
        for s in range(2):
            a_start(c, s, 0)
            a_start(c, s, 1)
        pl.when(c == 0)(lambda: t_start(0, 1))

    def a1(c):
        def forward(d):
            for s in range(2):
                a_wait(c, s, 0 if d == 1 else 1)
                a_start(c, s, 2, d)

        @pl.when(c == 0)
        def _():
            t_wait(0)
            t_start(2)

        pl.when(c % 2 == 0)(lambda: forward(1))
        pl.when(c % 2 == 1)(lambda: forward(-1))

    def a2(c):
        pl.when(c % 2 == 0)(lambda: [a_wait(c, s, 1) for s in range(2)] and None)
        pl.when(c % 2 == 1)(lambda: [a_wait(c, s, 0) for s in range(2)] and None)
        for s in range(2):
            a_wait(c, s, 2)
            a_start(c, s, 3)
            a_start(c, s, 4)

        @pl.when(c == 0)
        def _():
            t_wait(1, 2)
            t_start(3, 4)

    def a3(c):
        for s in range(2):
            a_wait(c, s, 3)
            a_start(c, s, 5)
            a_wait(c, s, 4)
            a_start(c, s, 6)

        @pl.when(c == 0)
        def _():
            t_wait(3)
            t_start(5)
            t_wait(4)
            t_start(6)

    def m1(c):
        for s in range(2):
            a_wait(c, s, 5)
            a_wait(c, s, 6)
        pl.when(c == 0)(lambda: t_wait(5, 6))
        ends = tg[:, :, pl.ds(pl.multiple_of(c // 2 * BLOCK, BLOCK), BLOCK), :].reshape(16 * BLOCK, 128)
        mine = lax.broadcasted_iota(jnp.int32, (16 * BLOCK, 128), 1) // 64 == c % 2
        ends = jnp.where(mine, ends.astype(F32), 0.0).astype(BF16)
        rows = ag[c].reshape(16 * BLOCK, main)
        middle = (width // 2 + 127) // 128 * 128
        last = (((1,), (1,)), ((), ()))
        for lo, hi in ((0, middle), (middle, width)):
            part = lax.dot_general(vt[lo:hi, :main], rows, last, preferred_element_type=F32)
            part = part + lax.dot_general(vtail[lo:hi], ends, last, preferred_element_type=F32)
            c1[c % SLOTS, :, lo:hi] = part.astype(BF16).T
        x_start(c, 0)

    def piece(step, start=0, size=32):
        return pl.ds(pl.multiple_of(strips[step] + start, 16), size)

    def x_send(c, k):
        if k == 0:
            return c1.at[c % SLOTS, pl.ds(pl.multiple_of(other, 128), 128)], cx.at[c % SLOTS], peer["core"]
        if k == 9:
            src = sg.at[c % SLOTS, pl.ds(pl.multiple_of(half, 128), 128)]
            return src, src, peer["core"]
        d = 1 if k % 2 == 1 else -1
        part = pl.ds(8 - 8 * d, 16)
        if k < 3:
            return c1.at[c % SLOTS, piece(2, 8 - 8 * d, 16)], xo.at[c, part], peer["x", d]
        if k < 5:
            return c1.at[c % SLOTS, piece(d)], xn.at[c, (k - 3)], peer["x", d]
        src = sg.at[c % SLOTS, piece(0) if k < 7 else piece(-d, 8 - 8 * d, 16)]
        return src, src, peer["x", d]

    def x_land(c, k):
        if k < 5:
            return x_send(c, k)[1]
        if k == 9:
            return sg.at[c % SLOTS, pl.ds(pl.multiple_of(other, 128), 128)]
        d = 1 if k % 2 == 1 else -1
        return sg.at[c % SLOTS, piece(-d) if k < 7 else piece(2, 8 - 8 * d, 16)]

    def x_start(c, k):
        src, dst, to = x_send(c, k)
        copy(c, X_KIND + k, src, dst, to).start()

    def x_wait(c, k):
        arrived(c, X_KIND + k, x_land(c, k))

    def b1(c):
        x_wait(c, 0)
        rows = pl.ds(pl.multiple_of(half, 128), 128)
        c1[c % SLOTS, rows, :] = (c1[c % SLOTS, rows, :].astype(F32) + cx[c % SLOTS].astype(F32)).astype(BF16)
        x_start(c, 1)
        x_start(c, 2)

    def b2(c):
        for k, step in ((1, 1), (2, -1)):
            x_wait(c, k)
            part, rows = pl.ds(16 * (k - 1), 16), piece(step, 16 * (k - 1), 16)
            c1[c % SLOTS, rows, :] = (c1[c % SLOTS, rows, :].astype(F32) + xo[c, part].astype(F32)).astype(BF16)
            x_start(c, k + 2)

    def b3(c):
        gap = rc[pl.ds(core * 8 + x * 2, 2), c].reshape(32, 128)
        x_wait(c, 3)
        x_wait(c, 4)
        rows = piece(0)
        total = c1[c % SLOTS, rows, :].astype(F32) + xn[c, 0].astype(F32) + xn[c, 1].astype(F32)
        sg[c % SLOTS, rows, :] = (total / (gap[:, :1] + cg[0:1, :width])).astype(BF16)
        x_start(c, 5)
        x_start(c, 6)

    def b4(c):
        for k in (5, 6):
            x_wait(c, k)
            x_start(c, k + 2)

    def b5(c):
        x_wait(c, 7)
        x_wait(c, 8)
        x_start(c, 9)

    def r_move(c, s, k):
        first, second = scatter[s]
        fs, gs = at[first], at[second]
        d = 1 if k % 2 == 0 else -1
        if k < 2:
            part = pl.ds(0, CUT) if k == 0 else pl.ds(CUT, group - CUT)
            return w1.at[s, c % SLOTS, fs[2], part], ro1.at[s, c, part], peer[first, d]
        if k < 4:
            return w1.at[s, c % SLOTS, fs[d]], rn1.at[s, c, k - 2], peer[first, d]
        if k < 6:
            part = pl.ds((k - 4) * (WINDOW // 2), WINDOW // 2)
            return w2.at[s, c, gs[2], part], ro2.at[s, c, part], peer[second, d]
        return w2.at[s, c, gs[d]], rn2.at[s, c, k - 6], peer[second, d]

    def r_start(c, s, k):
        src, dst, to = r_move(c, s, k)
        copy(c, RS_KIND + s * 8 + k, src, dst, to).start()

    def r_wait(c, s, k):
        arrived(c, RS_KIND + s * 8 + k, r_move(c, s, k)[1])

    def m2(c):
        x_wait(c, 9)

        turned[...] = sg[c % SLOTS].T

        for g in range(2):
            both = jnp.dot(v[2 * g * group : 2 * (g + 1) * group, :], turned[...], preferred_element_type=F32)
            for q in (2 * g, 2 * g + 1):
                part = both[(q - 2 * g) * group : (q - 2 * g + 1) * group]
                w1[0, c % SLOTS, q] = part[:, :128].astype(BF16)
                for p in range(4):
                    wq[p, q * final : (q + 1) * final] = part[p * final : (p + 1) * final, 128:]
        for p in range(4):
            w1[1, c % SLOTS, p] = wq[p].astype(BF16)
        for s in range(2):
            r_start(c, s, 0)
            r_start(c, s, 1)

    def r1(c):
        for s in range(2):
            up, down = at[scatter[s][0]][1], at[scatter[s][0]][-1]
            r_wait(c, s, 0)
            w1[s, c % SLOTS, up, :CUT] = (w1[s, c % SLOTS, up, :CUT].astype(F32) + ro1[s, c, :CUT].astype(F32)).astype(BF16)
            r_start(c, s, 2)
            r_wait(c, s, 1)
            w1[s, c % SLOTS, down, CUT:] = (w1[s, c % SLOTS, down, CUT:].astype(F32) + ro1[s, c, CUT:].astype(F32)).astype(BF16)
            r_start(c, s, 3)

    def r2(c):
        for s in range(2):
            f = at[scatter[s][0]][0]
            r_wait(c, s, 2)
            r_wait(c, s, 3)
            total = w1[s, c % SLOTS, f].astype(F32) + rn1[s, c, 0].astype(F32) + rn1[s, c, 1].astype(F32)
            total = total.astype(BF16)
            for p in range(4):
                w2[s, c, p] = total[p * STRIDE : p * STRIDE + WINDOW]
            r_start(c, s, 4)
            r_start(c, s, 5)

    def r3(c):
        h = WINDOW // 2
        for s in range(2):
            up, down = at[scatter[s][1]][1], at[scatter[s][1]][-1]
            r_wait(c, s, 4)
            w2[s, c, up, :h] = (w2[s, c, up, :h].astype(F32) + ro2[s, c, :h].astype(F32)).astype(BF16)
            r_start(c, s, 6)
            r_wait(c, s, 5)
            w2[s, c, down, h:] = (w2[s, c, down, h:].astype(F32) + ro2[s, c, h:].astype(F32)).astype(BF16)
            r_start(c, s, 7)

    def r4(c):
        sums = []
        for s in range(2):
            g = at[scatter[s][1]][0]
            r_wait(c, s, 6)
            r_wait(c, s, 7)
            total = w2[s, c, g].astype(F32) + rn2[s, c, 0].astype(F32) + rn2[s, c, 1].astype(F32)
            sums.append(pltpu.roll(total, lax.rem(WINDOW - 4 * g, WINDOW), 0))
        total = jnp.concatenate(sums, axis=1)
        total = jnp.concatenate([total, jnp.zeros((256 - WINDOW, 256), F32)], axis=0)
        gap = rc[:, c].reshape(256, 128)
        gap = jnp.concatenate([gap, gap], axis=1) + cf[0:1, :]
        out[:, c] = (total.T / gap).astype(BF16).reshape(16, BLOCK, 256)

    def rw(c):
        for s in range(2):
            for k in range(4):
                sent(c, RS_KIND + s * 8 + k, r_move(c, s, k)[0])

    def gw(c):
        for k in range(5, 10):
            sent(c, X_KIND + k, x_send(c, k)[0])

    def cw(c):
        for k in range(5):
            sent(c, X_KIND + k, x_send(c, k)[0])

    def sw(c):
        @pl.when(c == 0)
        def _():
            for k in range(7):
                t_copy(k, t_send(k)[0], peer["core"]).wait_send()

        for s in range(2):
            for k in range(7):
                sent(c, s * 7 + k, a_send(c, s, k)[0])
            for k in range(4, 8):
                sent(c, RS_KIND + s * 8 + k, r_move(c, s, k)[0])

    part = (width // 3 + 127) // 128 * 128

    def load(i):
        rows = pl.ds(i * part, min(part, width - i * part))
        return pltpu.make_async_copy(vt_hbm.at[rows], vt.at[rows], lsem.at[i])

    def tv(c):
        def turn(i, carry):
            tile = pl.ds(pl.multiple_of(i * TILE, TILE), TILE)
            v[:, tile] = vt[tile, :].T
            ends = vt[tile, main:]
            vtail[tile, :] = jnp.concatenate([ends, ends], axis=1)
            return carry

        for i in range(3):

            @pl.when(c == i)
            def _():
                load(i).wait()
                end = min((i + 1) * part, width)
                lax.fori_loop(i * part // TILE, end // TILE, turn, 0)
                if end % TILE:
                    start = end // TILE * TILE
                    v[:, start:] = vt[start:, :].T
                    ends = vt[start:, main:]
                    vtail[start:, :] = jnp.concatenate([ends, ends], axis=1)

    for i in range(3):
        load(i).start()
    for k in range(0, chunks, 2):
        pair = [a_ref[i * BLOCK : (i + 1) * BLOCK, main:] for i in (k, k + 1) if i < chunks]
        if len(pair) == 1:
            pair.append(jnp.zeros_like(pair[0]))
        tg[z, y, k // 2 * BLOCK : (k // 2 + 1) * BLOCK, :] = jnp.concatenate(pair, axis=1)

    def gp(c):
        inner, outer = col * width, (row * 16 + col) * final
        inner_row = inner // 128
        outer_row = jnp.minimum(outer // 128, col_ref.shape[0] - 3)
        for k in range(12):
            near[:, 128 * k : 128 * (k + 1)] = col_ref[pl.ds(inner_row + k, 1), :]
        for k in range(3):
            near[:, 1536 + 128 * k : 1664 + 128 * k] = col_ref[pl.ds(outer_row + k, 1), :]
        cg[...] = pltpu.roll(jnp.broadcast_to(near[:, :1536], (8, 1536)), (1536 - (inner - inner_row * 128)) % 1536, 1)
        shifted = pltpu.roll(jnp.broadcast_to(near[:, 1536:], (8, 384)), (384 - (outer - outer_row * 128)) % 384, 1)
        cf[...] = shifted[:, :256]
        flat = rc.reshape(16 * chunks * BLOCK, 128)
        for k in range(row_ref.shape[0]):
            flat[k * 128 : (k + 1) * 128, :] = jnp.broadcast_to(row_ref[k : k + 1, :], (128, 128)).T

    pl.semaphore_wait(barrier, len(peer))

    ops = dict(tv=tv, cw=cw, gw=gw, rw=rw, gp=gp, a0=a0, a1=a1, a2=a2, a3=a3, m1=m1, b1=b1, b2=b2, b3=b3, b4=b4, b5=b5, m2=m2, r1=r1, r2=r2, r3=r3, r4=r4, sw=sw)

    def step(t, carry):
        for name, late in PLAN:
            c = t - late
            pl.when(jnp.logical_and(c >= 0, c < {"tv": 3, "gp": 1}.get(name, chunks)))(functools.partial(ops[name], c))
        return carry

    lax.fori_loop(0, chunks + max(late for _, late in PLAN), step, 0)
    for k in range(chunks):
        lanes = pl.ds(k * 256, 256)
        rows = out.reshape(16 * chunks * BLOCK, 256)[lanes, :]
        o_ref[:, lanes] = rows.T[:final]


def on_device(amplitudes, integrals, row_gap, col_gap):
    rows, depth = amplitudes.shape
    width = integrals.shape[1]
    chunks = rows // BLOCK
    final = depth // 16

    vm = pl.BlockSpec(memory_space=pltpu.VMEM)
    anywhere = pl.BlockSpec(memory_space=pl.ANY)
    updated = pl.pallas_call(
        kernel,
        out_shape=jax.ShapeDtypeStruct((final, 16 * rows), BF16),
        in_specs=[vm, anywhere, vm, vm],
        out_specs=vm,
        scratch_shapes=[
            pltpu.VMEM((1, 1920), F32),
            pltpu.VMEM((8, 1536), F32),
            pltpu.VMEM((8, 256), F32),
            pltpu.VMEM((16, chunks, BLOCK, 128), F32),
            pltpu.VMEM((depth, width), BF16),
            pltpu.VMEM((width, depth), BF16),
            pltpu.VMEM((width, 128), BF16),
            pltpu.VMEM((width, 256), BF16),
            pltpu.VMEM((chunks, 4, 4, BLOCK, depth // 128 * 128), BF16),
            pltpu.VMEM((4, 4, (chunks + 1) // 2 * BLOCK, 128), BF16),
            pltpu.VMEM((SLOTS, 256, width), BF16),
            pltpu.VMEM((SLOTS, 128, width), BF16),
            pltpu.VMEM((chunks, 32, width), BF16),
            pltpu.VMEM((chunks, 2, 32, width), BF16),
            pltpu.VMEM((SLOTS, 256, width), BF16),
            pltpu.VMEM((4, depth // 4, 128), F32),
            pltpu.VMEM((2, SLOTS, 4, depth // 4, 128), BF16),
            pltpu.VMEM((2, chunks, 4, WINDOW, 128), BF16),
            pltpu.VMEM((2, chunks, depth // 4, 128), BF16),
            pltpu.VMEM((2, chunks, 2, depth // 4, 128), BF16),
            pltpu.VMEM((2, chunks, WINDOW, 128), BF16),
            pltpu.VMEM((2, chunks, 2, WINDOW, 128), BF16),
            pltpu.VMEM((16, chunks, BLOCK, 256), BF16),
            pltpu.SemaphoreType.DMA((3,)),
            pltpu.SemaphoreType.DMA((7,)),
            pltpu.SemaphoreType.DMA((7,)),
            pltpu.SemaphoreType.DMA((chunks, KINDS)),
            pltpu.SemaphoreType.DMA((chunks, KINDS)),
        ],
        compiler_params=pltpu.CompilerParams(
            collective_id=0, has_side_effects=True, vmem_limit_bytes=62 * 1024 * 1024
        ),
        cost_estimate=pl.CostEstimate(
            flops=4 * 16 * rows * depth * width, bytes_accessed=2 * depth * width, transcendentals=0
        ),
    )(amplitudes, integrals.T, row_gap.reshape(-1, 128), col_gap.reshape(-1, 128))
    return updated.T


def solution(mesh):
    return jax.shard_map(
        on_device,
        mesh=mesh,
        in_specs=(P("col", "row"), P("row", "col"), P(), P()),
        out_specs=P(None, ("row", "col")),
        check_vma=False,
    )
```

```python
import functools

import jax
import jax.numpy as jnp
from jax import lax
from jax.experimental import pallas as pl
from jax.experimental.pallas import tpu as pltpu
from jax.sharding import PartitionSpec as P

MESH = pl.DeviceIdType.MESH
F32 = jnp.float32
BF16 = jnp.bfloat16

BLOCK = 16
WINDOW = 192
STRIDE = 176
TILE = 128
SHARE = 1280
CUT = 368
SLOTS = 4
X_KIND = 14
RS_KIND = 24
KINDS = 40

PLAN = (
    ("r1", 8),
    ("r2", 10),
    ("a0", 0),
    ("cw", 7),
    ("m1", 3),
    ("b2", 4),
    ("b4", 5),
    ("r3", 12),
    ("a3", 2),
    ("a2", 1),
    ("r4", 14),
    ("sw", 14),
    ("tv", 0),
    ("gp", 3),
    ("a1", 0),
    ("rw", 10),
    ("m2", 6),
    ("gw", 7),
    ("b1", 3),
    ("b3", 4),
    ("b5", 5),
)


def kernel(
    a_ref, vt_hbm, row_ref, col_ref, o_ref,
    near, cg, cf, rc, v, vt, vtail, turned, ag, tg, c1, cx, xo, xn, sg, wq, w1, w2, ro1, rn1, ro2, rn2, out, lsem, tsend, trecv, send, recv,
):
    chunks = ag.shape[0]
    depth, width = a_ref.shape[1], v.shape[1]
    group, final = depth // 4, o_ref.shape[0]
    row, col = lax.axis_index("row"), lax.axis_index("col")
    x, core = row // 2, row % 2
    z, y = col // 4, col % 4
    half = core * 128
    other = 128 - half

    def around(index):
        return {0: index, 1: lax.rem(index + 1, 4), 2: lax.rem(index + 2, 4), -1: lax.rem(index + 3, 4)}

    xs, ys, zs = around(x), around(y), around(z)
    at = {"z": zs, "y": ys}
    peer = {
        ("x", 1): (xs[1] * 2 + core, col),
        ("x", -1): (xs[-1] * 2 + core, col),
        ("y", 1): (row, z * 4 + ys[1]),
        ("y", -1): (row, z * 4 + ys[-1]),
        ("z", 1): (row, zs[1] * 4 + y),
        ("z", -1): (row, zs[-1] * 4 + y),
        "core": (x * 2 + 1 - core, col),
    }
    strips = {step: half + index * 32 for step, index in xs.items()}
    main = ag.shape[-1]
    gather = (("y", "z", pl.ds(0, SHARE)), ("z", "y", pl.ds(SHARE, main - SHARE)))
    scatter = (("z", "y"), ("y", "z"))

    barrier = pltpu.get_barrier_semaphore()
    for to in peer.values():
        pl.semaphore_signal(barrier, inc=1, device_id=to, device_id_type=MESH)

    def copy(c, kind, src, dst, to):
        return pltpu.make_async_remote_copy(
            src_ref=src, dst_ref=dst, send_sem=send.at[c, kind], recv_sem=recv.at[c, kind],
            device_id=to, device_id_type=MESH,
        )

    def arrived(c, kind, dst):
        copy(c, kind, dst, dst, peer["core"]).wait_recv()

    def sent(c, kind, src):
        copy(c, kind, src, src, peer["core"]).wait_send()

    def block(s, c, step):
        first, _, lanes = gather[s]
        f = at[first][step]
        return ag.at[c, z, f, :, lanes] if first == "y" else ag.at[c, f, y, :, lanes]

    def line(s, c, step, start=0, size=4):
        first, second, lanes = gather[s]
        g, part = at[second][step], pl.ds(start, size)
        return ag.at[c, g, part, :, lanes] if first == "y" else ag.at[c, part, g, :, lanes]

    def a_send(c, s, k, d=1):
        first, second, _ = gather[s]
        if k == 0:
            return block(s, c, 0), peer[first, 1]
        if k == 1:
            return block(s, c, 0), peer[first, -1]
        if k == 2:
            return block(s, c, -d), peer[first, d]
        if k == 3:
            return line(s, c, 0), peer[second, 1]
        if k == 4:
            return line(s, c, 0), peer[second, -1]
        if k == 5:
            return line(s, c, -1, 0, 2), peer[second, 1]
        return line(s, c, 1, 2, 2), peer[second, -1]

    def a_land(c, s, k):
        if k < 3:
            return block(s, c, (-1, 1, 2)[k])
        if k < 5:
            return line(s, c, (-1, 1)[k - 3])
        return line(s, c, 2, 2 * (k - 5), 2)

    def a_start(c, s, k, d=1):
        src, to = a_send(c, s, k, d)
        copy(c, s * 7 + k, src, src, to).start()

    def a_wait(c, s, k):
        arrived(c, s * 7 + k, a_land(c, s, k))

    def t_line(step, start=0, size=4):
        return tg.at[pl.ds(start, size), ys[step]]

    def t_send(k):
        return (
            (tg.at[z, y], peer["z", 1]),
            (tg.at[z, y], peer["z", -1]),
            (tg.at[zs[-1], y], peer["z", 1]),
            (t_line(0), peer["y", 1]),
            (t_line(0), peer["y", -1]),
            (t_line(-1, 0, 2), peer["y", 1]),
            (t_line(1, 2, 2), peer["y", -1]),
        )[k]

    def t_land(k):
        return (
            tg.at[zs[-1], y], tg.at[zs[1], y], tg.at[zs[2], y],
            t_line(-1), t_line(1), t_line(2, 0, 2), t_line(2, 2, 2),
        )[k]

    def t_copy(k, src, to):
        return pltpu.make_async_remote_copy(
            src_ref=src, dst_ref=src, send_sem=tsend.at[k], recv_sem=trecv.at[k], device_id=to, device_id_type=MESH
        )

    def t_start(*kinds):
        for k in kinds:
            t_copy(k, *t_send(k)).start()

    def t_wait(*kinds):
        for k in kinds:
            t_copy(k, t_land(k), peer["core"]).wait_recv()

    def a0(c):
        ag[c, z, y] = a_ref[pl.ds(pl.multiple_of(c * BLOCK, BLOCK), BLOCK), :main]
        for s in range(2):
            a_start(c, s, 0)
            a_start(c, s, 1)
        pl.when(c == 0)(lambda: t_start(0, 1))

    def a1(c):
        def forward(d):
            for s in range(2):
                a_wait(c, s, 0 if d == 1 else 1)
                a_start(c, s, 2, d)

        @pl.when(c == 0)
        def _():
            t_wait(0)
            t_start(2)

        pl.when(c % 2 == 0)(lambda: forward(1))
        pl.when(c % 2 == 1)(lambda: forward(-1))

    def a2(c):
        pl.when(c % 2 == 0)(lambda: [a_wait(c, s, 1) for s in range(2)] and None)
        pl.when(c % 2 == 1)(lambda: [a_wait(c, s, 0) for s in range(2)] and None)
        for s in range(2):
            a_wait(c, s, 2)
            a_start(c, s, 3)
            a_start(c, s, 4)

        @pl.when(c == 0)
        def _():
            t_wait(1, 2)
            t_start(3, 4)

    def a3(c):
        for s in range(2):
            a_wait(c, s, 3)
            a_start(c, s, 5)
            a_wait(c, s, 4)
            a_start(c, s, 6)

        @pl.when(c == 0)
        def _():
            t_wait(3)
            t_start(5)
            t_wait(4)
            t_start(6)

    def m1(c):
        for s in range(2):
            a_wait(c, s, 5)
            a_wait(c, s, 6)
        pl.when(c == 0)(lambda: t_wait(5, 6))
        ends = tg[:, :, pl.ds(pl.multiple_of(c // 2 * BLOCK, BLOCK), BLOCK), :].reshape(16 * BLOCK, 128)
        mine = lax.broadcasted_iota(jnp.int32, (16 * BLOCK, 128), 1) // 64 == c % 2
        ends = jnp.where(mine, ends.astype(F32), 0.0).astype(BF16)
        rows = ag[c].reshape(16 * BLOCK, main)
        middle = (width // 2 + 127) // 128 * 128
        last = (((1,), (1,)), ((), ()))
        for lo, hi in ((0, middle), (middle, width)):
            part = lax.dot_general(vt[lo:hi, :main], rows, last, preferred_element_type=F32)
            part = part + lax.dot_general(vtail[lo:hi], ends, last, preferred_element_type=F32)
            c1[c % SLOTS, :, lo:hi] = part.astype(BF16).T
        x_start(c, 0)

    def piece(step, start=0, size=32):
        return pl.ds(pl.multiple_of(strips[step] + start, 16), size)

    def x_send(c, k):
        if k == 0:
            return c1.at[c % SLOTS, pl.ds(pl.multiple_of(other, 128), 128)], cx.at[c % SLOTS], peer["core"]
        if k == 9:
            src = sg.at[c % SLOTS, pl.ds(pl.multiple_of(half, 128), 128)]
            return src, src, peer["core"]
        d = 1 if k % 2 == 1 else -1
        part = pl.ds(8 - 8 * d, 16)
        if k < 3:
            return c1.at[c % SLOTS, piece(2, 8 - 8 * d, 16)], xo.at[c, part], peer["x", d]
        if k < 5:
            return c1.at[c % SLOTS, piece(d)], xn.at[c, (k - 3)], peer["x", d]
        src = sg.at[c % SLOTS, piece(0) if k < 7 else piece(-d, 8 - 8 * d, 16)]
        return src, src, peer["x", d]

    def x_land(c, k):
        if k < 5:
            return x_send(c, k)[1]
        if k == 9:
            return sg.at[c % SLOTS, pl.ds(pl.multiple_of(other, 128), 128)]
        d = 1 if k % 2 == 1 else -1
        return sg.at[c % SLOTS, piece(-d) if k < 7 else piece(2, 8 - 8 * d, 16)]

    def x_start(c, k):
        src, dst, to = x_send(c, k)
        copy(c, X_KIND + k, src, dst, to).start()

    def x_wait(c, k):
        arrived(c, X_KIND + k, x_land(c, k))

    def b1(c):
        x_wait(c, 0)
        rows = pl.ds(pl.multiple_of(half, 128), 128)
        c1[c % SLOTS, rows, :] = (c1[c % SLOTS, rows, :].astype(F32) + cx[c % SLOTS].astype(F32)).astype(BF16)
        x_start(c, 1)
        x_start(c, 2)

    def b2(c):
        for k, step in ((1, 1), (2, -1)):
            x_wait(c, k)
            part, rows = pl.ds(16 * (k - 1), 16), piece(step, 16 * (k - 1), 16)
            c1[c % SLOTS, rows, :] = (c1[c % SLOTS, rows, :].astype(F32) + xo[c, part].astype(F32)).astype(BF16)
            x_start(c, k + 2)

    def b3(c):
        gap = rc[pl.ds(core * 8 + x * 2, 2), c].reshape(32, 128)
        x_wait(c, 3)
        x_wait(c, 4)
        rows = piece(0)
        total = c1[c % SLOTS, rows, :].astype(F32) + xn[c, 0].astype(F32) + xn[c, 1].astype(F32)
        sg[c % SLOTS, rows, :] = (total / (gap[:, :1] + cg[0:1, :width])).astype(BF16)
        x_start(c, 5)
        x_start(c, 6)

    def b4(c):
        for k in (5, 6):
            x_wait(c, k)
            x_start(c, k + 2)

    def b5(c):
        x_wait(c, 7)
        x_wait(c, 8)
        x_start(c, 9)

    def r_move(c, s, k):
        first, second = scatter[s]
        fs, gs = at[first], at[second]
        d = 1 if k % 2 == 0 else -1
        if k < 2:
            part = pl.ds(0, CUT) if k == 0 else pl.ds(CUT, group - CUT)
            return w1.at[s, c % SLOTS, fs[2], part], ro1.at[s, c, part], peer[first, d]
        if k < 4:
            return w1.at[s, c % SLOTS, fs[d]], rn1.at[s, c, k - 2], peer[first, d]
        if k < 6:
            part = pl.ds((k - 4) * (WINDOW // 2), WINDOW // 2)
            return w2.at[s, c, gs[2], part], ro2.at[s, c, part], peer[second, d]
        return w2.at[s, c, gs[d]], rn2.at[s, c, k - 6], peer[second, d]

    def r_start(c, s, k):
        src, dst, to = r_move(c, s, k)
        copy(c, RS_KIND + s * 8 + k, src, dst, to).start()

    def r_wait(c, s, k):
        arrived(c, RS_KIND + s * 8 + k, r_move(c, s, k)[1])

    def m2(c):
        x_wait(c, 9)

        turned[...] = sg[c % SLOTS].T

        for g in range(2):
            both = jnp.dot(v[2 * g * group : 2 * (g + 1) * group, :], turned[...], preferred_element_type=F32)
            for q in (2 * g, 2 * g + 1):
                part = both[(q - 2 * g) * group : (q - 2 * g + 1) * group]
                w1[0, c % SLOTS, q] = part[:, :128].astype(BF16)
                for p in range(4):
                    wq[p, q * final : (q + 1) * final] = part[p * final : (p + 1) * final, 128:]
        for p in range(4):
            w1[1, c % SLOTS, p] = wq[p].astype(BF16)
        for s in range(2):
            r_start(c, s, 0)
            r_start(c, s, 1)

    def r1(c):
        for s in range(2):
            up, down = at[scatter[s][0]][1], at[scatter[s][0]][-1]
            r_wait(c, s, 0)
            w1[s, c % SLOTS, up, :CUT] = (w1[s, c % SLOTS, up, :CUT].astype(F32) + ro1[s, c, :CUT].astype(F32)).astype(BF16)
            r_start(c, s, 2)
            r_wait(c, s, 1)
            w1[s, c % SLOTS, down, CUT:] = (w1[s, c % SLOTS, down, CUT:].astype(F32) + ro1[s, c, CUT:].astype(F32)).astype(BF16)
            r_start(c, s, 3)

    def r2(c):
        for s in range(2):
            f = at[scatter[s][0]][0]
            r_wait(c, s, 2)
            r_wait(c, s, 3)
            total = w1[s, c % SLOTS, f].astype(F32) + rn1[s, c, 0].astype(F32) + rn1[s, c, 1].astype(F32)
            total = total.astype(BF16)
            for p in range(4):
                w2[s, c, p] = total[p * STRIDE : p * STRIDE + WINDOW]
            r_start(c, s, 4)
            r_start(c, s, 5)

    def r3(c):
        h = WINDOW // 2
        for s in range(2):
            up, down = at[scatter[s][1]][1], at[scatter[s][1]][-1]
            r_wait(c, s, 4)
            w2[s, c, up, :h] = (w2[s, c, up, :h].astype(F32) + ro2[s, c, :h].astype(F32)).astype(BF16)
            r_start(c, s, 6)
            r_wait(c, s, 5)
            w2[s, c, down, h:] = (w2[s, c, down, h:].astype(F32) + ro2[s, c, h:].astype(F32)).astype(BF16)
            r_start(c, s, 7)

    def r4(c):
        sums = []
        for s in range(2):
            g = at[scatter[s][1]][0]
            r_wait(c, s, 6)
            r_wait(c, s, 7)
            total = w2[s, c, g].astype(F32) + rn2[s, c, 0].astype(F32) + rn2[s, c, 1].astype(F32)
            sums.append(pltpu.roll(total, lax.rem(WINDOW - 4 * g, WINDOW), 0))
        total = jnp.concatenate(sums, axis=1)
        total = jnp.concatenate([total, jnp.zeros((256 - WINDOW, 256), F32)], axis=0)
        gap = rc[:, c].reshape(256, 128)
        gap = jnp.concatenate([gap, gap], axis=1) + cf[0:1, :]
        out[:, c] = (total.T / gap).astype(BF16).reshape(16, BLOCK, 256)

    def rw(c):
        for s in range(2):
            for k in range(4):
                sent(c, RS_KIND + s * 8 + k, r_move(c, s, k)[0])

    def gw(c):
        for k in range(5, 10):
            sent(c, X_KIND + k, x_send(c, k)[0])

    def cw(c):
        for k in range(5):
            sent(c, X_KIND + k, x_send(c, k)[0])

    def sw(c):
        @pl.when(c == 0)
        def _():
            for k in range(7):
                t_copy(k, t_send(k)[0], peer["core"]).wait_send()

        for s in range(2):
            for k in range(7):
                sent(c, s * 7 + k, a_send(c, s, k)[0])
            for k in range(4, 8):
                sent(c, RS_KIND + s * 8 + k, r_move(c, s, k)[0])

    part = (width // 3 + 127) // 128 * 128

    def load(i):
        rows = pl.ds(i * part, min(part, width - i * part))
        return pltpu.make_async_copy(vt_hbm.at[rows], vt.at[rows], lsem.at[i])

    def tv(c):
        def turn(i, carry):
            tile = pl.ds(pl.multiple_of(i * TILE, TILE), TILE)
            v[:, tile] = vt[tile, :].T
            ends = vt[tile, main:]
            vtail[tile, :] = jnp.concatenate([ends, ends], axis=1)
            return carry

        for i in range(3):

            @pl.when(c == i)
            def _():
                load(i).wait()
                end = min((i + 1) * part, width)
                lax.fori_loop(i * part // TILE, end // TILE, turn, 0)
                if end % TILE:
                    start = end // TILE * TILE
                    v[:, start:] = vt[start:, :].T
                    ends = vt[start:, main:]
                    vtail[start:, :] = jnp.concatenate([ends, ends], axis=1)

    for i in range(3):
        load(i).start()
    for k in range(0, chunks, 2):
        pair = [a_ref[i * BLOCK : (i + 1) * BLOCK, main:] for i in (k, k + 1) if i < chunks]
        if len(pair) == 1:
            pair.append(jnp.zeros_like(pair[0]))
        tg[z, y, k // 2 * BLOCK : (k // 2 + 1) * BLOCK, :] = jnp.concatenate(pair, axis=1)

    def gp(c):
        inner, outer = col * width, (row * 16 + col) * final
        inner_row = inner // 128
        outer_row = jnp.minimum(outer // 128, col_ref.shape[0] - 3)
        for k in range(12):
            near[:, 128 * k : 128 * (k + 1)] = col_ref[pl.ds(inner_row + k, 1), :]
        for k in range(3):
            near[:, 1536 + 128 * k : 1664 + 128 * k] = col_ref[pl.ds(outer_row + k, 1), :]
        cg[...] = pltpu.roll(jnp.broadcast_to(near[:, :1536], (8, 1536)), (1536 - (inner - inner_row * 128)) % 1536, 1)
        shifted = pltpu.roll(jnp.broadcast_to(near[:, 1536:], (8, 384)), (384 - (outer - outer_row * 128)) % 384, 1)
        cf[...] = shifted[:, :256]
        flat = rc.reshape(16 * chunks * BLOCK, 128)
        for k in range(row_ref.shape[0]):
            flat[k * 128 : (k + 1) * 128, :] = jnp.broadcast_to(row_ref[k : k + 1, :], (128, 128)).T

    pl.semaphore_wait(barrier, len(peer))

    ops = dict(tv=tv, cw=cw, gw=gw, rw=rw, gp=gp, a0=a0, a1=a1, a2=a2, a3=a3, m1=m1, b1=b1, b2=b2, b3=b3, b4=b4, b5=b5, m2=m2, r1=r1, r2=r2, r3=r3, r4=r4, sw=sw)

    def step(t, carry):
        for name, late in PLAN:
            c = t - late
            pl.when(jnp.logical_and(c >= 0, c < {"tv": 3, "gp": 1}.get(name, chunks)))(functools.partial(ops[name], c))
        return carry

    lax.fori_loop(0, chunks + max(late for _, late in PLAN), step, 0)
    for k in range(chunks):
        lanes = pl.ds(k * 256, 256)
        rows = out.reshape(16 * chunks * BLOCK, 256)[lanes, :]
        o_ref[:, lanes] = rows.T[:final]


def on_device(amplitudes, integrals, row_gap, col_gap):
    rows, depth = amplitudes.shape
    width = integrals.shape[1]
    chunks = rows // BLOCK
    final = depth // 16

    vm = pl.BlockSpec(memory_space=pltpu.VMEM)
    anywhere = pl.BlockSpec(memory_space=pl.ANY)
    updated = pl.pallas_call(
        kernel,
        out_shape=jax.ShapeDtypeStruct((final, 16 * rows), BF16),
        in_specs=[vm, anywhere, vm, vm],
        out_specs=vm,
        scratch_shapes=[
            pltpu.VMEM((1, 1920), F32),
            pltpu.VMEM((8, 1536), F32),
            pltpu.VMEM((8, 256), F32),
            pltpu.VMEM((16, chunks, BLOCK, 128), F32),
            pltpu.VMEM((depth, width), BF16),
            pltpu.VMEM((width, depth), BF16),
            pltpu.VMEM((width, 128), BF16),
            pltpu.VMEM((width, 256), BF16),
            pltpu.VMEM((chunks, 4, 4, BLOCK, depth // 128 * 128), BF16),
            pltpu.VMEM((4, 4, (chunks + 1) // 2 * BLOCK, 128), BF16),
            pltpu.VMEM((SLOTS, 256, width), BF16),
            pltpu.VMEM((SLOTS, 128, width), BF16),
            pltpu.VMEM((chunks, 32, width), BF16),
            pltpu.VMEM((chunks, 2, 32, width), BF16),
            pltpu.VMEM((SLOTS, 256, width), BF16),
            pltpu.VMEM((4, depth // 4, 128), F32),
            pltpu.VMEM((2, SLOTS, 4, depth // 4, 128), BF16),
            pltpu.VMEM((2, chunks, 4, WINDOW, 128), BF16),
            pltpu.VMEM((2, chunks, depth // 4, 128), BF16),
            pltpu.VMEM((2, chunks, 2, depth // 4, 128), BF16),
            pltpu.VMEM((2, chunks, WINDOW, 128), BF16),
            pltpu.VMEM((2, chunks, 2, WINDOW, 128), BF16),
            pltpu.VMEM((16, chunks, BLOCK, 256), BF16),
            pltpu.SemaphoreType.DMA((3,)),
            pltpu.SemaphoreType.DMA((7,)),
            pltpu.SemaphoreType.DMA((7,)),
            pltpu.SemaphoreType.DMA((chunks, KINDS)),
            pltpu.SemaphoreType.DMA((chunks, KINDS)),
        ],
        compiler_params=pltpu.CompilerParams(
            collective_id=0, has_side_effects=True, vmem_limit_bytes=62 * 1024 * 1024
        ),
        cost_estimate=pl.CostEstimate(
            flops=4 * 16 * rows * depth * width, bytes_accessed=2 * depth * width, transcendentals=0
        ),
    )(amplitudes, integrals.T, row_gap.reshape(-1, 128), col_gap.reshape(-1, 128))
    return updated.T


def solution(mesh):
    return jax.shard_map(
        on_device,
        mesh=mesh,
        in_specs=(P("col", "row"), P("row", "col"), P(), P()),
        out_specs=P(None, ("row", "col")),
        check_vma=False,
    )
```

```python
import functools

import jax
import jax.numpy as jnp
from jax import lax
from jax.experimental import pallas as pl
from jax.experimental.pallas import tpu as pltpu
from jax.sharding import PartitionSpec as P

MESH = pl.DeviceIdType.MESH
F32 = jnp.float32
BF16 = jnp.bfloat16

BLOCK = 16
WINDOW = 192
STRIDE = 176
TILE = 128
CUT = 368
SLOTS = 4
X_KIND = 14
RS_KIND = 24
KINDS = 40

PLAN = (
    ("b3", 6),
    ("cw", 8),
    ("m1", 4),
    ("b2", 5),
    ("a3", 3),
    ("a2", 2),
    ("r1", 9),
    ("rw", 12),
    ("m2", 8),
    ("b5", 7),
    ("a1", 1),
    ("a0", 0),
    ("r4", 13),
    ("sw", 13),
    ("tv", 2),
    ("gp", 5),
    ("gw", 8),
    ("b1", 4),
    ("b4", 6),
    ("r2", 10),
    ("r3", 11),
)


def kernel(
    a_hbm, vt_hbm, row_ref, col_ref, o_ref,
    a_ref, near, cg, cf, rc, v, vt, vtail, turned, ag, tg, c1, cx, xo, xn, sg, wq, w1, w2, ro1, rn1, ro2, rn2, lsem, tsend, trecv, send, recv,
):
    chunks = ag.shape[0]
    depth, width = a_ref.shape[1], v.shape[1]
    group, final = depth // 4, o_ref.shape[-1]
    row, col = lax.axis_index("row"), lax.axis_index("col")
    x, core = row // 2, row % 2
    z, y = col // 4, col % 4
    half = core * 128
    other = 128 - half

    def around(index):
        return {0: index, 1: lax.rem(index + 1, 4), 2: lax.rem(index + 2, 4), -1: lax.rem(index + 3, 4)}

    xs, ys, zs = around(x), around(y), around(z)
    at = {"z": zs, "y": ys}
    peer = {
        ("x", 1): (xs[1] * 2 + core, col),
        ("x", -1): (xs[-1] * 2 + core, col),
        ("y", 1): (row, z * 4 + ys[1]),
        ("y", -1): (row, z * 4 + ys[-1]),
        ("z", 1): (row, zs[1] * 4 + y),
        ("z", -1): (row, zs[-1] * 4 + y),
        "core": (x * 2 + 1 - core, col),
    }
    strips = {step: half + index * 32 for step, index in xs.items()}
    main = ag.shape[-1]
    gather = (("y", "z", pl.ds(0, main // 2)), ("z", "y", pl.ds(main // 2, main // 2)))
    scatter = (("z", "y"), ("y", "z"))

    barrier = pltpu.get_barrier_semaphore()
    for to in peer.values():
        pl.semaphore_signal(barrier, inc=1, device_id=to, device_id_type=MESH)

    def copy(c, kind, src, dst, to):
        return pltpu.make_async_remote_copy(
            src_ref=src, dst_ref=dst, send_sem=send.at[c, kind], recv_sem=recv.at[c, kind],
            device_id=to, device_id_type=MESH,
        )

    def arrived(c, kind, dst):
        copy(c, kind, dst, dst, peer["core"]).wait_recv()

    def sent(c, kind, src):
        copy(c, kind, src, src, peer["core"]).wait_send()

    def block(s, c, step):
        first, _, lanes = gather[s]
        f = at[first][step]
        return ag.at[c, z, f, :, lanes] if first == "y" else ag.at[c, f, y, :, lanes]

    def line(s, c, step, start=0, size=4):
        first, second, lanes = gather[s]
        g, part = at[second][step], pl.ds(start, size)
        return ag.at[c, g, part, :, lanes] if first == "y" else ag.at[c, part, g, :, lanes]

    def a_send(c, s, k, d=1):
        first, second, _ = gather[s]
        if k == 0:
            return block(s, c, 0), peer[first, 1]
        if k == 1:
            return block(s, c, 0), peer[first, -1]
        if k == 2:
            return block(s, c, -d), peer[first, d]
        if k == 3:
            return line(s, c, 0), peer[second, 1]
        if k == 4:
            return line(s, c, 0), peer[second, -1]
        if k == 5:
            return line(s, c, -1, 0, 2), peer[second, 1]
        return line(s, c, 1, 2, 2), peer[second, -1]

    def a_land(c, s, k):
        if k < 3:
            return block(s, c, (-1, 1, 2)[k])
        if k < 5:
            return line(s, c, (-1, 1)[k - 3])
        return line(s, c, 2, 2 * (k - 5), 2)

    def a_start(c, s, k, d=1):
        src, to = a_send(c, s, k, d)
        copy(c, s * 7 + k, src, src, to).start()

    def a_wait(c, s, k):
        arrived(c, s * 7 + k, a_land(c, s, k))

    def t_line(step, start=0, size=4):
        return tg.at[zs[step], pl.ds(start, size)]

    def t_send(k):
        return (
            (tg.at[z, y], peer["y", 1]),
            (tg.at[z, y], peer["y", -1]),
            (tg.at[z, ys[-1]], peer["y", 1]),
            (t_line(0), peer["z", 1]),
            (t_line(0), peer["z", -1]),
            (t_line(-1, 0, 2), peer["z", 1]),
            (t_line(1, 2, 2), peer["z", -1]),
        )[k]

    def t_land(k):
        return (
            tg.at[z, ys[-1]], tg.at[z, ys[1]], tg.at[z, ys[2]],
            t_line(-1), t_line(1), t_line(2, 0, 2), t_line(2, 2, 2),
        )[k]

    def t_copy(k, src, to):
        return pltpu.make_async_remote_copy(
            src_ref=src, dst_ref=src, send_sem=tsend.at[k], recv_sem=trecv.at[k], device_id=to, device_id_type=MESH
        )

    def t_start(*kinds):
        for k in kinds:
            t_copy(k, *t_send(k)).start()

    def t_wait(*kinds):
        for k in kinds:
            t_copy(k, t_land(k), peer["core"]).wait_recv()

    def a0(c):
        ag[c, z, y] = a_ref[pl.ds(pl.multiple_of(c * BLOCK, BLOCK), BLOCK), :main]
        for s in range(2):
            a_start(c, s, 0)
            a_start(c, s, 1)
        pl.when(c == 0)(lambda: t_start(0, 1))

    def a1(c):
        def forward(d):
            for s in range(2):
                a_wait(c, s, 0 if d == 1 else 1)
                a_start(c, s, 2, d)

        @pl.when(c == 0)
        def _():
            t_wait(0)
            t_start(2)

        pl.when(c % 2 == 0)(lambda: forward(1))
        pl.when(c % 2 == 1)(lambda: forward(-1))

    def a2(c):
        pl.when(c % 2 == 0)(lambda: [a_wait(c, s, 1) for s in range(2)] and None)
        pl.when(c % 2 == 1)(lambda: [a_wait(c, s, 0) for s in range(2)] and None)
        for s in range(2):
            a_wait(c, s, 2)
            a_start(c, s, 3)
            a_start(c, s, 4)

        @pl.when(c == 0)
        def _():
            t_wait(1, 2)
            t_start(3, 4)

    def a3(c):
        for s in range(2):
            a_wait(c, s, 3)
            a_start(c, s, 5)
            a_wait(c, s, 4)
            a_start(c, s, 6)

        @pl.when(c == 0)
        def _():
            t_wait(3)
            t_start(5)
            t_wait(4)
            t_start(6)

    def m1(c):
        for s in range(2):
            a_wait(c, s, 5)
            a_wait(c, s, 6)
        pl.when(c == 0)(lambda: t_wait(5, 6))
        ends = tg[:, :, pl.ds(pl.multiple_of(c // 2 * BLOCK, BLOCK), BLOCK), :].reshape(16 * BLOCK, 128)
        mine = lax.broadcasted_iota(jnp.int32, (16 * BLOCK, 128), 1) // 64 == c % 2
        ends = jnp.where(mine, ends.astype(F32), 0.0).astype(BF16)
        rows = ag[c].reshape(16 * BLOCK, main)
        middle = (width // 2 + 127) // 128 * 128
        last = (((1,), (1,)), ((), ()))
        for lo, hi in ((0, middle), (middle, width)):
            part = lax.dot_general(vt[lo:hi, :main], rows, last, preferred_element_type=F32)
            part = part + lax.dot_general(vtail[lo:hi], ends, last, preferred_element_type=F32)
            c1[c % SLOTS, :, lo:hi] = part.astype(BF16).T
        x_start(c, 0)

    def piece(step, start=0, size=32):
        return pl.ds(pl.multiple_of(strips[step] + start, 16), size)

    def x_send(c, k):
        if k == 0:
            return c1.at[c % SLOTS, pl.ds(pl.multiple_of(other, 128), 128)], cx.at[c % SLOTS], peer["core"]
        if k == 9:
            src = sg.at[c % SLOTS, pl.ds(pl.multiple_of(half, 128), 128)]
            return src, src, peer["core"]
        d = 1 if k % 2 == 1 else -1
        part = pl.ds(8 - 8 * d, 16)
        if k < 3:
            return c1.at[c % SLOTS, piece(2, 8 - 8 * d, 16)], xo.at[c, part], peer["x", d]
        if k < 5:
            return c1.at[c % SLOTS, piece(d)], xn.at[c, (k - 3)], peer["x", d]
        src = sg.at[c % SLOTS, piece(0) if k < 7 else piece(-d, 8 - 8 * d, 16)]
        return src, src, peer["x", d]

    def x_land(c, k):
        if k < 5:
            return x_send(c, k)[1]
        if k == 9:
            return sg.at[c % SLOTS, pl.ds(pl.multiple_of(other, 128), 128)]
        d = 1 if k % 2 == 1 else -1
        return sg.at[c % SLOTS, piece(-d) if k < 7 else piece(2, 8 - 8 * d, 16)]

    def x_start(c, k):
        src, dst, to = x_send(c, k)
        copy(c, X_KIND + k, src, dst, to).start()

    def x_wait(c, k):
        arrived(c, X_KIND + k, x_land(c, k))

    def b1(c):
        x_wait(c, 0)
        rows = pl.ds(pl.multiple_of(half, 128), 128)
        c1[c % SLOTS, rows, :] = (c1[c % SLOTS, rows, :].astype(F32) + cx[c % SLOTS].astype(F32)).astype(BF16)
        x_start(c, 1)
        x_start(c, 2)

    def b2(c):
        for k, step in ((1, 1), (2, -1)):
            x_wait(c, k)
            part, rows = pl.ds(16 * (k - 1), 16), piece(step, 16 * (k - 1), 16)
            c1[c % SLOTS, rows, :] = (c1[c % SLOTS, rows, :].astype(F32) + xo[c, part].astype(F32)).astype(BF16)
            x_start(c, k + 2)

    def b3(c):
        gap = rc[pl.ds(core * 8 + x * 2, 2), c].reshape(32, 128)
        x_wait(c, 3)
        x_wait(c, 4)
        rows = piece(0)
        total = c1[c % SLOTS, rows, :].astype(F32) + xn[c, 0].astype(F32) + xn[c, 1].astype(F32)
        sg[c % SLOTS, rows, :] = (total / (gap[:, :1] + cg[0:1, :width])).astype(BF16)
        x_start(c, 5)
        x_start(c, 6)

    def b4(c):
        for k in (5, 6):
            x_wait(c, k)
            x_start(c, k + 2)

    def b5(c):
        x_wait(c, 7)
        x_wait(c, 8)
        x_start(c, 9)

    def r_move(c, s, k):
        first, second = scatter[s]
        fs, gs = at[first], at[second]
        d = 1 if k % 2 == 0 else -1
        if k < 2:
            part = pl.ds(0, CUT) if k == 0 else pl.ds(CUT, group - CUT)
            return w1.at[s, c % SLOTS, fs[2], part], ro1.at[s, c, part], peer[first, d]
        if k < 4:
            return w1.at[s, c % SLOTS, fs[d]], rn1.at[s, c, k - 2], peer[first, d]
        if k < 6:
            part = pl.ds((k - 4) * (WINDOW // 2), WINDOW // 2)
            return w2.at[s, c, gs[2], part], ro2.at[s, c, part], peer[second, d]
        return w2.at[s, c, gs[d]], rn2.at[s, c, k - 6], peer[second, d]

    def r_start(c, s, k):
        src, dst, to = r_move(c, s, k)
        copy(c, RS_KIND + s * 8 + k, src, dst, to).start()

    def r_wait(c, s, k):
        arrived(c, RS_KIND + s * 8 + k, r_move(c, s, k)[1])

    def m2(c):
        x_wait(c, 9)

        turned[...] = sg[c % SLOTS].T

        for g in range(2):
            both = jnp.dot(v[2 * g * group : 2 * (g + 1) * group, :], turned[...], preferred_element_type=F32)
            for q in (2 * g, 2 * g + 1):
                part = both[(q - 2 * g) * group : (q - 2 * g + 1) * group]
                w1[0, c % SLOTS, q] = part[:, :128].astype(BF16)
                for p in range(4):
                    wq[p, q * final : (q + 1) * final] = part[p * final : (p + 1) * final, 128:]
        for p in range(4):
            w1[1, c % SLOTS, p] = wq[p].astype(BF16)
        for s in range(2):
            r_start(c, s, 0)
            r_start(c, s, 1)

    def r1(c):
        for s in range(2):
            up, down = at[scatter[s][0]][1], at[scatter[s][0]][-1]
            r_wait(c, s, 0)
            w1[s, c % SLOTS, up, :CUT] = (w1[s, c % SLOTS, up, :CUT].astype(F32) + ro1[s, c, :CUT].astype(F32)).astype(BF16)
            r_start(c, s, 2)
            r_wait(c, s, 1)
            w1[s, c % SLOTS, down, CUT:] = (w1[s, c % SLOTS, down, CUT:].astype(F32) + ro1[s, c, CUT:].astype(F32)).astype(BF16)
            r_start(c, s, 3)

    def r2(c):
        for s in range(2):
            f = at[scatter[s][0]][0]
            r_wait(c, s, 2)
            r_wait(c, s, 3)
            total = w1[s, c % SLOTS, f].astype(F32) + rn1[s, c, 0].astype(F32) + rn1[s, c, 1].astype(F32)
            total = total.astype(BF16)
            for p in range(4):
                w2[s, c, p] = total[p * STRIDE : p * STRIDE + WINDOW]
            r_start(c, s, 4)
            r_start(c, s, 5)

    def r3(c):
        h = WINDOW // 2
        for s in range(2):
            up, down = at[scatter[s][1]][1], at[scatter[s][1]][-1]
            r_wait(c, s, 4)
            w2[s, c, up, :h] = (w2[s, c, up, :h].astype(F32) + ro2[s, c, :h].astype(F32)).astype(BF16)
            r_start(c, s, 6)
            r_wait(c, s, 5)
            w2[s, c, down, h:] = (w2[s, c, down, h:].astype(F32) + ro2[s, c, h:].astype(F32)).astype(BF16)
            r_start(c, s, 7)

    def r4(c):
        sums = []
        for s in range(2):
            g = at[scatter[s][1]][0]
            r_wait(c, s, 6)
            r_wait(c, s, 7)
            total = w2[s, c, g].astype(F32) + rn2[s, c, 0].astype(F32) + rn2[s, c, 1].astype(F32)
            sums.append(pltpu.roll(total, lax.rem(WINDOW - 4 * g, WINDOW), 0))
        total = jnp.concatenate(sums, axis=1)
        total = jnp.concatenate([total, jnp.zeros((256 - WINDOW, 256), F32)], axis=0)
        gap = rc[:, c].reshape(256, 128)
        gap = jnp.concatenate([gap, gap], axis=1) + cf[0:1, :]
        o_ref[:, c] = (total.T / gap).astype(BF16)[:, :final].reshape(16, BLOCK, final)

    def rw(c):
        for s in range(2):
            for k in range(4):
                sent(c, RS_KIND + s * 8 + k, r_move(c, s, k)[0])

    def gw(c):
        for k in range(5, 10):
            sent(c, X_KIND + k, x_send(c, k)[0])

    def cw(c):
        for k in range(5):
            sent(c, X_KIND + k, x_send(c, k)[0])

    def sw(c):
        @pl.when(c == 0)
        def _():
            for k in range(7):
                t_copy(k, t_send(k)[0], peer["core"]).wait_send()

        for s in range(2):
            for k in range(7):
                sent(c, s * 7 + k, a_send(c, s, k)[0])
            for k in range(4, 8):
                sent(c, RS_KIND + s * 8 + k, r_move(c, s, k)[0])

    load = pltpu.make_async_copy(vt_hbm, vt, lsem.at[0])
    entry = pltpu.make_async_copy(a_hbm, a_ref, lsem.at[1])
    tiles = width // TILE

    def tv(c):
        @pl.when(c == 0)
        def _():
            load.wait()
            ends = vt[:, main:]
            vtail[...] = jnp.concatenate([ends, ends], axis=1)

        def turn(i, carry):
            tile = pl.ds(pl.multiple_of(i * TILE, TILE), TILE)
            v[:, tile] = vt[tile, :].T
            return carry

        lax.fori_loop(2 * c, jnp.minimum(2 * c + 2, tiles), turn, 0)

        @pl.when(c == 5)
        def _():
            v[:, tiles * TILE :] = vt[tiles * TILE :, :].T

    entry.start()
    load.start()
    entry.wait()
    for k in range(0, chunks, 2):
        pair = [a_ref[i * BLOCK : (i + 1) * BLOCK, main:] for i in (k, k + 1) if i < chunks]
        if len(pair) == 1:
            pair.append(jnp.zeros_like(pair[0]))
        tg[z, y, k // 2 * BLOCK : (k // 2 + 1) * BLOCK, :] = jnp.concatenate(pair, axis=1)

    def gp(c):
        inner, outer = col * width, (row * 16 + col) * final
        inner_row = inner // 128
        outer_row = jnp.minimum(outer // 128, col_ref.shape[0] - 3)
        for k in range(12):
            near[:, 128 * k : 128 * (k + 1)] = col_ref[pl.ds(inner_row + k, 1), :]
        for k in range(3):
            near[:, 1536 + 128 * k : 1664 + 128 * k] = col_ref[pl.ds(outer_row + k, 1), :]
        cg[...] = pltpu.roll(jnp.broadcast_to(near[:, :1536], (8, 1536)), (1536 - (inner - inner_row * 128)) % 1536, 1)
        shifted = pltpu.roll(jnp.broadcast_to(near[:, 1536:], (8, 384)), (384 - (outer - outer_row * 128)) % 384, 1)
        cf[...] = shifted[:, :256]
        flat = rc.reshape(16 * chunks * BLOCK, 128)
        for k in range(row_ref.shape[0]):
            flat[k * 128 : (k + 1) * 128, :] = jnp.broadcast_to(row_ref[k : k + 1, :], (128, 128)).T

    pl.semaphore_wait(barrier, len(peer))

    ops = dict(tv=tv, cw=cw, gw=gw, rw=rw, gp=gp, a0=a0, a1=a1, a2=a2, a3=a3, m1=m1, b1=b1, b2=b2, b3=b3, b4=b4, b5=b5, m2=m2, r1=r1, r2=r2, r3=r3, r4=r4, sw=sw)

    def step(t, carry):
        for name, late in PLAN:
            c = t - late
            pl.when(jnp.logical_and(c >= 0, c < {"tv": 6, "gp": 1}.get(name, chunks)))(functools.partial(ops[name], c))
        return carry

    lax.fori_loop(0, chunks + max(late for _, late in PLAN), step, 0)


def on_device(amplitudes, integrals, row_gap, col_gap):
    rows, depth = amplitudes.shape
    width = integrals.shape[1]
    chunks = rows // BLOCK
    final = depth // 16

    vm = pl.BlockSpec(memory_space=pltpu.VMEM)
    anywhere = pl.BlockSpec(memory_space=pl.ANY)
    updated = pl.pallas_call(
        kernel,
        out_shape=jax.ShapeDtypeStruct((16, chunks, BLOCK, final), BF16),
        in_specs=[anywhere, anywhere, vm, vm],
        out_specs=vm,
        scratch_shapes=[
            pltpu.VMEM((rows, depth), BF16),
            pltpu.VMEM((1, 1920), F32),
            pltpu.VMEM((8, 1536), F32),
            pltpu.VMEM((8, 256), F32),
            pltpu.VMEM((16, chunks, BLOCK, 128), F32),
            pltpu.VMEM((depth, width), BF16),
            pltpu.VMEM((width, depth), BF16),
            pltpu.VMEM((width, 128), BF16),
            pltpu.VMEM((width, 256), BF16),
            pltpu.VMEM((chunks, 4, 4, BLOCK, depth // 128 * 128), BF16),
            pltpu.VMEM((4, 4, (chunks + 1) // 2 * BLOCK, 128), BF16),
            pltpu.VMEM((SLOTS, 256, width), BF16),
            pltpu.VMEM((SLOTS, 128, width), BF16),
            pltpu.VMEM((chunks, 32, width), BF16),
            pltpu.VMEM((chunks, 2, 32, width), BF16),
            pltpu.VMEM((SLOTS, 256, width), BF16),
            pltpu.VMEM((4, depth // 4, 128), F32),
            pltpu.VMEM((2, SLOTS, 4, depth // 4, 128), BF16),
            pltpu.VMEM((2, chunks, 4, WINDOW, 128), BF16),
            pltpu.VMEM((2, chunks, depth // 4, 128), BF16),
            pltpu.VMEM((2, chunks, 2, depth // 4, 128), BF16),
            pltpu.VMEM((2, chunks, WINDOW, 128), BF16),
            pltpu.VMEM((2, chunks, 2, WINDOW, 128), BF16),
            pltpu.SemaphoreType.DMA((2,)),
            pltpu.SemaphoreType.DMA((7,)),
            pltpu.SemaphoreType.DMA((7,)),
            pltpu.SemaphoreType.DMA((chunks, KINDS)),
            pltpu.SemaphoreType.DMA((chunks, KINDS)),
        ],
        compiler_params=pltpu.CompilerParams(
            collective_id=0, has_side_effects=True, vmem_limit_bytes=62 * 1024 * 1024
        ),
        cost_estimate=pl.CostEstimate(
            flops=4 * 16 * rows * depth * width, bytes_accessed=2 * depth * width, transcendentals=0
        ),
    )(amplitudes, integrals.T, row_gap.reshape(-1, 128), col_gap.reshape(-1, 128))
    return updated.reshape(16 * rows, final)


def solution(mesh):
    return jax.shard_map(
        on_device,
        mesh=mesh,
        in_specs=(P("col", "row"), P("row", "col"), P(), P()),
        out_specs=P(None, ("row", "col")),
        check_vma=False,
    )
```

```python
import functools

import jax
import jax.numpy as jnp
from jax import lax
from jax.experimental import pallas as pl
from jax.experimental.pallas import tpu as pltpu
from jax.sharding import PartitionSpec as P

MESH = pl.DeviceIdType.MESH
F32 = jnp.float32
BF16 = jnp.bfloat16

BLOCK = 16
WINDOW = 192
STRIDE = 176
TILE = 128
CUT = 368
SLOTS = 4
X_KIND = 14
RS_KIND = 24
KINDS = 40

PLAN = (
    ("b3", 6),
    ("cw", 8),
    ("m1", 4),
    ("b2", 5),
    ("a3", 3),
    ("a2", 2),
    ("r1", 9),
    ("rw", 12),
    ("m2", 8),
    ("b5", 7),
    ("a1", 1),
    ("a0", 0),
    ("r4", 13),
    ("sw", 13),
    ("tv", 2),
    ("gp", 5),
    ("gw", 8),
    ("b1", 4),
    ("b4", 6),
    ("r2", 10),
    ("r3", 11),
)


def kernel(
    a_hbm, vt_hbm, row_ref, col_ref, o_ref,
    a_ref, near, cg, cf, rc, v, vt, vtail, turned, ag, tg, c1, cx, xo, xn, sg, wq, w1, w2, ro1, rn1, ro2, rn2, pace, lsem, tsend, trecv, send, recv,
):
    chunks = ag.shape[0]
    depth, width = a_ref.shape[1], v.shape[1]
    group, final = depth // 4, o_ref.shape[-1]
    row, col = lax.axis_index("row"), lax.axis_index("col")
    x, core = row // 2, row % 2
    z, y = col // 4, col % 4
    half = core * 128
    other = 128 - half

    def around(index):
        return {0: index, 1: lax.rem(index + 1, 4), 2: lax.rem(index + 2, 4), -1: lax.rem(index + 3, 4)}

    xs, ys, zs = around(x), around(y), around(z)
    at = {"z": zs, "y": ys}
    peer = {
        ("x", 1): (xs[1] * 2 + core, col),
        ("x", -1): (xs[-1] * 2 + core, col),
        ("y", 1): (row, z * 4 + ys[1]),
        ("y", -1): (row, z * 4 + ys[-1]),
        ("z", 1): (row, zs[1] * 4 + y),
        ("z", -1): (row, zs[-1] * 4 + y),
        "core": (x * 2 + 1 - core, col),
    }
    strips = {step: half + index * 32 for step, index in xs.items()}
    main = ag.shape[-1]
    gather = (("y", "z", pl.ds(0, main // 2)), ("z", "y", pl.ds(main // 2, main // 2)))
    scatter = (("z", "y"), ("y", "z"))

    barrier = pltpu.get_barrier_semaphore()
    for to in peer.values():
        pl.semaphore_signal(barrier, inc=1, device_id=to, device_id_type=MESH)

    def copy(c, kind, src, dst, to):
        return pltpu.make_async_remote_copy(
            src_ref=src, dst_ref=dst, send_sem=send.at[c, kind], recv_sem=recv.at[c, kind],
            device_id=to, device_id_type=MESH,
        )

    def arrived(c, kind, dst):
        copy(c, kind, dst, dst, peer["core"]).wait_recv()

    def sent(c, kind, src):
        copy(c, kind, src, src, peer["core"]).wait_send()

    def block(s, c, step):
        first, _, lanes = gather[s]
        f = at[first][step]
        return ag.at[c, z, f, :, lanes] if first == "y" else ag.at[c, f, y, :, lanes]

    def line(s, c, step, start=0, size=4):
        first, second, lanes = gather[s]
        g, part = at[second][step], pl.ds(start, size)
        return ag.at[c, g, part, :, lanes] if first == "y" else ag.at[c, part, g, :, lanes]

    def a_send(c, s, k, d=1):
        first, second, _ = gather[s]
        if k == 0:
            return block(s, c, 0), peer[first, 1]
        if k == 1:
            return block(s, c, 0), peer[first, -1]
        if k == 2:
            return block(s, c, -d), peer[first, d]
        if k == 3:
            return line(s, c, 0), peer[second, 1]
        if k == 4:
            return line(s, c, 0), peer[second, -1]
        if k == 5:
            return line(s, c, -1, 0, 2), peer[second, 1]
        return line(s, c, 1, 2, 2), peer[second, -1]

    def a_land(c, s, k):
        if k < 3:
            return block(s, c, (-1, 1, 2)[k])
        if k < 5:
            return line(s, c, (-1, 1)[k - 3])
        return line(s, c, 2, 2 * (k - 5), 2)

    def a_start(c, s, k, d=1):
        src, to = a_send(c, s, k, d)
        copy(c, s * 7 + k, src, src, to).start()

    def a_wait(c, s, k):
        arrived(c, s * 7 + k, a_land(c, s, k))

    def t_line(step, start=0, size=4):
        return tg.at[zs[step], pl.ds(start, size)]

    def t_send(k):
        return (
            (tg.at[z, y], peer["y", 1]),
            (tg.at[z, y], peer["y", -1]),
            (tg.at[z, ys[-1]], peer["y", 1]),
            (t_line(0), peer["z", 1]),
            (t_line(0), peer["z", -1]),
            (t_line(-1, 0, 2), peer["z", 1]),
            (t_line(1, 2, 2), peer["z", -1]),
        )[k]

    def t_land(k):
        return (
            tg.at[z, ys[-1]], tg.at[z, ys[1]], tg.at[z, ys[2]],
            t_line(-1), t_line(1), t_line(2, 0, 2), t_line(2, 2, 2),
        )[k]

    def t_copy(k, src, to):
        return pltpu.make_async_remote_copy(
            src_ref=src, dst_ref=src, send_sem=tsend.at[k], recv_sem=trecv.at[k], device_id=to, device_id_type=MESH
        )

    def t_start(*kinds):
        for k in kinds:
            t_copy(k, *t_send(k)).start()

    def t_wait(*kinds):
        for k in kinds:
            t_copy(k, t_land(k), peer["core"]).wait_recv()

    def a0(c):
        ag[c, z, y] = a_ref[pl.ds(pl.multiple_of(c * BLOCK, BLOCK), BLOCK), :main]
        for s in range(2):
            a_start(c, s, 0)
            a_start(c, s, 1)
        pl.when(c == 0)(lambda: t_start(0, 1))

    def a1(c):
        def forward(d):
            for s in range(2):
                a_wait(c, s, 0 if d == 1 else 1)
                a_start(c, s, 2, d)

        @pl.when(c == 0)
        def _():
            t_wait(0)
            t_start(2)

        pl.when(c % 2 == 0)(lambda: forward(1))
        pl.when(c % 2 == 1)(lambda: forward(-1))

    def a2(c):
        pl.when(c % 2 == 0)(lambda: [a_wait(c, s, 1) for s in range(2)] and None)
        pl.when(c % 2 == 1)(lambda: [a_wait(c, s, 0) for s in range(2)] and None)
        for s in range(2):
            a_wait(c, s, 2)
            a_start(c, s, 3)
            a_start(c, s, 4)

        @pl.when(c == 0)
        def _():
            t_wait(1, 2)
            t_start(3, 4)

    def a3(c):
        for s in range(2):
            a_wait(c, s, 3)
            a_start(c, s, 5)
            a_wait(c, s, 4)
            a_start(c, s, 6)

        @pl.when(c == 0)
        def _():
            t_wait(3)
            t_start(5)
            t_wait(4)
            t_start(6)

    def m1(c):
        for s in range(2):
            a_wait(c, s, 5)
            a_wait(c, s, 6)
        pl.when(c == 0)(lambda: t_wait(5, 6))
        ends = tg[:, :, pl.ds(pl.multiple_of(c // 2 * BLOCK, BLOCK), BLOCK), :].reshape(16 * BLOCK, 128)
        mine = lax.broadcasted_iota(jnp.int32, (16 * BLOCK, 128), 1) // 64 == c % 2
        ends = jnp.where(mine, ends.astype(F32), 0.0).astype(BF16)
        rows = ag[c].reshape(16 * BLOCK, main)
        middle = (width // 2 + 127) // 128 * 128
        last = (((1,), (1,)), ((), ()))
        for lo, hi in ((0, middle), (middle, width)):
            part = lax.dot_general(vt[lo:hi, :main], rows, last, preferred_element_type=F32)
            part = part + lax.dot_general(vtail[lo:hi], ends, last, preferred_element_type=F32)
            c1[c % SLOTS, :, lo:hi] = part.astype(BF16).T
        x_start(c, 0)

    def piece(step, start=0, size=32):
        return pl.ds(pl.multiple_of(strips[step] + start, 16), size)

    def x_send(c, k):
        if k == 0:
            return c1.at[c % SLOTS, pl.ds(pl.multiple_of(other, 128), 128)], cx.at[c % SLOTS], peer["core"]
        if k == 9:
            src = sg.at[c % SLOTS, pl.ds(pl.multiple_of(half, 128), 128)]
            return src, src, peer["core"]
        d = 1 if k % 2 == 1 else -1
        part = pl.ds(8 - 8 * d, 16)
        if k < 3:
            return c1.at[c % SLOTS, piece(2, 8 - 8 * d, 16)], xo.at[c, part], peer["x", d]
        if k < 5:
            return c1.at[c % SLOTS, piece(d)], xn.at[c, (k - 3)], peer["x", d]
        src = sg.at[c % SLOTS, piece(0) if k < 7 else piece(-d, 8 - 8 * d, 16)]
        return src, src, peer["x", d]

    def x_land(c, k):
        if k < 5:
            return x_send(c, k)[1]
        if k == 9:
            return sg.at[c % SLOTS, pl.ds(pl.multiple_of(other, 128), 128)]
        d = 1 if k % 2 == 1 else -1
        return sg.at[c % SLOTS, piece(-d) if k < 7 else piece(2, 8 - 8 * d, 16)]

    def x_start(c, k):
        src, dst, to = x_send(c, k)
        copy(c, X_KIND + k, src, dst, to).start()

    def x_wait(c, k):
        arrived(c, X_KIND + k, x_land(c, k))

    def b1(c):
        x_wait(c, 0)
        rows = pl.ds(pl.multiple_of(half, 128), 128)
        c1[c % SLOTS, rows, :] = (c1[c % SLOTS, rows, :].astype(F32) + cx[c % SLOTS].astype(F32)).astype(BF16)
        x_start(c, 1)
        x_start(c, 2)

    def b2(c):
        for k, step in ((1, 1), (2, -1)):
            x_wait(c, k)
            part, rows = pl.ds(16 * (k - 1), 16), piece(step, 16 * (k - 1), 16)
            c1[c % SLOTS, rows, :] = (c1[c % SLOTS, rows, :].astype(F32) + xo[c, part].astype(F32)).astype(BF16)
            x_start(c, k + 2)

    def b3(c):
        gap = rc[pl.ds(core * 8 + x * 2, 2), c].reshape(32, 128)
        x_wait(c, 3)
        x_wait(c, 4)
        rows = piece(0)
        total = c1[c % SLOTS, rows, :].astype(F32) + xn[c, 0].astype(F32) + xn[c, 1].astype(F32)
        sg[c % SLOTS, rows, :] = (total / (gap[:, :1] + cg[0:1, :width])).astype(BF16)
        x_start(c, 5)
        x_start(c, 6)

    def b4(c):
        for k in (5, 6):
            x_wait(c, k)
            x_start(c, k + 2)

    def b5(c):
        x_wait(c, 7)
        x_wait(c, 8)
        x_start(c, 9)

    def r_move(c, s, k):
        first, second = scatter[s]
        fs, gs = at[first], at[second]
        d = 1 if k % 2 == 0 else -1
        if k < 2:
            part = pl.ds(0, CUT) if k == 0 else pl.ds(CUT, group - CUT)
            return w1.at[s, c % SLOTS, fs[2], part], ro1.at[s, c, part], peer[first, d]
        if k < 4:
            return w1.at[s, c % SLOTS, fs[d]], rn1.at[s, c, k - 2], peer[first, d]
        if k < 6:
            part = pl.ds((k - 4) * (WINDOW // 2), WINDOW // 2)
            return w2.at[s, c, gs[2], part], ro2.at[s, c, part], peer[second, d]
        return w2.at[s, c, gs[d]], rn2.at[s, c, k - 6], peer[second, d]

    def r_start(c, s, k):
        src, dst, to = r_move(c, s, k)
        copy(c, RS_KIND + s * 8 + k, src, dst, to).start()

    def r_wait(c, s, k):
        arrived(c, RS_KIND + s * 8 + k, r_move(c, s, k)[1])

    def m2(c):
        x_wait(c, 9)

        turned[...] = sg[c % SLOTS].T

        for g in range(2):
            both = jnp.dot(v[2 * g * group : 2 * (g + 1) * group, :], turned[...], preferred_element_type=F32)
            for q in (2 * g, 2 * g + 1):
                part = both[(q - 2 * g) * group : (q - 2 * g + 1) * group]
                w1[0, c % SLOTS, q] = part[:, :128].astype(BF16)
                for p in range(4):
                    wq[p, q * final : (q + 1) * final] = part[p * final : (p + 1) * final, 128:]
        for p in range(4):
            w1[1, c % SLOTS, p] = wq[p].astype(BF16)
        for s in range(2):
            r_start(c, s, 0)
            r_start(c, s, 1)

    def r1(c):
        pl.semaphore_signal(pace.at[c], inc=1, device_id=peer["core"], device_id_type=MESH)
        pl.semaphore_wait(pace.at[c], 1)
        for s in range(2):
            up, down = at[scatter[s][0]][1], at[scatter[s][0]][-1]
            r_wait(c, s, 0)
            w1[s, c % SLOTS, up, :CUT] = (w1[s, c % SLOTS, up, :CUT].astype(F32) + ro1[s, c, :CUT].astype(F32)).astype(BF16)
            r_start(c, s, 2)
            r_wait(c, s, 1)
            w1[s, c % SLOTS, down, CUT:] = (w1[s, c % SLOTS, down, CUT:].astype(F32) + ro1[s, c, CUT:].astype(F32)).astype(BF16)
            r_start(c, s, 3)

    def r2(c):
        for s in range(2):
            f = at[scatter[s][0]][0]
            r_wait(c, s, 2)
            r_wait(c, s, 3)
            total = w1[s, c % SLOTS, f].astype(F32) + rn1[s, c, 0].astype(F32) + rn1[s, c, 1].astype(F32)
            total = total.astype(BF16)
            for p in range(4):
                w2[s, c, p] = total[p * STRIDE : p * STRIDE + WINDOW]
            r_start(c, s, 4)
            r_start(c, s, 5)

    def r3(c):
        h = WINDOW // 2
        for s in range(2):
            up, down = at[scatter[s][1]][1], at[scatter[s][1]][-1]
            r_wait(c, s, 4)
            w2[s, c, up, :h] = (w2[s, c, up, :h].astype(F32) + ro2[s, c, :h].astype(F32)).astype(BF16)
            r_start(c, s, 6)
            r_wait(c, s, 5)
            w2[s, c, down, h:] = (w2[s, c, down, h:].astype(F32) + ro2[s, c, h:].astype(F32)).astype(BF16)
            r_start(c, s, 7)

    def r4(c):
        sums = []
        for s in range(2):
            g = at[scatter[s][1]][0]
            r_wait(c, s, 6)
            r_wait(c, s, 7)
            total = w2[s, c, g].astype(F32) + rn2[s, c, 0].astype(F32) + rn2[s, c, 1].astype(F32)
            sums.append(pltpu.roll(total, lax.rem(WINDOW - 4 * g, WINDOW), 0))
        total = jnp.concatenate(sums, axis=1)
        total = jnp.concatenate([total, jnp.zeros((256 - WINDOW, 256), F32)], axis=0)
        gap = rc[:, c].reshape(256, 128)
        gap = jnp.concatenate([gap, gap], axis=1) + cf[0:1, :]
        o_ref[:, c] = (total.T / gap).astype(BF16)[:, :final].reshape(16, BLOCK, final)

    def rw(c):
        for s in range(2):
            for k in range(4):
                sent(c, RS_KIND + s * 8 + k, r_move(c, s, k)[0])

    def gw(c):
        for k in range(5, 10):
            sent(c, X_KIND + k, x_send(c, k)[0])

    def cw(c):
        for k in range(5):
            sent(c, X_KIND + k, x_send(c, k)[0])

    def sw(c):
        @pl.when(c == 0)
        def _():
            for k in range(7):
                t_copy(k, t_send(k)[0], peer["core"]).wait_send()

        for s in range(2):
            for k in range(7):
                sent(c, s * 7 + k, a_send(c, s, k)[0])
            for k in range(4, 8):
                sent(c, RS_KIND + s * 8 + k, r_move(c, s, k)[0])

    load = pltpu.make_async_copy(vt_hbm, vt, lsem.at[0])
    entry = pltpu.make_async_copy(a_hbm, a_ref, lsem.at[1])
    tiles = width // TILE

    def tv(c):
        @pl.when(c == 0)
        def _():
            load.wait()
            ends = vt[:, main:]
            vtail[...] = jnp.concatenate([ends, ends], axis=1)

        def turn(i, carry):
            tile = pl.ds(pl.multiple_of(i * TILE, TILE), TILE)
            v[:, tile] = vt[tile, :].T
            return carry

        lax.fori_loop(2 * c, jnp.minimum(2 * c + 2, tiles), turn, 0)

        @pl.when(c == 5)
        def _():
            v[:, tiles * TILE :] = vt[tiles * TILE :, :].T

    entry.start()
    load.start()
    entry.wait()
    for k in range(0, chunks, 2):
        pair = [a_ref[i * BLOCK : (i + 1) * BLOCK, main:] for i in (k, k + 1) if i < chunks]
        if len(pair) == 1:
            pair.append(jnp.zeros_like(pair[0]))
        tg[z, y, k // 2 * BLOCK : (k // 2 + 1) * BLOCK, :] = jnp.concatenate(pair, axis=1)

    def gp(c):
        inner, outer = col * width, (row * 16 + col) * final
        inner_row = inner // 128
        outer_row = jnp.minimum(outer // 128, col_ref.shape[0] - 3)
        for k in range(12):
            near[:, 128 * k : 128 * (k + 1)] = col_ref[pl.ds(inner_row + k, 1), :]
        for k in range(3):
            near[:, 1536 + 128 * k : 1664 + 128 * k] = col_ref[pl.ds(outer_row + k, 1), :]
        cg[...] = pltpu.roll(jnp.broadcast_to(near[:, :1536], (8, 1536)), (1536 - (inner - inner_row * 128)) % 1536, 1)
        shifted = pltpu.roll(jnp.broadcast_to(near[:, 1536:], (8, 384)), (384 - (outer - outer_row * 128)) % 384, 1)
        cf[...] = shifted[:, :256]
        flat = rc.reshape(16 * chunks * BLOCK, 128)
        for k in range(row_ref.shape[0]):
            flat[k * 128 : (k + 1) * 128, :] = jnp.broadcast_to(row_ref[k : k + 1, :], (128, 128)).T

    pl.semaphore_wait(barrier, len(peer))

    ops = dict(tv=tv, cw=cw, gw=gw, rw=rw, gp=gp, a0=a0, a1=a1, a2=a2, a3=a3, m1=m1, b1=b1, b2=b2, b3=b3, b4=b4, b5=b5, m2=m2, r1=r1, r2=r2, r3=r3, r4=r4, sw=sw)

    def step(t, carry):
        for name, late in PLAN:
            c = t - late
            pl.when(jnp.logical_and(c >= 0, c < {"tv": 6, "gp": 1}.get(name, chunks)))(functools.partial(ops[name], c))
        return carry

    lax.fori_loop(0, chunks + max(late for _, late in PLAN), step, 0)


def on_device(amplitudes, integrals, row_gap, col_gap):
    rows, depth = amplitudes.shape
    width = integrals.shape[1]
    chunks = rows // BLOCK
    final = depth // 16

    vm = pl.BlockSpec(memory_space=pltpu.VMEM)
    anywhere = pl.BlockSpec(memory_space=pl.ANY)
    updated = pl.pallas_call(
        kernel,
        out_shape=jax.ShapeDtypeStruct((16, chunks, BLOCK, final), BF16),
        in_specs=[anywhere, anywhere, vm, vm],
        out_specs=vm,
        scratch_shapes=[
            pltpu.VMEM((rows, depth), BF16),
            pltpu.VMEM((1, 1920), F32),
            pltpu.VMEM((8, 1536), F32),
            pltpu.VMEM((8, 256), F32),
            pltpu.VMEM((16, chunks, BLOCK, 128), F32),
            pltpu.VMEM((depth, width), BF16),
            pltpu.VMEM((width, depth), BF16),
            pltpu.VMEM((width, 128), BF16),
            pltpu.VMEM((width, 256), BF16),
            pltpu.VMEM((chunks, 4, 4, BLOCK, depth // 128 * 128), BF16),
            pltpu.VMEM((4, 4, (chunks + 1) // 2 * BLOCK, 128), BF16),
            pltpu.VMEM((SLOTS, 256, width), BF16),
            pltpu.VMEM((SLOTS, 128, width), BF16),
            pltpu.VMEM((chunks, 32, width), BF16),
            pltpu.VMEM((chunks, 2, 32, width), BF16),
            pltpu.VMEM((SLOTS, 256, width), BF16),
            pltpu.VMEM((4, depth // 4, 128), F32),
            pltpu.VMEM((2, SLOTS, 4, depth // 4, 128), BF16),
            pltpu.VMEM((2, chunks, 4, WINDOW, 128), BF16),
            pltpu.VMEM((2, chunks, depth // 4, 128), BF16),
            pltpu.VMEM((2, chunks, 2, depth // 4, 128), BF16),
            pltpu.VMEM((2, chunks, WINDOW, 128), BF16),
            pltpu.VMEM((2, chunks, 2, WINDOW, 128), BF16),
            pltpu.SemaphoreType.REGULAR((chunks,)),
            pltpu.SemaphoreType.DMA((2,)),
            pltpu.SemaphoreType.DMA((7,)),
            pltpu.SemaphoreType.DMA((7,)),
            pltpu.SemaphoreType.DMA((chunks, KINDS)),
            pltpu.SemaphoreType.DMA((chunks, KINDS)),
        ],
        compiler_params=pltpu.CompilerParams(
            collective_id=0, has_side_effects=True, vmem_limit_bytes=62 * 1024 * 1024
        ),
        cost_estimate=pl.CostEstimate(
            flops=4 * 16 * rows * depth * width, bytes_accessed=2 * depth * width, transcendentals=0
        ),
    )(amplitudes, integrals.T, row_gap.reshape(-1, 128), col_gap.reshape(-1, 128))
    return updated.reshape(16 * rows, final)


def solution(mesh):
    return jax.shard_map(
        on_device,
        mesh=mesh,
        in_specs=(P("col", "row"), P("row", "col"), P(), P()),
        out_specs=P(None, ("row", "col")),
        check_vma=False,
    )
```

```python
import functools

import jax
import jax.numpy as jnp
from jax import lax
from jax.experimental import pallas as pl
from jax.experimental.pallas import tpu as pltpu
from jax.sharding import PartitionSpec as P

MESH = pl.DeviceIdType.MESH
F32 = jnp.float32
BF16 = jnp.bfloat16

BLOCK = 16
WINDOW = 192
STRIDE = 176
TILE = 128
CUT = 368
SLOTS = 4
X_KIND = 14
RS_KIND = 24
KINDS = 40

PLAN = (
    ("a0", (0, 1, 2, 3, 5, 8, 10)),
    ("b5", (21, 24, 27, 29, 31, 33, 35)),
    ("m1", (10, 15, 16, 19, 21, 25, 27)),
    ("m2", (23, 26, 29, 31, 33, 34, 37)),
    ("b2", (13, 17, 20, 24, 26, 28, 31)),
    ("b4", (17, 22, 25, 26, 29, 32, 33)),
    ("a2", (5, 7, 10, 13, 14, 18, 21)),
    ("b1", (11, 16, 17, 21, 24, 27, 30)),
    ("r2", (27, 31, 35, 36, 39, 40, 42)),
    ("r3", (28, 36, 40, 41, 42, 43, 44)),
    ("tv", (3, 5, 6)),
    ("r4", (32, 37, 43, 44, 45, 46, 47)),
    ("b3", (15, 19, 21, 25, 27, 30, 32)),
    ("a1", (3, 4, 8, 9, 11, 12, 18)),
    ("a3", (5, 10, 12, 16, 17, 22, 24)),
    ("r1", (25, 29, 31, 32, 34, 37, 38)),
)


def kernel(
    a_hbm, vt_hbm, row_ref, col_ref, o_ref,
    a_ref, near, cg, cf, rc, v, vt, vtail, turned, ag, tg, c1, cx, xo, xn, sg, wq, w1, w2, ro1, rn1, ro2, rn2, lsem, tsend, trecv, send, recv,
):
    chunks = ag.shape[0]
    depth, width = a_ref.shape[1], v.shape[1]
    group, final = depth // 4, o_ref.shape[-1]
    row, col = lax.axis_index("row"), lax.axis_index("col")
    x, core = row // 2, row % 2
    z, y = col // 4, col % 4
    half = core * 128
    other = 128 - half

    def around(index):
        return {0: index, 1: lax.rem(index + 1, 4), 2: lax.rem(index + 2, 4), -1: lax.rem(index + 3, 4)}

    xs, ys, zs = around(x), around(y), around(z)
    at = {"z": zs, "y": ys}
    peer = {
        ("x", 1): (xs[1] * 2 + core, col),
        ("x", -1): (xs[-1] * 2 + core, col),
        ("y", 1): (row, z * 4 + ys[1]),
        ("y", -1): (row, z * 4 + ys[-1]),
        ("z", 1): (row, zs[1] * 4 + y),
        ("z", -1): (row, zs[-1] * 4 + y),
        "core": (x * 2 + 1 - core, col),
    }
    strips = {step: half + index * 32 for step, index in xs.items()}
    main = ag.shape[-1]
    gather = (("y", "z", pl.ds(0, main // 2)), ("z", "y", pl.ds(main // 2, main // 2)))
    scatter = (("z", "y"), ("y", "z"))

    barrier = pltpu.get_barrier_semaphore()
    for to in peer.values():
        pl.semaphore_signal(barrier, inc=1, device_id=to, device_id_type=MESH)

    def copy(c, kind, src, dst, to):
        return pltpu.make_async_remote_copy(
            src_ref=src, dst_ref=dst, send_sem=send.at[c, kind], recv_sem=recv.at[c, kind],
            device_id=to, device_id_type=MESH,
        )

    def arrived(c, kind, dst):
        copy(c, kind, dst, dst, peer["core"]).wait_recv()

    def sent(c, kind, src):
        copy(c, kind, src, src, peer["core"]).wait_send()

    def block(s, c, step):
        first, _, lanes = gather[s]
        f = at[first][step]
        return ag.at[c, z, f, :, lanes] if first == "y" else ag.at[c, f, y, :, lanes]

    def line(s, c, step, start=0, size=4):
        first, second, lanes = gather[s]
        g, part = at[second][step], pl.ds(start, size)
        return ag.at[c, g, part, :, lanes] if first == "y" else ag.at[c, part, g, :, lanes]

    def a_send(c, s, k, d=1):
        first, second, _ = gather[s]
        if k == 0:
            return block(s, c, 0), peer[first, 1]
        if k == 1:
            return block(s, c, 0), peer[first, -1]
        if k == 2:
            return block(s, c, -d), peer[first, d]
        if k == 3:
            return line(s, c, 0), peer[second, 1]
        if k == 4:
            return line(s, c, 0), peer[second, -1]
        if k == 5:
            return line(s, c, -1, 0, 2), peer[second, 1]
        return line(s, c, 1, 2, 2), peer[second, -1]

    def a_land(c, s, k):
        if k < 3:
            return block(s, c, (-1, 1, 2)[k])
        if k < 5:
            return line(s, c, (-1, 1)[k - 3])
        return line(s, c, 2, 2 * (k - 5), 2)

    def a_start(c, s, k, d=1):
        src, to = a_send(c, s, k, d)
        copy(c, s * 7 + k, src, src, to).start()

    def a_wait(c, s, k):
        arrived(c, s * 7 + k, a_land(c, s, k))

    def t_line(step, start=0, size=4):
        return tg.at[zs[step], pl.ds(start, size)]

    def t_send(k):
        return (
            (tg.at[z, y], peer["y", 1]),
            (tg.at[z, y], peer["y", -1]),
            (tg.at[z, ys[-1]], peer["y", 1]),
            (t_line(0), peer["z", 1]),
            (t_line(0), peer["z", -1]),
            (t_line(-1, 0, 2), peer["z", 1]),
            (t_line(1, 2, 2), peer["z", -1]),
        )[k]

    def t_land(k):
        return (
            tg.at[z, ys[-1]], tg.at[z, ys[1]], tg.at[z, ys[2]],
            t_line(-1), t_line(1), t_line(2, 0, 2), t_line(2, 2, 2),
        )[k]

    def t_copy(k, src, to):
        return pltpu.make_async_remote_copy(
            src_ref=src, dst_ref=src, send_sem=tsend.at[k], recv_sem=trecv.at[k], device_id=to, device_id_type=MESH
        )

    def t_start(*kinds):
        for k in kinds:
            t_copy(k, *t_send(k)).start()

    def t_wait(*kinds):
        for k in kinds:
            t_copy(k, t_land(k), peer["core"]).wait_recv()

    def a0(c):
        ag[c, z, y] = a_ref[pl.ds(pl.multiple_of(c * BLOCK, BLOCK), BLOCK), :main]
        for s in range(2):
            a_start(c, s, 0)
            a_start(c, s, 1)
        pl.when(c == 0)(lambda: t_start(0, 1))

    def a1(c):
        def forward(d):
            for s in range(2):
                a_wait(c, s, 0 if d == 1 else 1)
                a_start(c, s, 2, d)

        @pl.when(c == 0)
        def _():
            t_wait(0)
            t_start(2)

        pl.when(c % 2 == 0)(lambda: forward(1))
        pl.when(c % 2 == 1)(lambda: forward(-1))

    def a2(c):
        pl.when(c % 2 == 0)(lambda: [a_wait(c, s, 1) for s in range(2)] and None)
        pl.when(c % 2 == 1)(lambda: [a_wait(c, s, 0) for s in range(2)] and None)
        for s in range(2):
            a_wait(c, s, 2)
            a_start(c, s, 3)
            a_start(c, s, 4)

        @pl.when(c == 0)
        def _():
            t_wait(1, 2)
            t_start(3, 4)

    def a3(c):
        for s in range(2):
            a_wait(c, s, 3)
            a_start(c, s, 5)
            a_wait(c, s, 4)
            a_start(c, s, 6)

        @pl.when(c == 0)
        def _():
            t_wait(3)
            t_start(5)
            t_wait(4)
            t_start(6)

    def m1(c):
        pl.when(c >= SLOTS)(lambda: cw(c - SLOTS))
        for s in range(2):
            a_wait(c, s, 5)
            a_wait(c, s, 6)
        pl.when(c == 0)(lambda: t_wait(5, 6))
        ends = tg[:, :, pl.ds(pl.multiple_of(c // 2 * BLOCK, BLOCK), BLOCK), :].reshape(16 * BLOCK, 128)
        mine = lax.broadcasted_iota(jnp.int32, (16 * BLOCK, 128), 1) // 64 == c % 2
        ends = jnp.where(mine, ends.astype(F32), 0.0).astype(BF16)
        rows = ag[c].reshape(16 * BLOCK, main)
        middle = (width // 2 + 127) // 128 * 128
        last = (((1,), (1,)), ((), ()))
        for lo, hi in ((0, middle), (middle, width)):
            part = lax.dot_general(vt[lo:hi, :main], rows, last, preferred_element_type=F32)
            part = part + lax.dot_general(vtail[lo:hi], ends, last, preferred_element_type=F32)
            c1[c % SLOTS, :, lo:hi] = part.astype(BF16).T
        x_start(c, 0)

    def piece(step, start=0, size=32):
        return pl.ds(pl.multiple_of(strips[step] + start, 16), size)

    def x_send(c, k):
        if k == 0:
            return c1.at[c % SLOTS, pl.ds(pl.multiple_of(other, 128), 128)], cx.at[c % SLOTS], peer["core"]
        if k == 9:
            src = sg.at[c % SLOTS, pl.ds(pl.multiple_of(half, 128), 128)]
            return src, src, peer["core"]
        d = 1 if k % 2 == 1 else -1
        part = pl.ds(8 - 8 * d, 16)
        if k < 3:
            return c1.at[c % SLOTS, piece(2, 8 - 8 * d, 16)], xo.at[c, part], peer["x", d]
        if k < 5:
            return c1.at[c % SLOTS, piece(d)], xn.at[c, (k - 3)], peer["x", d]
        src = sg.at[c % SLOTS, piece(0) if k < 7 else piece(-d, 8 - 8 * d, 16)]
        return src, src, peer["x", d]

    def x_land(c, k):
        if k < 5:
            return x_send(c, k)[1]
        if k == 9:
            return sg.at[c % SLOTS, pl.ds(pl.multiple_of(other, 128), 128)]
        d = 1 if k % 2 == 1 else -1
        return sg.at[c % SLOTS, piece(-d) if k < 7 else piece(2, 8 - 8 * d, 16)]

    def x_start(c, k):
        src, dst, to = x_send(c, k)
        copy(c, X_KIND + k, src, dst, to).start()

    def x_wait(c, k):
        arrived(c, X_KIND + k, x_land(c, k))

    def b1(c):
        pl.when(c >= SLOTS)(lambda: gw(c - SLOTS))
        x_wait(c, 0)
        rows = pl.ds(pl.multiple_of(half, 128), 128)
        c1[c % SLOTS, rows, :] = (c1[c % SLOTS, rows, :].astype(F32) + cx[c % SLOTS].astype(F32)).astype(BF16)
        x_start(c, 1)
        x_start(c, 2)

    def b2(c):
        for k, step in ((1, 1), (2, -1)):
            x_wait(c, k)
            part, rows = pl.ds(16 * (k - 1), 16), piece(step, 16 * (k - 1), 16)
            c1[c % SLOTS, rows, :] = (c1[c % SLOTS, rows, :].astype(F32) + xo[c, part].astype(F32)).astype(BF16)
            x_start(c, k + 2)

    def b3(c):
        gap = rc[pl.ds(core * 8 + x * 2, 2), c].reshape(32, 128)
        x_wait(c, 3)
        x_wait(c, 4)
        rows = piece(0)
        total = c1[c % SLOTS, rows, :].astype(F32) + xn[c, 0].astype(F32) + xn[c, 1].astype(F32)
        sg[c % SLOTS, rows, :] = (total / (gap[:, :1] + cg[0:1, :width])).astype(BF16)
        x_start(c, 5)
        x_start(c, 6)

    def b4(c):
        for k in (5, 6):
            x_wait(c, k)
            x_start(c, k + 2)

    def b5(c):
        x_wait(c, 7)
        x_wait(c, 8)
        x_start(c, 9)

    def r_move(c, s, k):
        first, second = scatter[s]
        fs, gs = at[first], at[second]
        d = 1 if k % 2 == 0 else -1
        if k < 2:
            part = pl.ds(0, CUT) if k == 0 else pl.ds(CUT, group - CUT)
            return w1.at[s, c % SLOTS, fs[2], part], ro1.at[s, c, part], peer[first, d]
        if k < 4:
            return w1.at[s, c % SLOTS, fs[d]], rn1.at[s, c, k - 2], peer[first, d]
        if k < 6:
            part = pl.ds((k - 4) * (WINDOW // 2), WINDOW // 2)
            return w2.at[s, c, gs[2], part], ro2.at[s, c, part], peer[second, d]
        return w2.at[s, c, gs[d]], rn2.at[s, c, k - 6], peer[second, d]

    def r_start(c, s, k):
        src, dst, to = r_move(c, s, k)
        copy(c, RS_KIND + s * 8 + k, src, dst, to).start()

    def r_wait(c, s, k):
        arrived(c, RS_KIND + s * 8 + k, r_move(c, s, k)[1])

    def m2(c):
        pl.when(c >= SLOTS)(lambda: rw(c - SLOTS))
        x_wait(c, 9)

        turned[...] = sg[c % SLOTS].T

        for g in range(2):
            both = jnp.dot(v[2 * g * group : 2 * (g + 1) * group, :], turned[...], preferred_element_type=F32)
            for q in (2 * g, 2 * g + 1):
                part = both[(q - 2 * g) * group : (q - 2 * g + 1) * group]
                w1[0, c % SLOTS, q] = part[:, :128].astype(BF16)
                for p in range(4):
                    wq[p, q * final : (q + 1) * final] = part[p * final : (p + 1) * final, 128:]
        for p in range(4):
            w1[1, c % SLOTS, p] = wq[p].astype(BF16)
        for s in range(2):
            r_start(c, s, 0)
            r_start(c, s, 1)

    def r1(c):
        pl.when(c >= chunks - SLOTS)(lambda: cw(c))
        for s in range(2):
            up, down = at[scatter[s][0]][1], at[scatter[s][0]][-1]
            r_wait(c, s, 0)
            w1[s, c % SLOTS, up, :CUT] = (w1[s, c % SLOTS, up, :CUT].astype(F32) + ro1[s, c, :CUT].astype(F32)).astype(BF16)
            r_start(c, s, 2)
            r_wait(c, s, 1)
            w1[s, c % SLOTS, down, CUT:] = (w1[s, c % SLOTS, down, CUT:].astype(F32) + ro1[s, c, CUT:].astype(F32)).astype(BF16)
            r_start(c, s, 3)

    def r2(c):
        pl.when(c >= chunks - SLOTS)(lambda: gw(c))
        for s in range(2):
            f = at[scatter[s][0]][0]
            r_wait(c, s, 2)
            r_wait(c, s, 3)
            total = w1[s, c % SLOTS, f].astype(F32) + rn1[s, c, 0].astype(F32) + rn1[s, c, 1].astype(F32)
            total = total.astype(BF16)
            for p in range(4):
                w2[s, c, p] = total[p * STRIDE : p * STRIDE + WINDOW]
            r_start(c, s, 4)
            r_start(c, s, 5)

    def r3(c):
        h = WINDOW // 2
        for s in range(2):
            up, down = at[scatter[s][1]][1], at[scatter[s][1]][-1]
            r_wait(c, s, 4)
            w2[s, c, up, :h] = (w2[s, c, up, :h].astype(F32) + ro2[s, c, :h].astype(F32)).astype(BF16)
            r_start(c, s, 6)
            r_wait(c, s, 5)
            w2[s, c, down, h:] = (w2[s, c, down, h:].astype(F32) + ro2[s, c, h:].astype(F32)).astype(BF16)
            r_start(c, s, 7)

    def r4(c):
        pl.when(c >= chunks - SLOTS)(lambda: rw(c))
        pl.when(c >= 1)(lambda: sw(c - 1))
        sums = []
        for s in range(2):
            g = at[scatter[s][1]][0]
            r_wait(c, s, 6)
            r_wait(c, s, 7)
            total = w2[s, c, g].astype(F32) + rn2[s, c, 0].astype(F32) + rn2[s, c, 1].astype(F32)
            sums.append(pltpu.roll(total, lax.rem(WINDOW - 4 * g, WINDOW), 0))
        total = jnp.concatenate(sums, axis=1)
        total = jnp.concatenate([total, jnp.zeros((256 - WINDOW, 256), F32)], axis=0)
        gap = rc[:, c].reshape(256, 128)
        gap = jnp.concatenate([gap, gap], axis=1) + cf[0:1, :]
        o_ref[:, c] = (total.T / gap).astype(BF16)[:, :final].reshape(16, BLOCK, final)

    def rw(c):
        for s in range(2):
            for k in range(4):
                sent(c, RS_KIND + s * 8 + k, r_move(c, s, k)[0])

    def gw(c):
        for k in range(5, 10):
            sent(c, X_KIND + k, x_send(c, k)[0])

    def cw(c):
        for k in range(5):
            sent(c, X_KIND + k, x_send(c, k)[0])

    def sw(c):
        @pl.when(c == 0)
        def _():
            for k in range(7):
                t_copy(k, t_send(k)[0], peer["core"]).wait_send()

        for s in range(2):
            for k in range(7):
                sent(c, s * 7 + k, a_send(c, s, k)[0])
            for k in range(4, 8):
                sent(c, RS_KIND + s * 8 + k, r_move(c, s, k)[0])

    load = pltpu.make_async_copy(vt_hbm, vt, lsem.at[0])
    entry = pltpu.make_async_copy(a_hbm, a_ref, lsem.at[1])
    tiles = width // TILE

    def tv(c):
        @pl.when(c == 0)
        def _():
            load.wait()
            ends = vt[:, main:]
            vtail[...] = jnp.concatenate([ends, ends], axis=1)
            gp()

        def turn(i, carry):
            tile = pl.ds(pl.multiple_of(i * TILE, TILE), TILE)
            v[:, tile] = vt[tile, :].T
            return carry

        share = (tiles + 2) // 3
        lax.fori_loop(share * c, jnp.minimum(share * (c + 1), tiles), turn, 0)

        @pl.when(c == 2)
        def _():
            v[:, tiles * TILE :] = vt[tiles * TILE :, :].T

    entry.start()
    load.start()
    entry.wait()
    for k in range(0, chunks, 2):
        pair = [a_ref[i * BLOCK : (i + 1) * BLOCK, main:] for i in (k, k + 1) if i < chunks]
        if len(pair) == 1:
            pair.append(jnp.zeros_like(pair[0]))
        tg[z, y, k // 2 * BLOCK : (k // 2 + 1) * BLOCK, :] = jnp.concatenate(pair, axis=1)

    def gp():
        inner, outer = col * width, (row * 16 + col) * final
        inner_row = inner // 128
        outer_row = jnp.minimum(outer // 128, col_ref.shape[0] - 3)
        for k in range(12):
            near[:, 128 * k : 128 * (k + 1)] = col_ref[pl.ds(inner_row + k, 1), :]
        for k in range(3):
            near[:, 1536 + 128 * k : 1664 + 128 * k] = col_ref[pl.ds(outer_row + k, 1), :]
        cg[...] = pltpu.roll(jnp.broadcast_to(near[:, :1536], (8, 1536)), (1536 - (inner - inner_row * 128)) % 1536, 1)
        shifted = pltpu.roll(jnp.broadcast_to(near[:, 1536:], (8, 384)), (384 - (outer - outer_row * 128)) % 384, 1)
        cf[...] = shifted[:, :256]
        flat = rc.reshape(16 * chunks * BLOCK, 128)
        for k in range(row_ref.shape[0]):
            flat[k * 128 : (k + 1) * 128, :] = jnp.broadcast_to(row_ref[k : k + 1, :], (128, 128)).T

    pl.semaphore_wait(barrier, len(peer))

    ops = dict(
        tv=tv, a0=a0, a1=a1, a2=a2, a3=a3, m1=m1, b1=b1, b2=b2, b3=b3, b4=b4, b5=b5, m2=m2, r1=r1, r2=r2, r3=r3, r4=r4
    )

    def step(t, carry):
        for name, rounds in PLAN:

            @pl.when(functools.reduce(jnp.logical_or, [t == r for r in rounds]))
            def _():
                ops[name](sum((t > r).astype(jnp.int32) for r in rounds))

        return carry

    lax.fori_loop(0, 1 + max(rounds[-1] for _, rounds in PLAN), step, 0)
    sw(chunks - 1)


def on_device(amplitudes, integrals, row_gap, col_gap):
    rows, depth = amplitudes.shape
    width = integrals.shape[1]
    chunks = rows // BLOCK
    final = depth // 16

    vm = pl.BlockSpec(memory_space=pltpu.VMEM)
    anywhere = pl.BlockSpec(memory_space=pl.ANY)
    updated = pl.pallas_call(
        kernel,
        out_shape=jax.ShapeDtypeStruct((16, chunks, BLOCK, final), BF16),
        in_specs=[anywhere, anywhere, vm, vm],
        out_specs=vm,
        scratch_shapes=[
            pltpu.VMEM((rows, depth), BF16),
            pltpu.VMEM((1, 1920), F32),
            pltpu.VMEM((8, 1536), F32),
            pltpu.VMEM((8, 256), F32),
            pltpu.VMEM((16, chunks, BLOCK, 128), F32),
            pltpu.VMEM((depth, width), BF16),
            pltpu.VMEM((width, depth), BF16),
            pltpu.VMEM((width, 128), BF16),
            pltpu.VMEM((width, 256), BF16),
            pltpu.VMEM((chunks, 4, 4, BLOCK, depth // 128 * 128), BF16),
            pltpu.VMEM((4, 4, (chunks + 1) // 2 * BLOCK, 128), BF16),
            pltpu.VMEM((SLOTS, 256, width), BF16),
            pltpu.VMEM((SLOTS, 128, width), BF16),
            pltpu.VMEM((chunks, 32, width), BF16),
            pltpu.VMEM((chunks, 2, 32, width), BF16),
            pltpu.VMEM((SLOTS, 256, width), BF16),
            pltpu.VMEM((4, depth // 4, 128), F32),
            pltpu.VMEM((2, SLOTS, 4, depth // 4, 128), BF16),
            pltpu.VMEM((2, chunks, 4, WINDOW, 128), BF16),
            pltpu.VMEM((2, chunks, depth // 4, 128), BF16),
            pltpu.VMEM((2, chunks, 2, depth // 4, 128), BF16),
            pltpu.VMEM((2, chunks, WINDOW, 128), BF16),
            pltpu.VMEM((2, chunks, 2, WINDOW, 128), BF16),
            pltpu.SemaphoreType.DMA((2,)),
            pltpu.SemaphoreType.DMA((7,)),
            pltpu.SemaphoreType.DMA((7,)),
            pltpu.SemaphoreType.DMA((chunks, KINDS)),
            pltpu.SemaphoreType.DMA((chunks, KINDS)),
        ],
        compiler_params=pltpu.CompilerParams(
            collective_id=0, has_side_effects=True, vmem_limit_bytes=62 * 1024 * 1024
        ),
        cost_estimate=pl.CostEstimate(
            flops=4 * 16 * rows * depth * width, bytes_accessed=2 * depth * width, transcendentals=0
        ),
    )(amplitudes, integrals.T, row_gap.reshape(-1, 128), col_gap.reshape(-1, 128))
    return updated.reshape(16 * rows, final)


def solution(mesh):
    return jax.shard_map(
        on_device,
        mesh=mesh,
        in_specs=(P("col", "row"), P("row", "col"), P(), P()),
        out_specs=P(None, ("row", "col")),
        check_vma=False,
    )
```

```python
import functools

import jax
import jax.numpy as jnp
from jax import lax
from jax.experimental import pallas as pl
from jax.experimental.pallas import tpu as pltpu
from jax.sharding import PartitionSpec as P

MESH = pl.DeviceIdType.MESH
F32 = jnp.float32
BF16 = jnp.bfloat16

BLOCK = 16
WINDOW = 192
STRIDE = 176
TILE = 128
CUT = 368
SLOTS = 4
X_KIND = 14
RS_KIND = 24
KINDS = 40

PLAN = (
    ("r1", 8),
    ("r2", 10),
    ("a0", 0),
    ("cw", 7),
    ("m1", 3),
    ("b2", 4),
    ("b4", 5),
    ("r3", 12),
    ("a3", 2),
    ("a2", 1),
    ("r4", 14),
    ("sw", 14),
    ("a1", 0),
    ("tv", 0),
    ("gp", 3),
    ("rw", 10),
    ("m2", 6),
    ("gw", 7),
    ("b1", 3),
    ("b3", 4),
    ("b5", 5),
)


def kernel(
    a_hbm, vt_hbm, row_ref, col_ref, o_ref,
    a_ref, near, cg, cf, rc, v, vt, vtail, turned, ag, tg, c1, cx, xo, xn, sg, wq, w1, w2, ro1, rn1, ro2, rn2, lsem, tsend, trecv, send, recv,
):
    chunks = ag.shape[0]
    depth, width = a_ref.shape[1], v.shape[1]
    group, final = depth // 4, o_ref.shape[-1]
    row, col = lax.axis_index("row"), lax.axis_index("col")
    x, core = row // 2, row % 2
    z, y = col // 4, col % 4
    half = core * 128
    other = 128 - half

    def around(index):
        return {0: index, 1: lax.rem(index + 1, 4), 2: lax.rem(index + 2, 4), -1: lax.rem(index + 3, 4)}

    xs, ys, zs = around(x), around(y), around(z)
    at = {"z": zs, "y": ys}
    peer = {
        ("x", 1): (xs[1] * 2 + core, col),
        ("x", -1): (xs[-1] * 2 + core, col),
        ("y", 1): (row, z * 4 + ys[1]),
        ("y", -1): (row, z * 4 + ys[-1]),
        ("z", 1): (row, zs[1] * 4 + y),
        ("z", -1): (row, zs[-1] * 4 + y),
        ("y", 2): (row, z * 4 + ys[2]),
        ("z", 2): (row, zs[2] * 4 + y),
        "core": (x * 2 + 1 - core, col),
    }
    strips = {step: half + index * 32 for step, index in xs.items()}
    main = ag.shape[-1]
    gather = (("y", "z", pl.ds(0, main // 2)), ("z", "y", pl.ds(main // 2, main // 2)))
    scatter = (("z", "y"), ("y", "z"))

    barrier = pltpu.get_barrier_semaphore()
    for to in peer.values():
        pl.semaphore_signal(barrier, inc=1, device_id=to, device_id_type=MESH)

    def copy(c, kind, src, dst, to):
        return pltpu.make_async_remote_copy(
            src_ref=src, dst_ref=dst, send_sem=send.at[c, kind], recv_sem=recv.at[c, kind],
            device_id=to, device_id_type=MESH,
        )

    def arrived(c, kind, dst):
        copy(c, kind, dst, dst, peer["core"]).wait_recv()

    def sent(c, kind, src):
        copy(c, kind, src, src, peer["core"]).wait_send()

    def block(s, c, step):
        first, _, lanes = gather[s]
        f = at[first][step]
        return ag.at[c, z, f, :, lanes] if first == "y" else ag.at[c, f, y, :, lanes]

    def line(s, c, step, start=0, size=4):
        first, second, lanes = gather[s]
        g, part = at[second][step], pl.ds(start, size)
        return ag.at[c, g, part, :, lanes] if first == "y" else ag.at[c, part, g, :, lanes]

    def a_send(c, s, k, d=1):
        first, second, _ = gather[s]
        if k == 0:
            return block(s, c, 0), peer[first, 1]
        if k == 1:
            return block(s, c, 0), peer[first, -1]
        if k == 2:
            return block(s, c, -d), peer[first, d]
        if k == 3:
            return line(s, c, 0), peer[second, 1]
        if k == 4:
            return line(s, c, 0), peer[second, -1]
        if k == 5:
            return line(s, c, -1, 0, 2), peer[second, 1]
        return line(s, c, 1, 2, 2), peer[second, -1]

    def a_land(c, s, k):
        if k < 3:
            return block(s, c, (-1, 1, 2)[k])
        if k < 5:
            return line(s, c, (-1, 1)[k - 3])
        return line(s, c, 2, 2 * (k - 5), 2)

    def a_start(c, s, k, d=1):
        src, to = a_send(c, s, k, d)
        copy(c, s * 7 + k, src, src, to).start()

    def a_wait(c, s, k):
        arrived(c, s * 7 + k, a_land(c, s, k))

    def t_line(step, start=0, size=4):
        return tg.at[zs[step], pl.ds(start, size)]

    def t_send(k):
        return (
            (tg.at[z, y], peer["y", 1]),
            (tg.at[z, y], peer["y", -1]),
            (tg.at[z, y], peer["y", 2]),
            (t_line(0), peer["z", 1]),
            (t_line(0), peer["z", -1]),
            (t_line(-1, 0, 2), peer["z", 1]),
            (t_line(1, 2, 2), peer["z", -1]),
        )[k]

    def t_land(k):
        return (
            tg.at[z, ys[-1]], tg.at[z, ys[1]], tg.at[z, ys[2]],
            t_line(-1), t_line(1), t_line(2, 0, 2), t_line(2, 2, 2),
        )[k]

    def t_copy(k, src, to):
        return pltpu.make_async_remote_copy(
            src_ref=src, dst_ref=src, send_sem=tsend.at[k], recv_sem=trecv.at[k], device_id=to, device_id_type=MESH
        )

    def t_start(*kinds):
        for k in kinds:
            t_copy(k, *t_send(k)).start()

    def t_wait(*kinds):
        for k in kinds:
            t_copy(k, t_land(k), peer["core"]).wait_recv()

    def a0(c):
        ag[c, z, y] = a_ref[pl.ds(pl.multiple_of(c * BLOCK, BLOCK), BLOCK), :main]
        for s in range(2):
            a_start(c, s, 0)
            a_start(c, s, 1)

        @pl.when(c == 0)
        def _():
            for s in range(2):
                copy(c, s * 7 + 2, block(s, c, 0), block(s, c, 0), peer[gather[s][0], 2]).start()
            t_start(0, 1, 2)

    def a1(c):
        def forward(d):
            for s in range(2):
                a_wait(c, s, 0 if d == 1 else 1)
                a_start(c, s, 2, d)

        @pl.when(c == 0)
        def _():
            for s in range(2):
                a_wait(c, s, 0)

        pl.when(jnp.logical_and(c % 2 == 0, c > 0))(lambda: forward(1))
        pl.when(c % 2 == 1)(lambda: forward(-1))

    def a2(c):
        pl.when(c % 2 == 0)(lambda: [a_wait(c, s, 1) for s in range(2)] and None)
        pl.when(c % 2 == 1)(lambda: [a_wait(c, s, 0) for s in range(2)] and None)
        for s in range(2):
            a_wait(c, s, 2)
            a_start(c, s, 3)
            a_start(c, s, 4)

        @pl.when(c == 0)
        def _():
            t_wait(0, 1, 2)
            t_start(3, 4)

    def a3(c):
        for s in range(2):
            a_wait(c, s, 3)
            a_start(c, s, 5)
            a_wait(c, s, 4)
            a_start(c, s, 6)

        @pl.when(c == 0)
        def _():
            t_wait(3)
            t_start(5)
            t_wait(4)
            t_start(6)

    def m1(c):
        for s in range(2):
            a_wait(c, s, 5)
            a_wait(c, s, 6)
        pl.when(c == 0)(lambda: t_wait(5, 6))
        ends = tg[:, :, pl.ds(pl.multiple_of(c // 2 * BLOCK, BLOCK), BLOCK), :].reshape(16 * BLOCK, 128)
        mine = lax.broadcasted_iota(jnp.int32, (16 * BLOCK, 128), 1) // 64 == c % 2
        ends = jnp.where(mine, ends.astype(F32), 0.0).astype(BF16)
        rows = ag[c].reshape(16 * BLOCK, main)
        middle = (width // 2 + 127) // 128 * 128
        last = (((1,), (1,)), ((), ()))
        for lo, hi in ((0, middle), (middle, width)):
            part = lax.dot_general(vt[lo:hi, :main], rows, last, preferred_element_type=F32)
            part = part + lax.dot_general(vtail[lo:hi], ends, last, preferred_element_type=F32)
            c1[c % SLOTS, :, lo:hi] = part.astype(BF16).T
        x_start(c, 0)

    def piece(step, start=0, size=32):
        return pl.ds(pl.multiple_of(strips[step] + start, 16), size)

    def x_send(c, k):
        if k == 0:
            return c1.at[c % SLOTS, pl.ds(pl.multiple_of(other, 128), 128)], cx.at[c % SLOTS], peer["core"]
        if k == 9:
            src = sg.at[c % SLOTS, pl.ds(pl.multiple_of(half, 128), 128)]
            return src, src, peer["core"]
        d = 1 if k % 2 == 1 else -1
        part = pl.ds(8 - 8 * d, 16)
        if k < 3:
            return c1.at[c % SLOTS, piece(2, 8 - 8 * d, 16)], xo.at[c, part], peer["x", d]
        if k < 5:
            return c1.at[c % SLOTS, piece(d)], xn.at[c, (k - 3)], peer["x", d]
        src = sg.at[c % SLOTS, piece(0) if k < 7 else piece(-d, 8 - 8 * d, 16)]
        return src, src, peer["x", d]

    def x_land(c, k):
        if k < 5:
            return x_send(c, k)[1]
        if k == 9:
            return sg.at[c % SLOTS, pl.ds(pl.multiple_of(other, 128), 128)]
        d = 1 if k % 2 == 1 else -1
        return sg.at[c % SLOTS, piece(-d) if k < 7 else piece(2, 8 - 8 * d, 16)]

    def x_start(c, k):
        src, dst, to = x_send(c, k)
        copy(c, X_KIND + k, src, dst, to).start()

    def x_wait(c, k):
        arrived(c, X_KIND + k, x_land(c, k))

    def b1(c):
        x_wait(c, 0)
        rows = pl.ds(pl.multiple_of(half, 128), 128)
        c1[c % SLOTS, rows, :] = (c1[c % SLOTS, rows, :].astype(F32) + cx[c % SLOTS].astype(F32)).astype(BF16)
        x_start(c, 1)
        x_start(c, 2)

    def b2(c):
        for k, step in ((1, 1), (2, -1)):
            x_wait(c, k)
            part, rows = pl.ds(16 * (k - 1), 16), piece(step, 16 * (k - 1), 16)
            c1[c % SLOTS, rows, :] = (c1[c % SLOTS, rows, :].astype(F32) + xo[c, part].astype(F32)).astype(BF16)
            x_start(c, k + 2)

    def b3(c):
        gap = rc[pl.ds(core * 8 + x * 2, 2), c].reshape(32, 128)
        x_wait(c, 3)
        x_wait(c, 4)
        rows = piece(0)
        total = c1[c % SLOTS, rows, :].astype(F32) + xn[c, 0].astype(F32) + xn[c, 1].astype(F32)
        sg[c % SLOTS, rows, :] = (total / (gap[:, :1] + cg[0:1, :width])).astype(BF16)
        x_start(c, 5)
        x_start(c, 6)

    def b4(c):
        for k in (5, 6):
            x_wait(c, k)
            x_start(c, k + 2)

    def b5(c):
        x_wait(c, 7)
        x_wait(c, 8)
        x_start(c, 9)

    def r_move(c, s, k):
        first, second = scatter[s]
        fs, gs = at[first], at[second]
        d = 1 if k % 2 == 0 else -1
        if k < 2:
            part = pl.ds(0, CUT) if k == 0 else pl.ds(CUT, group - CUT)
            return w1.at[s, c % SLOTS, fs[2], part], ro1.at[s, c % SLOTS, part], peer[first, d]
        if k < 4:
            return w1.at[s, c % SLOTS, fs[d]], rn1.at[s, c % SLOTS, k - 2], peer[first, d]
        if k < 6:
            part = pl.ds((k - 4) * (WINDOW // 2), WINDOW // 2)
            return w2.at[s, c, gs[2], part], ro2.at[s, c, part], peer[second, d]
        return w2.at[s, c, gs[d]], rn2.at[s, c, k - 6], peer[second, d]

    def r_start(c, s, k):
        src, dst, to = r_move(c, s, k)
        copy(c, RS_KIND + s * 8 + k, src, dst, to).start()

    def far_copy(c, s):
        second = scatter[s][1]
        return copy(c, RS_KIND + s * 8 + 4, w2.at[s, c, at[second][2]], ro2.at[s, c], peer[second, 2])

    def r_wait(c, s, k):
        arrived(c, RS_KIND + s * 8 + k, r_move(c, s, k)[1])

    def m2(c):
        x_wait(c, 9)

        turned[...] = sg[c % SLOTS].T

        for g in range(2):
            both = jnp.dot(v[2 * g * group : 2 * (g + 1) * group, :], turned[...], preferred_element_type=F32)
            for q in (2 * g, 2 * g + 1):
                part = both[(q - 2 * g) * group : (q - 2 * g + 1) * group]
                w1[0, c % SLOTS, q] = part[:, :128].astype(BF16)
                for p in range(4):
                    wq[p, q * final : (q + 1) * final] = part[p * final : (p + 1) * final, 128:]
        for p in range(4):
            w1[1, c % SLOTS, p] = wq[p].astype(BF16)
        for s in range(2):
            r_start(c, s, 0)
            r_start(c, s, 1)

    def r1(c):
        o = c % SLOTS
        for s in range(2):
            r_wait(c, s, 0)
            r_wait(c, s, 1)
        for s in range(2):
            up, down = at[scatter[s][0]][1], at[scatter[s][0]][-1]
            w1[s, o, up, :CUT] = (w1[s, o, up, :CUT].astype(F32) + ro1[s, o, :CUT].astype(F32)).astype(BF16)
            r_start(c, s, 2)
            w1[s, o, down, CUT:] = (w1[s, o, down, CUT:].astype(F32) + ro1[s, o, CUT:].astype(F32)).astype(BF16)
            r_start(c, s, 3)

    def r2(c):
        o = c % SLOTS
        for s in range(2):
            f = at[scatter[s][0]][0]
            r_wait(c, s, 2)
            r_wait(c, s, 3)
            total = w1[s, o, f].astype(F32) + rn1[s, o, 0].astype(F32) + rn1[s, o, 1].astype(F32)
            total = total.astype(BF16)
            for p in range(4):
                w2[s, c, p] = total[p * STRIDE : p * STRIDE + WINDOW]

            @pl.when(c < chunks - 1)
            def _():
                r_start(c, s, 4)
                r_start(c, s, 5)

            @pl.when(c == chunks - 1)
            def _():
                far_copy(c, s).start()
                r_start(c, s, 6)
                r_start(c, s, 7)

    def r3(c):
        h = WINDOW // 2

        @pl.when(c < chunks - 1)
        def _():
            for s in range(2):
                up, down = at[scatter[s][1]][1], at[scatter[s][1]][-1]
                r_wait(c, s, 4)
                w2[s, c, up, :h] = (w2[s, c, up, :h].astype(F32) + ro2[s, c, :h].astype(F32)).astype(BF16)
                r_start(c, s, 6)
                r_wait(c, s, 5)
                w2[s, c, down, h:] = (w2[s, c, down, h:].astype(F32) + ro2[s, c, h:].astype(F32)).astype(BF16)
                r_start(c, s, 7)

    def r4(c):
        sums = []
        for s in range(2):
            g = at[scatter[s][1]][0]
            r_wait(c, s, 6)
            r_wait(c, s, 7)
            pl.when(c == chunks - 1)(lambda: far_copy(c, s).wait_recv())
            total = w2[s, c, g].astype(F32) + rn2[s, c, 0].astype(F32) + rn2[s, c, 1].astype(F32)
            total = total + jnp.where(c == chunks - 1, ro2[s, c].astype(F32), 0.0)
            sums.append(pltpu.roll(total, lax.rem(WINDOW - 4 * g, WINDOW), 0))
        total = jnp.concatenate(sums, axis=1)
        total = jnp.concatenate([total, jnp.zeros((256 - WINDOW, 256), F32)], axis=0)
        gap = rc[:, c].reshape(256, 128)
        gap = jnp.concatenate([gap, gap], axis=1) + cf[0:1, :]
        o_ref[:, c] = (total.T / gap).astype(BF16)[:, :final].reshape(16, BLOCK, final)

    def rw(c):
        for s in range(2):
            for k in range(4):
                sent(c, RS_KIND + s * 8 + k, r_move(c, s, k)[0])

    def gw(c):
        for k in range(5, 10):
            sent(c, X_KIND + k, x_send(c, k)[0])

    def cw(c):
        for k in range(5):
            sent(c, X_KIND + k, x_send(c, k)[0])

    def sw(c):
        @pl.when(c == 0)
        def _():
            for k in range(7):
                t_copy(k, t_send(k)[0], peer["core"]).wait_send()

        for s in range(2):
            for k in range(7):
                sent(c, s * 7 + k, a_send(c, s, k)[0])
            for k in (6, 7):
                sent(c, RS_KIND + s * 8 + k, r_move(c, s, k)[0])

            @pl.when(c < chunks - 1)
            def _():
                for k in (4, 5):
                    sent(c, RS_KIND + s * 8 + k, r_move(c, s, k)[0])

            pl.when(c == chunks - 1)(lambda: far_copy(c, s).wait_send())


    load = pltpu.make_async_copy(vt_hbm, vt, lsem.at[0])
    entry = pltpu.make_async_copy(a_hbm, a_ref, lsem.at[1])
    tiles = width // TILE

    def tv(c):
        @pl.when(c == 0)
        def _():
            load.wait()
            ends = vt[:, main:]
            vtail[...] = jnp.concatenate([ends, ends], axis=1)

        def turn(i, carry):
            tile = pl.ds(pl.multiple_of(i * TILE, TILE), TILE)
            v[:, tile] = vt[tile, :].T
            return carry

        lax.fori_loop(2 * c, jnp.minimum(2 * c + 2, tiles), turn, 0)

        @pl.when(c == 5)
        def _():
            v[:, tiles * TILE :] = vt[tiles * TILE :, :].T

    entry.start()
    load.start()
    entry.wait()
    for k in range(0, chunks, 2):
        pair = [a_ref[i * BLOCK : (i + 1) * BLOCK, main:] for i in (k, k + 1) if i < chunks]
        if len(pair) == 1:
            pair.append(jnp.zeros_like(pair[0]))
        tg[z, y, k // 2 * BLOCK : (k // 2 + 1) * BLOCK, :] = jnp.concatenate(pair, axis=1)

    def gp(c):
        inner, outer = col * width, (row * 16 + col) * final
        inner_row = inner // 128
        outer_row = jnp.minimum(outer // 128, col_ref.shape[0] - 3)
        for k in range(12):
            near[:, 128 * k : 128 * (k + 1)] = col_ref[pl.ds(inner_row + k, 1), :]
        for k in range(3):
            near[:, 1536 + 128 * k : 1664 + 128 * k] = col_ref[pl.ds(outer_row + k, 1), :]
        cg[...] = pltpu.roll(jnp.broadcast_to(near[:, :1536], (8, 1536)), (1536 - (inner - inner_row * 128)) % 1536, 1)
        shifted = pltpu.roll(jnp.broadcast_to(near[:, 1536:], (8, 384)), (384 - (outer - outer_row * 128)) % 384, 1)
        cf[...] = shifted[:, :256]
        flat = rc.reshape(16 * chunks * BLOCK, 128)
        for k in range(row_ref.shape[0]):
            flat[k * 128 : (k + 1) * 128, :] = jnp.broadcast_to(row_ref[k : k + 1, :], (128, 128)).T

    pl.semaphore_wait(barrier, len(peer))

    ops = dict(tv=tv, cw=cw, gw=gw, rw=rw, gp=gp, a0=a0, a1=a1, a2=a2, a3=a3, m1=m1, b1=b1, b2=b2, b3=b3, b4=b4, b5=b5, m2=m2, r1=r1, r2=r2, r3=r3, r4=r4, sw=sw)

    def step(t, carry):
        for name, late in PLAN:
            c = t - late
            pl.when(jnp.logical_and(c >= 0, c < {"tv": 6, "gp": 1}.get(name, chunks)))(functools.partial(ops[name], c))
        return carry

    lax.fori_loop(0, chunks + max(late for _, late in PLAN), step, 0)


def on_device(amplitudes, integrals, row_gap, col_gap):
    rows, depth = amplitudes.shape
    width = integrals.shape[1]
    chunks = rows // BLOCK
    final = depth // 16

    vm = pl.BlockSpec(memory_space=pltpu.VMEM)
    anywhere = pl.BlockSpec(memory_space=pl.ANY)
    updated = pl.pallas_call(
        kernel,
        out_shape=jax.ShapeDtypeStruct((16, chunks, BLOCK, final), BF16),
        in_specs=[anywhere, anywhere, vm, vm],
        out_specs=vm,
        scratch_shapes=[
            pltpu.VMEM((rows, depth), BF16),
            pltpu.VMEM((1, 1920), F32),
            pltpu.VMEM((8, 1536), F32),
            pltpu.VMEM((8, 256), F32),
            pltpu.VMEM((16, chunks, BLOCK, 128), F32),
            pltpu.VMEM((depth, width), BF16),
            pltpu.VMEM((width, depth), BF16),
            pltpu.VMEM((width, 128), BF16),
            pltpu.VMEM((width, 256), BF16),
            pltpu.VMEM((chunks, 4, 4, BLOCK, depth // 128 * 128), BF16),
            pltpu.VMEM((4, 4, (chunks + 1) // 2 * BLOCK, 128), BF16),
            pltpu.VMEM((SLOTS, 256, width), BF16),
            pltpu.VMEM((SLOTS, 128, width), BF16),
            pltpu.VMEM((chunks, 32, width), BF16),
            pltpu.VMEM((chunks, 2, 32, width), BF16),
            pltpu.VMEM((SLOTS, 256, width), BF16),
            pltpu.VMEM((4, depth // 4, 128), F32),
            pltpu.VMEM((2, SLOTS, 4, depth // 4, 128), BF16),
            pltpu.VMEM((2, chunks, 4, WINDOW, 128), BF16),
            pltpu.VMEM((2, SLOTS, depth // 4, 128), BF16),
            pltpu.VMEM((2, SLOTS, 2, depth // 4, 128), BF16),
            pltpu.VMEM((2, chunks, WINDOW, 128), BF16),
            pltpu.VMEM((2, chunks, 2, WINDOW, 128), BF16),
            pltpu.SemaphoreType.DMA((2,)),
            pltpu.SemaphoreType.DMA((7,)),
            pltpu.SemaphoreType.DMA((7,)),
            pltpu.SemaphoreType.DMA((chunks, KINDS)),
            pltpu.SemaphoreType.DMA((chunks, KINDS)),
        ],
        compiler_params=pltpu.CompilerParams(
            collective_id=0, has_side_effects=True, vmem_limit_bytes=62 * 1024 * 1024
        ),
        cost_estimate=pl.CostEstimate(
            flops=4 * 16 * rows * depth * width, bytes_accessed=2 * depth * width, transcendentals=0
        ),
    )(amplitudes, integrals.T, row_gap.reshape(-1, 128), col_gap.reshape(-1, 128))
    return updated.reshape(16 * rows, final)


def solution(mesh):
    return jax.shard_map(
        on_device,
        mesh=mesh,
        in_specs=(P("col", "row"), P("row", "col"), P(), P()),
        out_specs=P(None, ("row", "col")),
        check_vma=False,
    )
```

```python
import functools

import jax
import jax.numpy as jnp
from jax import lax
from jax.experimental import pallas as pl
from jax.experimental.pallas import tpu as pltpu
from jax.sharding import PartitionSpec as P

MESH = pl.DeviceIdType.MESH
F32 = jnp.float32
BF16 = jnp.bfloat16

BLOCK = 16
WINDOW = 192
STRIDE = 176
TILE = 128
CUT = 368
SLOTS = 4
X_KIND = 14
RS_KIND = 24
KINDS = 40

PLAN = (
    ("r1", 9),
    ("r3", 11),
    ("cw", 8),
    ("m1", 4),
    ("b2", 5),
    ("r2", 10),
    ("a3", 3),
    ("a0", 0),
    ("b4", 6),
    ("a1", 0),
    ("a2", 1),
    ("tv", 1),
    ("gp", 4),
    ("rw", 11),
    ("m2", 7),
    ("gw", 8),
    ("b1", 4),
    ("r4", 14),
    ("sw", 14),
    ("b3", 5),
    ("b5", 6),
)


def kernel(
    a_hbm, vt_hbm, row_ref, col_ref, o_ref,
    a_ref, near, cg, cf, rc, v, vt, vtail, turned, ag, tg, c1, cx, xo, xn, sg, wq, w1, w2, ro1, rn1, ro2, rn2, lsem, tsend, trecv, send, recv,
):
    chunks = ag.shape[0]
    depth, width = a_ref.shape[1], v.shape[1]
    group, final = depth // 4, o_ref.shape[-1]
    row, col = lax.axis_index("row"), lax.axis_index("col")
    x, core = row // 2, row % 2
    z, y = col // 4, col % 4
    half = core * 128
    other = 128 - half

    def around(index):
        return {0: index, 1: lax.rem(index + 1, 4), 2: lax.rem(index + 2, 4), -1: lax.rem(index + 3, 4)}

    xs, ys, zs = around(x), around(y), around(z)
    at = {"z": zs, "y": ys}
    peer = {
        ("x", 1): (xs[1] * 2 + core, col),
        ("x", -1): (xs[-1] * 2 + core, col),
        ("y", 1): (row, z * 4 + ys[1]),
        ("y", -1): (row, z * 4 + ys[-1]),
        ("z", 1): (row, zs[1] * 4 + y),
        ("z", -1): (row, zs[-1] * 4 + y),
        ("y", 2): (row, z * 4 + ys[2]),
        ("z", 2): (row, zs[2] * 4 + y),
        "core": (x * 2 + 1 - core, col),
    }
    strips = {step: half + index * 32 for step, index in xs.items()}
    main = ag.shape[-1]
    gather = (("y", "z", pl.ds(0, main // 2)), ("z", "y", pl.ds(main // 2, main // 2)))
    scatter = (("z", "y"), ("y", "z"))

    barrier = pltpu.get_barrier_semaphore()
    for to in peer.values():
        pl.semaphore_signal(barrier, inc=1, device_id=to, device_id_type=MESH)

    def copy(c, kind, src, dst, to):
        return pltpu.make_async_remote_copy(
            src_ref=src, dst_ref=dst, send_sem=send.at[c, kind], recv_sem=recv.at[c, kind],
            device_id=to, device_id_type=MESH,
        )

    def arrived(c, kind, dst):
        copy(c, kind, dst, dst, peer["core"]).wait_recv()

    def sent(c, kind, src):
        copy(c, kind, src, src, peer["core"]).wait_send()

    def block(s, c, step):
        first, _, lanes = gather[s]
        f = at[first][step]
        return ag.at[c, z, f, :, lanes] if first == "y" else ag.at[c, f, y, :, lanes]

    def line(s, c, step, start=0, size=4):
        first, second, lanes = gather[s]
        g, part = at[second][step], pl.ds(start, size)
        return ag.at[c, g, part, :, lanes] if first == "y" else ag.at[c, part, g, :, lanes]

    def a_send(c, s, k, d=1):
        first, second, _ = gather[s]
        if k == 0:
            return block(s, c, 0), peer[first, 1]
        if k == 1:
            return block(s, c, 0), peer[first, -1]
        if k == 2:
            return block(s, c, -d), peer[first, d]
        if k == 3:
            return line(s, c, 0), peer[second, 1]
        if k == 4:
            return line(s, c, 0), peer[second, -1]
        if k == 5:
            return line(s, c, -1, 0, 2), peer[second, 1]
        return line(s, c, 1, 2, 2), peer[second, -1]

    def a_land(c, s, k):
        if k < 3:
            return block(s, c, (-1, 1, 2)[k])
        if k < 5:
            return line(s, c, (-1, 1)[k - 3])
        return line(s, c, 2, 2 * (k - 5), 2)

    def a_start(c, s, k, d=1):
        src, to = a_send(c, s, k, d)
        copy(c, s * 7 + k, src, src, to).start()

    def a_wait(c, s, k):
        arrived(c, s * 7 + k, a_land(c, s, k))

    def t_line(step, start=0, size=4):
        return tg.at[zs[step], pl.ds(start, size)]

    def t_send(k):
        return (
            (tg.at[z, y], peer["y", 1]),
            (tg.at[z, y], peer["y", -1]),
            (tg.at[z, y], peer["y", 2]),
            (t_line(0), peer["z", 1]),
            (t_line(0), peer["z", -1]),
            (t_line(-1, 0, 2), peer["z", 1]),
            (t_line(1, 2, 2), peer["z", -1]),
        )[k]

    def t_land(k):
        return (
            tg.at[z, ys[-1]], tg.at[z, ys[1]], tg.at[z, ys[2]],
            t_line(-1), t_line(1), t_line(2, 0, 2), t_line(2, 2, 2),
        )[k]

    def t_copy(k, src, to):
        return pltpu.make_async_remote_copy(
            src_ref=src, dst_ref=src, send_sem=tsend.at[k], recv_sem=trecv.at[k], device_id=to, device_id_type=MESH
        )

    def t_start(*kinds):
        for k in kinds:
            t_copy(k, *t_send(k)).start()

    def t_wait(*kinds):
        for k in kinds:
            t_copy(k, t_land(k), peer["core"]).wait_recv()

    def a0(c):
        ag[c, z, y] = a_ref[pl.ds(pl.multiple_of(c * BLOCK, BLOCK), BLOCK), :main]
        for s in range(2):
            a_start(c, s, 0)
            a_start(c, s, 1)

        @pl.when(c == 0)
        def _():
            for s in range(2):
                copy(c, s * 7 + 2, block(s, c, 0), block(s, c, 0), peer[gather[s][0], 2]).start()
            t_start(0, 1, 2)

    def a1(c):
        def forward(d):
            for s in range(2):
                a_wait(c, s, 0 if d == 1 else 1)
                a_start(c, s, 2, d)

        @pl.when(c == 0)
        def _():
            for s in range(2):
                a_wait(c, s, 0)

        pl.when(jnp.logical_and(c % 2 == 0, c > 0))(lambda: forward(1))
        pl.when(c % 2 == 1)(lambda: forward(-1))

    def a2(c):
        pl.when(c % 2 == 0)(lambda: [a_wait(c, s, 1) for s in range(2)] and None)
        pl.when(c % 2 == 1)(lambda: [a_wait(c, s, 0) for s in range(2)] and None)
        for s in range(2):
            a_wait(c, s, 2)
            a_start(c, s, 3)
            a_start(c, s, 4)

        @pl.when(c == 0)
        def _():
            t_wait(0, 1, 2)
            t_start(3, 4)

    def a3(c):
        for s in range(2):
            a_wait(c, s, 3)
            a_start(c, s, 5)
            a_wait(c, s, 4)
            a_start(c, s, 6)

        @pl.when(c == 0)
        def _():
            t_wait(3)
            t_start(5)
            t_wait(4)
            t_start(6)

    def m1(c):
        for s in range(2):
            a_wait(c, s, 5)
            a_wait(c, s, 6)
        pl.when(c == 0)(lambda: t_wait(5, 6))
        ends = tg[:, :, pl.ds(pl.multiple_of(c // 2 * BLOCK, BLOCK), BLOCK), :].reshape(16 * BLOCK, 128)
        mine = lax.broadcasted_iota(jnp.int32, (16 * BLOCK, 128), 1) // 64 == c % 2
        ends = jnp.where(mine, ends.astype(F32), 0.0).astype(BF16)
        rows = ag[c].reshape(16 * BLOCK, main)
        middle = (width // 2 + 127) // 128 * 128
        last = (((1,), (1,)), ((), ()))
        for lo, hi in ((0, middle), (middle, width)):
            part = lax.dot_general(vt[lo:hi, :main], rows, last, preferred_element_type=F32)
            part = part + lax.dot_general(vtail[lo:hi], ends, last, preferred_element_type=F32)
            c1[c % SLOTS, :, lo:hi] = part.astype(BF16).T
        x_start(c, 0)

    def piece(step, start=0, size=32):
        return pl.ds(pl.multiple_of(strips[step] + start, 16), size)

    def x_send(c, k):
        if k == 0:
            return c1.at[c % SLOTS, pl.ds(pl.multiple_of(other, 128), 128)], cx.at[c % SLOTS], peer["core"]
        if k == 9:
            src = sg.at[c % SLOTS, pl.ds(pl.multiple_of(half, 128), 128)]
            return src, src, peer["core"]
        d = 1 if k % 2 == 1 else -1
        part = pl.ds(8 - 8 * d, 16)
        if k < 3:
            return c1.at[c % SLOTS, piece(2, 8 - 8 * d, 16)], xo.at[c, part], peer["x", d]
        if k < 5:
            return c1.at[c % SLOTS, piece(d)], xn.at[c, (k - 3)], peer["x", d]
        src = sg.at[c % SLOTS, piece(0) if k < 7 else piece(-d, 8 - 8 * d, 16)]
        return src, src, peer["x", d]

    def x_land(c, k):
        if k < 5:
            return x_send(c, k)[1]
        if k == 9:
            return sg.at[c % SLOTS, pl.ds(pl.multiple_of(other, 128), 128)]
        d = 1 if k % 2 == 1 else -1
        return sg.at[c % SLOTS, piece(-d) if k < 7 else piece(2, 8 - 8 * d, 16)]

    def x_start(c, k):
        src, dst, to = x_send(c, k)
        copy(c, X_KIND + k, src, dst, to).start()

    def x_wait(c, k):
        arrived(c, X_KIND + k, x_land(c, k))

    def b1(c):
        x_wait(c, 0)
        rows = pl.ds(pl.multiple_of(half, 128), 128)
        c1[c % SLOTS, rows, :] = (c1[c % SLOTS, rows, :].astype(F32) + cx[c % SLOTS].astype(F32)).astype(BF16)
        x_start(c, 1)
        x_start(c, 2)

    def b2(c):
        for k, step in ((1, 1), (2, -1)):
            x_wait(c, k)
            part, rows = pl.ds(16 * (k - 1), 16), piece(step, 16 * (k - 1), 16)
            c1[c % SLOTS, rows, :] = (c1[c % SLOTS, rows, :].astype(F32) + xo[c, part].astype(F32)).astype(BF16)
            x_start(c, k + 2)

    def b3(c):
        gap = rc[pl.ds(core * 8 + x * 2, 2), c].reshape(32, 128)
        x_wait(c, 3)
        x_wait(c, 4)
        rows = piece(0)
        total = c1[c % SLOTS, rows, :].astype(F32) + xn[c, 0].astype(F32) + xn[c, 1].astype(F32)
        sg[c % SLOTS, rows, :] = (total / (gap[:, :1] + cg[0:1, :width])).astype(BF16)
        x_start(c, 5)
        x_start(c, 6)

    def b4(c):
        for k in (5, 6):
            x_wait(c, k)
            x_start(c, k + 2)

    def b5(c):
        x_wait(c, 7)
        x_wait(c, 8)
        x_start(c, 9)

    def r_move(c, s, k):
        first, second = scatter[s]
        fs, gs = at[first], at[second]
        d = 1 if k % 2 == 0 else -1
        if k < 2:
            part = pl.ds(0, CUT) if k == 0 else pl.ds(CUT, group - CUT)
            return w1.at[s, c % SLOTS, fs[2], part], ro1.at[s, c % SLOTS, part], peer[first, d]
        if k < 4:
            return w1.at[s, c % SLOTS, fs[d]], rn1.at[s, c % SLOTS, k - 2], peer[first, d]
        if k < 6:
            part = pl.ds((k - 4) * (WINDOW // 2), WINDOW // 2)
            return w2.at[s, c, gs[2], part], ro2.at[s, c, part], peer[second, d]
        return w2.at[s, c, gs[d]], rn2.at[s, c, k - 6], peer[second, d]

    def r_start(c, s, k):
        src, dst, to = r_move(c, s, k)
        copy(c, RS_KIND + s * 8 + k, src, dst, to).start()

    def far_copy(c, s):
        second = scatter[s][1]
        return copy(c, RS_KIND + s * 8 + 4, w2.at[s, c, at[second][2]], ro2.at[s, c], peer[second, 2])

    def r_wait(c, s, k):
        arrived(c, RS_KIND + s * 8 + k, r_move(c, s, k)[1])

    def m2(c):
        x_wait(c, 9)

        turned[...] = sg[c % SLOTS].T

        for g in range(2):
            both = jnp.dot(v[2 * g * group : 2 * (g + 1) * group, :], turned[...], preferred_element_type=F32)
            for q in (2 * g, 2 * g + 1):
                part = both[(q - 2 * g) * group : (q - 2 * g + 1) * group]
                w1[0, c % SLOTS, q] = part[:, :128].astype(BF16)
                for p in range(4):
                    wq[p, q * final : (q + 1) * final] = part[p * final : (p + 1) * final, 128:]
        for p in range(4):
            w1[1, c % SLOTS, p] = wq[p].astype(BF16)
        for s in range(2):
            r_start(c, s, 0)
            r_start(c, s, 1)

    def r1(c):
        o = c % SLOTS
        for s in range(2):
            r_wait(c, s, 0)
            r_wait(c, s, 1)
        for s in range(2):
            up, down = at[scatter[s][0]][1], at[scatter[s][0]][-1]
            w1[s, o, up, :CUT] = (w1[s, o, up, :CUT].astype(F32) + ro1[s, o, :CUT].astype(F32)).astype(BF16)
            r_start(c, s, 2)
            w1[s, o, down, CUT:] = (w1[s, o, down, CUT:].astype(F32) + ro1[s, o, CUT:].astype(F32)).astype(BF16)
            r_start(c, s, 3)

    def r2(c):
        o = c % SLOTS
        for s in range(2):
            f = at[scatter[s][0]][0]
            r_wait(c, s, 2)
            r_wait(c, s, 3)
            total = w1[s, o, f].astype(F32) + rn1[s, o, 0].astype(F32) + rn1[s, o, 1].astype(F32)
            total = total.astype(BF16)
            for p in range(4):
                w2[s, c, p] = total[p * STRIDE : p * STRIDE + WINDOW]

            @pl.when(c < chunks - 1)
            def _():
                r_start(c, s, 4)
                r_start(c, s, 5)

            @pl.when(c == chunks - 1)
            def _():
                far_copy(c, s).start()
                r_start(c, s, 6)
                r_start(c, s, 7)

    def r3(c):
        h = WINDOW // 2

        @pl.when(c < chunks - 1)
        def _():
            for s in range(2):
                up, down = at[scatter[s][1]][1], at[scatter[s][1]][-1]
                r_wait(c, s, 4)
                w2[s, c, up, :h] = (w2[s, c, up, :h].astype(F32) + ro2[s, c, :h].astype(F32)).astype(BF16)
                r_start(c, s, 6)
                r_wait(c, s, 5)
                w2[s, c, down, h:] = (w2[s, c, down, h:].astype(F32) + ro2[s, c, h:].astype(F32)).astype(BF16)
                r_start(c, s, 7)

    def r4(c):
        sums = []
        for s in range(2):
            g = at[scatter[s][1]][0]
            r_wait(c, s, 6)
            r_wait(c, s, 7)
            pl.when(c == chunks - 1)(lambda: far_copy(c, s).wait_recv())
            total = w2[s, c, g].astype(F32) + rn2[s, c, 0].astype(F32) + rn2[s, c, 1].astype(F32)
            total = total + jnp.where(c == chunks - 1, ro2[s, c].astype(F32), 0.0)
            sums.append(pltpu.roll(total, lax.rem(WINDOW - 4 * g, WINDOW), 0))
        total = jnp.concatenate(sums, axis=1)
        total = jnp.concatenate([total, jnp.zeros((256 - WINDOW, 256), F32)], axis=0)
        gap = rc[:, c].reshape(256, 128)
        gap = jnp.concatenate([gap, gap], axis=1) + cf[0:1, :]
        o_ref[:, c] = (total.T / gap).astype(BF16)[:, :final].reshape(16, BLOCK, final)

    def rw(c):
        for s in range(2):
            for k in range(4):
                sent(c, RS_KIND + s * 8 + k, r_move(c, s, k)[0])

    def gw(c):
        for k in range(5, 10):
            sent(c, X_KIND + k, x_send(c, k)[0])

    def cw(c):
        for k in range(5):
            sent(c, X_KIND + k, x_send(c, k)[0])

    def sw(c):
        @pl.when(c == 0)
        def _():
            for k in range(7):
                t_copy(k, t_send(k)[0], peer["core"]).wait_send()

        for s in range(2):
            for k in range(7):
                sent(c, s * 7 + k, a_send(c, s, k)[0])
            for k in (6, 7):
                sent(c, RS_KIND + s * 8 + k, r_move(c, s, k)[0])

            @pl.when(c < chunks - 1)
            def _():
                for k in (4, 5):
                    sent(c, RS_KIND + s * 8 + k, r_move(c, s, k)[0])

            pl.when(c == chunks - 1)(lambda: far_copy(c, s).wait_send())


    load = pltpu.make_async_copy(vt_hbm, vt, lsem.at[0])
    entry = pltpu.make_async_copy(a_hbm, a_ref, lsem.at[1])
    tiles = width // TILE

    def tv(c):
        @pl.when(c == 0)
        def _():
            load.wait()
            ends = vt[:, main:]
            vtail[...] = jnp.concatenate([ends, ends], axis=1)

        def turn(i, carry):
            tile = pl.ds(pl.multiple_of(i * TILE, TILE), TILE)
            v[:, tile] = vt[tile, :].T
            return carry

        lax.fori_loop(2 * c, jnp.minimum(2 * c + 2, tiles), turn, 0)

        @pl.when(c == 5)
        def _():
            v[:, tiles * TILE :] = vt[tiles * TILE :, :].T

    entry.start()
    load.start()
    entry.wait()
    for k in range(0, chunks, 2):
        pair = [a_ref[i * BLOCK : (i + 1) * BLOCK, main:] for i in (k, k + 1) if i < chunks]
        if len(pair) == 1:
            pair.append(jnp.zeros_like(pair[0]))
        tg[z, y, k // 2 * BLOCK : (k // 2 + 1) * BLOCK, :] = jnp.concatenate(pair, axis=1)

    def gp(c):
        inner, outer = col * width, (row * 16 + col) * final
        inner_row = inner // 128
        outer_row = jnp.minimum(outer // 128, col_ref.shape[0] - 3)
        for k in range(12):
            near[:, 128 * k : 128 * (k + 1)] = col_ref[pl.ds(inner_row + k, 1), :]
        for k in range(3):
            near[:, 1536 + 128 * k : 1664 + 128 * k] = col_ref[pl.ds(outer_row + k, 1), :]
        cg[...] = pltpu.roll(jnp.broadcast_to(near[:, :1536], (8, 1536)), (1536 - (inner - inner_row * 128)) % 1536, 1)
        shifted = pltpu.roll(jnp.broadcast_to(near[:, 1536:], (8, 384)), (384 - (outer - outer_row * 128)) % 384, 1)
        cf[...] = shifted[:, :256]
        flat = rc.reshape(16 * chunks * BLOCK, 128)
        for k in range(row_ref.shape[0]):
            flat[k * 128 : (k + 1) * 128, :] = jnp.broadcast_to(row_ref[k : k + 1, :], (128, 128)).T

    pl.semaphore_wait(barrier, len(peer))

    ops = dict(tv=tv, cw=cw, gw=gw, rw=rw, gp=gp, a0=a0, a1=a1, a2=a2, a3=a3, m1=m1, b1=b1, b2=b2, b3=b3, b4=b4, b5=b5, m2=m2, r1=r1, r2=r2, r3=r3, r4=r4, sw=sw)

    def step(t, carry):
        for name, late in PLAN:
            c = t - late
            pl.when(jnp.logical_and(c >= 0, c < {"tv": 6, "gp": 1}.get(name, chunks)))(functools.partial(ops[name], c))
        return carry

    lax.fori_loop(0, chunks + max(late for _, late in PLAN), step, 0)


def on_device(amplitudes, integrals, row_gap, col_gap):
    rows, depth = amplitudes.shape
    width = integrals.shape[1]
    chunks = rows // BLOCK
    final = depth // 16

    vm = pl.BlockSpec(memory_space=pltpu.VMEM)
    anywhere = pl.BlockSpec(memory_space=pl.ANY)
    updated = pl.pallas_call(
        kernel,
        out_shape=jax.ShapeDtypeStruct((16, chunks, BLOCK, final), BF16),
        in_specs=[anywhere, anywhere, vm, vm],
        out_specs=vm,
        scratch_shapes=[
            pltpu.VMEM((rows, depth), BF16),
            pltpu.VMEM((1, 1920), F32),
            pltpu.VMEM((8, 1536), F32),
            pltpu.VMEM((8, 256), F32),
            pltpu.VMEM((16, chunks, BLOCK, 128), F32),
            pltpu.VMEM((depth, width), BF16),
            pltpu.VMEM((width, depth), BF16),
            pltpu.VMEM((width, 128), BF16),
            pltpu.VMEM((width, 256), BF16),
            pltpu.VMEM((chunks, 4, 4, BLOCK, depth // 128 * 128), BF16),
            pltpu.VMEM((4, 4, (chunks + 1) // 2 * BLOCK, 128), BF16),
            pltpu.VMEM((SLOTS, 256, width), BF16),
            pltpu.VMEM((SLOTS, 128, width), BF16),
            pltpu.VMEM((chunks, 32, width), BF16),
            pltpu.VMEM((chunks, 2, 32, width), BF16),
            pltpu.VMEM((SLOTS, 256, width), BF16),
            pltpu.VMEM((4, depth // 4, 128), F32),
            pltpu.VMEM((2, SLOTS, 4, depth // 4, 128), BF16),
            pltpu.VMEM((2, chunks, 4, WINDOW, 128), BF16),
            pltpu.VMEM((2, SLOTS, depth // 4, 128), BF16),
            pltpu.VMEM((2, SLOTS, 2, depth // 4, 128), BF16),
            pltpu.VMEM((2, chunks, WINDOW, 128), BF16),
            pltpu.VMEM((2, chunks, 2, WINDOW, 128), BF16),
            pltpu.SemaphoreType.DMA((2,)),
            pltpu.SemaphoreType.DMA((7,)),
            pltpu.SemaphoreType.DMA((7,)),
            pltpu.SemaphoreType.DMA((chunks, KINDS)),
            pltpu.SemaphoreType.DMA((chunks, KINDS)),
        ],
        compiler_params=pltpu.CompilerParams(
            collective_id=0, has_side_effects=True, vmem_limit_bytes=62 * 1024 * 1024
        ),
        cost_estimate=pl.CostEstimate(
            flops=4 * 16 * rows * depth * width, bytes_accessed=2 * depth * width, transcendentals=0
        ),
    )(amplitudes, integrals.T, row_gap.reshape(-1, 128), col_gap.reshape(-1, 128))
    return updated.reshape(16 * rows, final)


def solution(mesh):
    return jax.shard_map(
        on_device,
        mesh=mesh,
        in_specs=(P("col", "row"), P("row", "col"), P(), P()),
        out_specs=P(None, ("row", "col")),
        check_vma=False,
    )
```

```python
import functools

import jax
import jax.numpy as jnp
from jax import lax
from jax.experimental import pallas as pl
from jax.experimental.pallas import tpu as pltpu
from jax.sharding import PartitionSpec as P

MESH = pl.DeviceIdType.MESH
F32 = jnp.float32
BF16 = jnp.bfloat16

BLOCK = 16
WINDOW = 192
STRIDE = 176
TILE = 128
CUT = 368
SLOTS = 4
X_KIND = 14
RS_KIND = 24
KINDS = 40

PLAN = (
    ("a0", 0),
    ("r3", 20),
    ("b2", 12),
    ("rw", 19),
    ("m2", 15),
    ("a3", 8),
    ("b5", 14),
    ("gw", 15),
    ("b1", 11),
    ("tv", 6),
    ("gp", 11),
    ("a1", 3),
    ("cw", 13),
    ("m1", 9),
    ("r1", 16),
    ("r4", 22),
    ("sw", 22),
    ("r2", 18),
    ("b4", 13),
    ("b3", 12),
    ("a2", 6),
)


def kernel(
    a_hbm, vt_hbm, row_ref, col_ref, o_ref,
    a_ref, near, cg, cf, rc, v, vt, vtail, turned, ag, tg, c1, cx, xo, xn, sg, wq, w1, w2, ro1, rn1, ro2, rn2, lsem, tsend, trecv, send, recv,
):
    chunks = ag.shape[0]
    depth, width = a_ref.shape[1], v.shape[1]
    group, final = depth // 4, o_ref.shape[-1]
    row, col = lax.axis_index("row"), lax.axis_index("col")
    x, core = row // 2, row % 2
    z, y = col // 4, col % 4
    half = core * 128
    other = 128 - half

    def around(index):
        return {0: index, 1: lax.rem(index + 1, 4), 2: lax.rem(index + 2, 4), -1: lax.rem(index + 3, 4)}

    xs, ys, zs = around(x), around(y), around(z)
    at = {"z": zs, "y": ys}
    peer = {
        ("x", 1): (xs[1] * 2 + core, col),
        ("x", -1): (xs[-1] * 2 + core, col),
        ("y", 1): (row, z * 4 + ys[1]),
        ("y", -1): (row, z * 4 + ys[-1]),
        ("z", 1): (row, zs[1] * 4 + y),
        ("z", -1): (row, zs[-1] * 4 + y),
        ("y", 2): (row, z * 4 + ys[2]),
        ("z", 2): (row, zs[2] * 4 + y),
        "core": (x * 2 + 1 - core, col),
    }
    strips = {step: half + index * 32 for step, index in xs.items()}
    main = ag.shape[-1]
    gather = (("y", "z", pl.ds(0, main // 2)), ("z", "y", pl.ds(main // 2, main // 2)))
    scatter = (("z", "y"), ("y", "z"))

    barrier = pltpu.get_barrier_semaphore()
    for to in peer.values():
        pl.semaphore_signal(barrier, inc=1, device_id=to, device_id_type=MESH)

    def copy(c, kind, src, dst, to):
        return pltpu.make_async_remote_copy(
            src_ref=src, dst_ref=dst, send_sem=send.at[c, kind], recv_sem=recv.at[c, kind],
            device_id=to, device_id_type=MESH,
        )

    def arrived(c, kind, dst):
        copy(c, kind, dst, dst, peer["core"]).wait_recv()

    def sent(c, kind, src):
        copy(c, kind, src, src, peer["core"]).wait_send()

    def block(s, c, step):
        first, _, lanes = gather[s]
        f = at[first][step]
        return ag.at[c, z, f, :, lanes] if first == "y" else ag.at[c, f, y, :, lanes]

    def line(s, c, step, start=0, size=4):
        first, second, lanes = gather[s]
        g, part = at[second][step], pl.ds(start, size)
        return ag.at[c, g, part, :, lanes] if first == "y" else ag.at[c, part, g, :, lanes]

    def a_send(c, s, k, d=1):
        first, second, _ = gather[s]
        if k == 0:
            return block(s, c, 0), peer[first, 1]
        if k == 1:
            return block(s, c, 0), peer[first, -1]
        if k == 2:
            return block(s, c, -d), peer[first, d]
        if k == 3:
            return line(s, c, 0), peer[second, 1]
        if k == 4:
            return line(s, c, 0), peer[second, -1]
        if k == 5:
            return line(s, c, -1, 0, 2), peer[second, 1]
        return line(s, c, 1, 2, 2), peer[second, -1]

    def a_land(c, s, k):
        if k < 3:
            return block(s, c, (-1, 1, 2)[k])
        if k < 5:
            return line(s, c, (-1, 1)[k - 3])
        return line(s, c, 2, 2 * (k - 5), 2)

    def a_start(c, s, k, d=1):
        src, to = a_send(c, s, k, d)
        copy(c, s * 7 + k, src, src, to).start()

    def a_wait(c, s, k):
        arrived(c, s * 7 + k, a_land(c, s, k))

    def t_line(step, start=0, size=4):
        return tg.at[zs[step], pl.ds(start, size)]

    def t_send(k):
        return (
            (tg.at[z, y], peer["y", 1]),
            (tg.at[z, y], peer["y", -1]),
            (tg.at[z, y], peer["y", 2]),
            (t_line(0), peer["z", 1]),
            (t_line(0), peer["z", -1]),
            (t_line(-1, 0, 2), peer["z", 1]),
            (t_line(1, 2, 2), peer["z", -1]),
        )[k]

    def t_land(k):
        return (
            tg.at[z, ys[-1]], tg.at[z, ys[1]], tg.at[z, ys[2]],
            t_line(-1), t_line(1), t_line(2, 0, 2), t_line(2, 2, 2),
        )[k]

    def t_copy(k, src, to):
        return pltpu.make_async_remote_copy(
            src_ref=src, dst_ref=src, send_sem=tsend.at[k], recv_sem=trecv.at[k], device_id=to, device_id_type=MESH
        )

    def t_start(*kinds):
        for k in kinds:
            t_copy(k, *t_send(k)).start()

    def t_wait(*kinds):
        for k in kinds:
            t_copy(k, t_land(k), peer["core"]).wait_recv()

    def a0(c):
        ag[c, z, y] = a_ref[pl.ds(pl.multiple_of(c * BLOCK, BLOCK), BLOCK), :main]
        for s in range(2):
            a_start(c, s, 0)
            a_start(c, s, 1)

        @pl.when(c == 0)
        def _():
            for s in range(2):
                copy(c, s * 7 + 2, block(s, c, 0), block(s, c, 0), peer[gather[s][0], 2]).start()
            t_start(0, 1, 2)

    def a1(c):
        def forward(d):
            for s in range(2):
                a_wait(c, s, 0 if d == 1 else 1)
                a_start(c, s, 2, d)

        @pl.when(c == 0)
        def _():
            for s in range(2):
                a_wait(c, s, 0)

        pl.when(jnp.logical_and(c % 2 == 0, c > 0))(lambda: forward(1))
        pl.when(c % 2 == 1)(lambda: forward(-1))

    def a2(c):
        pl.when(c % 2 == 0)(lambda: [a_wait(c, s, 1) for s in range(2)] and None)
        pl.when(c % 2 == 1)(lambda: [a_wait(c, s, 0) for s in range(2)] and None)
        for s in range(2):
            a_wait(c, s, 2)
            a_start(c, s, 3)
            a_start(c, s, 4)

        @pl.when(c == 0)
        def _():
            t_wait(0, 1, 2)
            t_start(3, 4)

    def a3(c):
        for s in range(2):
            a_wait(c, s, 3)
            a_start(c, s, 5)
            a_wait(c, s, 4)
            a_start(c, s, 6)

        @pl.when(c == 0)
        def _():
            t_wait(3)
            t_start(5)
            t_wait(4)
            t_start(6)

    def m1(c):
        for s in range(2):
            a_wait(c, s, 5)
            a_wait(c, s, 6)
        pl.when(c == 0)(lambda: t_wait(5, 6))
        ends = tg[:, :, pl.ds(pl.multiple_of(c // 2 * BLOCK, BLOCK), BLOCK), :].reshape(16 * BLOCK, 128)
        mine = lax.broadcasted_iota(jnp.int32, (16 * BLOCK, 128), 1) // 64 == c % 2
        ends = jnp.where(mine, ends.astype(F32), 0.0).astype(BF16)
        rows = ag[c].reshape(16 * BLOCK, main)
        middle = (width // 2 + 127) // 128 * 128
        last = (((1,), (1,)), ((), ()))
        for lo, hi in ((0, middle), (middle, width)):
            part = lax.dot_general(vt[lo:hi, :main], rows, last, preferred_element_type=F32)
            part = part + lax.dot_general(vtail[lo:hi], ends, last, preferred_element_type=F32)
            c1[c % SLOTS, :, lo:hi] = part.astype(BF16).T
        x_start(c, 0)

    def piece(step, start=0, size=32):
        return pl.ds(pl.multiple_of(strips[step] + start, 16), size)

    def x_send(c, k):
        if k == 0:
            return c1.at[c % SLOTS, pl.ds(pl.multiple_of(other, 128), 128)], cx.at[c % SLOTS], peer["core"]
        if k == 9:
            src = sg.at[c % SLOTS, pl.ds(pl.multiple_of(half, 128), 128)]
            return src, src, peer["core"]
        d = 1 if k % 2 == 1 else -1
        part = pl.ds(8 - 8 * d, 16)
        if k < 3:
            return c1.at[c % SLOTS, piece(2, 8 - 8 * d, 16)], xo.at[c, part], peer["x", d]
        if k < 5:
            return c1.at[c % SLOTS, piece(d)], xn.at[c, (k - 3)], peer["x", d]
        src = sg.at[c % SLOTS, piece(0) if k < 7 else piece(-d, 8 - 8 * d, 16)]
        return src, src, peer["x", d]

    def x_land(c, k):
        if k < 5:
            return x_send(c, k)[1]
        if k == 9:
            return sg.at[c % SLOTS, pl.ds(pl.multiple_of(other, 128), 128)]
        d = 1 if k % 2 == 1 else -1
        return sg.at[c % SLOTS, piece(-d) if k < 7 else piece(2, 8 - 8 * d, 16)]

    def x_start(c, k):
        src, dst, to = x_send(c, k)
        copy(c, X_KIND + k, src, dst, to).start()

    def x_wait(c, k):
        arrived(c, X_KIND + k, x_land(c, k))

    def b1(c):
        x_wait(c, 0)
        rows = pl.ds(pl.multiple_of(half, 128), 128)
        c1[c % SLOTS, rows, :] = (c1[c % SLOTS, rows, :].astype(F32) + cx[c % SLOTS].astype(F32)).astype(BF16)
        x_start(c, 1)
        x_start(c, 2)

    def b2(c):
        for k, step in ((1, 1), (2, -1)):
            x_wait(c, k)
            part, rows = pl.ds(16 * (k - 1), 16), piece(step, 16 * (k - 1), 16)
            c1[c % SLOTS, rows, :] = (c1[c % SLOTS, rows, :].astype(F32) + xo[c, part].astype(F32)).astype(BF16)
            x_start(c, k + 2)

    def b3(c):
        gap = rc[pl.ds(core * 8 + x * 2, 2), c].reshape(32, 128)
        x_wait(c, 3)
        x_wait(c, 4)
        rows = piece(0)
        total = c1[c % SLOTS, rows, :].astype(F32) + xn[c, 0].astype(F32) + xn[c, 1].astype(F32)
        sg[c % SLOTS, rows, :] = (total / (gap[:, :1] + cg[0:1, :width])).astype(BF16)
        x_start(c, 5)
        x_start(c, 6)

    def b4(c):
        for k in (5, 6):
            x_wait(c, k)
            x_start(c, k + 2)

    def b5(c):
        x_wait(c, 7)
        x_wait(c, 8)
        x_start(c, 9)

    def r_move(c, s, k):
        first, second = scatter[s]
        fs, gs = at[first], at[second]
        d = 1 if k % 2 == 0 else -1
        if k < 2:
            part = pl.ds(0, CUT) if k == 0 else pl.ds(CUT, group - CUT)
            return w1.at[s, c % SLOTS, fs[2], part], ro1.at[s, c % SLOTS, part], peer[first, d]
        if k < 4:
            return w1.at[s, c % SLOTS, fs[d]], rn1.at[s, c % SLOTS, k - 2], peer[first, d]
        if k < 6:
            part = pl.ds((k - 4) * (WINDOW // 2), WINDOW // 2)
            return w2.at[s, c, gs[2], part], ro2.at[s, c, part], peer[second, d]
        return w2.at[s, c, gs[d]], rn2.at[s, c, k - 6], peer[second, d]

    def r_start(c, s, k):
        src, dst, to = r_move(c, s, k)
        copy(c, RS_KIND + s * 8 + k, src, dst, to).start()

    def far_copy(c, s):
        second = scatter[s][1]
        return copy(c, RS_KIND + s * 8 + 4, w2.at[s, c, at[second][2]], ro2.at[s, c], peer[second, 2])

    def r_wait(c, s, k):
        arrived(c, RS_KIND + s * 8 + k, r_move(c, s, k)[1])

    def m2(c):
        x_wait(c, 9)

        turned[...] = sg[c % SLOTS].T

        for g in range(2):
            both = jnp.dot(v[2 * g * group : 2 * (g + 1) * group, :], turned[...], preferred_element_type=F32)
            for q in (2 * g, 2 * g + 1):
                part = both[(q - 2 * g) * group : (q - 2 * g + 1) * group]
                w1[0, c % SLOTS, q] = part[:, :128].astype(BF16)
                for p in range(4):
                    wq[p, q * final : (q + 1) * final] = part[p * final : (p + 1) * final, 128:]
        for p in range(4):
            w1[1, c % SLOTS, p] = wq[p].astype(BF16)
        for s in range(2):
            r_start(c, s, 0)
            r_start(c, s, 1)

    def r1(c):
        o = c % SLOTS
        for s in range(2):
            r_wait(c, s, 0)
            r_wait(c, s, 1)
        for s in range(2):
            up, down = at[scatter[s][0]][1], at[scatter[s][0]][-1]
            w1[s, o, up, :CUT] = (w1[s, o, up, :CUT].astype(F32) + ro1[s, o, :CUT].astype(F32)).astype(BF16)
            r_start(c, s, 2)
            w1[s, o, down, CUT:] = (w1[s, o, down, CUT:].astype(F32) + ro1[s, o, CUT:].astype(F32)).astype(BF16)
            r_start(c, s, 3)

    def r2(c):
        o = c % SLOTS
        for s in range(2):
            f = at[scatter[s][0]][0]
            r_wait(c, s, 2)
            r_wait(c, s, 3)
            total = w1[s, o, f].astype(F32) + rn1[s, o, 0].astype(F32) + rn1[s, o, 1].astype(F32)
            total = total.astype(BF16)
            for p in range(4):
                w2[s, c, p] = total[p * STRIDE : p * STRIDE + WINDOW]

            @pl.when(c < chunks - 1)
            def _():
                r_start(c, s, 4)
                r_start(c, s, 5)

            @pl.when(c == chunks - 1)
            def _():
                far_copy(c, s).start()
                r_start(c, s, 6)
                r_start(c, s, 7)

    def r3(c):
        h = WINDOW // 2

        @pl.when(c < chunks - 1)
        def _():
            for s in range(2):
                up, down = at[scatter[s][1]][1], at[scatter[s][1]][-1]
                r_wait(c, s, 4)
                w2[s, c, up, :h] = (w2[s, c, up, :h].astype(F32) + ro2[s, c, :h].astype(F32)).astype(BF16)
                r_start(c, s, 6)
                r_wait(c, s, 5)
                w2[s, c, down, h:] = (w2[s, c, down, h:].astype(F32) + ro2[s, c, h:].astype(F32)).astype(BF16)
                r_start(c, s, 7)

    def r4(c):
        sums = []
        for s in range(2):
            g = at[scatter[s][1]][0]
            r_wait(c, s, 6)
            r_wait(c, s, 7)
            pl.when(c == chunks - 1)(lambda: far_copy(c, s).wait_recv())
            total = w2[s, c, g].astype(F32) + rn2[s, c, 0].astype(F32) + rn2[s, c, 1].astype(F32)
            total = total + jnp.where(c == chunks - 1, ro2[s, c].astype(F32), 0.0)
            sums.append(pltpu.roll(total, lax.rem(WINDOW - 4 * g, WINDOW), 0))
        total = jnp.concatenate(sums, axis=1)
        total = jnp.concatenate([total, jnp.zeros((256 - WINDOW, 256), F32)], axis=0)
        gap = rc[:, c].reshape(256, 128)
        gap = jnp.concatenate([gap, gap], axis=1) + cf[0:1, :]
        o_ref[:, c] = (total.T / gap).astype(BF16)[:, :final].reshape(16, BLOCK, final)

    def rw(c):
        for s in range(2):
            for k in range(4):
                sent(c, RS_KIND + s * 8 + k, r_move(c, s, k)[0])

    def gw(c):
        for k in range(5, 10):
            sent(c, X_KIND + k, x_send(c, k)[0])

    def cw(c):
        for k in range(5):
            sent(c, X_KIND + k, x_send(c, k)[0])

    def sw(c):
        @pl.when(c == 0)
        def _():
            for k in range(7):
                t_copy(k, t_send(k)[0], peer["core"]).wait_send()

        for s in range(2):
            for k in range(7):
                sent(c, s * 7 + k, a_send(c, s, k)[0])
            for k in (6, 7):
                sent(c, RS_KIND + s * 8 + k, r_move(c, s, k)[0])

            @pl.when(c < chunks - 1)
            def _():
                for k in (4, 5):
                    sent(c, RS_KIND + s * 8 + k, r_move(c, s, k)[0])

            pl.when(c == chunks - 1)(lambda: far_copy(c, s).wait_send())


    load = pltpu.make_async_copy(vt_hbm, vt, lsem.at[0])
    entry = pltpu.make_async_copy(a_hbm, a_ref, lsem.at[1])
    tiles = width // TILE

    def tv(c):
        @pl.when(c == 0)
        def _():
            load.wait()
            ends = vt[:, main:]
            vtail[...] = jnp.concatenate([ends, ends], axis=1)

        def turn(i, carry):
            tile = pl.ds(pl.multiple_of(i * TILE, TILE), TILE)
            v[:, tile] = vt[tile, :].T
            return carry

        lax.fori_loop(2 * c, jnp.minimum(2 * c + 2, tiles), turn, 0)

        @pl.when(c == 5)
        def _():
            v[:, tiles * TILE :] = vt[tiles * TILE :, :].T

    entry.start()
    load.start()
    entry.wait()
    for k in range(0, chunks, 2):
        pair = [a_ref[i * BLOCK : (i + 1) * BLOCK, main:] for i in (k, k + 1) if i < chunks]
        if len(pair) == 1:
            pair.append(jnp.zeros_like(pair[0]))
        tg[z, y, k // 2 * BLOCK : (k // 2 + 1) * BLOCK, :] = jnp.concatenate(pair, axis=1)

    def gp(c):
        inner, outer = col * width, (row * 16 + col) * final
        inner_row = inner // 128
        outer_row = jnp.minimum(outer // 128, col_ref.shape[0] - 3)
        for k in range(12):
            near[:, 128 * k : 128 * (k + 1)] = col_ref[pl.ds(inner_row + k, 1), :]
        for k in range(3):
            near[:, 1536 + 128 * k : 1664 + 128 * k] = col_ref[pl.ds(outer_row + k, 1), :]
        cg[...] = pltpu.roll(jnp.broadcast_to(near[:, :1536], (8, 1536)), (1536 - (inner - inner_row * 128)) % 1536, 1)
        shifted = pltpu.roll(jnp.broadcast_to(near[:, 1536:], (8, 384)), (384 - (outer - outer_row * 128)) % 384, 1)
        cf[...] = shifted[:, :256]
        flat = rc.reshape(16 * chunks * BLOCK, 128)
        for k in range(row_ref.shape[0]):
            flat[k * 128 : (k + 1) * 128, :] = jnp.broadcast_to(row_ref[k : k + 1, :], (128, 128)).T

    pl.semaphore_wait(barrier, len(peer))

    ops = dict(tv=tv, cw=cw, gw=gw, rw=rw, gp=gp, a0=a0, a1=a1, a2=a2, a3=a3, m1=m1, b1=b1, b2=b2, b3=b3, b4=b4, b5=b5, m2=m2, r1=r1, r2=r2, r3=r3, r4=r4, sw=sw)

    def step(t, carry):
        for name, late in PLAN:
            c = t - late
            pl.when(jnp.logical_and(c >= 0, c < {"tv": 6, "gp": 1}.get(name, chunks)))(functools.partial(ops[name], c))
        return carry

    lax.fori_loop(0, chunks + max(late for _, late in PLAN), step, 0)


def on_device(amplitudes, integrals, row_gap, col_gap):
    rows, depth = amplitudes.shape
    width = integrals.shape[1]
    chunks = rows // BLOCK
    final = depth // 16

    vm = pl.BlockSpec(memory_space=pltpu.VMEM)
    anywhere = pl.BlockSpec(memory_space=pl.ANY)
    updated = pl.pallas_call(
        kernel,
        out_shape=jax.ShapeDtypeStruct((16, chunks, BLOCK, final), BF16),
        in_specs=[anywhere, anywhere, vm, vm],
        out_specs=vm,
        scratch_shapes=[
            pltpu.VMEM((rows, depth), BF16),
            pltpu.VMEM((1, 1920), F32),
            pltpu.VMEM((8, 1536), F32),
            pltpu.VMEM((8, 256), F32),
            pltpu.VMEM((16, chunks, BLOCK, 128), F32),
            pltpu.VMEM((depth, width), BF16),
            pltpu.VMEM((width, depth), BF16),
            pltpu.VMEM((width, 128), BF16),
            pltpu.VMEM((width, 256), BF16),
            pltpu.VMEM((chunks, 4, 4, BLOCK, depth // 128 * 128), BF16),
            pltpu.VMEM((4, 4, (chunks + 1) // 2 * BLOCK, 128), BF16),
            pltpu.VMEM((SLOTS, 256, width), BF16),
            pltpu.VMEM((SLOTS, 128, width), BF16),
            pltpu.VMEM((chunks, 32, width), BF16),
            pltpu.VMEM((chunks, 2, 32, width), BF16),
            pltpu.VMEM((SLOTS, 256, width), BF16),
            pltpu.VMEM((4, depth // 4, 128), F32),
            pltpu.VMEM((2, SLOTS, 4, depth // 4, 128), BF16),
            pltpu.VMEM((2, chunks, 4, WINDOW, 128), BF16),
            pltpu.VMEM((2, SLOTS, depth // 4, 128), BF16),
            pltpu.VMEM((2, SLOTS, 2, depth // 4, 128), BF16),
            pltpu.VMEM((2, chunks, WINDOW, 128), BF16),
            pltpu.VMEM((2, chunks, 2, WINDOW, 128), BF16),
            pltpu.SemaphoreType.DMA((2,)),
            pltpu.SemaphoreType.DMA((7,)),
            pltpu.SemaphoreType.DMA((7,)),
            pltpu.SemaphoreType.DMA((chunks, KINDS)),
            pltpu.SemaphoreType.DMA((chunks, KINDS)),
        ],
        compiler_params=pltpu.CompilerParams(
            collective_id=0, has_side_effects=True, vmem_limit_bytes=62 * 1024 * 1024
        ),
        cost_estimate=pl.CostEstimate(
            flops=4 * 16 * rows * depth * width, bytes_accessed=2 * depth * width, transcendentals=0
        ),
    )(amplitudes, integrals.T, row_gap.reshape(-1, 128), col_gap.reshape(-1, 128))
    return updated.reshape(16 * rows, final)


def solution(mesh):
    return jax.shard_map(
        on_device,
        mesh=mesh,
        in_specs=(P("col", "row"), P("row", "col"), P(), P()),
        out_specs=P(None, ("row", "col")),
        check_vma=False,
    )
```

```python
import functools

import jax
import jax.numpy as jnp
from jax import lax
from jax.experimental import pallas as pl
from jax.experimental.pallas import tpu as pltpu
from jax.sharding import PartitionSpec as P

MESH = pl.DeviceIdType.MESH
F32 = jnp.float32
BF16 = jnp.bfloat16

BLOCK = 16
WINDOW = 192
STRIDE = 176
TILE = 128
CUT = 368
SLOTS = 4
X_KIND = 14
RS_KIND = 24
KINDS = 40

PLAN = (
    ("r1", 8),
    ("r2", 10),
    ("a0", 0),
    ("cw", 7),
    ("aw", 7),
    ("m1", 3),
    ("b2", 4),
    ("b4", 5),
    ("r3", 12),
    ("a3", 2),
    ("a2", 1),
    ("r4", 14),
    ("sw", 14),
    ("a1", 0),
    ("tv", 0),
    ("gp", 3),
    ("rw", 10),
    ("m2", 6),
    ("gw", 7),
    ("b1", 3),
    ("b3", 4),
    ("b5", 5),
)


def kernel(
    a_hbm, vt_hbm, row_ref, col_ref, o_ref,
    a_ref, near, cg, cf, rc, v, vt, vtail, turned, ag, tg, c1, cx, xo, xn, sg, wq, w1, w2, ro1, rn1, ro2, rn2, lsem, tsend, trecv, send, recv,
):
    chunks = ag.shape[0]
    depth, width = a_ref.shape[1], v.shape[1]
    group, final = depth // 4, o_ref.shape[-1]
    row, col = lax.axis_index("row"), lax.axis_index("col")
    x, core = row // 2, row % 2
    z, y = col // 4, col % 4
    half = core * 128
    other = 128 - half

    def around(index):
        return {0: index, 1: lax.rem(index + 1, 4), 2: lax.rem(index + 2, 4), -1: lax.rem(index + 3, 4)}

    xs, ys, zs = around(x), around(y), around(z)
    at = {"z": zs, "y": ys}
    peer = {
        ("x", 1): (xs[1] * 2 + core, col),
        ("x", -1): (xs[-1] * 2 + core, col),
        ("y", 1): (row, z * 4 + ys[1]),
        ("y", -1): (row, z * 4 + ys[-1]),
        ("z", 1): (row, zs[1] * 4 + y),
        ("z", -1): (row, zs[-1] * 4 + y),
        ("y", 2): (row, z * 4 + ys[2]),
        ("z", 2): (row, zs[2] * 4 + y),
        "core": (x * 2 + 1 - core, col),
    }
    strips = {step: half + index * 32 for step, index in xs.items()}
    main = ag.shape[-1]
    gather = (("y", "z", pl.ds(0, main // 2)), ("z", "y", pl.ds(main // 2, main // 2)))
    scatter = (("z", "y"), ("y", "z"))

    barrier = pltpu.get_barrier_semaphore()
    for to in peer.values():
        pl.semaphore_signal(barrier, inc=1, device_id=to, device_id_type=MESH)

    def copy(c, kind, src, dst, to):
        return pltpu.make_async_remote_copy(
            src_ref=src, dst_ref=dst, send_sem=send.at[c, kind], recv_sem=recv.at[c, kind],
            device_id=to, device_id_type=MESH,
        )

    def arrived(c, kind, dst):
        copy(c, kind, dst, dst, peer["core"]).wait_recv()

    def sent(c, kind, src):
        copy(c, kind, src, src, peer["core"]).wait_send()

    def block(s, c, step):
        first, _, lanes = gather[s]
        f = at[first][step]
        return ag.at[c, z, f, :, lanes] if first == "y" else ag.at[c, f, y, :, lanes]

    def line(s, c, step, start=0, size=4):
        first, second, lanes = gather[s]
        g, part = at[second][step], pl.ds(start, size)
        return ag.at[c, g, part, :, lanes] if first == "y" else ag.at[c, part, g, :, lanes]

    def a_send(c, s, k, d=1):
        first, second, _ = gather[s]
        if k == 0:
            return block(s, c, 0), peer[first, 1]
        if k == 1:
            return block(s, c, 0), peer[first, -1]
        if k == 2:
            return block(s, c, -d), peer[first, d]
        if k == 3:
            return line(s, c, 0), peer[second, 1]
        if k == 4:
            return line(s, c, 0), peer[second, -1]
        if k == 5:
            return line(s, c, -1, 0, 2), peer[second, 1]
        return line(s, c, 1, 2, 2), peer[second, -1]

    def a_land(c, s, k):
        if k < 3:
            return block(s, c, (-1, 1, 2)[k])
        if k < 5:
            return line(s, c, (-1, 1)[k - 3])
        return line(s, c, 2, 2 * (k - 5), 2)

    def a_start(c, s, k, d=1):
        src, to = a_send(c, s, k, d)
        copy(c, s * 7 + k, src, src, to).start()

    def a_wait(c, s, k):
        arrived(c, s * 7 + k, a_land(c, s, k))

    def t_line(step, start=0, size=4):
        return tg.at[zs[step], pl.ds(start, size)]

    def t_send(k):
        return (
            (tg.at[z, y], peer["y", 1]),
            (tg.at[z, y], peer["y", -1]),
            (tg.at[z, y], peer["y", 2]),
            (t_line(0), peer["z", 1]),
            (t_line(0), peer["z", -1]),
            (t_line(-1, 0, 2), peer["z", 1]),
            (t_line(1, 2, 2), peer["z", -1]),
        )[k]

    def t_land(k):
        return (
            tg.at[z, ys[-1]], tg.at[z, ys[1]], tg.at[z, ys[2]],
            t_line(-1), t_line(1), t_line(2, 0, 2), t_line(2, 2, 2),
        )[k]

    def t_copy(k, src, to):
        return pltpu.make_async_remote_copy(
            src_ref=src, dst_ref=src, send_sem=tsend.at[k], recv_sem=trecv.at[k], device_id=to, device_id_type=MESH
        )

    def t_start(*kinds):
        for k in kinds:
            t_copy(k, *t_send(k)).start()

    def t_wait(*kinds):
        for k in kinds:
            t_copy(k, t_land(k), peer["core"]).wait_recv()

    def a0(c):
        ag[c, z, y] = a_ref[pl.ds(pl.multiple_of(c * BLOCK, BLOCK), BLOCK), :main]
        for s in range(2):
            a_start(c, s, 0)
            a_start(c, s, 1)

        @pl.when(c == 0)
        def _():
            for s in range(2):
                copy(c, s * 7 + 2, block(s, c, 0), block(s, c, 0), peer[gather[s][0], 2]).start()
            t_start(0, 1, 2)

    def a1(c):
        def forward(d):
            for s in range(2):
                a_wait(c, s, 0 if d == 1 else 1)
                a_start(c, s, 2, d)

        @pl.when(c == 0)
        def _():
            for s in range(2):
                a_wait(c, s, 0)

        pl.when(jnp.logical_and(c % 2 == 0, c > 0))(lambda: forward(1))
        pl.when(c % 2 == 1)(lambda: forward(-1))

    def a2(c):
        pl.when(c % 2 == 0)(lambda: [a_wait(c, s, 1) for s in range(2)] and None)
        pl.when(c % 2 == 1)(lambda: [a_wait(c, s, 0) for s in range(2)] and None)
        for s in range(2):
            a_wait(c, s, 2)
            a_start(c, s, 3)
            a_start(c, s, 4)

        @pl.when(c == 0)
        def _():
            t_wait(0, 1, 2)
            t_start(3, 4)

    def a3(c):
        for s in range(2):
            a_wait(c, s, 3)
            a_start(c, s, 5)
            a_wait(c, s, 4)
            a_start(c, s, 6)

        @pl.when(c == 0)
        def _():
            t_wait(3)
            t_start(5)
            t_wait(4)
            t_start(6)

    def m1(c):
        for s in range(2):
            a_wait(c, s, 5)
            a_wait(c, s, 6)
        pl.when(c == 0)(lambda: t_wait(5, 6))
        ends = tg[:, :, pl.ds(pl.multiple_of(c // 2 * BLOCK, BLOCK), BLOCK), :].reshape(16 * BLOCK, 128)
        mine = lax.broadcasted_iota(jnp.int32, (16 * BLOCK, 128), 1) // 64 == c % 2
        ends = jnp.where(mine, ends.astype(F32), 0.0).astype(BF16)
        rows = jnp.concatenate([ag[c].reshape(16 * BLOCK, main), ends], axis=1)
        middle = (width // 2 + 127) // 128 * 128
        last = (((1,), (1,)), ((), ()))
        for lo, hi in ((0, middle), (middle, width)):
            left = jnp.concatenate([vt[lo:hi, :main], vtail[lo:hi]], axis=1)
            part = lax.dot_general(left, rows, last, preferred_element_type=F32)
            c1[c % SLOTS, :, lo:hi] = part.astype(BF16).T
        x_start(c, 0)

    def piece(step, start=0, size=32):
        return pl.ds(pl.multiple_of(strips[step] + start, 16), size)

    def x_send(c, k):
        if k == 0:
            return c1.at[c % SLOTS, pl.ds(pl.multiple_of(other, 128), 128)], cx.at[c % SLOTS], peer["core"]
        if k == 9:
            src = sg.at[c % SLOTS, pl.ds(pl.multiple_of(half, 128), 128)]
            return src, src, peer["core"]
        d = 1 if k % 2 == 1 else -1
        part = pl.ds(8 - 8 * d, 16)
        if k < 3:
            return c1.at[c % SLOTS, piece(2, 8 - 8 * d, 16)], xo.at[c, part], peer["x", d]
        if k < 5:
            return c1.at[c % SLOTS, piece(d)], xn.at[c, (k - 3)], peer["x", d]
        src = sg.at[c % SLOTS, piece(0) if k < 7 else piece(-d, 8 - 8 * d, 16)]
        return src, src, peer["x", d]

    def x_land(c, k):
        if k < 5:
            return x_send(c, k)[1]
        if k == 9:
            return sg.at[c % SLOTS, pl.ds(pl.multiple_of(other, 128), 128)]
        d = 1 if k % 2 == 1 else -1
        return sg.at[c % SLOTS, piece(-d) if k < 7 else piece(2, 8 - 8 * d, 16)]

    def x_start(c, k):
        src, dst, to = x_send(c, k)
        copy(c, X_KIND + k, src, dst, to).start()

    def x_wait(c, k):
        arrived(c, X_KIND + k, x_land(c, k))

    def b1(c):
        x_wait(c, 0)
        rows = pl.ds(pl.multiple_of(half, 128), 128)
        c1[c % SLOTS, rows, :] = c1[c % SLOTS, rows, :] + cx[c % SLOTS]
        x_start(c, 1)
        x_start(c, 2)

    def b2(c):
        for k, step in ((1, 1), (2, -1)):
            x_wait(c, k)
            part, rows = pl.ds(16 * (k - 1), 16), piece(step, 16 * (k - 1), 16)
            c1[c % SLOTS, rows, :] = c1[c % SLOTS, rows, :] + xo[c, part]
            x_start(c, k + 2)

    def b3(c):
        gap = rc[pl.ds(core * 8 + x * 2, 2), c].reshape(32, 128)
        x_wait(c, 3)
        x_wait(c, 4)
        rows = piece(0)
        total = c1[c % SLOTS, rows, :].astype(F32) + xn[c, 0].astype(F32) + xn[c, 1].astype(F32)
        sg[c % SLOTS, rows, :] = (total / (gap[:, :1] + cg[0:1, :width])).astype(BF16)
        x_start(c, 5)
        x_start(c, 6)

    def b4(c):
        for k in (5, 6):
            x_wait(c, k)
            x_start(c, k + 2)

    def b5(c):
        x_wait(c, 7)
        x_wait(c, 8)
        x_start(c, 9)

    def r_move(c, s, k):
        first, second = scatter[s]
        fs, gs = at[first], at[second]
        d = 1 if k % 2 == 0 else -1
        if k < 2:
            part = pl.ds(0, CUT) if k == 0 else pl.ds(CUT, group - CUT)
            return w1.at[s, c % SLOTS, fs[2], part], ro1.at[s, c % SLOTS, part], peer[first, d]
        if k < 4:
            return w1.at[s, c % SLOTS, fs[d]], rn1.at[s, c % SLOTS, k - 2], peer[first, d]
        if k < 6:
            part = pl.ds((k - 4) * (WINDOW // 2), WINDOW // 2)
            return w2.at[s, c, gs[2], part], ro2.at[s, c, part], peer[second, d]
        return w2.at[s, c, gs[d]], rn2.at[s, c, k - 6], peer[second, d]

    def r_start(c, s, k):
        src, dst, to = r_move(c, s, k)
        copy(c, RS_KIND + s * 8 + k, src, dst, to).start()

    def far_copy(c, s):
        second = scatter[s][1]
        return copy(c, RS_KIND + s * 8 + 4, w2.at[s, c, at[second][2]], ro2.at[s, c], peer[second, 2])

    def r_wait(c, s, k):
        arrived(c, RS_KIND + s * 8 + k, r_move(c, s, k)[1])

    def m2(c):
        x_wait(c, 9)

        turned[...] = sg[c % SLOTS].T

        for g in range(2):
            both = jnp.dot(v[2 * g * group : 2 * (g + 1) * group, :], turned[...], preferred_element_type=F32)
            for q in (2 * g, 2 * g + 1):
                part = both[(q - 2 * g) * group : (q - 2 * g + 1) * group]
                w1[0, c % SLOTS, q] = part[:, :128].astype(BF16)
                for p in range(4):
                    wq[p, q * final : (q + 1) * final] = part[p * final : (p + 1) * final, 128:]
        for p in range(4):
            w1[1, c % SLOTS, p] = wq[p].astype(BF16)
        for s in range(2):
            r_start(c, s, 0)
            r_start(c, s, 1)

    def r1(c):
        o = c % SLOTS
        for s in range(2):
            r_wait(c, s, 0)
            r_wait(c, s, 1)
        for s in range(2):
            up, down = at[scatter[s][0]][1], at[scatter[s][0]][-1]
            w1[s, o, up, :CUT] = w1[s, o, up, :CUT] + ro1[s, o, :CUT]
            r_start(c, s, 2)
            w1[s, o, down, CUT:] = w1[s, o, down, CUT:] + ro1[s, o, CUT:]
            r_start(c, s, 3)

    def r2(c):
        o = c % SLOTS
        for s in range(2):
            f = at[scatter[s][0]][0]
            r_wait(c, s, 2)
            r_wait(c, s, 3)
            total = w1[s, o, f].astype(F32) + rn1[s, o, 0].astype(F32) + rn1[s, o, 1].astype(F32)
            total = total.astype(BF16)
            for p in range(4):
                w2[s, c, p] = total[p * STRIDE : p * STRIDE + WINDOW]

            @pl.when(c < chunks - 1)
            def _():
                r_start(c, s, 4)
                r_start(c, s, 5)

            @pl.when(c == chunks - 1)
            def _():
                far_copy(c, s).start()
                r_start(c, s, 6)
                r_start(c, s, 7)

    def r3(c):
        h = WINDOW // 2

        @pl.when(c < chunks - 1)
        def _():
            for s in range(2):
                up, down = at[scatter[s][1]][1], at[scatter[s][1]][-1]
                r_wait(c, s, 4)
                w2[s, c, up, :h] = w2[s, c, up, :h] + ro2[s, c, :h]
                r_start(c, s, 6)
                r_wait(c, s, 5)
                w2[s, c, down, h:] = w2[s, c, down, h:] + ro2[s, c, h:]
                r_start(c, s, 7)

    def r4(c):
        sums = []
        for s in range(2):
            g = at[scatter[s][1]][0]
            r_wait(c, s, 6)
            r_wait(c, s, 7)
            pl.when(c == chunks - 1)(lambda: far_copy(c, s).wait_recv())
            total = w2[s, c, g].astype(F32) + rn2[s, c, 0].astype(F32) + rn2[s, c, 1].astype(F32)
            total = total + jnp.where(c == chunks - 1, ro2[s, c].astype(F32), 0.0)
            sums.append(pltpu.roll(total, lax.rem(WINDOW - 4 * g, WINDOW), 0))
        total = jnp.concatenate(sums, axis=1)
        total = jnp.concatenate([total, jnp.zeros((256 - WINDOW, 256), F32)], axis=0)
        gap = rc[:, c].reshape(256, 128)
        gap = jnp.concatenate([gap, gap], axis=1) + cf[0:1, :]
        o_ref[:, c] = (total.T / gap).astype(BF16)[:, :final].reshape(16, BLOCK, final)

    def rw(c):
        for s in range(2):
            for k in range(4):
                sent(c, RS_KIND + s * 8 + k, r_move(c, s, k)[0])

    def gw(c):
        for k in range(5, 10):
            sent(c, X_KIND + k, x_send(c, k)[0])

    def cw(c):
        for k in range(5):
            sent(c, X_KIND + k, x_send(c, k)[0])

    def aw(c):
        @pl.when(c == 0)
        def _():
            for k in range(7):
                t_copy(k, t_send(k)[0], peer["core"]).wait_send()

        for s in range(2):
            for k in range(7):
                sent(c, s * 7 + k, a_send(c, s, k)[0])

    def sw(c):
        for s in range(2):
            for k in (6, 7):
                sent(c, RS_KIND + s * 8 + k, r_move(c, s, k)[0])

            @pl.when(c < chunks - 1)
            def _():
                for k in (4, 5):
                    sent(c, RS_KIND + s * 8 + k, r_move(c, s, k)[0])

            pl.when(c == chunks - 1)(lambda: far_copy(c, s).wait_send())

    load = pltpu.make_async_copy(vt_hbm, vt, lsem.at[0])
    entry = pltpu.make_async_copy(a_hbm, a_ref, lsem.at[1])
    tiles = width // TILE

    def tv(c):
        @pl.when(c == 0)
        def _():
            load.wait()
            ends = vt[:, main:]
            vtail[...] = jnp.concatenate([ends, ends], axis=1)

        def turn(i, carry):
            tile = pl.ds(pl.multiple_of(i * TILE, TILE), TILE)
            v[:, tile] = vt[tile, :].T
            return carry

        lax.fori_loop(2 * c, jnp.minimum(2 * c + 2, tiles), turn, 0)

        @pl.when(c == 5)
        def _():
            v[:, tiles * TILE :] = vt[tiles * TILE :, :].T

    entry.start()
    load.start()
    entry.wait()
    for k in range(0, chunks, 2):
        pair = [a_ref[i * BLOCK : (i + 1) * BLOCK, main:] for i in (k, k + 1) if i < chunks]
        if len(pair) == 1:
            pair.append(jnp.zeros_like(pair[0]))
        tg[z, y, k // 2 * BLOCK : (k // 2 + 1) * BLOCK, :] = jnp.concatenate(pair, axis=1)

    def gp(c):
        inner, outer = col * width, (row * 16 + col) * final
        inner_row = inner // 128
        outer_row = jnp.minimum(outer // 128, col_ref.shape[0] - 3)
        for k in range(12):
            near[:, 128 * k : 128 * (k + 1)] = col_ref[pl.ds(inner_row + k, 1), :]
        for k in range(3):
            near[:, 1536 + 128 * k : 1664 + 128 * k] = col_ref[pl.ds(outer_row + k, 1), :]
        cg[...] = pltpu.roll(jnp.broadcast_to(near[:, :1536], (8, 1536)), (1536 - (inner - inner_row * 128)) % 1536, 1)
        shifted = pltpu.roll(jnp.broadcast_to(near[:, 1536:], (8, 384)), (384 - (outer - outer_row * 128)) % 384, 1)
        cf[...] = shifted[:, :256]
        flat = rc.reshape(16 * chunks * BLOCK, 128)
        for k in range(row_ref.shape[0]):
            flat[k * 128 : (k + 1) * 128, :] = jnp.broadcast_to(row_ref[k : k + 1, :], (128, 128)).T

    pl.semaphore_wait(barrier, len(peer))

    ops = dict(tv=tv, aw=aw, cw=cw, gw=gw, rw=rw, gp=gp, a0=a0, a1=a1, a2=a2, a3=a3, m1=m1, b1=b1, b2=b2, b3=b3, b4=b4, b5=b5, m2=m2, r1=r1, r2=r2, r3=r3, r4=r4, sw=sw)

    def step(t, carry):
        for name, late in PLAN:
            c = t - late
            pl.when(jnp.logical_and(c >= 0, c < {"tv": 6, "gp": 1}.get(name, chunks)))(functools.partial(ops[name], c))
        return carry

    lax.fori_loop(0, chunks + max(late for _, late in PLAN), step, 0)


def on_device(amplitudes, integrals, row_gap, col_gap):
    rows, depth = amplitudes.shape
    width = integrals.shape[1]
    chunks = rows // BLOCK
    final = depth // 16

    vm = pl.BlockSpec(memory_space=pltpu.VMEM)
    anywhere = pl.BlockSpec(memory_space=pl.ANY)
    updated = pl.pallas_call(
        kernel,
        out_shape=jax.ShapeDtypeStruct((16, chunks, BLOCK, final), BF16),
        in_specs=[anywhere, anywhere, vm, vm],
        out_specs=vm,
        scratch_shapes=[
            pltpu.VMEM((rows, depth), BF16),
            pltpu.VMEM((1, 1920), F32),
            pltpu.VMEM((8, 1536), F32),
            pltpu.VMEM((8, 256), F32),
            pltpu.VMEM((16, chunks, BLOCK, 128), F32),
            pltpu.VMEM((depth, width), BF16),
            pltpu.VMEM((width, depth), BF16),
            pltpu.VMEM((width, 128), BF16),
            pltpu.VMEM((width, 256), BF16),
            pltpu.VMEM((chunks, 4, 4, BLOCK, depth // 128 * 128), BF16),
            pltpu.VMEM((4, 4, (chunks + 1) // 2 * BLOCK, 128), BF16),
            pltpu.VMEM((SLOTS, 256, width), BF16),
            pltpu.VMEM((SLOTS, 128, width), BF16),
            pltpu.VMEM((chunks, 32, width), BF16),
            pltpu.VMEM((chunks, 2, 32, width), BF16),
            pltpu.VMEM((SLOTS, 256, width), BF16),
            pltpu.VMEM((4, depth // 4, 128), F32),
            pltpu.VMEM((2, SLOTS, 4, depth // 4, 128), BF16),
            pltpu.VMEM((2, chunks, 4, WINDOW, 128), BF16),
            pltpu.VMEM((2, SLOTS, depth // 4, 128), BF16),
            pltpu.VMEM((2, SLOTS, 2, depth // 4, 128), BF16),
            pltpu.VMEM((2, chunks, WINDOW, 128), BF16),
            pltpu.VMEM((2, chunks, 2, WINDOW, 128), BF16),
            pltpu.SemaphoreType.DMA((2,)),
            pltpu.SemaphoreType.DMA((7,)),
            pltpu.SemaphoreType.DMA((7,)),
            pltpu.SemaphoreType.DMA((chunks, KINDS)),
            pltpu.SemaphoreType.DMA((chunks, KINDS)),
        ],
        compiler_params=pltpu.CompilerParams(
            collective_id=0, has_side_effects=True, vmem_limit_bytes=62 * 1024 * 1024
        ),
        cost_estimate=pl.CostEstimate(
            flops=4 * 16 * rows * depth * width, bytes_accessed=2 * depth * width, transcendentals=0
        ),
    )(amplitudes, integrals.T, row_gap.reshape(-1, 128), col_gap.reshape(-1, 128))
    return updated.reshape(16 * rows, final)


def solution(mesh):
    return jax.shard_map(
        on_device,
        mesh=mesh,
        in_specs=(P("col", "row"), P("row", "col"), P(), P()),
        out_specs=P(None, ("row", "col")),
        check_vma=False,
    )
```

```python
import functools

import jax
import jax.numpy as jnp
from jax import lax
from jax.experimental import pallas as pl
from jax.experimental.pallas import tpu as pltpu
from jax.sharding import PartitionSpec as P

MESH = pl.DeviceIdType.MESH
F32 = jnp.float32
BF16 = jnp.bfloat16

BLOCK = 16
WINDOW = 192
STRIDE = 176
TILE = 128
CUT = 368
SLOTS = 4
X_KIND = 14
RS_KIND = 22
KINDS = 38
STEP = {1: 1, 2: 2, 3: -1}

PLAN = (
    ("r1", 7),
    ("r2", 9),
    ("a0", 0),
    ("cw", 7),
    ("aw", 7),
    ("m1", 3),
    ("gp", 3),
    ("b3", 4),
    ("r3", 11),
    ("a3", 2),
    ("a2", 1),
    ("b5", 4),
    ("r4", 13),
    ("sw", 13),
    ("a1", 0),
    ("tv", 0),
    ("rw", 9),
    ("m2", 5),
    ("gw", 7),
    ("b1", 3),
)


def kernel(
    a_hbm, vt_hbm, row_ref, col_ref, o_ref,
    a_ref, near, cg, cf, rc, v, vt, vtail, turned, ag, tg, c1, cx, xn, sg, wq, w1, w2, ro1, rn1, ro2, rn2, lsem, tsend, trecv, send, recv,
):
    chunks = ag.shape[0]
    depth, width = a_ref.shape[1], v.shape[1]
    group, final = depth // 4, o_ref.shape[-1]
    row, col = lax.axis_index("row"), lax.axis_index("col")
    x, core = row // 2, row % 2
    z, y = col // 4, col % 4
    half = core * 128
    other = 128 - half

    def around(index):
        return {0: index, 1: lax.rem(index + 1, 4), 2: lax.rem(index + 2, 4), -1: lax.rem(index + 3, 4)}

    xs, ys, zs = around(x), around(y), around(z)
    at = {"z": zs, "y": ys}
    peer = {
        ("x", 1): (xs[1] * 2 + core, col),
        ("x", -1): (xs[-1] * 2 + core, col),
        ("y", 1): (row, z * 4 + ys[1]),
        ("y", -1): (row, z * 4 + ys[-1]),
        ("z", 1): (row, zs[1] * 4 + y),
        ("z", -1): (row, zs[-1] * 4 + y),
        ("x", 2): (xs[2] * 2 + core, col),
        ("y", 2): (row, z * 4 + ys[2]),
        ("z", 2): (row, zs[2] * 4 + y),
        "core": (x * 2 + 1 - core, col),
    }
    strips = {step: half + index * 32 for step, index in xs.items()}
    main = ag.shape[-1]
    gather = (("y", "z", pl.ds(0, main // 2)), ("z", "y", pl.ds(main // 2, main // 2)))
    scatter = (("z", "y"), ("y", "z"))

    barrier = pltpu.get_barrier_semaphore()
    for to in peer.values():
        pl.semaphore_signal(barrier, inc=1, device_id=to, device_id_type=MESH)

    def copy(c, kind, src, dst, to):
        return pltpu.make_async_remote_copy(
            src_ref=src, dst_ref=dst, send_sem=send.at[c, kind], recv_sem=recv.at[c, kind],
            device_id=to, device_id_type=MESH,
        )

    def arrived(c, kind, dst):
        copy(c, kind, dst, dst, peer["core"]).wait_recv()

    def sent(c, kind, src):
        copy(c, kind, src, src, peer["core"]).wait_send()

    def block(s, c, step):
        first, _, lanes = gather[s]
        f = at[first][step]
        return ag.at[c, z, f, :, lanes] if first == "y" else ag.at[c, f, y, :, lanes]

    def line(s, c, step, start=0, size=4):
        first, second, lanes = gather[s]
        g, part = at[second][step], pl.ds(start, size)
        return ag.at[c, g, part, :, lanes] if first == "y" else ag.at[c, part, g, :, lanes]

    def a_send(c, s, k, d=1):
        first, second, _ = gather[s]
        if k == 0:
            return block(s, c, 0), peer[first, 1]
        if k == 1:
            return block(s, c, 0), peer[first, -1]
        if k == 2:
            return block(s, c, -d), peer[first, d]
        if k == 3:
            return line(s, c, 0), peer[second, 1]
        if k == 4:
            return line(s, c, 0), peer[second, -1]
        if k == 5:
            return line(s, c, -1, 0, 2), peer[second, 1]
        return line(s, c, 1, 2, 2), peer[second, -1]

    def a_land(c, s, k):
        if k < 3:
            return block(s, c, (-1, 1, 2)[k])
        if k < 5:
            return line(s, c, (-1, 1)[k - 3])
        return line(s, c, 2, 2 * (k - 5), 2)

    def a_start(c, s, k, d=1):
        src, to = a_send(c, s, k, d)
        copy(c, s * 7 + k, src, src, to).start()

    def a_wait(c, s, k):
        arrived(c, s * 7 + k, a_land(c, s, k))

    def t_line(step, start=0, size=4):
        return tg.at[zs[step], pl.ds(start, size)]

    def t_send(k):
        return (
            (tg.at[z, y], peer["y", 1]),
            (tg.at[z, y], peer["y", -1]),
            (tg.at[z, y], peer["y", 2]),
            (t_line(0), peer["z", 1]),
            (t_line(0), peer["z", -1]),
            (t_line(-1, 0, 2), peer["z", 1]),
            (t_line(1, 2, 2), peer["z", -1]),
        )[k]

    def t_land(k):
        return (
            tg.at[z, ys[-1]], tg.at[z, ys[1]], tg.at[z, ys[2]],
            t_line(-1), t_line(1), t_line(2, 0, 2), t_line(2, 2, 2),
        )[k]

    def t_copy(k, src, to):
        return pltpu.make_async_remote_copy(
            src_ref=src, dst_ref=src, send_sem=tsend.at[k], recv_sem=trecv.at[k], device_id=to, device_id_type=MESH
        )

    def t_start(*kinds):
        for k in kinds:
            t_copy(k, *t_send(k)).start()

    def t_wait(*kinds):
        for k in kinds:
            t_copy(k, t_land(k), peer["core"]).wait_recv()

    def a0(c):
        ag[c, z, y] = a_ref[pl.ds(pl.multiple_of(c * BLOCK, BLOCK), BLOCK), :main]
        for s in range(2):
            a_start(c, s, 0)
            a_start(c, s, 1)

        @pl.when(c == 0)
        def _():
            for s in range(2):
                copy(c, s * 7 + 2, block(s, c, 0), block(s, c, 0), peer[gather[s][0], 2]).start()
            t_start(0, 1, 2)

    def a1(c):
        def forward(d):
            for s in range(2):
                a_wait(c, s, 0 if d == 1 else 1)
                a_start(c, s, 2, d)

        @pl.when(c == 0)
        def _():
            for s in range(2):
                a_wait(c, s, 0)

        pl.when(jnp.logical_and(c % 2 == 0, c > 0))(lambda: forward(1))
        pl.when(c % 2 == 1)(lambda: forward(-1))

    def a2(c):
        pl.when(c % 2 == 0)(lambda: [a_wait(c, s, 1) for s in range(2)] and None)
        pl.when(c % 2 == 1)(lambda: [a_wait(c, s, 0) for s in range(2)] and None)
        for s in range(2):
            a_wait(c, s, 2)
            a_start(c, s, 3)
            a_start(c, s, 4)

        @pl.when(c == 0)
        def _():
            t_wait(0, 1, 2)
            t_start(3, 4)

    def a3(c):
        for s in range(2):
            a_wait(c, s, 3)
            a_start(c, s, 5)
            a_wait(c, s, 4)
            a_start(c, s, 6)

        @pl.when(c == 0)
        def _():
            t_wait(3)
            t_start(5)
            t_wait(4)
            t_start(6)

    def m1(c):
        for s in range(2):
            a_wait(c, s, 5)
            a_wait(c, s, 6)
        pl.when(c == 0)(lambda: t_wait(5, 6))
        ends = tg[:, :, pl.ds(pl.multiple_of(c // 2 * BLOCK, BLOCK), BLOCK), :].reshape(16 * BLOCK, 128)
        mine = lax.broadcasted_iota(jnp.int32, (16 * BLOCK, 128), 1) // 64 == c % 2
        ends = jnp.where(mine, ends.astype(F32), 0.0).astype(BF16)
        rows = jnp.concatenate([ag[c].reshape(16 * BLOCK, main), ends], axis=1)
        middle = (width // 2 + 127) // 128 * 128
        last = (((1,), (1,)), ((), ()))
        for lo, hi in ((0, middle), (middle, width)):
            left = jnp.concatenate([vt[lo:hi, :main], vtail[lo:hi]], axis=1)
            part = lax.dot_general(left, rows, last, preferred_element_type=F32)
            c1[c % SLOTS, :, lo:hi] = part.astype(BF16).T
        x_start(c, 0)

    def piece(step, start=0, size=32):
        return pl.ds(pl.multiple_of(strips[step] + start, 16), size)

    def x_send(c, k):
        if k == 0:
            return c1.at[c % SLOTS, pl.ds(pl.multiple_of(other, 128), 128)], cx.at[c % SLOTS], peer["core"]
        if k < 4:
            return c1.at[c % SLOTS, piece(STEP[k])], xn.at[c, k - 1], peer["x", STEP[k]]
        if k < 7:
            src = sg.at[c % SLOTS, piece(0)]
            return src, src, peer["x", STEP[k - 3]]
        src = sg.at[c % SLOTS, pl.ds(pl.multiple_of(half, 128), 128)]
        return src, src, peer["core"]

    def x_land(c, k):
        if k < 4:
            return x_send(c, k)[1]
        if k < 7:
            return sg.at[c % SLOTS, piece(STEP[7 - k])]
        return sg.at[c % SLOTS, pl.ds(pl.multiple_of(other, 128), 128)]

    def x_start(c, k):
        src, dst, to = x_send(c, k)
        copy(c, X_KIND + k, src, dst, to).start()

    def x_wait(c, k):
        arrived(c, X_KIND + k, x_land(c, k))

    def b1(c):
        x_wait(c, 0)
        rows = pl.ds(pl.multiple_of(half, 128), 128)
        c1[c % SLOTS, rows, :] = c1[c % SLOTS, rows, :] + cx[c % SLOTS]
        for k in (2, 1, 3):
            x_start(c, k)

    def b3(c):
        gap = rc[pl.ds(core * 8 + x * 2, 2), c].reshape(32, 128)
        rows = piece(0)
        total = c1[c % SLOTS, rows, :].astype(F32)
        for k in (1, 2, 3):
            x_wait(c, k)
            total = total + xn[c, k - 1].astype(F32)
        sg[c % SLOTS, rows, :] = (total / (gap[:, :1] + cg[0:1, :width])).astype(BF16)
        for k in (5, 4, 6):
            x_start(c, k)

    def b5(c):
        for k in (4, 5, 6):
            x_wait(c, k)
        x_start(c, 7)

    def r_move(c, s, k):
        first, second = scatter[s]
        fs, gs = at[first], at[second]
        d = 1 if k % 2 == 0 else -1
        if k < 2:
            part = pl.ds(0, CUT) if k == 0 else pl.ds(CUT, group - CUT)
            return w1.at[s, c % SLOTS, fs[2], part], ro1.at[s, c % SLOTS, part], peer[first, d]
        if k < 4:
            return w1.at[s, c % SLOTS, fs[d]], rn1.at[s, c % SLOTS, k - 2], peer[first, d]
        if k < 6:
            part = pl.ds((k - 4) * (WINDOW // 2), WINDOW // 2)
            return w2.at[s, c, gs[2], part], ro2.at[s, c, part], peer[second, d]
        return w2.at[s, c, gs[d]], rn2.at[s, c, k - 6], peer[second, d]

    def r_start(c, s, k):
        src, dst, to = r_move(c, s, k)
        copy(c, RS_KIND + s * 8 + k, src, dst, to).start()

    def far_copy(c, s):
        second = scatter[s][1]
        return copy(c, RS_KIND + s * 8 + 4, w2.at[s, c, at[second][2]], ro2.at[s, c], peer[second, 2])

    def r_wait(c, s, k):
        arrived(c, RS_KIND + s * 8 + k, r_move(c, s, k)[1])

    def m2(c):
        x_wait(c, 7)

        turned[...] = sg[c % SLOTS].T

        for g in range(2):
            both = jnp.dot(v[2 * g * group : 2 * (g + 1) * group, :], turned[...], preferred_element_type=F32)
            for q in (2 * g, 2 * g + 1):
                part = both[(q - 2 * g) * group : (q - 2 * g + 1) * group]
                w1[0, c % SLOTS, q] = part[:, :128].astype(BF16)
                for p in range(4):
                    wq[p, q * final : (q + 1) * final] = part[p * final : (p + 1) * final, 128:]
        for p in range(4):
            w1[1, c % SLOTS, p] = wq[p].astype(BF16)
        for s in range(2):
            r_start(c, s, 0)
            r_start(c, s, 1)

    def r1(c):
        o = c % SLOTS
        for s in range(2):
            r_wait(c, s, 0)
            r_wait(c, s, 1)
        for s in range(2):
            up, down = at[scatter[s][0]][1], at[scatter[s][0]][-1]
            w1[s, o, up, :CUT] = w1[s, o, up, :CUT] + ro1[s, o, :CUT]
            r_start(c, s, 2)
            w1[s, o, down, CUT:] = w1[s, o, down, CUT:] + ro1[s, o, CUT:]
            r_start(c, s, 3)

    def r2(c):
        o = c % SLOTS
        for s in range(2):
            f = at[scatter[s][0]][0]
            r_wait(c, s, 2)
            r_wait(c, s, 3)
            total = w1[s, o, f].astype(F32) + rn1[s, o, 0].astype(F32) + rn1[s, o, 1].astype(F32)
            total = total.astype(BF16)
            for p in range(4):
                w2[s, c, p] = total[p * STRIDE : p * STRIDE + WINDOW]

            @pl.when(c < chunks - 1)
            def _():
                r_start(c, s, 4)
                r_start(c, s, 5)

            @pl.when(c == chunks - 1)
            def _():
                far_copy(c, s).start()
                r_start(c, s, 6)
                r_start(c, s, 7)

    def r3(c):
        h = WINDOW // 2

        @pl.when(c < chunks - 1)
        def _():
            for s in range(2):
                up, down = at[scatter[s][1]][1], at[scatter[s][1]][-1]
                r_wait(c, s, 4)
                w2[s, c, up, :h] = w2[s, c, up, :h] + ro2[s, c, :h]
                r_start(c, s, 6)
                r_wait(c, s, 5)
                w2[s, c, down, h:] = w2[s, c, down, h:] + ro2[s, c, h:]
                r_start(c, s, 7)

    def r4(c):
        sums = []
        for s in range(2):
            g = at[scatter[s][1]][0]
            r_wait(c, s, 6)
            r_wait(c, s, 7)
            pl.when(c == chunks - 1)(lambda: far_copy(c, s).wait_recv())
            total = w2[s, c, g].astype(F32) + rn2[s, c, 0].astype(F32) + rn2[s, c, 1].astype(F32)
            total = total + jnp.where(c == chunks - 1, ro2[s, c].astype(F32), 0.0)
            sums.append(pltpu.roll(total, lax.rem(WINDOW - 4 * g, WINDOW), 0))
        total = jnp.concatenate(sums, axis=1)
        total = jnp.concatenate([total, jnp.zeros((256 - WINDOW, 256), F32)], axis=0)
        gap = rc[:, c].reshape(256, 128)
        gap = jnp.concatenate([gap, gap], axis=1) + cf[0:1, :]
        o_ref[:, c] = (total.T / gap).astype(BF16)[:, :final].reshape(16, BLOCK, final)

    def rw(c):
        for s in range(2):
            for k in range(4):
                sent(c, RS_KIND + s * 8 + k, r_move(c, s, k)[0])

    def gw(c):
        for k in range(4, 8):
            sent(c, X_KIND + k, x_send(c, k)[0])

    def cw(c):
        for k in range(4):
            sent(c, X_KIND + k, x_send(c, k)[0])

    def aw(c):
        @pl.when(c == 0)
        def _():
            for k in range(7):
                t_copy(k, t_send(k)[0], peer["core"]).wait_send()

        for s in range(2):
            for k in range(7):
                sent(c, s * 7 + k, a_send(c, s, k)[0])

    def sw(c):
        for s in range(2):
            for k in (6, 7):
                sent(c, RS_KIND + s * 8 + k, r_move(c, s, k)[0])

            @pl.when(c < chunks - 1)
            def _():
                for k in (4, 5):
                    sent(c, RS_KIND + s * 8 + k, r_move(c, s, k)[0])

            pl.when(c == chunks - 1)(lambda: far_copy(c, s).wait_send())

    load = pltpu.make_async_copy(vt_hbm, vt, lsem.at[0])
    entry = pltpu.make_async_copy(a_hbm, a_ref, lsem.at[1])
    tiles = width // TILE

    def tv(c):
        @pl.when(c == 0)
        def _():
            load.wait()
            ends = vt[:, main:]
            vtail[...] = jnp.concatenate([ends, ends], axis=1)

        def turn(i, carry):
            tile = pl.ds(pl.multiple_of(i * TILE, TILE), TILE)
            v[:, tile] = vt[tile, :].T
            return carry

        lax.fori_loop(2 * c, jnp.minimum(2 * c + 2, tiles), turn, 0)

        @pl.when(c == 5)
        def _():
            v[:, tiles * TILE :] = vt[tiles * TILE :, :].T

    entry.start()
    load.start()
    entry.wait()
    for k in range(0, chunks, 2):
        pair = [a_ref[i * BLOCK : (i + 1) * BLOCK, main:] for i in (k, k + 1) if i < chunks]
        if len(pair) == 1:
            pair.append(jnp.zeros_like(pair[0]))
        tg[z, y, k // 2 * BLOCK : (k // 2 + 1) * BLOCK, :] = jnp.concatenate(pair, axis=1)

    def gp(c):
        inner, outer = col * width, (row * 16 + col) * final
        inner_row = inner // 128
        outer_row = jnp.minimum(outer // 128, col_ref.shape[0] - 3)
        for k in range(12):
            near[:, 128 * k : 128 * (k + 1)] = col_ref[pl.ds(inner_row + k, 1), :]
        for k in range(3):
            near[:, 1536 + 128 * k : 1664 + 128 * k] = col_ref[pl.ds(outer_row + k, 1), :]
        cg[...] = pltpu.roll(jnp.broadcast_to(near[:, :1536], (8, 1536)), (1536 - (inner - inner_row * 128)) % 1536, 1)
        shifted = pltpu.roll(jnp.broadcast_to(near[:, 1536:], (8, 384)), (384 - (outer - outer_row * 128)) % 384, 1)
        cf[...] = shifted[:, :256]
        flat = rc.reshape(16 * chunks * BLOCK, 128)
        for k in range(row_ref.shape[0]):
            flat[k * 128 : (k + 1) * 128, :] = jnp.broadcast_to(row_ref[k : k + 1, :], (128, 128)).T

    pl.semaphore_wait(barrier, len(peer))

    ops = dict(tv=tv, aw=aw, cw=cw, gw=gw, rw=rw, gp=gp, a0=a0, a1=a1, a2=a2, a3=a3, m1=m1, b1=b1, b3=b3, b5=b5, m2=m2, r1=r1, r2=r2, r3=r3, r4=r4, sw=sw)

    def step(t, carry):
        for name, late in PLAN:
            c = t - late
            pl.when(jnp.logical_and(c >= 0, c < {"tv": 6, "gp": 1}.get(name, chunks)))(functools.partial(ops[name], c))
        return carry

    lax.fori_loop(0, chunks + max(late for _, late in PLAN), step, 0)


def on_device(amplitudes, integrals, row_gap, col_gap):
    rows, depth = amplitudes.shape
    width = integrals.shape[1]
    chunks = rows // BLOCK
    final = depth // 16

    vm = pl.BlockSpec(memory_space=pltpu.VMEM)
    anywhere = pl.BlockSpec(memory_space=pl.ANY)
    updated = pl.pallas_call(
        kernel,
        out_shape=jax.ShapeDtypeStruct((16, chunks, BLOCK, final), BF16),
        in_specs=[anywhere, anywhere, vm, vm],
        out_specs=vm,
        scratch_shapes=[
            pltpu.VMEM((rows, depth), BF16),
            pltpu.VMEM((1, 1920), F32),
            pltpu.VMEM((8, 1536), F32),
            pltpu.VMEM((8, 256), F32),
            pltpu.VMEM((16, chunks, BLOCK, 128), F32),
            pltpu.VMEM((depth, width), BF16),
            pltpu.VMEM((width, depth), BF16),
            pltpu.VMEM((width, 128), BF16),
            pltpu.VMEM((width, 256), BF16),
            pltpu.VMEM((chunks, 4, 4, BLOCK, depth // 128 * 128), BF16),
            pltpu.VMEM((4, 4, (chunks + 1) // 2 * BLOCK, 128), BF16),
            pltpu.VMEM((SLOTS, 256, width), BF16),
            pltpu.VMEM((SLOTS, 128, width), BF16),
            pltpu.VMEM((chunks, 3, 32, width), BF16),
            pltpu.VMEM((SLOTS, 256, width), BF16),
            pltpu.VMEM((4, depth // 4, 128), F32),
            pltpu.VMEM((2, SLOTS, 4, depth // 4, 128), BF16),
            pltpu.VMEM((2, chunks, 4, WINDOW, 128), BF16),
            pltpu.VMEM((2, SLOTS, depth // 4, 128), BF16),
            pltpu.VMEM((2, SLOTS, 2, depth // 4, 128), BF16),
            pltpu.VMEM((2, chunks, WINDOW, 128), BF16),
            pltpu.VMEM((2, chunks, 2, WINDOW, 128), BF16),
            pltpu.SemaphoreType.DMA((2,)),
            pltpu.SemaphoreType.DMA((7,)),
            pltpu.SemaphoreType.DMA((7,)),
            pltpu.SemaphoreType.DMA((chunks, KINDS)),
            pltpu.SemaphoreType.DMA((chunks, KINDS)),
        ],
        compiler_params=pltpu.CompilerParams(
            collective_id=0, has_side_effects=True, vmem_limit_bytes=62 * 1024 * 1024
        ),
        cost_estimate=pl.CostEstimate(
            flops=4 * 16 * rows * depth * width, bytes_accessed=2 * depth * width, transcendentals=0
        ),
    )(amplitudes, integrals.T, row_gap.reshape(-1, 128), col_gap.reshape(-1, 128))
    return updated.reshape(16 * rows, final)


def solution(mesh):
    return jax.shard_map(
        on_device,
        mesh=mesh,
        in_specs=(P("col", "row"), P("row", "col"), P(), P()),
        out_specs=P(None, ("row", "col")),
        check_vma=False,
    )
```

```python
import functools

import jax
import jax.numpy as jnp
from jax import lax
from jax.experimental import pallas as pl
from jax.experimental.pallas import tpu as pltpu
from jax.sharding import PartitionSpec as P

MESH = pl.DeviceIdType.MESH
F32 = jnp.float32
BF16 = jnp.bfloat16

BLOCK = 16
WINDOW = 192
STRIDE = 176
TILE = 128
CUT = 368
SLOTS = 4
X_KIND = 14
RS_KIND = 24
KINDS = 40

PLAN = (
    ("r1", 8),
    ("r2", 10),
    ("a0", 0),
    ("cw", 7),
    ("aw", 7),
    ("m1", 3),
    ("b2", 4),
    ("b4", 5),
    ("r3", 12),
    ("a3", 2),
    ("a2", 1),
    ("r4", 14),
    ("sw", 14),
    ("a1", 0),
    ("tv", 1),
    ("gp", 3),
    ("rw", 10),
    ("m2", 6),
    ("gw", 7),
    ("b1", 3),
    ("b3", 4),
    ("b5", 5),
)


def kernel(
    a_hbm, vt_hbm, row_ref, col_ref, o_ref,
    a_ref, near, cg, cf, rc, v, vt, vtail, turned, ag, tg, c1, cx, xo, xn, sg, wq, w1, w2, ro1, rn1, ro2, rn2, lsem, tsend, trecv, send, recv,
):
    chunks = ag.shape[0]
    depth, width = a_ref.shape[1], v.shape[1]
    group, final = depth // 4, o_ref.shape[-1]
    row, col = lax.axis_index("row"), lax.axis_index("col")
    x, core = row // 2, row % 2
    z, y = col // 4, col % 4
    half = core * 128
    other = 128 - half

    def around(index):
        return {0: index, 1: lax.rem(index + 1, 4), 2: lax.rem(index + 2, 4), -1: lax.rem(index + 3, 4)}

    xs, ys, zs = around(x), around(y), around(z)
    at = {"z": zs, "y": ys}
    peer = {
        ("x", 1): (xs[1] * 2 + core, col),
        ("x", -1): (xs[-1] * 2 + core, col),
        ("y", 1): (row, z * 4 + ys[1]),
        ("y", -1): (row, z * 4 + ys[-1]),
        ("z", 1): (row, zs[1] * 4 + y),
        ("z", -1): (row, zs[-1] * 4 + y),
        ("y", 2): (row, z * 4 + ys[2]),
        ("z", 2): (row, zs[2] * 4 + y),
        "core": (x * 2 + 1 - core, col),
    }
    strips = {step: half + index * 32 for step, index in xs.items()}
    main = ag.shape[-1]
    gather = (("y", "z", pl.ds(0, main // 2)), ("z", "y", pl.ds(main // 2, main // 2)))
    scatter = (("z", "y"), ("y", "z"))

    barrier = pltpu.get_barrier_semaphore()
    for to in peer.values():
        pl.semaphore_signal(barrier, inc=1, device_id=to, device_id_type=MESH)

    def copy(c, kind, src, dst, to):
        return pltpu.make_async_remote_copy(
            src_ref=src, dst_ref=dst, send_sem=send.at[c, kind], recv_sem=recv.at[c, kind],
            device_id=to, device_id_type=MESH,
        )

    def arrived(c, kind, dst):
        copy(c, kind, dst, dst, peer["core"]).wait_recv()

    def sent(c, kind, src):
        copy(c, kind, src, src, peer["core"]).wait_send()

    def block(s, c, step):
        first, _, lanes = gather[s]
        f = at[first][step]
        return ag.at[c, z, f, :, lanes] if first == "y" else ag.at[c, f, y, :, lanes]

    def line(s, c, step, start=0, size=4):
        first, second, lanes = gather[s]
        g, part = at[second][step], pl.ds(start, size)
        return ag.at[c, g, part, :, lanes] if first == "y" else ag.at[c, part, g, :, lanes]

    def a_send(c, s, k, d=1):
        first, second, _ = gather[s]
        if k == 0:
            return block(s, c, 0), peer[first, 1]
        if k == 1:
            return block(s, c, 0), peer[first, -1]
        if k == 2:
            return block(s, c, -d), peer[first, d]
        if k == 3:
            return line(s, c, 0), peer[second, 1]
        if k == 4:
            return line(s, c, 0), peer[second, -1]
        if k == 5:
            return line(s, c, -1, 0, 2), peer[second, 1]
        return line(s, c, 1, 2, 2), peer[second, -1]

    def a_land(c, s, k):
        if k < 3:
            return block(s, c, (-1, 1, 2)[k])
        if k < 5:
            return line(s, c, (-1, 1)[k - 3])
        return line(s, c, 2, 2 * (k - 5), 2)

    def a_start(c, s, k, d=1):
        src, to = a_send(c, s, k, d)
        copy(c, s * 7 + k, src, src, to).start()

    def a_wait(c, s, k):
        arrived(c, s * 7 + k, a_land(c, s, k))

    def t_line(step, start=0, size=4):
        return tg.at[zs[step], pl.ds(start, size)]

    def t_send(k):
        return (
            (tg.at[z, y], peer["y", 1]),
            (tg.at[z, y], peer["y", -1]),
            (tg.at[z, y], peer["y", 2]),
            (t_line(0), peer["z", 1]),
            (t_line(0), peer["z", -1]),
            (t_line(-1, 0, 2), peer["z", 1]),
            (t_line(1, 2, 2), peer["z", -1]),
        )[k]

    def t_land(k):
        return (
            tg.at[z, ys[-1]], tg.at[z, ys[1]], tg.at[z, ys[2]],
            t_line(-1), t_line(1), t_line(2, 0, 2), t_line(2, 2, 2),
        )[k]

    def t_copy(k, src, to):
        return pltpu.make_async_remote_copy(
            src_ref=src, dst_ref=src, send_sem=tsend.at[k], recv_sem=trecv.at[k], device_id=to, device_id_type=MESH
        )

    def t_start(*kinds):
        for k in kinds:
            t_copy(k, *t_send(k)).start()

    def t_wait(*kinds):
        for k in kinds:
            t_copy(k, t_land(k), peer["core"]).wait_recv()

    def a0(c):
        ag[c, z, y] = a_ref[pl.ds(pl.multiple_of(c * BLOCK, BLOCK), BLOCK), :main]
        for s in range(2):
            a_start(c, s, 0)
            a_start(c, s, 1)

        @pl.when(c == 0)
        def _():
            for s in range(2):
                copy(c, s * 7 + 2, block(s, c, 0), block(s, c, 0), peer[gather[s][0], 2]).start()
            t_start(0, 1, 2)

    def a1(c):
        def forward(d):
            for s in range(2):
                a_wait(c, s, 0 if d == 1 else 1)
                a_start(c, s, 2, d)

        @pl.when(c == 0)
        def _():
            for s in range(2):
                a_wait(c, s, 0)

        pl.when(jnp.logical_and(c % 2 == 0, c > 0))(lambda: forward(1))
        pl.when(c % 2 == 1)(lambda: forward(-1))

    def a2(c):
        pl.when(c % 2 == 0)(lambda: [a_wait(c, s, 1) for s in range(2)] and None)
        pl.when(c % 2 == 1)(lambda: [a_wait(c, s, 0) for s in range(2)] and None)
        for s in range(2):
            a_wait(c, s, 2)
            a_start(c, s, 3)
            a_start(c, s, 4)

        @pl.when(c == 0)
        def _():
            t_wait(0, 1, 2)
            t_start(3, 4)

    def a3(c):
        for s in range(2):
            a_wait(c, s, 3)
            a_start(c, s, 5)
            a_wait(c, s, 4)
            a_start(c, s, 6)

        @pl.when(c == 0)
        def _():
            t_wait(3)
            t_start(5)
            t_wait(4)
            t_start(6)

    def m1(c):
        for s in range(2):
            a_wait(c, s, 5)
            a_wait(c, s, 6)
        pl.when(c == 0)(lambda: t_wait(5, 6))
        ends = tg[:, :, pl.ds(pl.multiple_of(c // 2 * BLOCK, BLOCK), BLOCK), :].reshape(16 * BLOCK, 128)
        mine = lax.broadcasted_iota(jnp.int32, (16 * BLOCK, 128), 1) // 64 == c % 2
        ends = jnp.where(mine, ends.astype(F32), 0.0).astype(BF16)
        rows = jnp.concatenate([ag[c].reshape(16 * BLOCK, main), ends], axis=1)
        middle = (width // 2 + 127) // 128 * 128
        last = (((1,), (1,)), ((), ()))
        for lo, hi in ((0, middle), (middle, width)):
            left = jnp.concatenate([vt[lo:hi, :main], vtail[lo:hi]], axis=1)
            part = lax.dot_general(left, rows, last, preferred_element_type=F32)
            c1[c % SLOTS, :, lo:hi] = part.astype(BF16).T
        x_start(c, 0)

    def piece(step, start=0, size=32):
        return pl.ds(pl.multiple_of(strips[step] + start, 16), size)

    def x_send(c, k):
        if k == 0:
            return c1.at[c % SLOTS, pl.ds(pl.multiple_of(other, 128), 128)], cx.at[c % SLOTS], peer["core"]
        if k == 9:
            src = sg.at[c % SLOTS, pl.ds(pl.multiple_of(half, 128), 128)]
            return src, src, peer["core"]
        d = 1 if k % 2 == 1 else -1
        part = pl.ds(8 - 8 * d, 16)
        if k < 3:
            return c1.at[c % SLOTS, piece(2, 8 - 8 * d, 16)], xo.at[c, part], peer["x", d]
        if k < 5:
            return c1.at[c % SLOTS, piece(d)], xn.at[c, (k - 3)], peer["x", d]
        src = sg.at[c % SLOTS, piece(0) if k < 7 else piece(-d, 8 - 8 * d, 16)]
        return src, src, peer["x", d]

    def x_land(c, k):
        if k < 5:
            return x_send(c, k)[1]
        if k == 9:
            return sg.at[c % SLOTS, pl.ds(pl.multiple_of(other, 128), 128)]
        d = 1 if k % 2 == 1 else -1
        return sg.at[c % SLOTS, piece(-d) if k < 7 else piece(2, 8 - 8 * d, 16)]

    def x_start(c, k):
        src, dst, to = x_send(c, k)
        copy(c, X_KIND + k, src, dst, to).start()

    def x_wait(c, k):
        arrived(c, X_KIND + k, x_land(c, k))

    def b1(c):
        x_wait(c, 0)
        rows = pl.ds(pl.multiple_of(half, 128), 128)
        c1[c % SLOTS, rows, :] = c1[c % SLOTS, rows, :] + cx[c % SLOTS]
        x_start(c, 1)
        x_start(c, 2)

    def b2(c):
        for k, step in ((1, 1), (2, -1)):
            x_wait(c, k)
            part, rows = pl.ds(16 * (k - 1), 16), piece(step, 16 * (k - 1), 16)
            c1[c % SLOTS, rows, :] = c1[c % SLOTS, rows, :] + xo[c, part]
            x_start(c, k + 2)

    def b3(c):
        gap = rc[pl.ds(core * 8 + x * 2, 2), c].reshape(32, 128)
        x_wait(c, 3)
        x_wait(c, 4)
        rows = piece(0)
        total = c1[c % SLOTS, rows, :].astype(F32) + xn[c, 0].astype(F32) + xn[c, 1].astype(F32)
        sg[c % SLOTS, rows, :] = (total / (gap[:, :1] + cg[0:1, :width])).astype(BF16)
        x_start(c, 5)
        x_start(c, 6)

    def b4(c):
        for k in (5, 6):
            x_wait(c, k)
            x_start(c, k + 2)

    def b5(c):
        x_wait(c, 7)
        x_wait(c, 8)
        x_start(c, 9)

    def r_move(c, s, k):
        first, second = scatter[s]
        fs, gs = at[first], at[second]
        d = 1 if k % 2 == 0 else -1
        if k < 2:
            part = pl.ds(0, CUT) if k == 0 else pl.ds(CUT, group - CUT)
            return w1.at[s, c % SLOTS, fs[2], part], ro1.at[s, c % SLOTS, part], peer[first, d]
        if k < 4:
            return w1.at[s, c % SLOTS, fs[d]], rn1.at[s, c % SLOTS, k - 2], peer[first, d]
        if k < 6:
            part = pl.ds((k - 4) * (WINDOW // 2), WINDOW // 2)
            return w2.at[s, c, gs[2], part], ro2.at[s, c, part], peer[second, d]
        return w2.at[s, c, gs[d]], rn2.at[s, c, k - 6], peer[second, d]

    def r_start(c, s, k):
        src, dst, to = r_move(c, s, k)
        copy(c, RS_KIND + s * 8 + k, src, dst, to).start()

    def far_copy(c, s):
        second = scatter[s][1]
        return copy(c, RS_KIND + s * 8 + 4, w2.at[s, c, at[second][2]], ro2.at[s, c], peer[second, 2])

    def r_wait(c, s, k):
        arrived(c, RS_KIND + s * 8 + k, r_move(c, s, k)[1])

    def m2(c):
        x_wait(c, 9)

        turned[...] = sg[c % SLOTS].T

        for g in range(2):
            both = jnp.dot(v[2 * g * group : 2 * (g + 1) * group, :], turned[...], preferred_element_type=F32)
            for q in (2 * g, 2 * g + 1):
                part = both[(q - 2 * g) * group : (q - 2 * g + 1) * group]
                w1[0, c % SLOTS, q] = part[:, :128].astype(BF16)
                for p in range(4):
                    wq[p, q * final : (q + 1) * final] = part[p * final : (p + 1) * final, 128:]
        for p in range(4):
            w1[1, c % SLOTS, p] = wq[p].astype(BF16)
        for s in range(2):
            r_start(c, s, 0)
            r_start(c, s, 1)

    def r1(c):
        o = c % SLOTS
        for s in range(2):
            r_wait(c, s, 0)
            r_wait(c, s, 1)
        for s in range(2):
            up, down = at[scatter[s][0]][1], at[scatter[s][0]][-1]
            w1[s, o, up, :CUT] = w1[s, o, up, :CUT] + ro1[s, o, :CUT]
            r_start(c, s, 2)
            w1[s, o, down, CUT:] = w1[s, o, down, CUT:] + ro1[s, o, CUT:]
            r_start(c, s, 3)

    def r2(c):
        o = c % SLOTS
        for s in range(2):
            f = at[scatter[s][0]][0]
            r_wait(c, s, 2)
            r_wait(c, s, 3)
            total = w1[s, o, f].astype(F32) + rn1[s, o, 0].astype(F32) + rn1[s, o, 1].astype(F32)
            total = total.astype(BF16)
            for p in range(4):
                w2[s, c, p] = total[p * STRIDE : p * STRIDE + WINDOW]

            @pl.when(c < chunks - 1)
            def _():
                r_start(c, s, 4)
                r_start(c, s, 5)

            @pl.when(c == chunks - 1)
            def _():
                far_copy(c, s).start()
                r_start(c, s, 6)
                r_start(c, s, 7)

    def r3(c):
        h = WINDOW // 2

        @pl.when(c < chunks - 1)
        def _():
            for s in range(2):
                up, down = at[scatter[s][1]][1], at[scatter[s][1]][-1]
                r_wait(c, s, 4)
                w2[s, c, up, :h] = w2[s, c, up, :h] + ro2[s, c, :h]
                r_start(c, s, 6)
                r_wait(c, s, 5)
                w2[s, c, down, h:] = w2[s, c, down, h:] + ro2[s, c, h:]
                r_start(c, s, 7)

    def r4(c):
        sums = []
        for s in range(2):
            g = at[scatter[s][1]][0]
            r_wait(c, s, 6)
            r_wait(c, s, 7)
            pl.when(c == chunks - 1)(lambda: far_copy(c, s).wait_recv())
            total = w2[s, c, g].astype(F32) + rn2[s, c, 0].astype(F32) + rn2[s, c, 1].astype(F32)
            total = total + jnp.where(c == chunks - 1, ro2[s, c].astype(F32), 0.0)
            sums.append(pltpu.roll(total, lax.rem(WINDOW - 4 * g, WINDOW), 0))
        total = jnp.concatenate(sums, axis=1)
        total = jnp.concatenate([total, jnp.zeros((256 - WINDOW, 256), F32)], axis=0)
        gap = rc[:, c].reshape(256, 128)
        gap = jnp.concatenate([gap, gap], axis=1) + cf[0:1, :]
        o_ref[:, c] = (total.T / gap).astype(BF16)[:, :final].reshape(16, BLOCK, final)

    def rw(c):
        for s in range(2):
            for k in range(4):
                sent(c, RS_KIND + s * 8 + k, r_move(c, s, k)[0])

    def gw(c):
        for k in range(5, 10):
            sent(c, X_KIND + k, x_send(c, k)[0])

    def cw(c):
        for k in range(5):
            sent(c, X_KIND + k, x_send(c, k)[0])

    def aw(c):
        @pl.when(c == 0)
        def _():
            for k in range(7):
                t_copy(k, t_send(k)[0], peer["core"]).wait_send()

        for s in range(2):
            for k in range(7):
                sent(c, s * 7 + k, a_send(c, s, k)[0])

    def sw(c):
        for s in range(2):
            for k in (6, 7):
                sent(c, RS_KIND + s * 8 + k, r_move(c, s, k)[0])

            @pl.when(c < chunks - 1)
            def _():
                for k in (4, 5):
                    sent(c, RS_KIND + s * 8 + k, r_move(c, s, k)[0])

            pl.when(c == chunks - 1)(lambda: far_copy(c, s).wait_send())

    load = pltpu.make_async_copy(vt_hbm, vt, lsem.at[0])
    entry = pltpu.make_async_copy(a_hbm, a_ref, lsem.at[1])
    tiles = width // TILE

    def tv(c):
        @pl.when(c == 0)
        def _():
            load.wait()
            ends = vt[:, main:]
            vtail[...] = jnp.concatenate([ends, ends], axis=1)

        def turn(i, carry):
            tile = pl.ds(pl.multiple_of(i * TILE, TILE), TILE)
            v[:, tile] = vt[tile, :].T
            return carry

        lax.fori_loop(2 * c, jnp.minimum(2 * c + 2, tiles), turn, 0)

        @pl.when(c == 5)
        def _():
            v[:, tiles * TILE :] = vt[tiles * TILE :, :].T

    entry.start()
    load.start()
    entry.wait()
    for k in range(0, chunks, 2):
        pair = [a_ref[i * BLOCK : (i + 1) * BLOCK, main:] for i in (k, k + 1) if i < chunks]
        if len(pair) == 1:
            pair.append(jnp.zeros_like(pair[0]))
        tg[z, y, k // 2 * BLOCK : (k // 2 + 1) * BLOCK, :] = jnp.concatenate(pair, axis=1)

    def gp(c):
        inner, outer = col * width, (row * 16 + col) * final
        inner_row = inner // 128
        outer_row = jnp.minimum(outer // 128, col_ref.shape[0] - 3)
        for k in range(12):
            near[:, 128 * k : 128 * (k + 1)] = col_ref[pl.ds(inner_row + k, 1), :]
        for k in range(3):
            near[:, 1536 + 128 * k : 1664 + 128 * k] = col_ref[pl.ds(outer_row + k, 1), :]
        cg[...] = pltpu.roll(jnp.broadcast_to(near[:, :1536], (8, 1536)), (1536 - (inner - inner_row * 128)) % 1536, 1)
        shifted = pltpu.roll(jnp.broadcast_to(near[:, 1536:], (8, 384)), (384 - (outer - outer_row * 128)) % 384, 1)
        cf[...] = shifted[:, :256]
        flat = rc.reshape(16 * chunks * BLOCK, 128)
        for k in range(row_ref.shape[0]):
            flat[k * 128 : (k + 1) * 128, :] = jnp.broadcast_to(row_ref[k : k + 1, :], (128, 128)).T

    pl.semaphore_wait(barrier, len(peer))

    ops = dict(tv=tv, aw=aw, cw=cw, gw=gw, rw=rw, gp=gp, a0=a0, a1=a1, a2=a2, a3=a3, m1=m1, b1=b1, b2=b2, b3=b3, b4=b4, b5=b5, m2=m2, r1=r1, r2=r2, r3=r3, r4=r4, sw=sw)

    def step(t, carry):
        for name, late in PLAN:
            c = t - late
            pl.when(jnp.logical_and(c >= 0, c < {"tv": 6, "gp": 1}.get(name, chunks)))(functools.partial(ops[name], c))
        return carry

    lax.fori_loop(0, chunks + max(late for _, late in PLAN), step, 0)


def on_device(amplitudes, integrals, row_gap, col_gap):
    rows, depth = amplitudes.shape
    width = integrals.shape[1]
    chunks = rows // BLOCK
    final = depth // 16

    vm = pl.BlockSpec(memory_space=pltpu.VMEM)
    anywhere = pl.BlockSpec(memory_space=pl.ANY)
    updated = pl.pallas_call(
        kernel,
        out_shape=jax.ShapeDtypeStruct((16, chunks, BLOCK, final), BF16),
        in_specs=[anywhere, anywhere, vm, vm],
        out_specs=vm,
        scratch_shapes=[
            pltpu.VMEM((rows, depth), BF16),
            pltpu.VMEM((1, 1920), F32),
            pltpu.VMEM((8, 1536), F32),
            pltpu.VMEM((8, 256), F32),
            pltpu.VMEM((16, chunks, BLOCK, 128), F32),
            pltpu.VMEM((depth, width), BF16),
            pltpu.VMEM((width, depth), BF16),
            pltpu.VMEM((width, 128), BF16),
            pltpu.VMEM((width, 256), BF16),
            pltpu.VMEM((chunks, 4, 4, BLOCK, depth // 128 * 128), BF16),
            pltpu.VMEM((4, 4, (chunks + 1) // 2 * BLOCK, 128), BF16),
            pltpu.VMEM((SLOTS, 256, width), BF16),
            pltpu.VMEM((SLOTS, 128, width), BF16),
            pltpu.VMEM((chunks, 32, width), BF16),
            pltpu.VMEM((chunks, 2, 32, width), BF16),
            pltpu.VMEM((SLOTS, 256, width), BF16),
            pltpu.VMEM((4, depth // 4, 128), F32),
            pltpu.VMEM((2, SLOTS, 4, depth // 4, 128), BF16),
            pltpu.VMEM((2, chunks, 4, WINDOW, 128), BF16),
            pltpu.VMEM((2, SLOTS, depth // 4, 128), BF16),
            pltpu.VMEM((2, SLOTS, 2, depth // 4, 128), BF16),
            pltpu.VMEM((2, chunks, WINDOW, 128), BF16),
            pltpu.VMEM((2, chunks, 2, WINDOW, 128), BF16),
            pltpu.SemaphoreType.DMA((2,)),
            pltpu.SemaphoreType.DMA((7,)),
            pltpu.SemaphoreType.DMA((7,)),
            pltpu.SemaphoreType.DMA((chunks, KINDS)),
            pltpu.SemaphoreType.DMA((chunks, KINDS)),
        ],
        compiler_params=pltpu.CompilerParams(
            collective_id=0, has_side_effects=True, vmem_limit_bytes=62 * 1024 * 1024
        ),
        cost_estimate=pl.CostEstimate(
            flops=4 * 16 * rows * depth * width, bytes_accessed=2 * depth * width, transcendentals=0
        ),
    )(amplitudes, integrals.T, row_gap.reshape(-1, 128), col_gap.reshape(-1, 128))
    return updated.reshape(16 * rows, final)


def solution(mesh):
    return jax.shard_map(
        on_device,
        mesh=mesh,
        in_specs=(P("col", "row"), P("row", "col"), P(), P()),
        out_specs=P(None, ("row", "col")),
        check_vma=False,
    )
```

```python
import functools

import jax
import jax.numpy as jnp
from jax import lax
from jax.experimental import pallas as pl
from jax.experimental.pallas import tpu as pltpu
from jax.sharding import PartitionSpec as P

MESH = pl.DeviceIdType.MESH
F32 = jnp.float32
BF16 = jnp.bfloat16

BLOCK = 16
WINDOW = 192
STRIDE = 176
TILE = 128
CUT = 368
SLOTS = 4
X_KIND = 14
RS_KIND = 24
KINDS = 40

PLAN = (
    ("r1", 8),
    ("r2", 10),
    ("a0", 0),
    ("a1", 1),
    ("cw", 7),
    ("aw", 7),
    ("m1", 3),
    ("b2", 4),
    ("b4", 5),
    ("r3", 12),
    ("a3", 2),
    ("a2", 1),
    ("r4", 14),
    ("sw", 14),
    ("tv", 1),
    ("gp", 3),
    ("rw", 10),
    ("m2", 6),
    ("gw", 7),
    ("b1", 3),
    ("b3", 4),
    ("b5", 5),
)


def kernel(
    a_hbm, vt_hbm, row_ref, col_ref, o_ref,
    a_ref, near, cg, cf, rc, v, vt, vtail, turned, ag, tg, c1, cx, xo, xn, sg, wq, w1, w2, ro1, rn1, ro2, rn2, lsem, tsend, trecv, send, recv,
):
    chunks = ag.shape[0]
    depth, width = a_ref.shape[1], v.shape[1]
    group, final = depth // 4, o_ref.shape[-1]
    row, col = lax.axis_index("row"), lax.axis_index("col")
    x, core = row // 2, row % 2
    z, y = col // 4, col % 4
    half = core * 128
    other = 128 - half

    def around(index):
        return {0: index, 1: lax.rem(index + 1, 4), 2: lax.rem(index + 2, 4), -1: lax.rem(index + 3, 4)}

    xs, ys, zs = around(x), around(y), around(z)
    at = {"z": zs, "y": ys}
    peer = {
        ("x", 1): (xs[1] * 2 + core, col),
        ("x", -1): (xs[-1] * 2 + core, col),
        ("y", 1): (row, z * 4 + ys[1]),
        ("y", -1): (row, z * 4 + ys[-1]),
        ("z", 1): (row, zs[1] * 4 + y),
        ("z", -1): (row, zs[-1] * 4 + y),
        ("y", 2): (row, z * 4 + ys[2]),
        ("z", 2): (row, zs[2] * 4 + y),
        "core": (x * 2 + 1 - core, col),
    }
    strips = {step: half + index * 32 for step, index in xs.items()}
    main = ag.shape[-1]
    gather = (("y", "z", pl.ds(0, main // 2)), ("z", "y", pl.ds(main // 2, main // 2)))
    scatter = (("z", "y"), ("y", "z"))

    barrier = pltpu.get_barrier_semaphore()
    for to in peer.values():
        pl.semaphore_signal(barrier, inc=1, device_id=to, device_id_type=MESH)

    def copy(c, kind, src, dst, to):
        return pltpu.make_async_remote_copy(
            src_ref=src, dst_ref=dst, send_sem=send.at[c, kind], recv_sem=recv.at[c, kind],
            device_id=to, device_id_type=MESH,
        )

    def arrived(c, kind, dst):
        copy(c, kind, dst, dst, peer["core"]).wait_recv()

    def sent(c, kind, src):
        copy(c, kind, src, src, peer["core"]).wait_send()

    def block(s, c, step):
        first, _, lanes = gather[s]
        f = at[first][step]
        return ag.at[c, z, f, :, lanes] if first == "y" else ag.at[c, f, y, :, lanes]

    def line(s, c, step, start=0, size=4):
        first, second, lanes = gather[s]
        g, part = at[second][step], pl.ds(start, size)
        return ag.at[c, g, part, :, lanes] if first == "y" else ag.at[c, part, g, :, lanes]

    def a_send(c, s, k, d=1):
        first, second, _ = gather[s]
        if k == 0:
            return block(s, c, 0), peer[first, 1]
        if k == 1:
            return block(s, c, 0), peer[first, -1]
        if k == 2:
            return block(s, c, -d), peer[first, d]
        if k == 3:
            return line(s, c, 0), peer[second, 1]
        if k == 4:
            return line(s, c, 0), peer[second, -1]
        if k == 5:
            return line(s, c, -1, 0, 2), peer[second, 1]
        return line(s, c, 1, 2, 2), peer[second, -1]

    def a_land(c, s, k):
        if k < 3:
            return block(s, c, (-1, 1, 2)[k])
        if k < 5:
            return line(s, c, (-1, 1)[k - 3])
        return line(s, c, 2, 2 * (k - 5), 2)

    def a_start(c, s, k, d=1):
        src, to = a_send(c, s, k, d)
        copy(c, s * 7 + k, src, src, to).start()

    def a_wait(c, s, k):
        arrived(c, s * 7 + k, a_land(c, s, k))

    def t_line(step, start=0, size=4):
        return tg.at[zs[step], pl.ds(start, size)]

    def t_send(k):
        return (
            (tg.at[z, y], peer["y", 1]),
            (tg.at[z, y], peer["y", -1]),
            (tg.at[z, y], peer["y", 2]),
            (t_line(0), peer["z", 1]),
            (t_line(0), peer["z", -1]),
            (t_line(-1, 0, 2), peer["z", 1]),
            (t_line(1, 2, 2), peer["z", -1]),
        )[k]

    def t_land(k):
        return (
            tg.at[z, ys[-1]], tg.at[z, ys[1]], tg.at[z, ys[2]],
            t_line(-1), t_line(1), t_line(2, 0, 2), t_line(2, 2, 2),
        )[k]

    def t_copy(k, src, to):
        return pltpu.make_async_remote_copy(
            src_ref=src, dst_ref=src, send_sem=tsend.at[k], recv_sem=trecv.at[k], device_id=to, device_id_type=MESH
        )

    def t_start(*kinds):
        for k in kinds:
            t_copy(k, *t_send(k)).start()

    def t_wait(*kinds):
        for k in kinds:
            t_copy(k, t_land(k), peer["core"]).wait_recv()

    def a0(c):
        ag[c, z, y] = a_ref[pl.ds(pl.multiple_of(c * BLOCK, BLOCK), BLOCK), :main]
        for s in range(2):
            a_start(c, s, 0)
            a_start(c, s, 1)

        @pl.when(c == 0)
        def _():
            for s in range(2):
                copy(c, s * 7 + 2, block(s, c, 0), block(s, c, 0), peer[gather[s][0], 2]).start()
            t_start(0, 1, 2)

    def a1(c):
        def forward(d):
            for s in range(2):
                a_wait(c, s, 0 if d == 1 else 1)
                a_start(c, s, 2, d)

        @pl.when(c == 0)
        def _():
            for s in range(2):
                a_wait(c, s, 0)

        pl.when(jnp.logical_and(c % 2 == 0, c > 0))(lambda: forward(1))
        pl.when(c % 2 == 1)(lambda: forward(-1))

    def a2(c):
        pl.when(c % 2 == 0)(lambda: [a_wait(c, s, 1) for s in range(2)] and None)
        pl.when(c % 2 == 1)(lambda: [a_wait(c, s, 0) for s in range(2)] and None)
        for s in range(2):
            a_wait(c, s, 2)
            a_start(c, s, 3)
            a_start(c, s, 4)

        @pl.when(c == 0)
        def _():
            t_wait(0, 1, 2)
            t_start(3, 4)

    def a3(c):
        for s in range(2):
            a_wait(c, s, 3)
            a_start(c, s, 5)
            a_wait(c, s, 4)
            a_start(c, s, 6)

        @pl.when(c == 0)
        def _():
            t_wait(3)
            t_start(5)
            t_wait(4)
            t_start(6)

    def m1(c):
        for s in range(2):
            a_wait(c, s, 5)
            a_wait(c, s, 6)
        pl.when(c == 0)(lambda: t_wait(5, 6))
        ends = tg[:, :, pl.ds(pl.multiple_of(c // 2 * BLOCK, BLOCK), BLOCK), :].reshape(16 * BLOCK, 128)
        mine = lax.broadcasted_iota(jnp.int32, (16 * BLOCK, 128), 1) // 64 == c % 2
        ends = jnp.where(mine, ends.astype(F32), 0.0).astype(BF16)
        rows = jnp.concatenate([ag[c].reshape(16 * BLOCK, main), ends], axis=1)
        middle = (width // 2 + 127) // 128 * 128
        last = (((1,), (1,)), ((), ()))
        for lo, hi in ((0, middle), (middle, width)):
            left = jnp.concatenate([vt[lo:hi, :main], vtail[lo:hi]], axis=1)
            part = lax.dot_general(left, rows, last, preferred_element_type=F32)
            c1[c % SLOTS, :, lo:hi] = part.astype(BF16).T
        x_start(c, 0)

    def piece(step, start=0, size=32):
        return pl.ds(pl.multiple_of(strips[step] + start, 16), size)

    def x_send(c, k):
        if k == 0:
            return c1.at[c % SLOTS, pl.ds(pl.multiple_of(other, 128), 128)], cx.at[c % SLOTS], peer["core"]
        if k == 9:
            src = sg.at[c % SLOTS, pl.ds(pl.multiple_of(half, 128), 128)]
            return src, src, peer["core"]
        d = 1 if k % 2 == 1 else -1
        part = pl.ds(8 - 8 * d, 16)
        if k < 3:
            return c1.at[c % SLOTS, piece(2, 8 - 8 * d, 16)], xo.at[c, part], peer["x", d]
        if k < 5:
            return c1.at[c % SLOTS, piece(d)], xn.at[c, (k - 3)], peer["x", d]
        src = sg.at[c % SLOTS, piece(0) if k < 7 else piece(-d, 8 - 8 * d, 16)]
        return src, src, peer["x", d]

    def x_land(c, k):
        if k < 5:
            return x_send(c, k)[1]
        if k == 9:
            return sg.at[c % SLOTS, pl.ds(pl.multiple_of(other, 128), 128)]
        d = 1 if k % 2 == 1 else -1
        return sg.at[c % SLOTS, piece(-d) if k < 7 else piece(2, 8 - 8 * d, 16)]

    def x_start(c, k):
        src, dst, to = x_send(c, k)
        copy(c, X_KIND + k, src, dst, to).start()

    def x_wait(c, k):
        arrived(c, X_KIND + k, x_land(c, k))

    def b1(c):
        x_wait(c, 0)
        rows = pl.ds(pl.multiple_of(half, 128), 128)
        c1[c % SLOTS, rows, :] = c1[c % SLOTS, rows, :] + cx[c % SLOTS]
        x_start(c, 1)
        x_start(c, 2)

    def b2(c):
        for k, step in ((1, 1), (2, -1)):
            x_wait(c, k)
            part, rows = pl.ds(16 * (k - 1), 16), piece(step, 16 * (k - 1), 16)
            c1[c % SLOTS, rows, :] = c1[c % SLOTS, rows, :] + xo[c, part]
            x_start(c, k + 2)

    def b3(c):
        gap = rc[pl.ds(core * 8 + x * 2, 2), c].reshape(32, 128)
        x_wait(c, 3)
        x_wait(c, 4)
        rows = piece(0)
        total = c1[c % SLOTS, rows, :].astype(F32) + xn[c, 0].astype(F32) + xn[c, 1].astype(F32)
        sg[c % SLOTS, rows, :] = (total / (gap[:, :1] + cg[0:1, :width])).astype(BF16)
        x_start(c, 5)
        x_start(c, 6)

    def b4(c):
        for k in (5, 6):
            x_wait(c, k)
            x_start(c, k + 2)

    def b5(c):
        x_wait(c, 7)
        x_wait(c, 8)
        x_start(c, 9)

    def r_move(c, s, k):
        first, second = scatter[s]
        fs, gs = at[first], at[second]
        d = 1 if k % 2 == 0 else -1
        if k < 2:
            part = pl.ds(0, CUT) if k == 0 else pl.ds(CUT, group - CUT)
            return w1.at[s, c % SLOTS, fs[2], part], ro1.at[s, c % SLOTS, part], peer[first, d]
        if k < 4:
            return w1.at[s, c % SLOTS, fs[d]], rn1.at[s, c % SLOTS, k - 2], peer[first, d]
        if k < 6:
            part = pl.ds((k - 4) * (WINDOW // 2), WINDOW // 2)
            return w2.at[s, c, gs[2], part], ro2.at[s, c, part], peer[second, d]
        return w2.at[s, c, gs[d]], rn2.at[s, c, k - 6], peer[second, d]

    def r_start(c, s, k):
        src, dst, to = r_move(c, s, k)
        copy(c, RS_KIND + s * 8 + k, src, dst, to).start()

    def far_copy(c, s):
        second = scatter[s][1]
        return copy(c, RS_KIND + s * 8 + 4, w2.at[s, c, at[second][2]], ro2.at[s, c], peer[second, 2])

    def r_wait(c, s, k):
        arrived(c, RS_KIND + s * 8 + k, r_move(c, s, k)[1])

    def m2(c):
        x_wait(c, 9)

        turned[...] = sg[c % SLOTS].T

        for g in range(2):
            both = jnp.dot(v[2 * g * group : 2 * (g + 1) * group, :], turned[...], preferred_element_type=F32)
            for q in (2 * g, 2 * g + 1):
                part = both[(q - 2 * g) * group : (q - 2 * g + 1) * group]
                w1[0, c % SLOTS, q] = part[:, :128].astype(BF16)
                for p in range(4):
                    wq[p, q * final : (q + 1) * final] = part[p * final : (p + 1) * final, 128:]
        for p in range(4):
            w1[1, c % SLOTS, p] = wq[p].astype(BF16)
        for s in range(2):
            r_start(c, s, 0)
            r_start(c, s, 1)

    def r1(c):
        o = c % SLOTS
        for s in range(2):
            r_wait(c, s, 0)
            r_wait(c, s, 1)
        for s in range(2):
            up, down = at[scatter[s][0]][1], at[scatter[s][0]][-1]
            w1[s, o, up, :CUT] = w1[s, o, up, :CUT] + ro1[s, o, :CUT]
            r_start(c, s, 2)
            w1[s, o, down, CUT:] = w1[s, o, down, CUT:] + ro1[s, o, CUT:]
            r_start(c, s, 3)

    def r2(c):
        o = c % SLOTS
        for s in range(2):
            f = at[scatter[s][0]][0]
            r_wait(c, s, 2)
            r_wait(c, s, 3)
            total = w1[s, o, f].astype(F32) + rn1[s, o, 0].astype(F32) + rn1[s, o, 1].astype(F32)
            total = total.astype(BF16)
            for p in range(4):
                w2[s, c, p] = total[p * STRIDE : p * STRIDE + WINDOW]

            @pl.when(c < chunks - 1)
            def _():
                r_start(c, s, 4)
                r_start(c, s, 5)

            @pl.when(c == chunks - 1)
            def _():
                far_copy(c, s).start()
                r_start(c, s, 6)
                r_start(c, s, 7)

    def r3(c):
        h = WINDOW // 2

        @pl.when(c < chunks - 1)
        def _():
            for s in range(2):
                up, down = at[scatter[s][1]][1], at[scatter[s][1]][-1]
                r_wait(c, s, 4)
                w2[s, c, up, :h] = w2[s, c, up, :h] + ro2[s, c, :h]
                r_start(c, s, 6)
                r_wait(c, s, 5)
                w2[s, c, down, h:] = w2[s, c, down, h:] + ro2[s, c, h:]
                r_start(c, s, 7)

    def r4(c):
        sums = []
        for s in range(2):
            g = at[scatter[s][1]][0]
            r_wait(c, s, 6)
            r_wait(c, s, 7)
            pl.when(c == chunks - 1)(lambda: far_copy(c, s).wait_recv())
            total = w2[s, c, g].astype(F32) + rn2[s, c, 0].astype(F32) + rn2[s, c, 1].astype(F32)
            total = total + jnp.where(c == chunks - 1, ro2[s, c].astype(F32), 0.0)
            sums.append(pltpu.roll(total, lax.rem(WINDOW - 4 * g, WINDOW), 0))
        total = jnp.concatenate(sums, axis=1)
        total = jnp.concatenate([total, jnp.zeros((256 - WINDOW, 256), F32)], axis=0)
        gap = rc[:, c].reshape(256, 128)
        gap = jnp.concatenate([gap, gap], axis=1) + cf[0:1, :]
        o_ref[:, c] = (total.T / gap).astype(BF16)[:, :final].reshape(16, BLOCK, final)

    def rw(c):
        for s in range(2):
            for k in range(4):
                sent(c, RS_KIND + s * 8 + k, r_move(c, s, k)[0])

    def gw(c):
        for k in range(5, 10):
            sent(c, X_KIND + k, x_send(c, k)[0])

    def cw(c):
        for k in range(5):
            sent(c, X_KIND + k, x_send(c, k)[0])

    def aw(c):
        @pl.when(c == 0)
        def _():
            for k in range(7):
                t_copy(k, t_send(k)[0], peer["core"]).wait_send()

        for s in range(2):
            for k in range(7):
                sent(c, s * 7 + k, a_send(c, s, k)[0])

    def sw(c):
        for s in range(2):
            for k in (6, 7):
                sent(c, RS_KIND + s * 8 + k, r_move(c, s, k)[0])

            @pl.when(c < chunks - 1)
            def _():
                for k in (4, 5):
                    sent(c, RS_KIND + s * 8 + k, r_move(c, s, k)[0])

            pl.when(c == chunks - 1)(lambda: far_copy(c, s).wait_send())

    load = pltpu.make_async_copy(vt_hbm, vt, lsem.at[0])
    entry = pltpu.make_async_copy(a_hbm, a_ref, lsem.at[1])
    tiles = width // TILE

    def tv(c):
        @pl.when(c == 0)
        def _():
            load.wait()
            ends = vt[:, main:]
            vtail[...] = jnp.concatenate([ends, ends], axis=1)

        def turn(i, carry):
            tile = pl.ds(pl.multiple_of(i * TILE, TILE), TILE)
            v[:, tile] = vt[tile, :].T
            return carry

        lax.fori_loop(2 * c, jnp.minimum(2 * c + 2, tiles), turn, 0)

        @pl.when(c == 5)
        def _():
            v[:, tiles * TILE :] = vt[tiles * TILE :, :].T

    entry.start()
    load.start()
    entry.wait()
    for k in range(0, chunks, 2):
        pair = [a_ref[i * BLOCK : (i + 1) * BLOCK, main:] for i in (k, k + 1) if i < chunks]
        if len(pair) == 1:
            pair.append(jnp.zeros_like(pair[0]))
        tg[z, y, k // 2 * BLOCK : (k // 2 + 1) * BLOCK, :] = jnp.concatenate(pair, axis=1)

    def gp(c):
        inner, outer = col * width, (row * 16 + col) * final
        inner_row = inner // 128
        outer_row = jnp.minimum(outer // 128, col_ref.shape[0] - 3)
        for k in range(12):
            near[:, 128 * k : 128 * (k + 1)] = col_ref[pl.ds(inner_row + k, 1), :]
        for k in range(3):
            near[:, 1536 + 128 * k : 1664 + 128 * k] = col_ref[pl.ds(outer_row + k, 1), :]
        cg[...] = pltpu.roll(jnp.broadcast_to(near[:, :1536], (8, 1536)), (1536 - (inner - inner_row * 128)) % 1536, 1)
        shifted = pltpu.roll(jnp.broadcast_to(near[:, 1536:], (8, 384)), (384 - (outer - outer_row * 128)) % 384, 1)
        cf[...] = shifted[:, :256]
        flat = rc.reshape(16 * chunks * BLOCK, 128)
        for k in range(row_ref.shape[0]):
            flat[k * 128 : (k + 1) * 128, :] = jnp.broadcast_to(row_ref[k : k + 1, :], (128, 128)).T

    pl.semaphore_wait(barrier, len(peer))

    ops = dict(tv=tv, aw=aw, cw=cw, gw=gw, rw=rw, gp=gp, a0=a0, a1=a1, a2=a2, a3=a3, m1=m1, b1=b1, b2=b2, b3=b3, b4=b4, b5=b5, m2=m2, r1=r1, r2=r2, r3=r3, r4=r4, sw=sw)

    def step(t, carry):
        for name, late in PLAN:
            c = t - late
            pl.when(jnp.logical_and(c >= 0, c < {"tv": 6, "gp": 1}.get(name, chunks)))(functools.partial(ops[name], c))
        return carry

    lax.fori_loop(0, chunks + max(late for _, late in PLAN), step, 0)


def on_device(amplitudes, integrals, row_gap, col_gap):
    rows, depth = amplitudes.shape
    width = integrals.shape[1]
    chunks = rows // BLOCK
    final = depth // 16

    vm = pl.BlockSpec(memory_space=pltpu.VMEM)
    anywhere = pl.BlockSpec(memory_space=pl.ANY)
    updated = pl.pallas_call(
        kernel,
        out_shape=jax.ShapeDtypeStruct((16, chunks, BLOCK, final), BF16),
        in_specs=[anywhere, anywhere, vm, vm],
        out_specs=vm,
        scratch_shapes=[
            pltpu.VMEM((rows, depth), BF16),
            pltpu.VMEM((1, 1920), F32),
            pltpu.VMEM((8, 1536), F32),
            pltpu.VMEM((8, 256), F32),
            pltpu.VMEM((16, chunks, BLOCK, 128), F32),
            pltpu.VMEM((depth, width), BF16),
            pltpu.VMEM((width, depth), BF16),
            pltpu.VMEM((width, 128), BF16),
            pltpu.VMEM((width, 256), BF16),
            pltpu.VMEM((chunks, 4, 4, BLOCK, depth // 128 * 128), BF16),
            pltpu.VMEM((4, 4, (chunks + 1) // 2 * BLOCK, 128), BF16),
            pltpu.VMEM((SLOTS, 256, width), BF16),
            pltpu.VMEM((SLOTS, 128, width), BF16),
            pltpu.VMEM((chunks, 32, width), BF16),
            pltpu.VMEM((chunks, 2, 32, width), BF16),
            pltpu.VMEM((SLOTS, 256, width), BF16),
            pltpu.VMEM((4, depth // 4, 128), F32),
            pltpu.VMEM((2, SLOTS, 4, depth // 4, 128), BF16),
            pltpu.VMEM((2, chunks, 4, WINDOW, 128), BF16),
            pltpu.VMEM((2, SLOTS, depth // 4, 128), BF16),
            pltpu.VMEM((2, SLOTS, 2, depth // 4, 128), BF16),
            pltpu.VMEM((2, chunks, WINDOW, 128), BF16),
            pltpu.VMEM((2, chunks, 2, WINDOW, 128), BF16),
            pltpu.SemaphoreType.DMA((2,)),
            pltpu.SemaphoreType.DMA((7,)),
            pltpu.SemaphoreType.DMA((7,)),
            pltpu.SemaphoreType.DMA((chunks, KINDS)),
            pltpu.SemaphoreType.DMA((chunks, KINDS)),
        ],
        compiler_params=pltpu.CompilerParams(
            collective_id=0, has_side_effects=True, vmem_limit_bytes=62 * 1024 * 1024
        ),
        cost_estimate=pl.CostEstimate(
            flops=4 * 16 * rows * depth * width, bytes_accessed=2 * depth * width, transcendentals=0
        ),
    )(amplitudes, integrals.T, row_gap.reshape(-1, 128), col_gap.reshape(-1, 128))
    return updated.reshape(16 * rows, final)


def solution(mesh):
    return jax.shard_map(
        on_device,
        mesh=mesh,
        in_specs=(P("col", "row"), P("row", "col"), P(), P()),
        out_specs=P(None, ("row", "col")),
        check_vma=False,
    )
```

```python
import functools

import jax
import jax.numpy as jnp
from jax import lax
from jax.experimental import pallas as pl
from jax.experimental.pallas import tpu as pltpu
from jax.sharding import PartitionSpec as P

MESH = pl.DeviceIdType.MESH
F32 = jnp.float32
BF16 = jnp.bfloat16

BLOCK = 16
WINDOW = 192
STRIDE = 176
TILE = 128
CUT = 368
SLOTS = 4
X_KIND = 14
RS_KIND = 24
KINDS = 40

PLAN = (
    ("r1", 8),
    ("r2", 10),
    ("a0", 0),
    ("a2", 1),
    ("cw", 7),
    ("aw", 7),
    ("m1", 3),
    ("b2", 4),
    ("b4", 5),
    ("r3", 12),
    ("a3", 2),
    ("r4", 14),
    ("sw", 14),
    ("a1", 0),
    ("tv", 1),
    ("gp", 3),
    ("rw", 10),
    ("m2", 6),
    ("gw", 7),
    ("b1", 3),
    ("b3", 4),
    ("b5", 5),
)


def kernel(
    a_hbm, vt_hbm, row_ref, col_ref, o_ref,
    a_ref, near, cg, cf, rc, v, vt, vtail, turned, ag, tg, c1, cx, xo, xn, sg, wq, w1, w2, ro1, rn1, ro2, rn2, lsem, tsend, trecv, send, recv,
):
    chunks = ag.shape[0]
    depth, width = a_ref.shape[1], v.shape[1]
    group, final = depth // 4, o_ref.shape[-1]
    row, col = lax.axis_index("row"), lax.axis_index("col")
    x, core = row // 2, row % 2
    z, y = col // 4, col % 4
    half = core * 128
    other = 128 - half

    def around(index):
        return {0: index, 1: lax.rem(index + 1, 4), 2: lax.rem(index + 2, 4), -1: lax.rem(index + 3, 4)}

    xs, ys, zs = around(x), around(y), around(z)
    at = {"z": zs, "y": ys}
    peer = {
        ("x", 1): (xs[1] * 2 + core, col),
        ("x", -1): (xs[-1] * 2 + core, col),
        ("y", 1): (row, z * 4 + ys[1]),
        ("y", -1): (row, z * 4 + ys[-1]),
        ("z", 1): (row, zs[1] * 4 + y),
        ("z", -1): (row, zs[-1] * 4 + y),
        ("y", 2): (row, z * 4 + ys[2]),
        ("z", 2): (row, zs[2] * 4 + y),
        "core": (x * 2 + 1 - core, col),
    }
    strips = {step: half + index * 32 for step, index in xs.items()}
    main = ag.shape[-1]
    gather = (("y", "z", pl.ds(0, main // 2)), ("z", "y", pl.ds(main // 2, main // 2)))
    scatter = (("z", "y"), ("y", "z"))

    barrier = pltpu.get_barrier_semaphore()
    for to in peer.values():
        pl.semaphore_signal(barrier, inc=1, device_id=to, device_id_type=MESH)

    def copy(c, kind, src, dst, to):
        return pltpu.make_async_remote_copy(
            src_ref=src, dst_ref=dst, send_sem=send.at[c, kind], recv_sem=recv.at[c, kind],
            device_id=to, device_id_type=MESH,
        )

    def arrived(c, kind, dst):
        copy(c, kind, dst, dst, peer["core"]).wait_recv()

    def sent(c, kind, src):
        copy(c, kind, src, src, peer["core"]).wait_send()

    def block(s, c, step):
        first, _, lanes = gather[s]
        f = at[first][step]
        return ag.at[c, z, f, :, lanes] if first == "y" else ag.at[c, f, y, :, lanes]

    def line(s, c, step, start=0, size=4):
        first, second, lanes = gather[s]
        g, part = at[second][step], pl.ds(start, size)
        return ag.at[c, g, part, :, lanes] if first == "y" else ag.at[c, part, g, :, lanes]

    def a_send(c, s, k, d=1):
        first, second, _ = gather[s]
        if k == 0:
            return block(s, c, 0), peer[first, 1]
        if k == 1:
            return block(s, c, 0), peer[first, -1]
        if k == 2:
            return block(s, c, -d), peer[first, d]
        if k == 3:
            return line(s, c, 0), peer[second, 1]
        if k == 4:
            return line(s, c, 0), peer[second, -1]
        if k == 5:
            return line(s, c, -1, 0, 2), peer[second, 1]
        return line(s, c, 1, 2, 2), peer[second, -1]

    def a_land(c, s, k):
        if k < 3:
            return block(s, c, (-1, 1, 2)[k])
        if k < 5:
            return line(s, c, (-1, 1)[k - 3])
        return line(s, c, 2, 2 * (k - 5), 2)

    def a_start(c, s, k, d=1):
        src, to = a_send(c, s, k, d)
        copy(c, s * 7 + k, src, src, to).start()

    def a_wait(c, s, k):
        arrived(c, s * 7 + k, a_land(c, s, k))

    def t_line(step, start=0, size=4):
        return tg.at[zs[step], pl.ds(start, size)]

    def t_send(k):
        return (
            (tg.at[z, y], peer["y", 1]),
            (tg.at[z, y], peer["y", -1]),
            (tg.at[z, y], peer["y", 2]),
            (t_line(0), peer["z", 1]),
            (t_line(0), peer["z", -1]),
            (t_line(-1, 0, 2), peer["z", 1]),
            (t_line(1, 2, 2), peer["z", -1]),
        )[k]

    def t_land(k):
        return (
            tg.at[z, ys[-1]], tg.at[z, ys[1]], tg.at[z, ys[2]],
            t_line(-1), t_line(1), t_line(2, 0, 2), t_line(2, 2, 2),
        )[k]

    def t_copy(k, src, to):
        return pltpu.make_async_remote_copy(
            src_ref=src, dst_ref=src, send_sem=tsend.at[k], recv_sem=trecv.at[k], device_id=to, device_id_type=MESH
        )

    def t_start(*kinds):
        for k in kinds:
            t_copy(k, *t_send(k)).start()

    def t_wait(*kinds):
        for k in kinds:
            t_copy(k, t_land(k), peer["core"]).wait_recv()

    def a0(c):
        ag[c, z, y] = a_ref[pl.ds(pl.multiple_of(c * BLOCK, BLOCK), BLOCK), :main]
        for s in range(2):
            a_start(c, s, 0)
            a_start(c, s, 1)

        @pl.when(c == 0)
        def _():
            for s in range(2):
                copy(c, s * 7 + 2, block(s, c, 0), block(s, c, 0), peer[gather[s][0], 2]).start()
            t_start(0, 1, 2)

    def a1(c):
        def forward(d):
            for s in range(2):
                a_wait(c, s, 0 if d == 1 else 1)
                a_start(c, s, 2, d)

        @pl.when(c == 0)
        def _():
            for s in range(2):
                a_wait(c, s, 0)

        pl.when(jnp.logical_and(c % 2 == 0, c > 0))(lambda: forward(1))
        pl.when(c % 2 == 1)(lambda: forward(-1))

    def a2(c):
        pl.when(c % 2 == 0)(lambda: [a_wait(c, s, 1) for s in range(2)] and None)
        pl.when(c % 2 == 1)(lambda: [a_wait(c, s, 0) for s in range(2)] and None)
        for s in range(2):
            a_wait(c, s, 2)
            a_start(c, s, 3)
            a_start(c, s, 4)

        @pl.when(c == 0)
        def _():
            t_wait(0, 1, 2)
            t_start(3, 4)

    def a3(c):
        for s in range(2):
            a_wait(c, s, 3)
            a_start(c, s, 5)
            a_wait(c, s, 4)
            a_start(c, s, 6)

        @pl.when(c == 0)
        def _():
            t_wait(3)
            t_start(5)
            t_wait(4)
            t_start(6)

    def m1(c):
        for s in range(2):
            a_wait(c, s, 5)
            a_wait(c, s, 6)
        pl.when(c == 0)(lambda: t_wait(5, 6))
        ends = tg[:, :, pl.ds(pl.multiple_of(c // 2 * BLOCK, BLOCK), BLOCK), :].reshape(16 * BLOCK, 128)
        mine = lax.broadcasted_iota(jnp.int32, (16 * BLOCK, 128), 1) // 64 == c % 2
        ends = jnp.where(mine, ends.astype(F32), 0.0).astype(BF16)
        rows = jnp.concatenate([ag[c].reshape(16 * BLOCK, main), ends], axis=1)
        middle = (width // 2 + 127) // 128 * 128
        last = (((1,), (1,)), ((), ()))
        for lo, hi in ((0, middle), (middle, width)):
            left = jnp.concatenate([vt[lo:hi, :main], vtail[lo:hi]], axis=1)
            part = lax.dot_general(left, rows, last, preferred_element_type=F32)
            c1[c % SLOTS, :, lo:hi] = part.astype(BF16).T
        x_start(c, 0)

    def piece(step, start=0, size=32):
        return pl.ds(pl.multiple_of(strips[step] + start, 16), size)

    def x_send(c, k):
        if k == 0:
            return c1.at[c % SLOTS, pl.ds(pl.multiple_of(other, 128), 128)], cx.at[c % SLOTS], peer["core"]
        if k == 9:
            src = sg.at[c % SLOTS, pl.ds(pl.multiple_of(half, 128), 128)]
            return src, src, peer["core"]
        d = 1 if k % 2 == 1 else -1
        part = pl.ds(8 - 8 * d, 16)
        if k < 3:
            return c1.at[c % SLOTS, piece(2, 8 - 8 * d, 16)], xo.at[c, part], peer["x", d]
        if k < 5:
            return c1.at[c % SLOTS, piece(d)], xn.at[c, (k - 3)], peer["x", d]
        src = sg.at[c % SLOTS, piece(0) if k < 7 else piece(-d, 8 - 8 * d, 16)]
        return src, src, peer["x", d]

    def x_land(c, k):
        if k < 5:
            return x_send(c, k)[1]
        if k == 9:
            return sg.at[c % SLOTS, pl.ds(pl.multiple_of(other, 128), 128)]
        d = 1 if k % 2 == 1 else -1
        return sg.at[c % SLOTS, piece(-d) if k < 7 else piece(2, 8 - 8 * d, 16)]

    def x_start(c, k):
        src, dst, to = x_send(c, k)
        copy(c, X_KIND + k, src, dst, to).start()

    def x_wait(c, k):
        arrived(c, X_KIND + k, x_land(c, k))

    def b1(c):
        x_wait(c, 0)
        rows = pl.ds(pl.multiple_of(half, 128), 128)
        c1[c % SLOTS, rows, :] = c1[c % SLOTS, rows, :] + cx[c % SLOTS]
        x_start(c, 1)
        x_start(c, 2)

    def b2(c):
        for k, step in ((1, 1), (2, -1)):
            x_wait(c, k)
            part, rows = pl.ds(16 * (k - 1), 16), piece(step, 16 * (k - 1), 16)
            c1[c % SLOTS, rows, :] = c1[c % SLOTS, rows, :] + xo[c, part]
            x_start(c, k + 2)

    def b3(c):
        gap = rc[pl.ds(core * 8 + x * 2, 2), c].reshape(32, 128)
        x_wait(c, 3)
        x_wait(c, 4)
        rows = piece(0)
        total = c1[c % SLOTS, rows, :].astype(F32) + xn[c, 0].astype(F32) + xn[c, 1].astype(F32)
        sg[c % SLOTS, rows, :] = (total / (gap[:, :1] + cg[0:1, :width])).astype(BF16)
        x_start(c, 5)
        x_start(c, 6)

    def b4(c):
        for k in (5, 6):
            x_wait(c, k)
            x_start(c, k + 2)

    def b5(c):
        x_wait(c, 7)
        x_wait(c, 8)
        x_start(c, 9)

    def r_move(c, s, k):
        first, second = scatter[s]
        fs, gs = at[first], at[second]
        d = 1 if k % 2 == 0 else -1
        if k < 2:
            part = pl.ds(0, CUT) if k == 0 else pl.ds(CUT, group - CUT)
            return w1.at[s, c % SLOTS, fs[2], part], ro1.at[s, c % SLOTS, part], peer[first, d]
        if k < 4:
            return w1.at[s, c % SLOTS, fs[d]], rn1.at[s, c % SLOTS, k - 2], peer[first, d]
        if k < 6:
            part = pl.ds((k - 4) * (WINDOW // 2), WINDOW // 2)
            return w2.at[s, c, gs[2], part], ro2.at[s, c, part], peer[second, d]
        return w2.at[s, c, gs[d]], rn2.at[s, c, k - 6], peer[second, d]

    def r_start(c, s, k):
        src, dst, to = r_move(c, s, k)
        copy(c, RS_KIND + s * 8 + k, src, dst, to).start()

    def far_copy(c, s):
        second = scatter[s][1]
        return copy(c, RS_KIND + s * 8 + 4, w2.at[s, c, at[second][2]], ro2.at[s, c], peer[second, 2])

    def r_wait(c, s, k):
        arrived(c, RS_KIND + s * 8 + k, r_move(c, s, k)[1])

    def m2(c):
        x_wait(c, 9)

        turned[...] = sg[c % SLOTS].T

        for g in range(2):
            both = jnp.dot(v[2 * g * group : 2 * (g + 1) * group, :], turned[...], preferred_element_type=F32)
            for q in (2 * g, 2 * g + 1):
                part = both[(q - 2 * g) * group : (q - 2 * g + 1) * group]
                w1[0, c % SLOTS, q] = part[:, :128].astype(BF16)
                for p in range(4):
                    wq[p, q * final : (q + 1) * final] = part[p * final : (p + 1) * final, 128:]
        for p in range(4):
            w1[1, c % SLOTS, p] = wq[p].astype(BF16)
        for s in range(2):
            r_start(c, s, 0)
            r_start(c, s, 1)

    def r1(c):
        o = c % SLOTS
        for s in range(2):
            r_wait(c, s, 0)
            r_wait(c, s, 1)
        for s in range(2):
            up, down = at[scatter[s][0]][1], at[scatter[s][0]][-1]
            w1[s, o, up, :CUT] = w1[s, o, up, :CUT] + ro1[s, o, :CUT]
            r_start(c, s, 2)
            w1[s, o, down, CUT:] = w1[s, o, down, CUT:] + ro1[s, o, CUT:]
            r_start(c, s, 3)

    def r2(c):
        o = c % SLOTS
        for s in range(2):
            f = at[scatter[s][0]][0]
            r_wait(c, s, 2)
            r_wait(c, s, 3)
            total = w1[s, o, f].astype(F32) + rn1[s, o, 0].astype(F32) + rn1[s, o, 1].astype(F32)
            total = total.astype(BF16)
            for p in range(4):
                w2[s, c, p] = total[p * STRIDE : p * STRIDE + WINDOW]

            @pl.when(c < chunks - 1)
            def _():
                r_start(c, s, 4)
                r_start(c, s, 5)

            @pl.when(c == chunks - 1)
            def _():
                far_copy(c, s).start()
                r_start(c, s, 6)
                r_start(c, s, 7)

    def r3(c):
        h = WINDOW // 2

        @pl.when(c < chunks - 1)
        def _():
            for s in range(2):
                up, down = at[scatter[s][1]][1], at[scatter[s][1]][-1]
                r_wait(c, s, 4)
                w2[s, c, up, :h] = w2[s, c, up, :h] + ro2[s, c, :h]
                r_start(c, s, 6)
                r_wait(c, s, 5)
                w2[s, c, down, h:] = w2[s, c, down, h:] + ro2[s, c, h:]
                r_start(c, s, 7)

    def r4(c):
        sums = []
        for s in range(2):
            g = at[scatter[s][1]][0]
            r_wait(c, s, 6)
            r_wait(c, s, 7)
            pl.when(c == chunks - 1)(lambda: far_copy(c, s).wait_recv())
            total = w2[s, c, g].astype(F32) + rn2[s, c, 0].astype(F32) + rn2[s, c, 1].astype(F32)
            total = total + jnp.where(c == chunks - 1, ro2[s, c].astype(F32), 0.0)
            sums.append(pltpu.roll(total, lax.rem(WINDOW - 4 * g, WINDOW), 0))
        total = jnp.concatenate(sums, axis=1)
        total = jnp.concatenate([total, jnp.zeros((256 - WINDOW, 256), F32)], axis=0)
        gap = rc[:, c].reshape(256, 128)
        gap = jnp.concatenate([gap, gap], axis=1) + cf[0:1, :]
        o_ref[:, c] = (total.T / gap).astype(BF16)[:, :final].reshape(16, BLOCK, final)

    def rw(c):
        for s in range(2):
            for k in range(4):
                sent(c, RS_KIND + s * 8 + k, r_move(c, s, k)[0])

    def gw(c):
        for k in range(5, 10):
            sent(c, X_KIND + k, x_send(c, k)[0])

    def cw(c):
        for k in range(5):
            sent(c, X_KIND + k, x_send(c, k)[0])

    def aw(c):
        @pl.when(c == 0)
        def _():
            for k in range(7):
                t_copy(k, t_send(k)[0], peer["core"]).wait_send()

        for s in range(2):
            for k in range(7):
                sent(c, s * 7 + k, a_send(c, s, k)[0])

    def sw(c):
        for s in range(2):
            for k in (6, 7):
                sent(c, RS_KIND + s * 8 + k, r_move(c, s, k)[0])

            @pl.when(c < chunks - 1)
            def _():
                for k in (4, 5):
                    sent(c, RS_KIND + s * 8 + k, r_move(c, s, k)[0])

            pl.when(c == chunks - 1)(lambda: far_copy(c, s).wait_send())

    load = pltpu.make_async_copy(vt_hbm, vt, lsem.at[0])
    entry = pltpu.make_async_copy(a_hbm, a_ref, lsem.at[1])
    tiles = width // TILE

    def tv(c):
        @pl.when(c == 0)
        def _():
            load.wait()
            ends = vt[:, main:]
            vtail[...] = jnp.concatenate([ends, ends], axis=1)

        def turn(i, carry):
            tile = pl.ds(pl.multiple_of(i * TILE, TILE), TILE)
            v[:, tile] = vt[tile, :].T
            return carry

        lax.fori_loop(2 * c, jnp.minimum(2 * c + 2, tiles), turn, 0)

        @pl.when(c == 5)
        def _():
            v[:, tiles * TILE :] = vt[tiles * TILE :, :].T

    entry.start()
    load.start()
    entry.wait()
    for k in range(0, chunks, 2):
        pair = [a_ref[i * BLOCK : (i + 1) * BLOCK, main:] for i in (k, k + 1) if i < chunks]
        if len(pair) == 1:
            pair.append(jnp.zeros_like(pair[0]))
        tg[z, y, k // 2 * BLOCK : (k // 2 + 1) * BLOCK, :] = jnp.concatenate(pair, axis=1)

    def gp(c):
        inner, outer = col * width, (row * 16 + col) * final
        inner_row = inner // 128
        outer_row = jnp.minimum(outer // 128, col_ref.shape[0] - 3)
        for k in range(12):
            near[:, 128 * k : 128 * (k + 1)] = col_ref[pl.ds(inner_row + k, 1), :]
        for k in range(3):
            near[:, 1536 + 128 * k : 1664 + 128 * k] = col_ref[pl.ds(outer_row + k, 1), :]
        cg[...] = pltpu.roll(jnp.broadcast_to(near[:, :1536], (8, 1536)), (1536 - (inner - inner_row * 128)) % 1536, 1)
        shifted = pltpu.roll(jnp.broadcast_to(near[:, 1536:], (8, 384)), (384 - (outer - outer_row * 128)) % 384, 1)
        cf[...] = shifted[:, :256]
        flat = rc.reshape(16 * chunks * BLOCK, 128)
        for k in range(row_ref.shape[0]):
            flat[k * 128 : (k + 1) * 128, :] = jnp.broadcast_to(row_ref[k : k + 1, :], (128, 128)).T

    pl.semaphore_wait(barrier, len(peer))

    ops = dict(tv=tv, aw=aw, cw=cw, gw=gw, rw=rw, gp=gp, a0=a0, a1=a1, a2=a2, a3=a3, m1=m1, b1=b1, b2=b2, b3=b3, b4=b4, b5=b5, m2=m2, r1=r1, r2=r2, r3=r3, r4=r4, sw=sw)

    def step(t, carry):
        for name, late in PLAN:
            c = t - late
            pl.when(jnp.logical_and(c >= 0, c < {"tv": 6, "gp": 1}.get(name, chunks)))(functools.partial(ops[name], c))
        return carry

    lax.fori_loop(0, chunks + max(late for _, late in PLAN), step, 0)


def on_device(amplitudes, integrals, row_gap, col_gap):
    rows, depth = amplitudes.shape
    width = integrals.shape[1]
    chunks = rows // BLOCK
    final = depth // 16

    vm = pl.BlockSpec(memory_space=pltpu.VMEM)
    anywhere = pl.BlockSpec(memory_space=pl.ANY)
    updated = pl.pallas_call(
        kernel,
        out_shape=jax.ShapeDtypeStruct((16, chunks, BLOCK, final), BF16),
        in_specs=[anywhere, anywhere, vm, vm],
        out_specs=vm,
        scratch_shapes=[
            pltpu.VMEM((rows, depth), BF16),
            pltpu.VMEM((1, 1920), F32),
            pltpu.VMEM((8, 1536), F32),
            pltpu.VMEM((8, 256), F32),
            pltpu.VMEM((16, chunks, BLOCK, 128), F32),
            pltpu.VMEM((depth, width), BF16),
            pltpu.VMEM((width, depth), BF16),
            pltpu.VMEM((width, 128), BF16),
            pltpu.VMEM((width, 256), BF16),
            pltpu.VMEM((chunks, 4, 4, BLOCK, depth // 128 * 128), BF16),
            pltpu.VMEM((4, 4, (chunks + 1) // 2 * BLOCK, 128), BF16),
            pltpu.VMEM((SLOTS, 256, width), BF16),
            pltpu.VMEM((SLOTS, 128, width), BF16),
            pltpu.VMEM((chunks, 32, width), BF16),
            pltpu.VMEM((chunks, 2, 32, width), BF16),
            pltpu.VMEM((SLOTS, 256, width), BF16),
            pltpu.VMEM((4, depth // 4, 128), F32),
            pltpu.VMEM((2, SLOTS, 4, depth // 4, 128), BF16),
            pltpu.VMEM((2, chunks, 4, WINDOW, 128), BF16),
            pltpu.VMEM((2, SLOTS, depth // 4, 128), BF16),
            pltpu.VMEM((2, SLOTS, 2, depth // 4, 128), BF16),
            pltpu.VMEM((2, chunks, WINDOW, 128), BF16),
            pltpu.VMEM((2, chunks, 2, WINDOW, 128), BF16),
            pltpu.SemaphoreType.DMA((2,)),
            pltpu.SemaphoreType.DMA((7,)),
            pltpu.SemaphoreType.DMA((7,)),
            pltpu.SemaphoreType.DMA((chunks, KINDS)),
            pltpu.SemaphoreType.DMA((chunks, KINDS)),
        ],
        compiler_params=pltpu.CompilerParams(
            collective_id=0, has_side_effects=True, vmem_limit_bytes=62 * 1024 * 1024
        ),
        cost_estimate=pl.CostEstimate(
            flops=4 * 16 * rows * depth * width, bytes_accessed=2 * depth * width, transcendentals=0
        ),
    )(amplitudes, integrals.T, row_gap.reshape(-1, 128), col_gap.reshape(-1, 128))
    return updated.reshape(16 * rows, final)


def solution(mesh):
    return jax.shard_map(
        on_device,
        mesh=mesh,
        in_specs=(P("col", "row"), P("row", "col"), P(), P()),
        out_specs=P(None, ("row", "col")),
        check_vma=False,
    )
```
